32 devices in a mesh: dp: 16 (over z, y, x), tensor: 2 (over core).
Axes of the slice: x: 2, y: 2, z: 4, core: 2. Of those that a mesh axis runs over, the one named last changes fastest.
Arguments:
- tokens: bfloat16 [16384, 1280], P('dp'), may hold values from -6 to 6
- cotangent: bfloat16 [16384, 1280], P('dp'), may hold values from -6 to 6
- segment_ids: int32 [32, 512], P('dp'), may hold values from 0 to 7, never falling along the last dimension, each value on 1 to 256 neighbouring positions
- pad_mask: int32 [32, 512], P('dp'), may hold values 0 or 1
- inward_master: float32 [3, 1280, 1280], P(None, 'dp', 'tensor'), may hold values from -8 to 8
- inward_first: bfloat16 [3, 1280, 1280], P(None, 'dp', 'tensor'), may hold values from -3 to 3
- inward_second: float32 [3, 1280, 1280], P(None, 'dp', 'tensor'), may hold values from 0.16384 to 0.65536
- outward_master: float32 [1280, 1280], P('tensor', 'dp'), may hold values from -8 to 8
- outward_first: bfloat16 [1280, 1280], P('tensor', 'dp'), may hold values from -3 to 3
- outward_second: float32 [1280, 1280], P('tensor', 'dp'), may hold values from 0.16384 to 0.65536
- expand_master: float32 [2, 1280, 5120], P(None, 'dp', 'tensor'), may hold values from -8 to 8
- expand_first: bfloat16 [2, 1280, 5120], P(None, 'dp', 'tensor'), may hold values from -1 to 1
- expand_second: float32 [2, 1280, 5120], P(None, 'dp', 'tensor'), may hold values from 0.0262144 to 0.1048576
- shrink_master: float32 [5120, 1280], P('tensor', 'dp'), may hold values from -8 to 8
- shrink_first: bfloat16 [5120, 1280], P('tensor', 'dp'), may hold values from -1 to 1
- shrink_second: float32 [5120, 1280], P('tensor', 'dp'), may hold values from 0.0262144 to 0.1048576
- alpha_master: float32 [2, 1280], P(None, 'dp'), may hold values from 0.15 to 0.6
- alpha_first: bfloat16 [2, 1280], P(None, 'dp'), may hold values from -160 to 160
- alpha_second: float32 [2, 1280], P(None, 'dp'), may hold values from 3276.8 to 13107.2
- scale_master: float32 [9, 1280], P(None, 'dp'), may hold values from 0.4 to 1.6
- scale_first: bfloat16 [9, 1280], P(None, 'dp'), may hold values from -24 to 24
- scale_second: float32 [9, 1280], P(None, 'dp'), may hold values from 81.92 to 327.68
Outputs:
- block_output: bfloat16 [16384, 1280], P('dp')
- input_grad: float32 [16384, 1280], P('dp', 'tensor')
- inward_gradient: float32 [3, 1280, 1280], P(None, 'dp', 'tensor')
- inward_variance: float32 [3, 1280, 1280], P(None, 'dp', 'tensor')
- inward_updated: float32 [3, 1280, 1280], P(None, 'dp', 'tensor')
- outward_gradient: float32 [1280, 1280], P('tensor', 'dp')
- outward_variance: float32 [1280, 1280], P('tensor', 'dp')
- outward_updated: float32 [1280, 1280], P('tensor', 'dp')
- expand_gradient: float32 [2, 1280, 5120], P(None, 'dp', 'tensor')
- expand_variance: float32 [2, 1280, 5120], P(None, 'dp', 'tensor')
- expand_updated: float32 [2, 1280, 5120], P(None, 'dp', 'tensor')
- shrink_gradient: float32 [5120, 1280], P('tensor', 'dp')
- shrink_variance: float32 [5120, 1280], P('tensor', 'dp')
- shrink_updated: float32 [5120, 1280], P('tensor', 'dp')
- alpha_gradient: float32 [2, 1280], P(None, 'dp')
- alpha_variance: float32 [2, 1280], P(None, 'dp')
- alpha_updated: float32 [2, 1280], P(None, 'dp')
- scale_gradient: float32 [9, 1280], P(None, 'dp')
- scale_variance: float32 [9, 1280], P(None, 'dp')
- scale_updated: float32 [9, 1280], P(None, 'dp')
The draws below stay inside these ranges and needn't reach their ends.
All inputs are finite; a program needn't handle non-finite values. No bound on the sum of `pad_mask` on one device may be relied on, other than what follows from the above.
Results may differ from the reference program's by a relative error of at most 0.015.
The reference program's roundings to bfloat16 on the way count: a program that leaves them out, or rounds other values in their place, can miss the bound.
Values may be sent and summed in bfloat16 or wider, within the bound.
A program may use at most 256 MiB of HBM per device.

```python
import math
import jax
import jax.numpy as jnp
import numpy as np
from jax import lax

D = 1280
HEADS = 20
HD = 64
FF = 5120
SEQ = 512
DOCS = 8
STEP = 10
SEQS = 32
TOKENS = 16384
NSC = 9


def ramp_scale(array_shape, axis, low_end, high_end):
    length = array_shape[axis]
    ramp_shape = [1] * len(array_shape)
    ramp_shape[axis] = length
    fraction = jnp.arange(length, dtype=jnp.float32).reshape(ramp_shape) / (length - 1)
    return low_end + (high_end - low_end) * fraction


def draw_inward_master(key, part):
    key = jax.random.fold_in(key, 11)
    array_shape = (3, D, HEADS * HD)
    return jnp.clip(jax.random.normal(key, array_shape, jnp.float32), -4.0, 4.0) * ramp_scale(array_shape, 1, 0.6, 1.8)


def draw_outward_master(key, part):
    key = jax.random.fold_in(key, 12)
    array_shape = (HEADS * HD, D)
    return jnp.clip(jax.random.normal(key, array_shape, jnp.float32), -4.0, 4.0) * ramp_scale(array_shape, 1, 0.6, 1.8)


def draw_expand_master(key, part):
    key = jax.random.fold_in(key, 13)
    array_shape = (2, D, FF)
    return jnp.clip(jax.random.normal(key, array_shape, jnp.float32), -4.0, 4.0) * ramp_scale(array_shape, 1, 0.6, 1.8)


def draw_shrink_master(key, part):
    key = jax.random.fold_in(key, 14)
    array_shape = (FF, D)
    return jnp.clip(jax.random.normal(key, array_shape, jnp.float32), -4.0, 4.0) * ramp_scale(array_shape, 1, 0.6, 1.8)


def with_ends(entries, key, low, largest):
    extent = entries.shape
    index_at = [jax.random.randint(jax.random.fold_in(key, axis), (), 0, extent[axis]) for axis in range(len(extent))]
    entries = entries.at[tuple(index_at)].set(low)
    longest = extent.index(max(extent))
    index_at[longest] = (index_at[longest] + 1) % extent[longest]
    return entries.at[tuple(index_at)].set(largest)


def level_of(stream_key, extent, shards, smallest, largest):
    def one(axis_at, shards_of):
        draws = jax.random.uniform(jax.random.fold_in(jax.random.fold_in(stream_key, 6), axis_at), (shards_of,), jnp.float32, smallest / len(shards), largest / len(shards))
        return jnp.repeat(jnp.exp(draws), extent[axis_at] // shards_of).reshape((-1,) + (1,) * (len(extent) - axis_at - 1))

    factor_of = one(*shards[0])
    for cut in shards[1:]:
        factor_of = factor_of * one(*cut)
    return factor_of


def split_up(count, total, limit, skew):
    loads = [(1 << 20) // math.isqrt(standing ** skew) + 1 for standing in range(2, count + 1)]
    rest, given = total - limit - (count - 1), [1] * (count - 1)
    while rest > 0:
        movable = [i for i in range(count - 1) if given[i] < limit]
        mass, remaining = sum([loads[i] for i in movable]), rest
        for i in movable:
            addition = min(limit - given[i], max(1, remaining * loads[i] // mass), rest)
            given[i] = given[i] + addition
            rest = rest - addition
    return np.array([limit] + given)


def uneven(rng, amount, total, bound, lean):
    if amount == 2:
        one = jax.random.randint(rng, (), max(1, total - bound), min(bound, total - 1) + 1)
        return jnp.stack([one, total - one])
    tallies = jnp.asarray(split_up(amount, total, bound, lean), jnp.int32)
    twos = (amount - 1) // 2
    source_of, receiver = tallies[1:1 + 2 * twos:2], tallies[2:2 + 2 * twos:2]
    slack = jnp.minimum(source_of - 1, bound - receiver)
    passed = jax.random.randint(jax.random.fold_in(rng, 1), (twos,), 0, 1 << 20) % (slack + 1)
    tallies = tallies.at[1:1 + 2 * twos:2].set(source_of - passed).at[2:2 + 2 * twos:2].set(receiver + passed)
    return tallies[jax.random.permutation(jax.random.fold_in(rng, 2), amount)]


def scatter_about(rng, dims, deviation, limit, split=(), kind=jnp.bfloat16):
    array = jax.random.normal(rng, dims, jnp.float32) * deviation
    if len(split) > 0:
        array = level_of(rng, dims, split, -0.22, 0.18) * array
    return jnp.clip(array, min=-limit, max=limit).astype(kind)


def setup_inputs(seed: int = 0) -> dict:
    seeds = jax.random.split(jax.random.key(seed), 23)
    return {
        "tokens": scatter_about(seeds[0], (TOKENS, D), 1.0, 6.0, ((0, 16),)),
        "cotangent": scatter_about(seeds[1], (TOKENS, D), 1.0, 6.0, ((0, 16),)),
        "segment_ids": jax.vmap(lambda own: jnp.searchsorted(jnp.cumsum(uneven(own, DOCS, SEQ, SEQ // 2, 2)), jnp.arange(SEQ), side="right"))(jax.random.split(seeds[2], SEQS)).reshape((SEQS, SEQ)).astype(jnp.int32),
        "pad_mask": with_ends((jax.random.randint(seeds[3], (SEQS, SEQ), 0, 8) < 1).astype(jnp.int32), jax.random.fold_in(seeds[3], 1), 0, 1),
        "inward_master": draw_inward_master(jax.random.fold_in(seeds[22], 71), 0),
        "inward_first": scatter_about(seeds[5], (3, D, HEADS * HD), (0.0015 * TOKENS ** 0.5), 3.0, ((1, 16), (2, 2))),
        "inward_second": jnp.clip(jnp.exp(math.log(0.65536) - 1.3862944 * jax.random.uniform(seeds[6], (3, D, HEADS * HD), jnp.float32) ** level_of(seeds[6], (3, D, HEADS * HD), ((1, 16), (2, 2)), -0.2, 0.2)), 0.16384, 0.65536),
        "outward_master": draw_outward_master(jax.random.fold_in(seeds[22], 71), 0),
        "outward_first": scatter_about(seeds[8], (HEADS * HD, D), (0.0015 * TOKENS ** 0.5), 3.0, ((0, 2), (1, 16))),
        "outward_second": jnp.clip(jnp.exp(math.log(0.65536) - 1.3862944 * jax.random.uniform(seeds[9], (HEADS * HD, D), jnp.float32) ** level_of(seeds[9], (HEADS * HD, D), ((0, 2), (1, 16)), -0.2, 0.2)), 0.16384, 0.65536),
        "expand_master": draw_expand_master(jax.random.fold_in(seeds[22], 71), 0),
        "expand_first": scatter_about(seeds[11], (2, D, FF), (0.0006 * TOKENS ** 0.5), 1.0, ((1, 16), (2, 2))),
        "expand_second": jnp.clip(jnp.exp(math.log(0.1048576) - 1.3862944 * jax.random.uniform(seeds[12], (2, D, FF), jnp.float32) ** level_of(seeds[12], (2, D, FF), ((1, 16), (2, 2)), -0.2, 0.2)), 0.0262144, 0.1048576),
        "shrink_master": draw_shrink_master(jax.random.fold_in(seeds[22], 71), 0),
        "shrink_first": scatter_about(seeds[14], (FF, D), (0.0006 * TOKENS ** 0.5), 1.0, ((0, 2), (1, 16))),
        "shrink_second": jnp.clip(jnp.exp(math.log(0.1048576) - 1.3862944 * jax.random.uniform(seeds[15], (FF, D), jnp.float32) ** level_of(seeds[15], (FF, D), ((0, 2), (1, 16)), -0.2, 0.2)), 0.0262144, 0.1048576),
        "alpha_master": jnp.clip(jnp.exp(math.log(0.6) - 1.3862944 * jax.random.uniform(seeds[16], (2, D), jnp.float32) ** level_of(seeds[16], (2, D), ((1, 16),), -0.2, 0.2)), 0.15, 0.6),
        "alpha_first": scatter_about(seeds[17], (2, D), (0.22 * TOKENS ** 0.5), 160.0, ((1, 16),)),
        "alpha_second": jnp.clip(jnp.exp(math.log(13107.2) - 1.3862944 * jax.random.uniform(seeds[18], (2, D), jnp.float32) ** level_of(seeds[18], (2, D), ((1, 16),), -0.2, 0.2)), 3276.8, 13107.2),
        "scale_master": jnp.clip(1.0 + 0.12 * jax.random.normal(seeds[19], (NSC, D), jnp.float32), 0.4, 1.6),
        "scale_first": scatter_about(seeds[20], (NSC, D), (0.033 * TOKENS ** 0.5), 24.0, ((1, 16),)),
        "scale_second": jnp.clip(jnp.exp(math.log(327.68) - 1.3862944 * jax.random.uniform(seeds[21], (NSC, D), jnp.float32) ** level_of(seeds[21], (NSC, D), ((1, 16),), -0.2, 0.2)), 81.92, 327.68),
    }


EPS_NORM = 1e-06
BETA_ONE = 0.9
BETA_TWO = 0.95
ADAM_EPS = 1e-08
RATE_MATRIX = 0.3
RATE_ALPHA = 0.08
RATE_SCALE = 0.25
MASKED = -1e+30
HIGHEST = lax.Precision.HIGHEST

@jax.custom_vjp
def low(v):
    return lax.optimization_barrier(v.astype(jnp.bfloat16)).astype(jnp.float32)

@jax.custom_vjp
def low_back(v):
    return v

def low_keep(v):
    return (low(v), None)

def low_pass(kept, grad):
    return (grad,)

def back_keep(v):
    return (v, None)

def back_low(kept, grad):
    return (low(grad),)
low.defvjp(low_keep, low_pass)
low_back.defvjp(back_keep, back_low)

def row_norm(values):
    return values * lax.rsqrt(lax.optimization_barrier(jnp.mean(values * values, axis=-1, keepdims=True)) + EPS_NORM)

def unit_scaled(values, gains):
    return gains * values * lax.rsqrt(lax.optimization_barrier(jnp.sum(values * values, axis=-1, keepdims=True)) + EPS_NORM)

def allowed_mask(segment_row, pad_row):
    positions = jnp.arange(segment_row.shape[0])
    same_doc = segment_row[:, None] == segment_row[None, :]
    earlier = positions[None, :] <= positions[:, None]
    live_key = pad_row[None, :] == 0
    return same_doc & earlier & live_key | (positions[:, None] == positions[None, :])

def block(inputs, w_inward, w_outward, w_expand, w_shrink, alphas, scale_rows, allowed):
    row_count = inputs.shape[0]
    inv_root = D ** (-0.5)
    raw_proj = low_back(jnp.einsum('rd,jdc->jrc', inputs, w_inward, precision=HIGHEST) * inv_root)
    split_heads = raw_proj.reshape(3, row_count, HEADS, HD)
    query_gain = scale_rows[0].reshape(HEADS, HD)
    queries = low(unit_scaled(split_heads[0], query_gain))
    keys_low = low(unit_scaled(split_heads[1], query_gain))
    values_low = low(split_heads[2])
    scores = jnp.einsum('qhe,khe->hqk', queries, keys_low, precision=HIGHEST) * HD ** 0.5
    scores = low_back(jnp.where(allowed[None], scores, MASKED))
    probs = low(jax.nn.softmax(scores, axis=-1))
    mixed = jnp.einsum('hqk,khe->qhe', probs, values_low, precision=HIGHEST)
    mixed = low_back(low(mixed)).reshape(row_count, HEADS * HD)
    branch = low_back(jnp.dot(mixed, w_outward, precision=HIGHEST))
    h_attn = row_norm(branch)
    first = row_norm(inputs + alphas[0] * (h_attn - inputs))
    first_low = low(first)
    expand_proj = low_back(jnp.einsum('rd,jdf->jrf', first_low, w_expand, precision=HIGHEST) * inv_root)
    ratio_rows = FF // D
    gain_up = scale_rows[1:1 + ratio_rows].reshape(FF)
    gain_gate = scale_rows[1 + ratio_rows:].reshape(FF)
    up_branch = gain_up * expand_proj[0]
    gate_branch = gain_gate * expand_proj[1]
    hidden = low(up_branch * jax.nn.silu(gate_branch))
    shrunk = low_back(jnp.dot(hidden, w_shrink, precision=HIGHEST))
    h_mlp = row_norm(shrunk)
    return row_norm(first + alphas[1] * (h_mlp - first))

def adam_step(master, first_moment, second_moment, gradient, rate):
    first_new = BETA_ONE * first_moment.astype(jnp.float32) + (1.0 - BETA_ONE) * gradient
    second_new = BETA_TWO * second_moment + (1.0 - BETA_TWO) * gradient * gradient
    ratio = first_new / (1.0 - BETA_ONE ** STEP) / (jnp.sqrt(second_new / (1.0 - BETA_TWO ** STEP)) + ADAM_EPS)
    return (master - rate * ratio, second_new)

def renormed(matrix, axis):
    return matrix * lax.rsqrt(lax.optimization_barrier(jnp.mean(matrix * matrix, axis=axis, keepdims=True)) + EPS_NORM)

def reference(tokens, cotangent, segment_ids, pad_mask, inward_master, inward_first, inward_second, outward_master, outward_first, outward_second, expand_master, expand_first, expand_second, shrink_master, shrink_first, shrink_second, alpha_master, alpha_first, alpha_second, scale_master, scale_first, scale_second):
    masters = (inward_master, outward_master, expand_master, shrink_master, alpha_master, scale_master)
    copies = tuple((master.astype(jnp.bfloat16).astype(jnp.float32) for master in masters))
    seq_count = segment_ids.shape[0]
    inputs_all = tokens.astype(jnp.float32).reshape(seq_count, SEQ, D)
    cot_all = cotangent.astype(jnp.float32).reshape(seq_count, SEQ, D)

    def per_sequence(carry, item):
        inputs, cot_rows, segment_row, pad_row = item
        allowed = allowed_mask(segment_row, pad_row)
        output, pullback = jax.vjp(lambda inputs_in, *weights: block(inputs_in, *weights, allowed), inputs, *copies)
        keep_rows = (1 - pad_row).astype(jnp.float32)[:, None]
        grads_all = pullback(cot_rows * keep_rows)
        carry = tuple((accum_sum + new_part for accum_sum, new_part in zip(carry, grads_all[1:])))
        return (carry, (output.astype(jnp.bfloat16), grads_all[0]))
    zero_grads = tuple((jnp.zeros_like(weight_copy) for weight_copy in copies))
    sums, (outputs, input_grads) = lax.scan(per_sequence, zero_grads, (inputs_all, cot_all, segment_ids, pad_mask))
    inward_g, outward_g, expand_g, shrink_g, alpha_g, scale_g = sums
    inward_pre, inward_var = adam_step(inward_master, inward_first, inward_second, inward_g, RATE_MATRIX)
    outward_pre, outward_var = adam_step(outward_master, outward_first, outward_second, outward_g, RATE_MATRIX)
    expand_pre, expand_var = adam_step(expand_master, expand_first, expand_second, expand_g, RATE_MATRIX)
    shrink_pre, shrink_var = adam_step(shrink_master, shrink_first, shrink_second, shrink_g, RATE_MATRIX)
    alpha_new, alpha_var = adam_step(alpha_master, alpha_first, alpha_second, alpha_g, RATE_ALPHA)
    scale_new, scale_var = adam_step(scale_master, scale_first, scale_second, scale_g, RATE_SCALE)
    return (outputs.reshape(seq_count * SEQ, D), input_grads.reshape(seq_count * SEQ, D), inward_g, inward_var, renormed(inward_pre, 1), outward_g, outward_var, renormed(outward_pre, 1), expand_g, expand_var, renormed(expand_pre, 1), shrink_g, shrink_var, renormed(shrink_pre, 1), alpha_g, alpha_var, alpha_new, scale_g, scale_var, scale_new)
```

```python
import functools

import jax
import jax.numpy as jnp
from jax import lax
from jax.experimental import pallas as pl
from jax.experimental.pallas import tpu as pltpu
from jax.sharding import PartitionSpec as P

D = 1280
HEADS = 20
HD = 64
FF = 5120
STEP = 10
LONGEST = 256


EPS_NORM = 1e-06
BETA_ONE = 0.9
BETA_TWO = 0.95
ADAM_EPS = 1e-08
RATE_MATRIX = 0.3
RATE_ALPHA = 0.08
RATE_SCALE = 0.25
MASKED = -1e30
F32 = jnp.float32
BF16 = jnp.bfloat16


def row_norm(values):
    factor = lax.rsqrt(jnp.mean(values * values, axis=-1, keepdims=True) + EPS_NORM)
    return (values * factor, factor)


def row_norm_back(upstream, normed, factor):
    return factor * (upstream - normed * jnp.mean(upstream * normed, axis=-1, keepdims=True))


def adam_step(master, first_moment, second_moment, gradient, rate):
    first_new = BETA_ONE * first_moment.astype(F32) + (1.0 - BETA_ONE) * gradient
    second_new = BETA_TWO * second_moment + (1.0 - BETA_TWO) * gradient * gradient
    ratio = (
        first_new
        / (1.0 - BETA_ONE**STEP)
        / (jnp.sqrt(second_new / (1.0 - BETA_TWO**STEP)) + ADAM_EPS)
    )
    return (master - rate * ratio, second_new)


LANES = 128
PLACES = (2, 1, 4, 8)
ROUTES = ((3, 2, 1, 0), (3, 2, 0, 1), (1, 0, 3, 2), (0, 1, 3, 2))
EVERY = 4
LAG = 2
RING = 4


def partner_of(me, bit):
    return me + bit - 2 * bit * ((me // bit) % 2)


def greet(me):
    barrier = pltpu.get_barrier_semaphore()
    for bit in PLACES:
        pl.semaphore_signal(
            barrier,
            inc=1,
            device_id={"dp": partner_of(me, bit)},
            device_id_type=pl.DeviceIdType.MESH,
        )
    pl.semaphore_wait(barrier, len(PLACES))


def tile_plan(columns):
    tiles = columns // LANES
    rare = tiles // 10
    often = (tiles - 2 * rare) // 2
    return (
        (0, 2, often, 1),
        (1, 2, often, 1),
        (2 * often, 1, rare, EVERY),
        (2 * often + rare, 1, rare, EVERY),
    )


def for_tiles(step, hop, plan, body):
    for route, (_, _, number, every) in enumerate(plan):
        if number == 0:
            continue
        at = step - hop * LAG
        due = (at >= 0) & (at < number * every)
        if every > 1:
            due = due & (at % every == 0)

        @pl.when(due)
        def _():
            body(route, at // every)


def lanes_of(plan, route, tile):
    first, stride, _, _ = plan[route]
    return pl.ds(pl.multiple_of((first + stride * tile) * LANES, LANES), LANES)


def steps_of(plan, hops):
    return max((number - 1) * every + 1 for _, _, number, every in plan if number) + hops * LAG


def gather_kernel(plan, block, out, own_sem, send_sem, recv_sem):
    me = lax.axis_index("dp")
    own = pltpu.make_async_copy(block, out.at[0, 0, 0, 0], own_sem)
    own.start()
    greet(me)

    def piece(hop, route, tile):
        lanes = lanes_of(plan, route, tile)
        crossed, place = ROUTES[route][:hop], ROUTES[route][hop]
        source = [slice(None) if axis in crossed else 0 for axis in range(4)]
        target = [1 if axis == place else source[axis] for axis in range(4)]
        if hop == 0:
            source_ref = block.at[:, lanes]
        else:
            source_ref = out.at[(*source, slice(None), lanes)]
        return pltpu.make_async_remote_copy(
            src_ref=source_ref,
            dst_ref=out.at[(*target, slice(None), lanes)],
            send_sem=send_sem.at[hop, route, tile % RING],
            recv_sem=recv_sem.at[hop, route, tile],
            device_id={"dp": partner_of(me, PLACES[place])},
            device_id_type=pl.DeviceIdType.MESH,
        )

    def step(index, _):
        for hop in range(5):

            def body(route, tile, hop=hop):
                if hop > 0:
                    piece(hop - 1, route, tile).wait_recv()
                if hop < 4:

                    @pl.when(tile >= RING)
                    def _():
                        piece(hop, route, tile - RING).wait_send()

                    piece(hop, route, tile).start()

            for_tiles(index, hop, plan, body)
        return 0

    lax.fori_loop(0, LAG, step, 0)
    own.wait()
    lax.fori_loop(LAG, steps_of(plan, 4), step, 0)
    for route, (_, _, number, _) in enumerate(plan):
        for tile in range(max(0, number - RING), number):
            for hop in range(4):
                piece(hop, route, tile).wait_send()


def gather_columns(block, collective_id):
    rows, columns = block.shape
    plan = tile_plan(columns)
    most = max(number for _, _, number, _ in plan)
    out = pl.pallas_call(
        functools.partial(gather_kernel, plan),
        out_shape=jax.ShapeDtypeStruct((2, 2, 2, 2, rows, columns), BF16),
        in_specs=[pl.BlockSpec(memory_space=pltpu.VMEM)],
        out_specs=pl.BlockSpec(memory_space=pl.ANY),
        scratch_shapes=[
            pltpu.SemaphoreType.DMA,
            pltpu.SemaphoreType.DMA((4, 4, RING)),
            pltpu.SemaphoreType.DMA((4, 4, most)),
        ],
        compiler_params=pltpu.CompilerParams(
            collective_id=collective_id, has_side_effects=True, vmem_limit_bytes=16 << 20
        ),
        name="gather_columns",
    )(block)
    return out.reshape(16 * rows, columns)


def sum_kernel(plan, left_of, scale, left, right, out, work, arrived, send_sem, recv_sem):
    me = lax.axis_index("dp")
    greet(me)
    rows = out.shape[0]

    def piece(hop, route, tile):
        place = ROUTES[route][3 - hop]
        slot = tile % RING
        return pltpu.make_async_remote_copy(
            src_ref=work[hop].at[route, slot, 1],
            dst_ref=arrived[hop].at[route, tile],
            send_sem=send_sem.at[hop, route, slot],
            recv_sem=recv_sem.at[hop, route, tile],
            device_id={"dp": partner_of(me, PLACES[place])},
            device_id_type=pl.DeviceIdType.MESH,
        )

    def send(hop, route, tile, fill):
        @pl.when(tile >= RING)
        def _():
            piece(hop, route, tile - RING).wait_send()

        fill(work[hop].at[route, tile % RING])
        piece(hop, route, tile).start()

    def product(route, tile):
        part = (
            lax.dot_general(
                left[left_of(route, tile)],
                right[:, lanes_of(plan, route, tile)],
                (((1,), (0,)), ((), ())),
                preferred_element_type=F32,
            )
            * scale
        ).astype(BF16)

        def fill(slot):
            axes = ROUTES[route][::-1]
            for block in range(16):
                bits = [(block >> (3 - axis)) & 1 for axis in axes]
                index = bits[1] * 4 + bits[2] * 2 + bits[3]
                slot[bits[0], index * rows : (index + 1) * rows, :] = part[
                    block * rows : (block + 1) * rows
                ]

        send(0, route, tile, fill)

    def add(hop, route, tile):
        piece(hop - 1, route, tile).wait_recv()
        kept = work[hop - 1][route, tile % RING, 0].astype(F32)
        total = kept + arrived[hop - 1][route, tile].astype(F32)
        if hop == 4:
            out[:, lanes_of(plan, route, tile)] = total
            return
        half = total.shape[0] // 2

        def fill(slot):
            slot[0] = total[:half].astype(BF16)
            slot[1] = total[half:].astype(BF16)

        send(hop, route, tile, fill)

    def step(index, _):
        for hop in range(4, 0, -1):
            for_tiles(index, hop, plan, functools.partial(add, hop))
        for_tiles(index, 0, plan, product)
        return 0

    lax.fori_loop(0, steps_of(plan, 4), step, 0)
    for route, (_, _, number, _) in enumerate(plan):
        for tile in range(max(0, number - RING), number):
            for hop in range(4):
                piece(hop, route, tile).wait_send()


def sum_products(left, right, left_of, scale, collective_id):
    rows = left.shape[1] // 16
    columns = right.shape[1]
    plan = tile_plan(columns)
    most = max(number for _, _, number, _ in plan)
    halves = [rows * 8 >> hop for hop in range(4)]
    return pl.pallas_call(
        functools.partial(sum_kernel, plan, left_of, scale),
        out_shape=jax.ShapeDtypeStruct((rows, columns), F32),
        in_specs=[pl.BlockSpec(memory_space=pltpu.VMEM)] * 2,
        out_specs=pl.BlockSpec(memory_space=pltpu.VMEM),
        scratch_shapes=[
            [pltpu.VMEM((4, RING, 2, half, LANES), BF16) for half in halves],
            [pltpu.VMEM((4, most, half, LANES), BF16) for half in halves],
            pltpu.SemaphoreType.DMA((4, 4, RING)),
            pltpu.SemaphoreType.DMA((4, 4, most)),
        ],
        compiler_params=pltpu.CompilerParams(
            collective_id=collective_id, has_side_effects=True, vmem_limit_bytes=56 << 20
        ),
        name="sum_products",
    )(left, right)


def extra_bits(count):
    return [bit for bit in (1 << k for k in range(4, count.bit_length() - 1))]


def exchange(array, bit, count):
    return lax.ppermute(array, "dp", [(i, i ^ bit) for i in range(count)])


def swap_cores(array):
    return lax.ppermute(array, "tensor", [(0, 1), (1, 0)])


def gather(block, count, collective_id):
    for bit in extra_bits(count)[::-1]:
        block = jnp.concatenate([block, exchange(block, bit, count)], axis=0)
    return gather_columns(block, collective_id)


def scatter_rest(partial, count):
    for bit in extra_bits(count):
        half = partial.shape[0] // 2
        partial = partial[:half] + exchange(partial[half:], bit, count)
    return partial


def butterfly_sum(array, count):
    for bit in list(PLACES) + extra_bits(count):
        array = array + exchange(array, bit, count)
    return array


def scatter_sum(partial, count):
    for bit in PLACES:
        half = partial.shape[0] // 2
        partial = partial[:half] + exchange(partial[half:], bit, count)
    return scatter_rest(partial, count)


def place_matrix(me, count):
    places = list(PLACES) + extra_bits(count)
    width = D // count
    natural = lax.broadcasted_iota(jnp.int32, (D, D), 0)
    placed = lax.broadcasted_iota(jnp.int32, (D, D), 1)
    position, offset = placed // width, placed % width
    relative = jnp.zeros_like(position)
    for axis, bit in enumerate(places):
        value = (position >> (len(places) - 1 - axis)) & 1
        relative = relative + value * bit
    return (natural == (relative ^ me) * width + offset).astype(BF16)


def nn(a, b):
    return lax.dot_general(a, b, (((1,), (0,)), ((), ())), preferred_element_type=F32)


def nt(a, b):
    return lax.dot_general(a, b, (((1,), (1,)), ((), ())), preferred_element_type=F32)


def tn(a, b):
    return lax.dot_general(a, b, (((0,), (0,)), ((), ())), preferred_element_type=F32)


def head_factors(raw, low_lanes):
    squares = raw * raw
    low = jnp.sum(jnp.where(low_lanes, squares, 0.0), axis=-1, keepdims=True)
    high = jnp.sum(jnp.where(low_lanes, 0.0, squares), axis=-1, keepdims=True)
    return jnp.where(low_lanes, lax.rsqrt(low + EPS_NORM), lax.rsqrt(high + EPS_NORM))


def head_sums(values, low_lanes):
    low = jnp.sum(jnp.where(low_lanes, values, 0.0), axis=-1, keepdims=True)
    high = jnp.sum(jnp.where(low_lanes, 0.0, values), axis=-1, keepdims=True)
    return jnp.where(low_lanes, low, high)


Q_TILE = 128


def key_range(tile):
    start = max(0, tile * Q_TILE - LONGEST)
    return start, (tile + 1) * Q_TILE


def attend_kernel(raw_q, raw_k, raw_v, gain, bias, mixed):
    length = raw_q.shape[0]
    low_lanes = lax.broadcasted_iota(jnp.int32, (1, 2 * HD), 1) < HD
    query = raw_q[...]
    key = raw_k[...]
    query = (gain[...] * (query * head_factors(query, low_lanes))).astype(BF16) * 8
    key = (gain[...] * (key * head_factors(key, low_lanes))).astype(BF16)
    value = raw_v[...].astype(BF16)
    zero = jnp.zeros_like(query)
    parts = (jnp.where(low_lanes, query, zero), jnp.where(low_lanes, zero, query))
    for tile in range(length // Q_TILE):
        start, end = key_range(tile)
        rows = slice(tile * Q_TILE, (tile + 1) * Q_TILE)
        tile_bias = bias[0, rows, start:end]
        results = []
        for part in parts:
            expo = jnp.exp(nt(part[rows], key[start:end]) + tile_bias)
            total = jnp.sum(expo, axis=-1, keepdims=True)
            results.append(nn(expo.astype(BF16), value[start:end]) * (1.0 / total))
        mixed[rows, :] = jnp.where(low_lanes, results[0], results[1]).astype(BF16)


def attend_back_kernel(
    raw_q, raw_k, raw_v, d_mixed, gain, bias, d_raw_q, d_raw_k, d_raw_v, gain_grad, sum_k, sum_v
):
    length = raw_q.shape[0]
    low_lanes = lax.broadcasted_iota(jnp.int32, (1, 2 * HD), 1) < HD
    gains = gain[...]
    key_raw = raw_k[...]
    key_factor = head_factors(key_raw, low_lanes)
    key_unit = key_raw * key_factor
    key = (gains * key_unit).astype(BF16)
    key_eight = key * 8
    value = raw_v[...].astype(BF16)
    sum_k[...] = jnp.zeros_like(sum_k)
    sum_v[...] = jnp.zeros_like(sum_v)
    gain_total = jnp.zeros((1, 2 * HD), F32)

    def back(upstream, unit, factor):
        scaled = gains * upstream
        return (factor * (scaled - unit * head_sums(scaled * unit, low_lanes))).astype(BF16)

    for tile in range(length // Q_TILE):
        start, end = key_range(tile)
        rows = slice(tile * Q_TILE, (tile + 1) * Q_TILE)
        query_raw = raw_q[rows, :]
        query_factor = head_factors(query_raw, low_lanes)
        query_unit = query_raw * query_factor
        query = (gains * query_unit).astype(BF16) * 8
        upstream = d_mixed[rows, :].astype(F32)
        tile_bias = bias[0, rows, start:end]
        d_query = []
        for low in (True, False):
            lanes = low_lanes if low else jnp.logical_not(low_lanes)
            own_query = jnp.where(lanes, query, jnp.zeros_like(query))
            expo = jnp.exp(nt(own_query, key[start:end]) + tile_bias)
            inverse = 1.0 / jnp.sum(expo, axis=-1, keepdims=True)
            expo_low = expo.astype(BF16)
            result = nn(expo_low, value[start:end]) * inverse
            own_up = jnp.where(lanes, upstream, 0.0)
            delta = jnp.sum(result * own_up, axis=-1, keepdims=True) * inverse
            own_up = (own_up * inverse).astype(BF16)
            sum_v[start:end, :] += tn(expo_low, own_up)
            d_scores = (expo * (nt(own_up, value[start:end]) - delta)).astype(BF16)
            d_query.append(nn(d_scores, key_eight[start:end]))
            sum_k[start:end, :] += tn(d_scores, own_query)
        d_query = jnp.where(low_lanes, d_query[0], d_query[1])
        gain_total += jnp.sum(d_query * query_unit, axis=0, keepdims=True)
        d_raw_q[rows, :] = back(d_query, query_unit, query_factor)
    d_key = sum_k[...]
    gain_total += jnp.sum(d_key * key_unit, axis=0, keepdims=True)
    d_raw_k[...] = back(d_key, key_unit, key_factor)
    d_raw_v[...] = sum_v[...].astype(BF16)
    gain_grad[...] = jnp.broadcast_to(gain_total[None], gain_grad.shape)


def attend_specs(length):
    lanes = pl.BlockSpec((length, 2 * HD), lambda s, h: (s, h))
    gain = pl.BlockSpec((1, 2 * HD), lambda s, h: (0, h))
    bias = pl.BlockSpec((1, length, length), lambda s, h: (s, 0, 0))
    return lanes, gain, bias


def attend(raw, gain, bias):
    count, length, _ = bias.shape
    rows, columns = raw[0].shape
    lanes, gain_spec, bias_spec = attend_specs(length)
    return pl.pallas_call(
        attend_kernel,
        grid=(count, columns // (2 * HD)),
        in_specs=[lanes, lanes, lanes, gain_spec, bias_spec],
        out_specs=lanes,
        out_shape=jax.ShapeDtypeStruct((rows, columns), BF16),
        compiler_params=pltpu.CompilerParams(vmem_limit_bytes=40 << 20),
        cost_estimate=pl.CostEstimate(
            flops=4 * rows * length * columns, bytes_accessed=14 * rows * columns, transcendentals=0
        ),
        name="attend",
    )(*raw, gain, bias)


def attend_back(raw, d_mixed, gain, bias):
    count, length, _ = bias.shape
    rows, columns = raw[0].shape
    lanes, gain_spec, bias_spec = attend_specs(length)
    out = jax.ShapeDtypeStruct((rows, columns), BF16)
    result = pl.pallas_call(
        attend_back_kernel,
        grid=(count, columns // (2 * HD)),
        in_specs=[lanes, lanes, lanes, lanes, gain_spec, bias_spec],
        out_specs=[lanes, lanes, lanes, pl.BlockSpec((1, 8, 2 * HD), lambda s, h: (s, 0, h))],
        out_shape=[out, out, out, jax.ShapeDtypeStruct((count, 8, columns), F32)],
        scratch_shapes=[pltpu.VMEM((length, 2 * HD), F32)] * 2,
        compiler_params=pltpu.CompilerParams(vmem_limit_bytes=40 << 20),
        cost_estimate=pl.CostEstimate(
            flops=12 * rows * length * columns, bytes_accessed=20 * rows * columns, transcendentals=0
        ),
        name="attend_back",
    )(*raw, d_mixed, gain, bias)
    return result[:3], jnp.sum(result[3][:, 0, :], axis=0)


def bias_of(segment_ids, pad_mask):
    positions = jnp.arange(segment_ids.shape[1])
    key_code = jnp.where(pad_mask == 0, segment_ids, -1)
    earlier = positions[None, :] <= positions[:, None]
    same = positions[None, :] == positions[:, None]
    allowed = (segment_ids[:, :, None] == key_code[:, None, :]) & earlier[None] | same[None]
    return jnp.where(allowed, 0.0, MASKED).astype(F32)


def one_left(route, tile):
    return 0


def attention_left_of(route, tile):
    if route < 2:
        return jnp.where(tile < 2, 0, 1)
    return jnp.where(tile < 1, 0, 1) if route == 2 else 1


def per_device(
    tokens,
    cotangent,
    segment_ids,
    pad_mask,
    inward_master,
    inward_first,
    inward_second,
    outward_master,
    outward_first,
    outward_second,
    expand_master,
    expand_first,
    expand_second,
    shrink_master,
    shrink_first,
    shrink_second,
    alpha_master,
    alpha_first,
    alpha_second,
    scale_master,
    scale_first,
    scale_second,
):
    count = lax.axis_size("dp")
    me = lax.axis_index("dp")
    core = lax.axis_index("tensor")
    inv_root = D ** (-0.5)
    rows = tokens.shape[0]
    own_rows = rows // 2
    heads_width = inward_master.shape[2]
    units = expand_master.shape[2]

    small = jnp.concatenate([alpha_master, scale_master], axis=0).astype(BF16)
    small_count = small.shape[0]
    small = jnp.pad(small, ((0, 128 - small_count), (0, 0))).T
    attention_copies = jnp.concatenate(
        [
            inward_master[0].astype(BF16),
            inward_master[1].astype(BF16),
            inward_master[2].astype(BF16),
            outward_master.astype(BF16).T,
            jnp.pad(small, ((0, 0), (0, 128))),
        ],
        axis=1,
    )
    attention_copies = gather(attention_copies, count, 0)
    w_inward = attention_copies[:, : 3 * heads_width]
    w_outward = attention_copies[:, 3 * heads_width : 4 * heads_width]
    small = attention_copies[:, 4 * heads_width : 4 * heads_width + 128]

    places = place_matrix(me, count)
    tokens_in = nn(tokens, places).astype(BF16)
    cot_own = lax.dynamic_slice_in_dim(cotangent, core * own_rows, own_rows, 0)
    cot_own = nn(cot_own, places)
    keep = (1 - pad_mask).astype(F32).reshape(rows, 1)
    cot_own = cot_own * lax.dynamic_slice_in_dim(keep, core * own_rows, own_rows, 0)
    tokens_own = lax.dynamic_slice_in_dim(tokens_in, core * own_rows, own_rows, 0).astype(F32)
    alphas = small[:, :2].T.astype(F32)
    scale_rows = tn(small, places.T)[2:small_count]
    query_gain = lax.dynamic_slice_in_dim(scale_rows[0], core * heads_width, heads_width, 0)[None]
    ratio_rows = FF // D
    gain_up = lax.dynamic_slice_in_dim(
        scale_rows[1 : 1 + ratio_rows].reshape(FF), core * units, units, 0
    )
    gain_gate = lax.dynamic_slice_in_dim(
        scale_rows[1 + ratio_rows :].reshape(FF), core * units, units, 0
    )
    bias = bias_of(segment_ids, pad_mask)

    def sum_own(partial):
        send = lax.dynamic_slice_in_dim(partial, (1 - core) * own_rows, own_rows, 0)
        kept = lax.dynamic_slice_in_dim(partial, core * own_rows, own_rows, 0)
        return kept + swap_cores(send)

    def both(own):
        other = swap_cores(own)
        full = jnp.zeros((rows, own.shape[1]), own.dtype)
        full = lax.dynamic_update_slice_in_dim(full, own, core * own_rows, 0)
        return lax.dynamic_update_slice_in_dim(full, other, (1 - core) * own_rows, 0)

    raw = nn(tokens_in, w_inward) * inv_root
    raw = [raw[:, k * heads_width : (k + 1) * heads_width] for k in range(3)]
    mixed = attend(raw, query_gain, bias)
    branch = sum_own(nt(mixed, w_outward))
    h_attn, attn_factor = row_norm(branch)
    first, first_factor = row_norm(tokens_own + alphas[0] * (h_attn - tokens_own))
    first_low = both(first.astype(BF16))
    unit_copies = jnp.concatenate(
        [
            expand_master[0].astype(BF16),
            expand_master[1].astype(BF16),
            shrink_master.astype(BF16).T,
        ],
        axis=1,
    )
    unit_copies, first_low = lax.optimization_barrier((unit_copies, first_low))
    unit_copies = gather(unit_copies, count, 1)
    w_up = unit_copies[:, :units]
    w_gate = unit_copies[:, units : 2 * units]
    w_shrink = unit_copies[:, 2 * units :]
    proj_up = nn(first_low, w_up) * inv_root
    proj_gate = nn(first_low, w_gate) * inv_root
    up_branch = gain_up * proj_up
    gate_branch = gain_gate * proj_gate
    sigmoid_gate = jax.nn.sigmoid(gate_branch)
    activation = gate_branch * sigmoid_gate
    hidden = (up_branch * activation).astype(BF16)
    shrunk = sum_own(nt(hidden, w_shrink))
    h_mlp, mlp_factor = row_norm(shrunk)
    output, out_factor = row_norm(first + alphas[1] * (h_mlp - first))

    d_two = row_norm_back(cot_own, output, out_factor)
    alpha_mlp_grad = jnp.sum(d_two * (h_mlp - first), axis=0)
    d_shrunk = both(row_norm_back(alphas[1] * d_two, h_mlp, mlp_factor).astype(BF16))
    shrink_grad = sum_products(d_shrunk.T[None], hidden, one_left, 1.0, 2)
    shrink_grad = scatter_rest(shrink_grad, count).T
    d_hidden = nn(d_shrunk, w_shrink)
    d_up = d_hidden * activation
    d_gate = d_hidden * up_branch * sigmoid_gate * (1.0 + gate_branch * (1.0 - sigmoid_gate))
    up_gain_grad = jnp.sum(d_up * proj_up, axis=0)
    gate_gain_grad = jnp.sum(d_gate * proj_gate, axis=0)
    d_proj_up = (d_up * gain_up).astype(BF16)
    d_proj_gate = (d_gate * gain_gate).astype(BF16)
    d_expand = jnp.concatenate([d_proj_up, d_proj_gate], axis=1)
    expand_grad = sum_products(first_low.T[None], d_expand, one_left, inv_root, 3)
    expand_grad = scatter_rest(expand_grad, count)
    expand_grad = jnp.stack([expand_grad[:, :units], expand_grad[:, units:]])
    first_part = sum_own((nt(d_proj_up, w_up) + nt(d_proj_gate, w_gate)) * inv_root)
    d_first = (1.0 - alphas[1]) * d_two + first_part
    d_one = row_norm_back(d_first, first, first_factor)
    alpha_attn_grad = jnp.sum(d_one * (h_attn - tokens_own), axis=0)
    d_branch = both(row_norm_back(alphas[0] * d_one, h_attn, attn_factor).astype(BF16))
    d_mixed = nn(d_branch, w_outward).astype(BF16)
    d_raw, query_gain_grad = attend_back(raw, d_mixed, query_gain, bias)
    attention_right = jnp.concatenate(
        [mixed[:, :512], *d_raw[:2], d_raw[2][:, :256], mixed[:, 512:], d_raw[2][:, 256:]], axis=1
    )
    attention_left = jnp.stack([d_branch.T, tokens_in.T])
    attention_grad = sum_products(attention_left, attention_right, attention_left_of, 1.0, 4)
    attention_grad = scatter_rest(attention_grad, count)
    input_part = (nt(jnp.concatenate(d_raw, axis=1), w_inward)) * inv_root

    block_output = both(nt(output.astype(BF16), places).astype(BF16))
    residual = (1.0 - alphas[0]) * d_one
    residual_high = residual.astype(BF16)
    residual_low = (residual - residual_high.astype(F32)).astype(BF16)
    residual = nt(residual_high, places) + nt(residual_low, places)
    own_width = D // lax.axis_size("tensor")
    input_part = nt(input_part.astype(BF16), places)
    input_part = lax.dynamic_update_slice_in_dim(
        input_part,
        lax.dynamic_slice_in_dim(input_part, core * own_rows, own_rows, 0) + residual,
        core * own_rows,
        0,
    )
    input_grad = lax.dynamic_slice_in_dim(input_part, core * own_width, own_width, 1) + swap_cores(
        lax.dynamic_slice_in_dim(input_part, (1 - core) * own_width, own_width, 1)
    )

    alpha_grad = jnp.stack([alpha_attn_grad, alpha_mlp_grad])
    query_full = lax.dynamic_update_slice_in_dim(
        jnp.zeros((D,), F32), query_gain_grad, core * heads_width, 0
    )
    up_full = lax.dynamic_update_slice_in_dim(jnp.zeros((FF,), F32), up_gain_grad, core * units, 0)
    gate_full = lax.dynamic_update_slice_in_dim(
        jnp.zeros((FF,), F32), gate_gain_grad, core * units, 0
    )
    scale_grad = jnp.concatenate(
        [query_full.reshape(1, D), up_full.reshape(FF // D, D), gate_full.reshape(FF // D, D)],
        axis=0,
    )
    alpha_grad = alpha_grad + swap_cores(alpha_grad)
    scale_grad = scale_grad + swap_cores(scale_grad)
    width = D // count
    alpha_grad = scatter_sum(alpha_grad.T, count).T
    scale_grad = lax.dynamic_slice_in_dim(butterfly_sum(scale_grad, count), me * width, width, 1)

    outward_grad = jnp.concatenate(
        [attention_grad[:, :512], attention_grad[:, 2048:2176]], axis=1
    ).T
    inward_grad = jnp.stack(
        [
            attention_grad[:, 512:1152],
            attention_grad[:, 1152:1792],
            jnp.concatenate([attention_grad[:, 1792:2048], attention_grad[:, 2176:]], axis=1),
        ]
    ) * inv_root
    inward_pre, inward_var = adam_step(
        inward_master, inward_first, inward_second, inward_grad, RATE_MATRIX
    )
    outward_pre, outward_var = adam_step(
        outward_master, outward_first, outward_second, outward_grad, RATE_MATRIX
    )
    expand_pre, expand_var = adam_step(
        expand_master, expand_first, expand_second, expand_grad, RATE_MATRIX
    )
    shrink_pre, shrink_var = adam_step(
        shrink_master, shrink_first, shrink_second, shrink_grad, RATE_MATRIX
    )
    alpha_new, alpha_var = adam_step(
        alpha_master, alpha_first, alpha_second, alpha_grad, RATE_ALPHA
    )
    scale_new, scale_var = adam_step(
        scale_master, scale_first, scale_second, scale_grad, RATE_SCALE
    )

    def renormed(pre, axis):
        squares = butterfly_sum(jnp.sum(pre * pre, axis=axis), count)
        return pre * lax.rsqrt(jnp.expand_dims(squares, axis) / D + EPS_NORM)

    return (
        block_output,
        input_grad,
        inward_grad,
        inward_var,
        renormed(inward_pre, 1),
        outward_grad,
        outward_var,
        renormed(outward_pre, 1),
        expand_grad,
        expand_var,
        renormed(expand_pre, 1),
        shrink_grad,
        shrink_var,
        renormed(shrink_pre, 1),
        alpha_grad,
        alpha_var,
        alpha_new,
        scale_grad,
        scale_var,
        scale_new,
    )


def solution(mesh):
    rows = P("dp", None)
    deep = P(None, "dp", "tensor")
    flat = P("tensor", "dp")
    vector = P(None, "dp")
    in_specs = (rows,) * 4 + (deep,) * 3 + (flat,) * 3 + (deep,) * 3 + (flat,) * 3 + (vector,) * 6
    out_specs = (
        (rows, P("dp", "tensor"))
        + (deep,) * 3
        + (flat,) * 3
        + (deep,) * 3
        + (flat,) * 3
        + (vector,) * 6
    )
    return jax.shard_map(
        per_device, mesh=mesh, in_specs=in_specs, out_specs=out_specs, check_vma=False
    )
```

```python
import functools

import jax
import jax.numpy as jnp
import numpy as np
from jax import lax
from jax.experimental import pallas as pl
from jax.experimental.pallas import tpu as pltpu
from jax.sharding import PartitionSpec as P

D = 1280
HEADS = 20
HD = 64
FF = 5120
STEP = 10
LONGEST = 256


EPS_NORM = 1e-06
BETA_ONE = 0.9
BETA_TWO = 0.95
ADAM_EPS = 1e-08
RATE_MATRIX = 0.3
RATE_ALPHA = 0.08
RATE_SCALE = 0.25
MASKED = -1e30
F32 = jnp.float32
BF16 = jnp.bfloat16


def row_norm(values):
    factor = lax.rsqrt(jnp.mean(values * values, axis=-1, keepdims=True) + EPS_NORM)
    return (values * factor, factor)


def row_norm_back(upstream, normed, factor):
    return factor * (upstream - normed * jnp.mean(upstream * normed, axis=-1, keepdims=True))


def adam_step(master, first_moment, second_moment, gradient, rate):
    first_new = BETA_ONE * first_moment.astype(F32) + (1.0 - BETA_ONE) * gradient
    second_new = BETA_TWO * second_moment + (1.0 - BETA_TWO) * gradient * gradient
    ratio = (
        first_new
        / (1.0 - BETA_ONE**STEP)
        / (jnp.sqrt(second_new / (1.0 - BETA_TWO**STEP)) + ADAM_EPS)
    )
    return (master - rate * ratio, second_new)


LANES = 128
PLACES = (2, 1, 4, 8)
ROUTES = ((3, 2, 1, 0), (3, 2, 0, 1), (1, 0, 3, 2), (0, 1, 3, 2))
EVERY = 4
LAG = 2
RING = 4


def partner_of(me, bit):
    return me + bit - 2 * bit * ((me // bit) % 2)


def greet(me, core=None):
    barrier = pltpu.get_barrier_semaphore()
    partners = [{"dp": partner_of(me, bit)} for bit in PLACES]
    if core is not None:
        partners.append({"tensor": 1 - core})
    for partner in partners:
        pl.semaphore_signal(
            barrier, inc=1, device_id=partner, device_id_type=pl.DeviceIdType.MESH
        )
    pl.semaphore_wait(barrier, len(partners))


def tile_plan(columns):
    tiles = columns // LANES
    rare = tiles // 10
    often = (tiles - 2 * rare) // 2
    return (
        (0, 2, often, 1),
        (1, 2, often, 1),
        (2 * often, 1, rare, EVERY),
        (2 * often + rare, 1, rare, EVERY),
    )


def for_tiles(step, hop, plan, body):
    for route, (_, _, number, every) in enumerate(plan):
        if number == 0:
            continue
        at = step - hop * LAG
        due = (at >= 0) & (at < number * every)
        if every > 1:
            due = due & (at % every == 0)

        @pl.when(due)
        def _():
            body(route, at // every)


def lanes_of(plan, route, tile):
    first, stride, _, _ = plan[route]
    return pl.ds(pl.multiple_of((first + stride * tile) * LANES, LANES), LANES)


def steps_of(plan, hops):
    return max((number - 1) * every + 1 for _, _, number, every in plan if number) + hops * LAG


def extra_bits(count):
    return [bit for bit in (1 << k for k in range(4, count.bit_length() - 1))]


def exchange(array, bit, count):
    return lax.ppermute(array, "dp", [(i, i ^ bit) for i in range(count)])


def swap_cores(array):
    return lax.ppermute(array, "tensor", [(0, 1), (1, 0)])


def gather_rest(block, count):
    for bit in extra_bits(count)[::-1]:
        block = jnp.concatenate([block, exchange(block, bit, count)], axis=0)
    return block


def scatter_rest(partial, count):
    for bit in extra_bits(count):
        half = partial.shape[0] // 2
        partial = partial[:half] + exchange(partial[half:], bit, count)
    return partial


def butterfly_sum(array, count):
    for bit in list(PLACES) + extra_bits(count):
        array = array + exchange(array, bit, count)
    return array


def scatter_sum(partial, count):
    for bit in PLACES:
        half = partial.shape[0] // 2
        partial = partial[:half] + exchange(partial[half:], bit, count)
    return scatter_rest(partial, count)


def place_row_of(me, count):
    places = list(PLACES) + extra_bits(count)
    width = D // count
    placed = np.arange(D, dtype=np.int32)
    position, offset = placed // width, placed % width
    relative = np.zeros_like(position)
    for axis, bit in enumerate(places):
        relative = relative + ((position >> (len(places) - 1 - axis)) & 1) * bit
    return ((jnp.asarray(relative) ^ me) * width + jnp.asarray(offset))[None]


def place_matrix(place_row):
    natural = lax.broadcasted_iota(jnp.int32, (D, D), 0)
    return (natural == place_row).astype(BF16)


def nn(a, b):
    return lax.dot_general(a, b, (((1,), (0,)), ((), ())), preferred_element_type=F32)


def nt(a, b):
    return lax.dot_general(a, b, (((1,), (1,)), ((), ())), preferred_element_type=F32)


def tn(a, b):
    return lax.dot_general(a, b, (((0,), (0,)), ((), ())), preferred_element_type=F32)


def head_factors(raw, low_lanes):
    squares = raw * raw
    low = jnp.sum(jnp.where(low_lanes, squares, 0.0), axis=-1, keepdims=True)
    high = jnp.sum(jnp.where(low_lanes, 0.0, squares), axis=-1, keepdims=True)
    return jnp.where(low_lanes, lax.rsqrt(low + EPS_NORM), lax.rsqrt(high + EPS_NORM))


def head_sums(values, low_lanes):
    low = jnp.sum(jnp.where(low_lanes, values, 0.0), axis=-1, keepdims=True)
    high = jnp.sum(jnp.where(low_lanes, 0.0, values), axis=-1, keepdims=True)
    return jnp.where(low_lanes, low, high)


Q_TILE = 128


def key_range(tile):
    start = max(0, tile * Q_TILE - LONGEST)
    return start, (tile + 1) * Q_TILE


def attend_pair(query, key, value, gain, bias, mixed):
    length = query.shape[0]
    low_lanes = lax.broadcasted_iota(jnp.int32, (1, 2 * HD), 1) < HD
    query = (gain * (query * head_factors(query, low_lanes))).astype(BF16) * 8
    key = (gain * (key * head_factors(key, low_lanes))).astype(BF16)
    value = value.astype(BF16)
    zero = jnp.zeros_like(query)
    parts = (jnp.where(low_lanes, query, zero), jnp.where(low_lanes, zero, query))
    for tile in range(length // Q_TILE):
        start, end = key_range(tile)
        rows = slice(tile * Q_TILE, (tile + 1) * Q_TILE)
        tile_bias = bias[rows, start:end]
        results = []
        for part in parts:
            expo = jnp.exp(nt(part[rows], key[start:end]) + tile_bias)
            total = jnp.sum(expo, axis=-1, keepdims=True)
            results.append(nn(expo.astype(BF16), value[start:end]) * (1.0 / total))
        mixed[rows, :] = jnp.where(low_lanes, results[0], results[1]).astype(BF16)


def attend_pair_back(
    raw_q, raw_k, raw_v, d_mixed, gains, bias, d_raw_q, d_raw_k, d_raw_v, sum_k, sum_v
):
    length = raw_q.shape[0]
    low_lanes = lax.broadcasted_iota(jnp.int32, (1, 2 * HD), 1) < HD
    key_raw = raw_k[...]
    key_factor = head_factors(key_raw, low_lanes)
    key_unit = key_raw * key_factor
    key = (gains * key_unit).astype(BF16)
    key_eight = key * 8
    value = raw_v[...].astype(BF16)
    sum_k[...] = jnp.zeros_like(sum_k)
    sum_v[...] = jnp.zeros_like(sum_v)
    gain_total = jnp.zeros((1, 2 * HD), F32)

    def back(upstream, unit, factor):
        scaled = gains * upstream
        return (factor * (scaled - unit * head_sums(scaled * unit, low_lanes))).astype(BF16)

    for tile in range(length // Q_TILE):
        start, end = key_range(tile)
        rows = slice(tile * Q_TILE, (tile + 1) * Q_TILE)
        query_raw = raw_q[rows, :]
        query_factor = head_factors(query_raw, low_lanes)
        query_unit = query_raw * query_factor
        query = (gains * query_unit).astype(BF16) * 8
        upstream = d_mixed[rows].astype(F32)
        tile_bias = bias[rows, start:end]
        d_query = []
        for low in (True, False):
            lanes = low_lanes if low else jnp.logical_not(low_lanes)
            own_query = jnp.where(lanes, query, jnp.zeros_like(query))
            expo = jnp.exp(nt(own_query, key[start:end]) + tile_bias)
            inverse = 1.0 / jnp.sum(expo, axis=-1, keepdims=True)
            expo_low = expo.astype(BF16)
            result = nn(expo_low, value[start:end]) * inverse
            own_up = jnp.where(lanes, upstream, 0.0)
            delta = jnp.sum(result * own_up, axis=-1, keepdims=True) * inverse
            own_up = (own_up * inverse).astype(BF16)
            sum_v[start:end, :] += tn(expo_low, own_up)
            d_scores = (expo * (nt(own_up, value[start:end]) - delta)).astype(BF16)
            d_query.append(nn(d_scores, key_eight[start:end]))
            sum_k[start:end, :] += tn(d_scores, own_query)
        d_query = jnp.where(low_lanes, d_query[0], d_query[1])
        gain_total += jnp.sum(d_query * query_unit, axis=0, keepdims=True)
        d_raw_q[rows, :] = back(d_query, query_unit, query_factor)
    d_key = sum_k[...]
    gain_total += jnp.sum(d_key * key_unit, axis=0, keepdims=True)
    d_raw_k[...] = back(d_key, key_unit, key_factor)
    d_raw_v[...] = sum_v[...].astype(BF16)
    return gain_total


def bias_of(segment_ids, pad_mask):
    positions = jnp.arange(segment_ids.shape[1])
    key_code = jnp.where(pad_mask == 0, segment_ids, -1)
    earlier = positions[None, :] <= positions[:, None]
    same = positions[None, :] == positions[:, None]
    allowed = (segment_ids[:, :, None] == key_code[:, None, :]) & earlier[None] | same[None]
    return jnp.where(allowed, 0.0, MASKED).astype(F32)


ARRIVE = 4 * LAG
UNIT_GROUP = 4
FIRST_UNIT_PAIR = 8
RARE_UNITS = 3


def head_tiles():
    return HEADS * HD // 2 // LANES


def unit_tiles():
    return FF // 2 // LANES


def forward_plan():
    groups = unit_tiles() // UNIT_GROUP
    return tile_plan((2 * (FIRST_UNIT_PAIR + 5 * groups) + 2 * (RARE_UNITS + groups)) * LANES)


def pair_tile(unit):
    return 2 * (FIRST_UNIT_PAIR + 5 * (unit // UNIT_GROUP) + unit % UNIT_GROUP)


def shrink_tile_static(unit):
    plan = forward_plan()
    group, place = unit // UNIT_GROUP, unit % UNIT_GROUP
    if place < 2:
        return plan[2][0] + place * plan[2][2] + RARE_UNITS + group
    return 2 * (FIRST_UNIT_PAIR + 5 * group + UNIT_GROUP) + place - 2


def shrink_tile(unit):
    plan = forward_plan()
    group, place = unit // UNIT_GROUP, unit % UNIT_GROUP
    rare = plan[2][0] + place * plan[2][2] + RARE_UNITS + group
    often = 2 * (FIRST_UNIT_PAIR + 5 * group + UNIT_GROUP) + place - 2
    return jnp.where(place < 2, rare, often)


def forward_columns(inward, outward, expand, shrink, small):
    rows = small.shape[0]
    groups = unit_tiles() // UNIT_GROUP
    heads = 3 * head_tiles() - 1
    units = jnp.stack([expand[0], expand[1]], axis=1).reshape(
        rows, 2, groups, UNIT_GROUP, LANES
    )
    units = units.transpose(0, 2, 3, 1, 4).reshape(rows, groups, 2 * UNIT_GROUP, LANES)
    shrink = shrink.reshape(rows, groups, UNIT_GROUP, LANES)
    units = jnp.concatenate([units, shrink[:, :, 2:]], axis=2).reshape(rows, -1)
    return jnp.concatenate(
        [
            inward[:, : heads * LANES],
            outward[:, 2 * LANES : 4 * LANES],
            units,
            inward[:, heads * LANES :],
            outward[:, :LANES],
            outward[:, 4 * LANES :],
            shrink[:, :, 0].reshape(rows, -1),
            small,
            outward[:, LANES : 2 * LANES],
            jnp.zeros((rows, LANES), BF16),
            shrink[:, :, 1].reshape(rows, -1),
        ],
        axis=1,
    )


def forward_kernel(
    plan,
    block,
    tokens,
    place_row,
    bias,
    out,
    tokens_out,
    raw_out,
    mixed_out,
    h_attn_out,
    first_out,
    first_low_out,
    tokens_turned_out,
    first_turned_out,
    proj_out,
    hidden_out,
    factors,
    alphas,
    scales,
    gains,
    shrunk,
    place,
    tokens_in,
    raw,
    stage_pair,
    stage_one,
    stage_outward,
    mixed,
    branch_in,
    h_attn,
    first,
    first_low,
    stage_proj,
    stage_hidden,
    own_sem,
    send_sem,
    recv_sem,
    pair_sem,
    one_sem,
    outward_sem,
    proj_sem,
    hidden_sem,
    result_sem,
    core_send,
    core_recv,
):
    me = lax.axis_index("dp")
    core = lax.axis_index("tensor")
    inv_root = D ** (-0.5)
    rows = tokens.shape[0]
    own_rows = rows // 2
    own_at = pl.multiple_of(core * own_rows, own_rows)
    other_at = pl.multiple_of((1 - core) * own_rows, own_rows)
    heads = head_tiles()
    units = unit_tiles()
    attend_at = 3 * heads // 2 + ARRIVE + 1
    pairs_each = 2
    sequences = bias.shape[0]
    length = bias.shape[1]
    head_pairs = sequences * heads
    branch_at = attend_at + -(-head_pairs // pairs_each)
    units_at = branch_at + 2

    own = pltpu.make_async_copy(block, out.at[0, 0, 0, 0], own_sem)
    own.start()
    greet(me, core)

    def piece(hop, route, tile):
        lanes = lanes_of(plan, route, tile)
        crossed, axis = ROUTES[route][:hop], ROUTES[route][hop]
        source = [slice(None) if k in crossed else 0 for k in range(4)]
        target = [1 if k == axis else source[k] for k in range(4)]
        if hop == 0:
            source_ref = block.at[:, lanes]
        else:
            source_ref = out.at[(*source, slice(None), lanes)]
        return pltpu.make_async_remote_copy(
            src_ref=source_ref,
            dst_ref=out.at[(*target, slice(None), lanes)],
            send_sem=send_sem.at[hop, route, tile % RING],
            recv_sem=recv_sem.at[hop, route, tile],
            device_id={"dp": partner_of(me, PLACES[axis])},
            device_id_type=pl.DeviceIdType.MESH,
        )

    def forward_hop(hop, route, tile):
        if hop > 0:
            piece(hop - 1, route, tile).wait_recv()
        if hop < 4:

            @pl.when(tile >= RING)
            def _():
                piece(hop, route, tile - RING).wait_send()

            piece(hop, route, tile).start()

    def staged(tile, width, target, sem):
        lanes = pl.ds(pl.multiple_of(tile * LANES, LANES), width * LANES)
        return pltpu.make_async_copy(out.at[:, :, :, :, :, lanes], target, sem)

    def pair_copy(tile, slot):
        return staged(tile, 2, stage_pair.at[slot], pair_sem.at[slot])

    def one_copy(tile, slot):
        return staged(tile, 1, stage_one.at[slot], one_sem.at[slot])

    rare = plan[2][0]
    rarer = plan[3][0]

    def outward_copies():
        return [
            staged(tile, width, stage_outward.at[:, :, :, :, :, pl.ds(at * LANES, width * LANES)], outward_sem.at[k])
            for k, (tile, width, at) in enumerate(
                ((rare + 1, 1, 0), (rarer + 1, 1, 1), (3 * heads - 1, 2, 2), (rare + 2, 1, 4))
            )
        ]

    def core_copy(source, target, which):
        return pltpu.make_async_remote_copy(
            src_ref=source,
            dst_ref=target,
            send_sem=core_send.at[which],
            recv_sem=core_recv.at[which],
            device_id={"tensor": 1 - core},
            device_id_type=pl.DeviceIdType.MESH,
        )

    def branch_copy():
        return core_copy(shrunk.at[pl.ds(0, own_rows)], branch_in, 0)

    def first_copy():
        return core_copy(
            first_low.at[pl.ds(own_at, own_rows)], first_low.at[pl.ds(own_at, own_rows)], 1
        )

    result_pairs = (
        (tokens_in, tokens_out),
        (raw, raw_out),
        (mixed, mixed_out),
        (h_attn, h_attn_out),
        (first, first_out),
        (first_low, first_low_out),
        (place.at[:, pl.ds(0, rows)], tokens_turned_out),
        (place.at[:, pl.ds(0, rows)], first_turned_out),
    )

    def result(k):
        return pltpu.make_async_copy(*result_pairs[k], result_sem.at[k])

    def chunks(total, size, body):
        def one(k, _):
            body(pl.ds(pl.multiple_of(k * size, size), size))
            return 0

        lax.fori_loop(0, total // size, one, 0)

    def in_order():
        natural = place_row[...]

        def fill(at):
            here = lax.broadcasted_iota(jnp.int32, (LANES, D), 0) + at.start
            place[at, :] = jnp.where(here == natural, 1.0, 0.0).astype(BF16)

        chunks(D, LANES, fill)

        def move(at):
            tokens_in[at, :] = nn(tokens[at, :], place[...]).astype(BF16)

        chunks(rows, 256, move)
        result(0).start()

    def turn(source):
        def some(at):
            place[:, at] = source[at, :].astype(F32).T.astype(BF16)

        chunks(rows, LANES, some)

    def project(weights, lanes):
        def some(at):
            raw[at, lanes] = nn(tokens_in[at, :], weights) * inv_root

        chunks(rows, 256, some)

    def small_vectors():
        small = stage_one[1].reshape(D, LANES).astype(F32).T
        alphas[...] = small[: alphas.shape[0]]
        scales[...] = nt(small.astype(BF16), place[...])[: scales.shape[0]]
        each = units * LANES // D
        for row in range(2):
            for k in range(each):
                at = 3 + row * 2 * each + k
                gains[row : row + 1, k * D : (k + 1) * D] = jnp.where(
                    core == 0, scales[at : at + 1, :], scales[at + each : at + each + 1, :]
                )

    def attend_one(number):
        sequence, head = number // heads, number % heads
        at = pl.ds(pl.multiple_of(sequence * length, length), length)
        lanes = [
            pl.ds(pl.multiple_of((k * heads + head) * LANES, LANES), LANES) for k in range(3)
        ]
        gain_lanes = pl.ds(pl.multiple_of((core * heads + head) * LANES, LANES), LANES)
        attend_pair(
            raw[at, lanes[0]],
            raw[at, lanes[1]],
            raw[at, lanes[2]],
            scales[2:3, gain_lanes],
            bias.at[sequence],
            mixed.at[at, lanes[0]],
        )

    def branch():
        weights = stage_outward[...].reshape(D, heads * LANES)
        for target, source in ((0, other_at), (own_rows, own_at)):
            for k in range(2):
                half = own_rows // 2
                at = pl.ds(pl.multiple_of(source + k * half, half), half)
                shrunk[pl.ds(target + k * half, half), :] = nt(mixed[at, :], weights)
            if target == 0:
                branch_copy().start()

    def norms():
        branch_copy().wait()
        alpha = alphas[0:1, :]

        def some(at):
            total = shrunk[pl.ds(pl.multiple_of(own_rows + at.start, 64), 64), :] + branch_in[at, :]
            normed, factor = row_norm(total)
            here = pl.ds(pl.multiple_of(own_at + at.start, 64), 64)
            inputs = tokens_in[here, :].astype(F32)
            result, result_factor = row_norm(inputs + alpha * (normed - inputs))
            h_attn[at, :] = normed
            first[at, :] = result
            first_low[here, :] = result.astype(BF16)
            factors[at, :LANES] = jnp.broadcast_to(factor, (64, LANES))
            factors[at, LANES:] = jnp.broadcast_to(result_factor, (64, LANES))

        chunks(own_rows, 64, some)
        first_copy().start()
        for k in (3, 4):
            result(k).start()

    def gain_of(unit, row):
        return gains[row : row + 1, pl.ds(pl.multiple_of(unit * LANES, LANES), LANES)]

    def proj_copy(unit):
        lanes = pl.ds(pl.multiple_of(unit * 2 * LANES, 2 * LANES), 2 * LANES)
        slot = unit % 2
        return pltpu.make_async_copy(stage_proj.at[slot], proj_out.at[:, lanes], proj_sem.at[slot])

    def hidden_copy(unit):
        lanes = pl.ds(pl.multiple_of(unit * LANES, LANES), LANES)
        slot = unit % 2
        return pltpu.make_async_copy(
            stage_hidden.at[slot], hidden_out.at[:, lanes], hidden_sem.at[slot]
        )

    def fetch_unit(unit):
        pair_copy(pair_tile(unit), unit % 2).start()
        one_copy(shrink_tile(unit), unit % 2).start()

    def one_unit(unit):
        slot = unit % 2

        @pl.when(unit == 0)
        def _():
            first_copy().wait()
            result(5).start()
            shrunk[...] = jnp.zeros_like(shrunk)

        @pl.when(unit >= 2)
        def _():
            proj_copy(unit - 2).wait()
            hidden_copy(unit - 2).wait()

        pair_copy(0, slot).wait()
        one_copy(0, slot).wait()
        weights = stage_pair[slot].reshape(D, 2 * LANES)
        down = stage_one[slot].reshape(D, LANES)
        gain_up = gain_of(unit, 0)
        gain_gate = gain_of(unit, 1)

        def some(at):
            proj = nn(first_low[at, :], weights) * inv_root
            stage_proj[slot, at, :] = proj
            gate = gain_gate * proj[:, LANES:]
            hidden = (gain_up * proj[:, :LANES] * (gate * jax.nn.sigmoid(gate))).astype(BF16)
            stage_hidden[slot, at, :] = hidden
            shrunk[at, :] += nt(hidden, down)

        chunks(rows, 256, some)
        proj_copy(unit).start()
        hidden_copy(unit).start()

    def step(index, _):
        for hop in range(5):
            for_tiles(index, hop, plan, functools.partial(forward_hop, hop))

        @pl.when(index == 0)
        def _():
            in_order()

        @pl.when(index == LAG - 1)
        def _():
            own.wait()

        pair = index - ARRIVE

        @pl.when((pair >= 0) & (pair < 3 * heads // 2))
        def _():
            pair_copy(2 * pair, pair % 2).start()

        @pl.when(pair == 0)
        def _():
            one_copy(rare, 0).start()
            one_copy(rarer, 1).start()

        @pl.when((pair >= 1) & (pair <= 3 * heads // 2))
        def _():
            done = pair - 1
            pair_copy(0, done % 2).wait()
            lanes = pl.ds(pl.multiple_of(done * 2 * LANES, 2 * LANES), 2 * LANES)
            project(stage_pair[done % 2].reshape(D, 2 * LANES), lanes)

        @pl.when(pair == 1)
        def _():
            one_copy(0, 0).wait()
            one_copy(0, 1).wait()
            project(stage_one[0].reshape(D, LANES), pl.ds((3 * heads - 1) * LANES, LANES))
            small_vectors()

        @pl.when(pair == 2)
        def _():
            turn(tokens_in)
            result(6).start()

        @pl.when(index == units_at + 1)
        def _():
            result(6).wait()
            turn(first_low)
            result(7).start()

        @pl.when(index == attend_at)
        def _():
            result(1).start()
            for copy in outward_copies():
                copy.start()

        @pl.when((index >= attend_at) & (index < branch_at))
        def _():
            for k in range(pairs_each):
                attend_one((index - attend_at) * pairs_each + k)

        @pl.when(index == branch_at)
        def _():
            result(2).start()
            for copy in outward_copies():
                copy.wait()
            branch()

        @pl.when(index == branch_at + 1)
        def _():
            norms()

        unit = index - units_at

        @pl.when((unit >= -1) & (unit < units - 1))
        def _():
            fetch_unit(unit + 1)

        @pl.when((unit >= 0) & (unit < units))
        def _():
            one_unit(unit)

        return 0

    lax.fori_loop(0, max(steps_of(plan, 4), units_at + units), step, 0)
    for unit in (units - 2, units - 1):
        proj_copy(unit).wait()
        hidden_copy(unit).wait()
    for k in range(len(result_pairs)):
        if k != 6:
            result(k).wait()
    for route, (_, _, number, _) in enumerate(plan):
        for tile in range(max(0, number - RING), number):
            for hop in range(4):
                piece(hop, route, tile).wait_send()


def forward_pass(block, tokens, place_row, bias, collective_id):
    plan = forward_plan()
    rows, columns = block.shape
    count = tokens.shape[0]
    own = count // 2
    heads = head_tiles() * LANES
    units = unit_tiles() * LANES
    most = max(number for _, _, number, _ in plan)
    place = (2, 2, 2, 2, rows)
    hbm = pl.BlockSpec(memory_space=pl.ANY)
    vmem = pl.BlockSpec(memory_space=pltpu.VMEM)
    dma = pltpu.SemaphoreType.DMA
    return pl.pallas_call(
        functools.partial(forward_kernel, plan),
        out_shape=[
            jax.ShapeDtypeStruct((*place, columns), BF16),
            jax.ShapeDtypeStruct((count, D), BF16),
            jax.ShapeDtypeStruct((count, 3 * heads), F32),
            jax.ShapeDtypeStruct((count, heads), BF16),
            jax.ShapeDtypeStruct((own, D), F32),
            jax.ShapeDtypeStruct((own, D), F32),
            jax.ShapeDtypeStruct((count, D), BF16),
            jax.ShapeDtypeStruct((D, count), BF16),
            jax.ShapeDtypeStruct((D, count), BF16),
            jax.ShapeDtypeStruct((count, 2 * units), F32),
            jax.ShapeDtypeStruct((count, units), BF16),
            jax.ShapeDtypeStruct((own, 2 * LANES), F32),
            jax.ShapeDtypeStruct((8, D), F32),
            jax.ShapeDtypeStruct((16, D), F32),
            jax.ShapeDtypeStruct((8, units), F32),
            jax.ShapeDtypeStruct((count, D), F32),
        ],
        in_specs=[vmem] * 4,
        out_specs=[hbm] * 11 + [vmem] * 5,
        scratch_shapes=[
            pltpu.VMEM((D, D), BF16),
            pltpu.VMEM((count, D), BF16),
            pltpu.VMEM((count, 3 * heads), F32),
            pltpu.VMEM((2, *place, 2 * LANES), BF16),
            pltpu.VMEM((2, *place, LANES), BF16),
            pltpu.VMEM((*place, heads), BF16),
            pltpu.VMEM((count, heads), BF16),
            pltpu.VMEM((own, D), F32),
            pltpu.VMEM((own, D), F32),
            pltpu.VMEM((own, D), F32),
            pltpu.VMEM((count, D), BF16),
            pltpu.VMEM((2, count, 2 * LANES), F32),
            pltpu.VMEM((2, count, LANES), BF16),
            dma,
            dma((4, 4, RING)),
            dma((4, 4, most)),
            dma((2,)),
            dma((2,)),
            dma((4,)),
            dma((2,)),
            dma((2,)),
            dma((8,)),
            dma((2,)),
            dma((2,)),
        ],
        compiler_params=pltpu.CompilerParams(
            collective_id=collective_id, has_side_effects=True, vmem_limit_bytes=60 << 20
        ),
        name="forward_pass",
    )(block, tokens, place_row, bias)


SLOTS = 2 * RING + 4


def backward_plan():
    return tile_plan((4 * head_tiles() + 3 * unit_tiles()) * LANES)


def slot_of(route, tile):
    if route < 2:
        return route * RING + tile % RING
    return 2 * RING + (route - 2) * 2 + tile % 2


def ring_of(route):
    return RING if route < 2 else 2


def backward_kernel(
    plan,
    copies,
    d_shrunk,
    d_shrunk_turned,
    first_turned,
    tokens_turned,
    hidden,
    proj,
    raw,
    mixed,
    d_two,
    h_attn,
    first,
    tokens_in,
    factors,
    alphas,
    scales,
    gains,
    bias,
    d_raw_out,
    d_one_out,
    grads,
    alpha_grad,
    unit_grad,
    query_grad,
    work,
    arrived,
    lefts,
    d_low,
    d_proj,
    first_part,
    core_in,
    stage_hidden,
    stage_rows,
    wide,
    outward,
    right,
    sum_k,
    sum_v,
    send_sem,
    recv_sem,
    load_sem,
    unit_sem,
    raw_sem,
    result_sem,
    core_send,
    core_recv,
):
    me = lax.axis_index("dp")
    core = lax.axis_index("tensor")
    inv_root = D ** (-0.5)
    rows = tokens_in.shape[0]
    own_rows = rows // 2
    own_at = pl.multiple_of(core * own_rows, own_rows)
    other_at = pl.multiple_of((1 - core) * own_rows, own_rows)
    heads = head_tiles()
    units = unit_tiles()
    block = D // 16
    unit_steps = units // 2
    shrink_steps = unit_steps - 1
    late_units = units // 4
    expand_steps = units - late_units
    attention_at = shrink_steps + expand_steps
    rare_units = 1 + late_units
    exchange_at = unit_steps
    attend_at = exchange_at + 3
    sequences = bias.shape[0]
    length = bias.shape[1]
    head_pairs = sequences * heads

    greet(me, core)

    def copy(source, target, sem):
        return pltpu.make_async_copy(source, target, sem)

    def chunks(total, size, body):
        def one(k, _):
            body(pl.ds(pl.multiple_of(k * size, size), size))
            return 0

        lax.fori_loop(0, total // size, one, 0)


    def piece(hop, route, tile):
        axis = ROUTES[route][3 - hop]
        slot = slot_of(route, tile)
        return pltpu.make_async_remote_copy(
            src_ref=work[hop].at[slot, 1],
            dst_ref=arrived[hop].at[slot],
            send_sem=send_sem.at[hop, slot],
            recv_sem=recv_sem.at[hop, slot],
            device_id={"dp": partner_of(me, PLACES[axis])},
            device_id_type=pl.DeviceIdType.MESH,
        )

    def free(hop, route, tile):
        @pl.when(tile >= ring_of(route))
        def _():
            piece(hop, route, tile - ring_of(route)).wait_send()

    def add(hop, route, tile):
        piece(hop - 1, route, tile).wait_recv()
        slot = slot_of(route, tile)
        total = work[hop - 1][slot, 0].astype(F32) + arrived[hop - 1][slot].astype(F32)
        if hop == 4:
            grads[:, lanes_of(plan, route, tile)] = total
            return
        half = total.shape[0] // 2
        free(hop, route, tile)
        work[hop][slot, 0] = total[:half].astype(BF16)
        work[hop][slot, 1] = total[half:].astype(BF16)
        piece(hop, route, tile).start()

    def keep_quarter(route, slot, quarter, part):
        axes = ROUTES[route][::-1]
        if route < 2:
            bits = [quarter >> 1, quarter & 1]
            at = bits[axes[1]] * 4 * block
            work[0][slot, bits[axes[0]], at : at + 4 * block, :] = part
            return
        for low in range(4):
            bits = [quarter >> 1, quarter & 1, low >> 1, low & 1]
            index = bits[axes[1]] * 4 + bits[axes[2]] * 2 + bits[axes[3]]
            work[0][slot, bits[axes[0]], index * block : (index + 1) * block, :] = part[
                low * block : (low + 1) * block
            ]

    def quarter_rows(quarter):
        return slice(quarter * 4 * block, (quarter + 1) * 4 * block)

    def often_product(tile):
        for route in (0, 1):
            free(0, route, tile)
        is_shrink = tile < shrink_steps
        is_expand = (tile >= shrink_steps) & (tile < attention_at)
        late = tile - attention_at
        is_outward = (late >= 0) & (late < 2)

        @pl.when(is_shrink)
        def _():
            right[0] = stage_hidden[tile % 2]

        @pl.when(is_expand)
        def _():
            unit = tile - shrink_steps + late_units
            right[0] = d_proj[:, pl.ds(pl.multiple_of(unit * 2 * LANES, 2 * LANES), 2 * LANES)]

        @pl.when(late >= 0)
        def _():
            first_tile = jnp.where(late < 2, 2 * late, 2 * late + 1)
            right[0] = wide[:rows, pl.ds(pl.multiple_of(first_tile * LANES, LANES), 2 * LANES)]

        which = jnp.where(is_expand | is_outward, 1, 0)
        scale = jnp.where(is_shrink | is_outward, 1.0, inv_root)
        for quarter in range(4):
            part = (nn(lefts[which, quarter_rows(quarter), :], right[0]) * scale).astype(BF16)
            for route in (0, 1):
                keep_quarter(
                    route, slot_of(route, tile), quarter, part[:, route * LANES : (route + 1) * LANES]
                )
        for route in (0, 1):
            piece(0, route, tile).start()

    def rare_product(tile):
        late = tile - rare_units

        @pl.when(tile == 0)
        def _():
            right[1] = stage_hidden[2]

        @pl.when((tile > 0) & (late < 0))
        def _():
            lanes = pl.ds(pl.multiple_of((tile - 1) * 2 * LANES, 2 * LANES), 2 * LANES)
            right[1] = d_proj[:, lanes]

        @pl.when(late == 0)
        def _():
            right[1, :, :LANES] = wide[:rows, (heads - 1) * LANES : heads * LANES]
            right[1, :, LANES:] = wide[:rows, (heads + 12) * LANES : (heads + 13) * LANES]

        @pl.when(late == 1)
        def _():
            right[1] = wide[:rows, (heads + 13) * LANES : (heads + 15) * LANES]

        for route in (2, 3):
            free(0, route, tile)
            of_units = (tile > 0) & (late < 0)
            of_outward = (late == 0) if route == 2 else (late < -rare_units)
            which = jnp.where(of_units | of_outward, 1, 0)
            scale = jnp.where((tile == 0) | of_outward, 1.0, inv_root)
            at = (route - 2) * LANES
            for quarter in range(4):
                part = nn(lefts[which, quarter_rows(quarter), :], right[1, :, at : at + LANES])
                keep_quarter(route, slot_of(route, tile), quarter, (part * scale).astype(BF16))
            piece(0, route, tile).start()


    def unit_copies(pair):
        slot = pair % 2
        unit = 2 * pair
        at = pl.multiple_of(slot * 6 * LANES, 2 * LANES)
        result = [
            (
                copies.at[:, pl.ds(pl.multiple_of(pair_tile(unit) * LANES, LANES), 4 * LANES)],
                wide.at[:, pl.ds(at, 4 * LANES)],
            )
        ]
        for k in range(2):
            tile = shrink_tile(unit + k)
            result.append(
                (
                    copies.at[:, pl.ds(pl.multiple_of(tile * LANES, LANES), LANES)],
                    wide.at[:, pl.ds(pl.multiple_of(at + (4 + k) * LANES, LANES), LANES)],
                )
            )
        lanes = pl.ds(pl.multiple_of(pair * 4 * LANES, 4 * LANES), 4 * LANES)
        for k in range(2):
            result.append(
                (
                    proj.at[pl.ds(k * own_rows, own_rows), lanes],
                    stage_rows.at[slot, :, pl.ds(k * 4 * LANES, 4 * LANES)],
                )
            )
        return [copy(source, target, unit_sem.at[k, slot]) for k, (source, target) in enumerate(result)]

    def hidden_copy(tile):
        lanes = pl.ds(pl.multiple_of((2 * tile + 2) * LANES, 2 * LANES), 2 * LANES)
        return copy(hidden.at[:, lanes], stage_hidden.at[tile % 2], unit_sem.at[5, tile % 2])

    def unit_pair(pair):
        slot = pair % 2
        for part in unit_copies(pair):
            part.wait()
        at = pl.multiple_of(slot * 6 * LANES, 2 * LANES)
        expand = wide[:, pl.ds(at, 4 * LANES)]
        down = wide[:, pl.ds(pl.multiple_of(at + 4 * LANES, 2 * LANES), 2 * LANES)]

        def some(row_at, row_from, proj_lanes):
            d_hidden = nn(d_low[row_at, :], down)
            for k in range(2):
                lanes = pl.ds(pl.multiple_of((2 * pair + k) * LANES, LANES), LANES)
                gain_up, gain_gate = gains[0:1, lanes], gains[1:2, lanes]
                start = proj_lanes + 2 * k * LANES
                proj_up = stage_rows[slot, row_from, start : start + LANES]
                proj_gate = stage_rows[slot, row_from, start + LANES : start + 2 * LANES]
                upstream = d_hidden[:, k * LANES : (k + 1) * LANES]
                gate = gain_gate * proj_gate
                sigmoid = jax.nn.sigmoid(gate)
                d_up = upstream * (gate * sigmoid)
                d_gate = upstream * (gain_up * proj_up) * sigmoid * (1.0 + gate * (1.0 - sigmoid))
                unit_grad[0:1, lanes] += jnp.sum(d_up * proj_up, axis=0, keepdims=True)
                unit_grad[1:2, lanes] += jnp.sum(d_gate * proj_gate, axis=0, keepdims=True)
                at = pl.multiple_of((2 * pair + k) * 2 * LANES, 2 * LANES)
                d_proj[row_at, pl.ds(at, LANES)] = (d_up * gain_up).astype(BF16)
                d_proj[row_at, pl.ds(pl.multiple_of(at + LANES, LANES), LANES)] = (
                    d_gate * gain_gate
                ).astype(BF16)
            lanes = pl.ds(pl.multiple_of(pair * 4 * LANES, 4 * LANES), 4 * LANES)
            first_part[row_at, :] += nt(d_proj[row_at, lanes], expand)

        size = own_rows // 2
        for half in range(2):

            def one(k, _, half=half):
                row_from = pl.multiple_of(k * size, size)
                row_at = pl.multiple_of(half * own_rows + row_from, size)
                some(pl.ds(row_at, size), pl.ds(row_from, size), half * 4 * LANES)
                return 0

            lax.fori_loop(0, 2, one, 0)


    def core_copy(source, target, which):
        return pltpu.make_async_remote_copy(
            src_ref=source,
            dst_ref=target,
            send_sem=core_send.at[which],
            recv_sem=core_recv.at[which],
            device_id={"tensor": 1 - core},
            device_id_type=pl.DeviceIdType.MESH,
        )

    def part_copy():
        return core_copy(first_part.at[pl.ds(other_at, own_rows)], core_in, 0)

    def branch_copy():
        own = d_low.at[pl.ds(own_at, own_rows)]
        return core_copy(own, own, 1)

    tokens_place = wide.at[pl.ds(0, own_rows), pl.ds(D, D)]
    rare, rarer = forward_plan()[2][0], forward_plan()[3][0]
    outward_tiles = ((rare + 1, 1, 0), (rarer + 1, 1, 1), (3 * heads - 1, 2, 2), (rare + 2, 1, 4))

    def load(k):
        if k == 0:
            return copy(d_two, stage_rows.at[0], load_sem.at[0])
        if k == 1:
            return copy(h_attn, stage_rows.at[1], load_sem.at[1])
        if k == 2:
            return copy(tokens_in.at[pl.ds(own_at, own_rows)], tokens_place, load_sem.at[2])
        if k == 3:
            return copy(
                mixed, wide.at[pl.ds(0, rows), pl.ds(0, heads * LANES)], load_sem.at[3]
            )
        if k == 4:
            return copy(first, first_part.at[pl.ds(other_at, own_rows)], load_sem.at[4])
        if k == 5:
            return copy(d_shrunk, d_low, load_sem.at[5])
        if k == 6:
            return copy(d_shrunk_turned, lefts.at[0], load_sem.at[6])
        if k == 7:
            return copy(first_turned, lefts.at[1], load_sem.at[7])
        if k == 8:
            return copy(tokens_turned, lefts.at[0], load_sem.at[8])
        if k == 9:
            return copy(hidden.at[:, pl.ds(0, 2 * LANES)], stage_hidden.at[2], load_sem.at[9])
        tile, width, at = outward_tiles[k - 10]
        return copy(
            copies.at[:, pl.ds(tile * LANES, width * LANES)],
            outward.at[:, pl.ds(at * LANES, width * LANES)],
            load_sem.at[k],
        )

    def branch_gradient():
        part_copy().wait_send()
        load(4).start()
        part_copy().wait_recv()
        for k in (0, 1, 2, 4):
            load(k).wait()
        alpha_attn, alpha_mlp = alphas[0:1, :], alphas[1:2, :]

        def some(at):
            here = pl.ds(pl.multiple_of(own_at + at.start, 64), 64)
            there = pl.ds(pl.multiple_of(other_at + at.start, 64), 64)
            part = (first_part[here, :] + core_in[at, :]) * inv_root
            d_first = (1.0 - alpha_mlp) * stage_rows[0, at, :] + part
            normed = stage_rows[1, at, :]
            d_one = row_norm_back(
                d_first, first_part[there, :], factors[at, LANES : LANES + 1]
            )
            inputs = wide[at, D : 2 * D].astype(F32)
            alpha_grad[0:1, :] += jnp.sum(d_one * (normed - inputs), axis=0, keepdims=True)
            stage_rows[0, at, :] = d_one
            d_low[here, :] = row_norm_back(alpha_attn * d_one, normed, factors[at, 0:1]).astype(
                BF16
            )

        chunks(own_rows, 64, some)
        branch_copy().start()
        copy(stage_rows.at[0], d_one_out, result_sem.at[0]).start()


    def raw_copies(number):
        sequence, head = number // heads, number % heads
        at = pl.ds(pl.multiple_of(sequence * length, length), length)
        slot = number % 2
        target_rows = pl.ds(pl.multiple_of(slot * own_rows, own_rows), length)
        return [
            copy(
                raw.at[at, pl.ds(pl.multiple_of((k * heads + head) * LANES, LANES), LANES)],
                first_part.at[target_rows, pl.ds(k * LANES, LANES)],
                raw_sem.at[k, slot],
            )
            for k in range(3)
        ]

    def attend_one(number):
        sequence, head = number // heads, number % heads
        for part in raw_copies(number):
            part.wait()
        at = pl.ds(pl.multiple_of(sequence * length, length), length)
        source_rows = pl.ds(pl.multiple_of((number % 2) * own_rows, own_rows), length)
        head_lanes = pl.ds(pl.multiple_of(head * LANES, LANES), LANES)
        gain_lanes = pl.ds(pl.multiple_of((core * heads + head) * LANES, LANES), LANES)
        d_mixed = nn(d_low[at, :], outward[:, head_lanes]).astype(BF16)
        targets = [
            wide.at[at, pl.ds(pl.multiple_of(((k + 1) * heads + head) * LANES, LANES), LANES)]
            for k in range(3)
        ]
        total = attend_pair_back(
            *[first_part.at[source_rows, pl.ds(k * LANES, LANES)] for k in range(3)],
            d_mixed,
            scales[2:3, gain_lanes],
            bias.at[sequence],
            *targets,
            sum_k,
            sum_v,
        )
        query_grad[0:1, head_lanes] += total

    def d_raw_copy():
        return copy(
            wide.at[pl.ds(0, rows), pl.ds(heads * LANES, 3 * heads * LANES)],
            d_raw_out,
            result_sem.at[1],
        )


    for k in (5, 6, 9, 7):
        load(k).start()
    for part in unit_copies(0):
        part.start()
    hidden_copy(0).start()
    alpha_grad[...] = jnp.zeros_like(alpha_grad)
    unit_grad[...] = jnp.zeros_like(unit_grad)
    query_grad[...] = jnp.zeros_like(query_grad)
    first_part[...] = jnp.zeros_like(first_part)
    for k in (5, 6, 9, 7):
        load(k).wait()

    def step(index, _):
        for hop in range(4, 0, -1):
            for_tiles(index, hop, plan, functools.partial(add, hop))

        @pl.when(index < shrink_steps)
        def _():
            hidden_copy(index).wait()

        @pl.when(index == attention_at)
        def _():
            load(8).wait()
            chunks(rows, LANES, turn)

        @pl.when(index < plan[0][2])
        def _():
            often_product(index)

        @pl.when((index % EVERY == 0) & (index < plan[2][2] * EVERY))
        def _():
            rare_product(index // EVERY)

        @pl.when(index + 1 < shrink_steps)
        def _():
            hidden_copy(index + 1).start()

        @pl.when(index + 1 < unit_steps)
        def _():
            for part in unit_copies(index + 1):
                part.start()

        @pl.when(index < unit_steps)
        def _():
            unit_pair(index)

        @pl.when(index == exchange_at)
        def _():
            part_copy().start()
            for k in (0, 1, 2, 3, 8, 10, 11, 12, 13):
                load(k).start()

        @pl.when(index == exchange_at + 1)
        def _():
            branch_gradient()

        @pl.when(index == exchange_at + 2)
        def _():
            branch_copy().wait()
            for k in (3, 10, 11, 12, 13):
                load(k).wait()

        number = index - attend_at

        @pl.when((number >= -1) & (number < head_pairs - 1))
        def _():
            for part in raw_copies(number + 1):
                part.start()

        @pl.when((number >= 0) & (number < head_pairs))
        def _():
            attend_one(number)

        @pl.when(number == head_pairs)
        def _():
            d_raw_copy().start()

        return 0

    def turn(at):
        lefts[1, :, at] = d_low[at, :].astype(F32).T.astype(BF16)

    lax.fori_loop(0, steps_of(plan, 4), step, 0)
    copy(stage_rows.at[0], d_one_out, result_sem.at[0]).wait()
    d_raw_copy().wait()
    for route, (_, _, number, _) in enumerate(plan):
        for tile in range(max(0, number - ring_of(route)), number):
            for hop in range(4):
                piece(hop, route, tile).wait_send()


def backward_pass(*operands, collective_id):
    plan = backward_plan()
    copies = operands[0]
    count = operands[1].shape[0]
    own = count // 2
    heads = head_tiles() * LANES
    units = unit_tiles() * LANES
    length = operands[-1].shape[1]
    block = D // 16
    halves = [block * 8 >> hop for hop in range(4)]
    hbm = pl.BlockSpec(memory_space=pl.ANY)
    vmem = pl.BlockSpec(memory_space=pltpu.VMEM)
    dma = pltpu.SemaphoreType.DMA
    return pl.pallas_call(
        functools.partial(backward_kernel, plan),
        out_shape=[
            jax.ShapeDtypeStruct((count, 3 * heads), BF16),
            jax.ShapeDtypeStruct((own, D), F32),
            jax.ShapeDtypeStruct((block, 4 * heads + 3 * units), F32),
            jax.ShapeDtypeStruct((8, D), F32),
            jax.ShapeDtypeStruct((8, units), F32),
            jax.ShapeDtypeStruct((8, heads), F32),
        ],
        in_specs=[hbm] * 13 + [vmem] * 5,
        out_specs=[hbm] * 2 + [vmem] * 4,
        scratch_shapes=[
            [pltpu.VMEM((SLOTS, 2, half, LANES), BF16) for half in halves],
            [pltpu.VMEM((SLOTS, half, LANES), BF16) for half in halves],
            pltpu.VMEM((2, D, count), BF16),
            pltpu.VMEM((count, D), BF16),
            pltpu.VMEM((count, 2 * units), BF16),
            pltpu.VMEM((count, D), F32),
            pltpu.VMEM((own, D), F32),
            pltpu.VMEM((3, count, 2 * LANES), BF16),
            pltpu.VMEM((2, own, D), F32),
            pltpu.VMEM((D, 4 * heads), BF16),
            pltpu.VMEM((D, heads), BF16),
            pltpu.VMEM((2, count, 2 * LANES), BF16),
            pltpu.VMEM((length, LANES), F32),
            pltpu.VMEM((length, LANES), F32),
            dma((4, SLOTS)),
            dma((4, SLOTS)),
            dma((14,)),
            dma((6, 2)),
            dma((3, 2)),
            dma((2,)),
            dma((2,)),
            dma((2,)),
        ],
        compiler_params=pltpu.CompilerParams(
            collective_id=collective_id, has_side_effects=True, vmem_limit_bytes=62 << 20
        ),
        name="backward_pass",
    )(*operands)


def columns_of(grads):
    plan = backward_plan()
    rows = grads.shape[0]
    heads, units = head_tiles(), unit_tiles()
    shrink_steps, late = units // 2 - 1, units // 4
    rare, rarer = plan[2][0], plan[3][0]

    def tiles(start, number):
        return grads[:, start * LANES : (start + number) * LANES]

    attention_at = 2 * (shrink_steps + units - late)
    pairs = tiles(2 * shrink_steps, 2 * (units - late)).reshape(rows, units - late, 2, LANES)
    shrink = jnp.concatenate([tiles(rare, 1), tiles(rarer, 1), tiles(0, 2 * shrink_steps)], axis=1)
    up = jnp.concatenate([tiles(rare + 1, late), pairs[:, :, 0].reshape(rows, -1)], axis=1)
    gate = jnp.concatenate([tiles(rarer + 1, late), pairs[:, :, 1].reshape(rows, -1)], axis=1)
    last = late + 1
    outward = jnp.concatenate([tiles(attention_at, 4), tiles(rare + last, 1)], axis=1)
    inward = jnp.concatenate(
        [
            tiles(attention_at + 4, 12),
            tiles(rarer + last, 1),
            tiles(rare + last + 1, 1),
            tiles(rarer + last + 1, 1),
        ],
        axis=1,
    )
    return inward, outward, up, gate, shrink


def per_device(
    tokens,
    cotangent,
    segment_ids,
    pad_mask,
    inward_master,
    inward_first,
    inward_second,
    outward_master,
    outward_first,
    outward_second,
    expand_master,
    expand_first,
    expand_second,
    shrink_master,
    shrink_first,
    shrink_second,
    alpha_master,
    alpha_first,
    alpha_second,
    scale_master,
    scale_first,
    scale_second,
):
    count = lax.axis_size("dp")
    me = lax.axis_index("dp")
    core = lax.axis_index("tensor")
    inv_root = D ** (-0.5)
    rows = tokens.shape[0]
    own_rows = rows // 2
    heads_width = inward_master.shape[2]
    units = expand_master.shape[2]

    small = jnp.concatenate([alpha_master, scale_master], axis=0).astype(BF16)
    small = jnp.pad(small, ((0, LANES - small.shape[0]), (0, 0))).T
    inward_low = inward_master.astype(BF16)
    block = forward_columns(
        jnp.concatenate([inward_low[0], inward_low[1], inward_low[2]], axis=1),
        outward_master.astype(BF16).T,
        expand_master.astype(BF16),
        shrink_master.astype(BF16).T,
        small,
    )
    block = gather_rest(block, count)
    place_row = place_row_of(me, count)
    bias = bias_of(segment_ids, pad_mask)
    (
        copies,
        tokens_in,
        raw,
        mixed,
        h_attn,
        first,
        first_low,
        tokens_turned,
        first_turned,
        proj,
        hidden,
        factors,
        alphas,
        scale_rows,
        gains,
        shrunk,
    ) = forward_pass(block, tokens, place_row, bias, 0)
    copies = copies.reshape(D, -1)
    attn_factor, first_factor = factors[:, :1], factors[:, LANES : LANES + 1]
    places = place_matrix(place_row)
    cot_own = lax.dynamic_slice_in_dim(cotangent, core * own_rows, own_rows, 0)
    cot_own = nn(cot_own, places)
    keep = (1 - pad_mask).astype(F32).reshape(rows, 1)
    cot_own = cot_own * lax.dynamic_slice_in_dim(keep, core * own_rows, own_rows, 0)
    tokens_own = lax.dynamic_slice_in_dim(tokens_in, core * own_rows, own_rows, 0).astype(F32)
    def sum_own(partial):
        send = lax.dynamic_slice_in_dim(partial, (1 - core) * own_rows, own_rows, 0)
        kept = lax.dynamic_slice_in_dim(partial, core * own_rows, own_rows, 0)
        return kept + swap_cores(send)

    def both(own):
        other = swap_cores(own)
        full = jnp.zeros((rows, own.shape[1]), own.dtype)
        full = lax.dynamic_update_slice_in_dim(full, own, core * own_rows, 0)
        return lax.dynamic_update_slice_in_dim(full, other, (1 - core) * own_rows, 0)

    shrunk = sum_own(shrunk)
    h_mlp, mlp_factor = row_norm(shrunk)
    output, out_factor = row_norm(first + alphas[1] * (h_mlp - first))

    d_two = row_norm_back(cot_own, output, out_factor)
    alpha_mlp_grad = jnp.sum(d_two * (h_mlp - first), axis=0)
    d_shrunk = both(row_norm_back(alphas[1] * d_two, h_mlp, mlp_factor).astype(BF16))
    d_raw, d_one, grads, alpha_attn_grad, unit_grad, query_gain_grad = backward_pass(
        copies,
        d_shrunk,
        d_shrunk.T,
        first_turned,
        tokens_turned,
        hidden,
        proj,
        raw,
        mixed,
        d_two,
        h_attn,
        first,
        tokens_in,
        factors,
        alphas,
        scale_rows,
        gains,
        bias,
        collective_id=1,
    )
    alpha_attn_grad, query_gain_grad = alpha_attn_grad[0], query_gain_grad[0]
    up_gain_grad, gate_gain_grad = unit_grad[0], unit_grad[1]
    grads = scatter_rest(grads, count)
    inward_grad, outward_grad, up_grad, gate_grad, shrink_grad = columns_of(grads)
    last = forward_plan()[2][0]
    w_inward = jnp.concatenate(
        [copies[:, : 3 * heads_width - LANES], copies[:, last * LANES : (last + 1) * LANES]], axis=1
    )
    input_part = nt(d_raw, w_inward) * inv_root

    block_output = both(nt(output.astype(BF16), places).astype(BF16))
    residual = (1.0 - alphas[0]) * d_one
    residual_high = residual.astype(BF16)
    residual_low = (residual - residual_high.astype(F32)).astype(BF16)
    residual = nt(residual_high, places) + nt(residual_low, places)
    own_width = D // lax.axis_size("tensor")
    input_part = nt(input_part.astype(BF16), places)
    input_part = lax.dynamic_update_slice_in_dim(
        input_part,
        lax.dynamic_slice_in_dim(input_part, core * own_rows, own_rows, 0) + residual,
        core * own_rows,
        0,
    )
    input_grad = lax.dynamic_slice_in_dim(input_part, core * own_width, own_width, 1) + swap_cores(
        lax.dynamic_slice_in_dim(input_part, (1 - core) * own_width, own_width, 1)
    )

    alpha_grad = jnp.stack([alpha_attn_grad, alpha_mlp_grad])
    query_full = lax.dynamic_update_slice_in_dim(
        jnp.zeros((D,), F32), query_gain_grad, core * heads_width, 0
    )
    up_full = lax.dynamic_update_slice_in_dim(jnp.zeros((FF,), F32), up_gain_grad, core * units, 0)
    gate_full = lax.dynamic_update_slice_in_dim(
        jnp.zeros((FF,), F32), gate_gain_grad, core * units, 0
    )
    scale_grad = jnp.concatenate(
        [query_full.reshape(1, D), up_full.reshape(FF // D, D), gate_full.reshape(FF // D, D)],
        axis=0,
    )
    alpha_grad = alpha_grad + swap_cores(alpha_grad)
    scale_grad = scale_grad + swap_cores(scale_grad)
    width = D // count
    alpha_grad = scatter_sum(alpha_grad.T, count).T
    scale_grad = lax.dynamic_slice_in_dim(butterfly_sum(scale_grad, count), me * width, width, 1)

    outward_grad = outward_grad.T
    shrink_grad = shrink_grad.T
    expand_grad = jnp.stack([up_grad, gate_grad])
    inward_grad = jnp.stack(
        [inward_grad[:, k * heads_width : (k + 1) * heads_width] for k in range(3)]
    )
    inward_pre, inward_var = adam_step(
        inward_master, inward_first, inward_second, inward_grad, RATE_MATRIX
    )
    outward_pre, outward_var = adam_step(
        outward_master, outward_first, outward_second, outward_grad, RATE_MATRIX
    )
    expand_pre, expand_var = adam_step(
        expand_master, expand_first, expand_second, expand_grad, RATE_MATRIX
    )
    shrink_pre, shrink_var = adam_step(
        shrink_master, shrink_first, shrink_second, shrink_grad, RATE_MATRIX
    )
    alpha_new, alpha_var = adam_step(
        alpha_master, alpha_first, alpha_second, alpha_grad, RATE_ALPHA
    )
    scale_new, scale_var = adam_step(
        scale_master, scale_first, scale_second, scale_grad, RATE_SCALE
    )

    def renormed(pre, axis):
        squares = butterfly_sum(jnp.sum(pre * pre, axis=axis), count)
        return pre * lax.rsqrt(jnp.expand_dims(squares, axis) / D + EPS_NORM)

    return (
        block_output,
        input_grad,
        inward_grad,
        inward_var,
        renormed(inward_pre, 1),
        outward_grad,
        outward_var,
        renormed(outward_pre, 1),
        expand_grad,
        expand_var,
        renormed(expand_pre, 1),
        shrink_grad,
        shrink_var,
        renormed(shrink_pre, 1),
        alpha_grad,
        alpha_var,
        alpha_new,
        scale_grad,
        scale_var,
        scale_new,
    )


def solution(mesh):
    rows = P("dp", None)
    deep = P(None, "dp", "tensor")
    flat = P("tensor", "dp")
    vector = P(None, "dp")
    in_specs = (rows,) * 4 + (deep,) * 3 + (flat,) * 3 + (deep,) * 3 + (flat,) * 3 + (vector,) * 6
    out_specs = (
        (rows, P("dp", "tensor"))
        + (deep,) * 3
        + (flat,) * 3
        + (deep,) * 3
        + (flat,) * 3
        + (vector,) * 6
    )
    return jax.shard_map(
        per_device, mesh=mesh, in_specs=in_specs, out_specs=out_specs, check_vma=False
    )
```

```python
import functools

import jax
import jax.numpy as jnp
import numpy as np
from jax import lax
from jax.experimental import pallas as pl
from jax.experimental.pallas import tpu as pltpu
from jax.sharding import PartitionSpec as P

D = 1280
HEADS = 20
HD = 64
FF = 5120
STEP = 10
LONGEST = 256


EPS_NORM = 1e-06
BETA_ONE = 0.9
BETA_TWO = 0.95
ADAM_EPS = 1e-08
RATE_MATRIX = 0.3
RATE_ALPHA = 0.08
RATE_SCALE = 0.25
MASKED = -1e30
F32 = jnp.float32
BF16 = jnp.bfloat16


def row_norm(values):
    factor = lax.rsqrt(jnp.mean(values * values, axis=-1, keepdims=True) + EPS_NORM)
    return (values * factor, factor)


def row_norm_back(upstream, normed, factor):
    return factor * (upstream - normed * jnp.mean(upstream * normed, axis=-1, keepdims=True))


def adam_step(master, first_moment, second_moment, gradient, rate):
    first_new = BETA_ONE * first_moment.astype(F32) + (1.0 - BETA_ONE) * gradient
    second_new = BETA_TWO * second_moment + (1.0 - BETA_TWO) * gradient * gradient
    ratio = (
        first_new
        / (1.0 - BETA_ONE**STEP)
        / (jnp.sqrt(second_new / (1.0 - BETA_TWO**STEP)) + ADAM_EPS)
    )
    return (master - rate * ratio, second_new)


LANES = 128
PLACES = (2, 1, 4, 8)
ROUTES = ((3, 2, 1, 0), (3, 2, 0, 1), (1, 0, 3, 2), (0, 1, 3, 2))
EVERY = 4
LAG = 2
RING = 4


def partner_of(me, bit):
    return me + bit - 2 * bit * ((me // bit) % 2)


def greet(me, core=None):
    barrier = pltpu.get_barrier_semaphore()
    partners = [{"dp": partner_of(me, bit)} for bit in PLACES]
    if core is not None:
        partners.append({"tensor": 1 - core})
    for partner in partners:
        pl.semaphore_signal(
            barrier, inc=1, device_id=partner, device_id_type=pl.DeviceIdType.MESH
        )
    pl.semaphore_wait(barrier, len(partners))


def tile_plan(columns):
    tiles = columns // LANES
    rare = tiles // 10
    often = (tiles - 2 * rare) // 2
    return (
        (0, 2, often, 1),
        (1, 2, often, 1),
        (2 * often, 1, rare, EVERY),
        (2 * often + rare, 1, rare, EVERY),
    )


def for_tiles(step, hop, plan, body):
    for route, (_, _, number, every) in enumerate(plan):
        if number == 0:
            continue
        at = step - hop * LAG
        due = (at >= 0) & (at < number * every)
        if every > 1:
            due = due & (at % every == 0)

        @pl.when(due)
        def _():
            body(route, at // every)


def lanes_of(plan, route, tile):
    first, stride, _, _ = plan[route]
    return pl.ds(pl.multiple_of((first + stride * tile) * LANES, LANES), LANES)


def steps_of(plan, hops):
    return max((number - 1) * every + 1 for _, _, number, every in plan if number) + hops * LAG


def extra_bits(count):
    return [bit for bit in (1 << k for k in range(4, count.bit_length() - 1))]


def exchange(array, bit, count):
    return lax.ppermute(array, "dp", [(i, i ^ bit) for i in range(count)])


def gather_rest(block, count):
    for bit in extra_bits(count)[::-1]:
        block = jnp.concatenate([block, exchange(block, bit, count)], axis=-2)
    return block


def scatter_rest(partial, count):
    for bit in extra_bits(count):
        half = partial.shape[0] // 2
        partial = partial[:half] + exchange(partial[half:], bit, count)
    return partial


def place_row_of(me, count):
    places = list(PLACES) + extra_bits(count)
    width = D // count
    placed = np.arange(D, dtype=np.int32)
    position, offset = placed // width, placed % width
    relative = np.zeros_like(position)
    for axis, bit in enumerate(places):
        relative = relative + ((position >> (len(places) - 1 - axis)) & 1) * bit
    return ((jnp.asarray(relative) ^ me) * width + jnp.asarray(offset))[None]


def nn(a, b):
    return lax.dot_general(a, b, (((1,), (0,)), ((), ())), preferred_element_type=F32)


def nt(a, b):
    return lax.dot_general(a, b, (((1,), (1,)), ((), ())), preferred_element_type=F32)


def tn(a, b):
    return lax.dot_general(a, b, (((0,), (0,)), ((), ())), preferred_element_type=F32)


def head_factors(raw, low_lanes):
    squares = raw * raw
    low = jnp.sum(jnp.where(low_lanes, squares, 0.0), axis=-1, keepdims=True)
    high = jnp.sum(jnp.where(low_lanes, 0.0, squares), axis=-1, keepdims=True)
    return jnp.where(low_lanes, lax.rsqrt(low + EPS_NORM), lax.rsqrt(high + EPS_NORM))


def head_sums(values, low_lanes):
    low = jnp.sum(jnp.where(low_lanes, values, 0.0), axis=-1, keepdims=True)
    high = jnp.sum(jnp.where(low_lanes, 0.0, values), axis=-1, keepdims=True)
    return jnp.where(low_lanes, low, high)


Q_TILE = 128


def key_range(tile):
    start = max(0, tile * Q_TILE - LONGEST)
    return start, (tile + 1) * Q_TILE


def attend_pair(query, key, value, gain, bias, mixed):
    length = query.shape[0]
    low_lanes = lax.broadcasted_iota(jnp.int32, (1, 2 * HD), 1) < HD
    query = (gain * (query * head_factors(query, low_lanes))).astype(BF16) * 8
    key = (gain * (key * head_factors(key, low_lanes))).astype(BF16)
    value = value.astype(BF16)
    zero = jnp.zeros_like(query)
    parts = (jnp.where(low_lanes, query, zero), jnp.where(low_lanes, zero, query))
    for tile in range(length // Q_TILE):
        start, end = key_range(tile)
        rows = slice(tile * Q_TILE, (tile + 1) * Q_TILE)
        tile_bias = bias[rows, start:end]
        results = []
        for part in parts:
            expo = jnp.exp(nt(part[rows], key[start:end]) + tile_bias)
            total = jnp.sum(expo, axis=-1, keepdims=True)
            results.append(nn(expo.astype(BF16), value[start:end]) * (1.0 / total))
        mixed[rows, :] = jnp.where(low_lanes, results[0], results[1]).astype(BF16)


def attend_pair_back(
    raw_q, raw_k, raw_v, d_mixed, gains, bias, d_raw_q, d_raw_k, d_raw_v, sum_k, sum_v
):
    length = raw_q.shape[0]
    low_lanes = lax.broadcasted_iota(jnp.int32, (1, 2 * HD), 1) < HD
    key_raw = raw_k[...]
    key_factor = head_factors(key_raw, low_lanes)
    key_unit = key_raw * key_factor
    key = (gains * key_unit).astype(BF16)
    key_eight = key * 8
    value = raw_v[...].astype(BF16)
    sum_k[...] = jnp.zeros_like(sum_k)
    sum_v[...] = jnp.zeros_like(sum_v)
    gain_total = jnp.zeros((1, 2 * HD), F32)

    def back(upstream, unit, factor):
        scaled = gains * upstream
        return (factor * (scaled - unit * head_sums(scaled * unit, low_lanes))).astype(BF16)

    for tile in range(length // Q_TILE):
        start, end = key_range(tile)
        rows = slice(tile * Q_TILE, (tile + 1) * Q_TILE)
        query_raw = raw_q[rows, :]
        query_factor = head_factors(query_raw, low_lanes)
        query_unit = query_raw * query_factor
        query = (gains * query_unit).astype(BF16) * 8
        upstream = d_mixed[rows].astype(F32)
        tile_bias = bias[rows, start:end]
        d_query = []
        for low in (True, False):
            lanes = low_lanes if low else jnp.logical_not(low_lanes)
            own_query = jnp.where(lanes, query, jnp.zeros_like(query))
            expo = jnp.exp(nt(own_query, key[start:end]) + tile_bias)
            inverse = 1.0 / jnp.sum(expo, axis=-1, keepdims=True)
            expo_low = expo.astype(BF16)
            result = nn(expo_low, value[start:end]) * inverse
            own_up = jnp.where(lanes, upstream, 0.0)
            delta = jnp.sum(result * own_up, axis=-1, keepdims=True) * inverse
            own_up = (own_up * inverse).astype(BF16)
            sum_v[start:end, :] += tn(expo_low, own_up)
            d_scores = (expo * (nt(own_up, value[start:end]) - delta)).astype(BF16)
            d_query.append(nn(d_scores, key_eight[start:end]))
            sum_k[start:end, :] += tn(d_scores, own_query)
        d_query = jnp.where(low_lanes, d_query[0], d_query[1])
        gain_total += jnp.sum(d_query * query_unit, axis=0, keepdims=True)
        d_raw_q[rows, :] = back(d_query, query_unit, query_factor)
    d_key = sum_k[...]
    gain_total += jnp.sum(d_key * key_unit, axis=0, keepdims=True)
    d_raw_k[...] = back(d_key, key_unit, key_factor)
    d_raw_v[...] = sum_v[...].astype(BF16)
    return gain_total


ARRIVE = 4 * LAG
UNIT_GROUP = 4
FIRST_UNIT_PAIR = 8
RARE_UNITS = 3


def head_tiles():
    return HEADS * HD // 2 // LANES


def unit_tiles():
    return FF // 2 // LANES


def forward_plan():
    groups = unit_tiles() // UNIT_GROUP
    return tile_plan((2 * (FIRST_UNIT_PAIR + 5 * groups) + 2 * (RARE_UNITS + groups)) * LANES)


def pair_tile(unit):
    return 2 * (FIRST_UNIT_PAIR + 5 * (unit // UNIT_GROUP) + unit % UNIT_GROUP)


def shrink_tile_static(unit):
    plan = forward_plan()
    group, place = unit // UNIT_GROUP, unit % UNIT_GROUP
    if place < 2:
        return plan[2][0] + place * plan[2][2] + RARE_UNITS + group
    return 2 * (FIRST_UNIT_PAIR + 5 * group + UNIT_GROUP) + place - 2


def shrink_tile(unit):
    plan = forward_plan()
    group, place = unit // UNIT_GROUP, unit % UNIT_GROUP
    rare = plan[2][0] + place * plan[2][2] + RARE_UNITS + group
    often = 2 * (FIRST_UNIT_PAIR + 5 * group + UNIT_GROUP) + place - 2
    return jnp.where(place < 2, rare, often)


def forward_sources():
    plan = forward_plan()
    heads, units = head_tiles(), unit_tiles()
    rare, rarer = plan[2][0], plan[3][0]
    inward = [("inward", k // heads, k % heads) for k in range(3 * heads)]
    sources = dict(enumerate(inward[:-1]))
    sources[rare] = inward[-1]
    sources[rarer] = ("small", None, 0)
    for tile, place in ((rare + 1, 0), (rarer + 1, 1), (3 * heads - 1, 2), (3 * heads, 3), (rare + 2, 4)):
        sources[tile] = ("outward", None, place)
    for unit in range(units):
        sources[pair_tile(unit)] = ("expand", 0, unit)
        sources[pair_tile(unit) + 1] = ("expand", 1, unit)
        sources[shrink_tile_static(unit)] = ("shrink", None, unit)
    return sources


def shrink_tile_static(unit):
    plan = forward_plan()
    group, place = unit // UNIT_GROUP, unit % UNIT_GROUP
    if place < 2:
        return plan[2][0] + place * plan[2][2] + RARE_UNITS + group
    return 2 * (FIRST_UNIT_PAIR + 5 * group + UNIT_GROUP) + place - 2


def forward_kernel(
    plan,
    inward,
    outward,
    expand,
    shrink,
    small_copies,
    tokens,
    cotangent,
    segments,
    pads,
    place_row,
    out,
    tokens_out,
    raw_out,
    mixed_out,
    h_attn_out,
    first_out,
    first_low_out,
    tokens_turned_out,
    first_turned_out,
    bias_out,
    d_two_out,
    output_out,
    d_shrunk_out,
    d_shrunk_turned_out,
    proj_out,
    hidden_out,
    factors,
    alphas,
    scales,
    gains,
    alpha_grad,
    block,
    shrunk,
    place,
    tokens_in,
    cot_in,
    bias,
    raw,
    stage_pair,
    stage_one,
    stage_outward,
    mixed,
    branch_in,
    h_attn,
    first,
    first_low,
    stage_proj,
    stage_hidden,
    own_sem,
    send_sem,
    recv_sem,
    pair_sem,
    one_sem,
    outward_sem,
    proj_sem,
    hidden_sem,
    result_sem,
    core_send,
    core_recv,
):
    me = lax.axis_index("dp")
    core = lax.axis_index("tensor")
    inv_root = D ** (-0.5)
    rows = tokens.shape[0]
    own_rows = rows // 2
    own_at = pl.multiple_of(core * own_rows, own_rows)
    other_at = pl.multiple_of((1 - core) * own_rows, own_rows)
    heads = head_tiles()
    units = unit_tiles()
    attend_at = 3 * heads // 2 + ARRIVE + 1
    pairs_each = 2
    sequences, length = segments.shape
    head_pairs = sequences * heads
    branch_at = attend_at + -(-head_pairs // pairs_each)
    units_at = branch_at + 2

    cot_copy = pltpu.make_async_copy(cotangent.at[pl.ds(own_at, own_rows)], cot_in, result_sem.at[13])
    cot_copy.start()
    operands = {
        "inward": inward,
        "outward": outward,
        "expand": expand,
        "shrink": shrink,
        "small": small_copies,
    }
    for tile, (name, row_block, at) in forward_sources().items():
        source = operands[name] if row_block is None else operands[name].at[row_block]
        block[:, tile * LANES : (tile + 1) * LANES] = source[
            :, at * LANES : (at + 1) * LANES
        ].astype(BF16)
    unused = plan[3][0] + 2
    block[:, unused * LANES : (unused + 1) * LANES] = jnp.zeros((block.shape[0], LANES), BF16)
    own = pltpu.make_async_copy(block, out.at[0, 0, 0, 0], own_sem)
    own.start()
    greet(me, core)

    def piece(hop, route, tile):
        lanes = lanes_of(plan, route, tile)
        crossed, axis = ROUTES[route][:hop], ROUTES[route][hop]
        source = [slice(None) if k in crossed else 0 for k in range(4)]
        target = [1 if k == axis else source[k] for k in range(4)]
        if hop == 0:
            source_ref = block.at[:, lanes]
        else:
            source_ref = out.at[(*source, slice(None), lanes)]
        return pltpu.make_async_remote_copy(
            src_ref=source_ref,
            dst_ref=out.at[(*target, slice(None), lanes)],
            send_sem=send_sem.at[hop, route, tile % RING],
            recv_sem=recv_sem.at[hop, route, tile],
            device_id={"dp": partner_of(me, PLACES[axis])},
            device_id_type=pl.DeviceIdType.MESH,
        )

    def forward_hop(hop, route, tile):
        if hop > 0:
            piece(hop - 1, route, tile).wait_recv()
        if hop < 4:

            @pl.when(tile >= RING)
            def _():
                piece(hop, route, tile - RING).wait_send()

            piece(hop, route, tile).start()

    def staged(tile, width, target, sem):
        lanes = pl.ds(pl.multiple_of(tile * LANES, LANES), width * LANES)
        return pltpu.make_async_copy(out.at[:, :, :, :, :, lanes], target, sem)

    def pair_copy(tile, slot):
        return staged(tile, 2, stage_pair.at[slot], pair_sem.at[slot])

    def one_copy(tile, slot):
        return staged(tile, 1, stage_one.at[slot], one_sem.at[slot])

    rare = plan[2][0]
    rarer = plan[3][0]

    def outward_copies():
        return [
            staged(tile, width, stage_outward.at[:, :, :, :, :, pl.ds(at * LANES, width * LANES)], outward_sem.at[k])
            for k, (tile, width, at) in enumerate(
                ((rare + 1, 1, 0), (rarer + 1, 1, 1), (3 * heads - 1, 2, 2), (rare + 2, 1, 4))
            )
        ]

    def core_copy(source, target, which):
        return pltpu.make_async_remote_copy(
            src_ref=source,
            dst_ref=target,
            send_sem=core_send.at[which],
            recv_sem=core_recv.at[which],
            device_id={"tensor": 1 - core},
            device_id_type=pl.DeviceIdType.MESH,
        )

    def branch_copy():
        return core_copy(shrunk.at[pl.ds(0, own_rows)], branch_in, 0)

    def first_copy():
        return core_copy(
            first_low.at[pl.ds(own_at, own_rows)], first_low.at[pl.ds(own_at, own_rows)], 1
        )

    def shrunk_copy():
        return core_copy(shrunk.at[pl.ds(other_at, own_rows)], branch_in, 2)

    def d_shrunk_copy():
        own = first_low.at[pl.ds(own_at, own_rows)]
        return core_copy(own, own, 3)

    result_pairs = (
        (tokens_in, tokens_out),
        (raw, raw_out),
        (mixed, mixed_out),
        (h_attn, h_attn_out),
        (first, first_out),
        (first_low, first_low_out),
        (place.at[:, pl.ds(0, rows)], tokens_turned_out),
        (place.at[:, pl.ds(0, rows)], first_turned_out),
        (bias, bias_out),
        (h_attn, d_two_out),
        (tokens_in.at[pl.ds(own_at, own_rows)], output_out),
        (first_low, d_shrunk_out),
        (place.at[:, pl.ds(0, rows)], d_shrunk_turned_out),
    )

    def result(k):
        return pltpu.make_async_copy(*result_pairs[k], result_sem.at[k])

    def chunks(total, size, body):
        def one(k, _):
            body(pl.ds(pl.multiple_of(k * size, size), size))
            return 0

        lax.fori_loop(0, total // size, one, 0)

    def in_order():
        natural = place_row[...]

        def fill(at):
            here = lax.broadcasted_iota(jnp.int32, (LANES, D), 0) + at.start
            place[at, :] = jnp.where(here == natural, 1.0, 0.0).astype(BF16)

        chunks(D, LANES, fill)

        def move(at):
            tokens_in[at, :] = nn(tokens[at, :], place[...]).astype(BF16)

        chunks(rows, 256, move)
        result(0).start()

    def cot_in_order():
        cot_copy.wait()

        def move(at):
            cot_in[at, :] = nn(cot_in[at, :], place[...]).astype(BF16)

        chunks(own_rows, 256, move)

    def column_of(row):
        return jnp.broadcast_to(row.astype(F32), (LANES, length)).T

    def make_bias():
        for sequence in range(sequences):
            segment = segments[sequence : sequence + 1, :]
            pad = pads[sequence : sequence + 1, :]
            own_segment = column_of(segment)
            for tile in range(length // LANES):
                lanes = slice(tile * LANES, (tile + 1) * LANES)
                query = lax.broadcasted_iota(jnp.int32, (length, LANES), 0)
                key = lax.broadcasted_iota(jnp.int32, (length, LANES), 1) + tile * LANES
                open_key = jnp.where(pad[:, lanes] == 0, segment[:, lanes], -1).astype(F32)
                allowed = ((own_segment == open_key) & (key <= query)) | (key == query)
                bias[sequence, :, lanes] = jnp.where(allowed, 0.0, MASKED)
        result(8).start()

    def finish():
        shrunk_copy().start()
        result(3).wait()
        keep = jnp.where(
            core == 0, column_of(1 - pads[0:1, :]), column_of(1 - pads[1:2, :])
        )
        stage_proj[0, :own_rows, :LANES] = keep
        alpha = alphas[1:2, :]
        alpha_grad[...] = jnp.zeros_like(alpha_grad)
        shrunk_copy().wait()

        def some(at):
            here = pl.ds(pl.multiple_of(own_at + at.start, 64), 64)
            normed, factor = row_norm(shrunk[here, :] + branch_in[at, :])
            start = first[at, :]
            output, output_factor = row_norm(start + alpha * (normed - start))
            upstream = cot_in[at, :].astype(F32) * stage_proj[0, at, 0:1]
            d_two = row_norm_back(upstream, output, output_factor)
            alpha_grad[0:1, :] += jnp.sum(d_two * (normed - start), axis=0, keepdims=True)
            h_attn[at, :] = d_two
            tokens_in[here, :] = output.astype(BF16)
            first_low[here, :] = row_norm_back(alpha * d_two, normed, factor).astype(BF16)

        chunks(own_rows, 64, some)
        d_shrunk_copy().start()
        result(9).start()
        result(10).start()
        result(7).wait()
        d_shrunk_copy().wait()
        result(11).start()
        turn(first_low)
        result(12).start()
        for k in (9, 10, 11, 12):
            result(k).wait()

    def turn(source):
        def some(at):
            place[:, at] = source[at, :].astype(F32).T.astype(BF16)

        chunks(rows, LANES, some)

    def project(weights, lanes):
        def some(at):
            raw[at, lanes] = nn(tokens_in[at, :], weights) * inv_root

        chunks(rows, 256, some)

    def small_vectors():
        small = stage_one[1].reshape(D, LANES).astype(F32).T
        alphas[...] = small[: alphas.shape[0]]
        scales[...] = nt(small.astype(BF16), place[...])[: scales.shape[0]]
        each = units * LANES // D
        for row in range(2):
            for k in range(each):
                at = 3 + row * 2 * each + k
                gains[row : row + 1, k * D : (k + 1) * D] = jnp.where(
                    core == 0, scales[at : at + 1, :], scales[at + each : at + each + 1, :]
                )

    def attend_one(number):
        sequence, head = number // heads, number % heads
        at = pl.ds(pl.multiple_of(sequence * length, length), length)
        lanes = [
            pl.ds(pl.multiple_of((k * heads + head) * LANES, LANES), LANES) for k in range(3)
        ]
        gain_lanes = pl.ds(pl.multiple_of((core * heads + head) * LANES, LANES), LANES)
        attend_pair(
            raw[at, lanes[0]],
            raw[at, lanes[1]],
            raw[at, lanes[2]],
            scales[2:3, gain_lanes],
            bias.at[sequence],
            mixed.at[at, lanes[0]],
        )

    def branch():
        weights = stage_outward[...].reshape(D, heads * LANES)
        for target, source in ((0, other_at), (own_rows, own_at)):
            for k in range(2):
                half = own_rows // 2
                at = pl.ds(pl.multiple_of(source + k * half, half), half)
                shrunk[pl.ds(target + k * half, half), :] = nt(mixed[at, :], weights)
            if target == 0:
                branch_copy().start()

    def norms():
        branch_copy().wait()
        alpha = alphas[0:1, :]

        def some(at):
            total = shrunk[pl.ds(pl.multiple_of(own_rows + at.start, 64), 64), :] + branch_in[at, :]
            normed, factor = row_norm(total)
            here = pl.ds(pl.multiple_of(own_at + at.start, 64), 64)
            inputs = tokens_in[here, :].astype(F32)
            result, result_factor = row_norm(inputs + alpha * (normed - inputs))
            h_attn[at, :] = normed
            first[at, :] = result
            first_low[here, :] = result.astype(BF16)
            factors[at, :LANES] = jnp.broadcast_to(factor, (64, LANES))
            factors[at, LANES:] = jnp.broadcast_to(result_factor, (64, LANES))

        chunks(own_rows, 64, some)
        first_copy().start()
        for k in (3, 4):
            result(k).start()

    def gain_of(unit, row):
        return gains[row : row + 1, pl.ds(pl.multiple_of(unit * LANES, LANES), LANES)]

    def proj_copy(unit):
        lanes = pl.ds(pl.multiple_of(unit * 2 * LANES, 2 * LANES), 2 * LANES)
        slot = unit % 2
        return pltpu.make_async_copy(stage_proj.at[slot], proj_out.at[:, lanes], proj_sem.at[slot])

    def hidden_copy(unit):
        lanes = pl.ds(pl.multiple_of(unit * LANES, LANES), LANES)
        slot = unit % 2
        return pltpu.make_async_copy(
            stage_hidden.at[slot], hidden_out.at[:, lanes], hidden_sem.at[slot]
        )

    def fetch_unit(unit):
        pair_copy(pair_tile(unit), unit % 2).start()
        one_copy(shrink_tile(unit), unit % 2).start()

    def one_unit(unit):
        slot = unit % 2

        @pl.when(unit == 0)
        def _():
            first_copy().wait()
            result(5).start()
            shrunk[...] = jnp.zeros_like(shrunk)

        @pl.when(unit >= 2)
        def _():
            proj_copy(unit - 2).wait()
            hidden_copy(unit - 2).wait()

        pair_copy(0, slot).wait()
        one_copy(0, slot).wait()
        weights = stage_pair[slot].reshape(D, 2 * LANES)
        down = stage_one[slot].reshape(D, LANES)
        gain_up = gain_of(unit, 0)
        gain_gate = gain_of(unit, 1)

        def some(at):
            proj = nn(first_low[at, :], weights) * inv_root
            stage_proj[slot, at, :] = proj
            gate = gain_gate * proj[:, LANES:]
            hidden = (gain_up * proj[:, :LANES] * (gate * jax.nn.sigmoid(gate))).astype(BF16)
            stage_hidden[slot, at, :] = hidden
            shrunk[at, :] += nt(hidden, down)

        chunks(rows, 256, some)
        proj_copy(unit).start()
        hidden_copy(unit).start()

    def step(index, _):
        for hop in range(5):
            for_tiles(index, hop, plan, functools.partial(forward_hop, hop))

        @pl.when(index == 0)
        def _():
            in_order()

        @pl.when(index == LAG - 1)
        def _():
            own.wait()
            cot_in_order()

        @pl.when(index == LAG)
        def _():
            make_bias()

        pair = index - ARRIVE

        @pl.when((pair >= 0) & (pair < 3 * heads // 2))
        def _():
            pair_copy(2 * pair, pair % 2).start()

        @pl.when(pair == 0)
        def _():
            one_copy(rare, 0).start()
            one_copy(rarer, 1).start()

        @pl.when((pair >= 1) & (pair <= 3 * heads // 2))
        def _():
            done = pair - 1
            pair_copy(0, done % 2).wait()
            lanes = pl.ds(pl.multiple_of(done * 2 * LANES, 2 * LANES), 2 * LANES)
            project(stage_pair[done % 2].reshape(D, 2 * LANES), lanes)

        @pl.when(pair == 1)
        def _():
            one_copy(0, 0).wait()
            one_copy(0, 1).wait()
            project(stage_one[0].reshape(D, LANES), pl.ds((3 * heads - 1) * LANES, LANES))
            small_vectors()

        @pl.when(pair == 2)
        def _():
            turn(tokens_in)
            result(6).start()

        @pl.when(index == units_at + 1)
        def _():
            result(6).wait()
            turn(first_low)
            result(7).start()

        @pl.when(index == attend_at)
        def _():
            result(1).start()
            for copy in outward_copies():
                copy.start()

        @pl.when((index >= attend_at) & (index < branch_at))
        def _():
            for k in range(pairs_each):
                attend_one((index - attend_at) * pairs_each + k)

        @pl.when(index == branch_at)
        def _():
            result(2).start()
            for copy in outward_copies():
                copy.wait()
            branch()

        @pl.when(index == branch_at + 1)
        def _():
            norms()

        unit = index - units_at

        @pl.when((unit >= -1) & (unit < units - 1))
        def _():
            fetch_unit(unit + 1)

        @pl.when((unit >= 0) & (unit < units))
        def _():
            one_unit(unit)

        return 0

    lax.fori_loop(0, max(steps_of(plan, 4), units_at + units), step, 0)
    for unit in (units - 2, units - 1):
        proj_copy(unit).wait()
        hidden_copy(unit).wait()
    for k in (0, 1, 2, 4, 5, 8):
        result(k).wait()
    finish()
    for route, (_, _, number, _) in enumerate(plan):
        for tile in range(max(0, number - RING), number):
            for hop in range(4):
                piece(hop, route, tile).wait_send()


def forward_pass(*operands, collective_id):
    plan = forward_plan()
    rows = operands[1].shape[0]
    count = operands[5].shape[0]
    sequences, length = operands[7].shape
    columns = sum(number for _, _, number, _ in plan) * LANES
    own = count // 2
    heads = head_tiles() * LANES
    units = unit_tiles() * LANES
    most = max(number for _, _, number, _ in plan)
    place = (2, 2, 2, 2, rows)
    hbm = pl.BlockSpec(memory_space=pl.ANY)
    vmem = pl.BlockSpec(memory_space=pltpu.VMEM)
    dma = pltpu.SemaphoreType.DMA
    return pl.pallas_call(
        functools.partial(forward_kernel, plan),
        out_shape=[
            jax.ShapeDtypeStruct((*place, columns), BF16),
            jax.ShapeDtypeStruct((count, D), BF16),
            jax.ShapeDtypeStruct((count, 3 * heads), F32),
            jax.ShapeDtypeStruct((count, heads), BF16),
            jax.ShapeDtypeStruct((own, D), F32),
            jax.ShapeDtypeStruct((own, D), F32),
            jax.ShapeDtypeStruct((count, D), BF16),
            jax.ShapeDtypeStruct((D, count), BF16),
            jax.ShapeDtypeStruct((D, count), BF16),
            jax.ShapeDtypeStruct((sequences, length, length), F32),
            jax.ShapeDtypeStruct((own, D), F32),
            jax.ShapeDtypeStruct((own, D), BF16),
            jax.ShapeDtypeStruct((count, D), BF16),
            jax.ShapeDtypeStruct((D, count), BF16),
            jax.ShapeDtypeStruct((count, 2 * units), F32),
            jax.ShapeDtypeStruct((count, units), BF16),
            jax.ShapeDtypeStruct((own, 2 * LANES), F32),
            jax.ShapeDtypeStruct((8, D), F32),
            jax.ShapeDtypeStruct((16, D), F32),
            jax.ShapeDtypeStruct((8, units), F32),
            jax.ShapeDtypeStruct((8, D), F32),
        ],
        in_specs=[vmem] * 6 + [hbm] + [vmem] * 3,
        out_specs=[hbm] * 16 + [vmem] * 5,
        scratch_shapes=[
            pltpu.VMEM((rows, columns), BF16),
            pltpu.VMEM((count, D), F32),
            pltpu.VMEM((D, D), BF16),
            pltpu.VMEM((count, D), BF16),
            pltpu.VMEM((own, D), BF16),
            pltpu.VMEM((sequences, length, length), F32),
            pltpu.VMEM((count, 3 * heads), F32),
            pltpu.VMEM((2, *place, 2 * LANES), BF16),
            pltpu.VMEM((2, *place, LANES), BF16),
            pltpu.VMEM((*place, heads), BF16),
            pltpu.VMEM((count, heads), BF16),
            pltpu.VMEM((own, D), F32),
            pltpu.VMEM((own, D), F32),
            pltpu.VMEM((own, D), F32),
            pltpu.VMEM((count, D), BF16),
            pltpu.VMEM((2, count, 2 * LANES), F32),
            pltpu.VMEM((2, count, LANES), BF16),
            dma,
            dma((4, 4, RING)),
            dma((4, 4, most)),
            dma((2,)),
            dma((2,)),
            dma((4,)),
            dma((2,)),
            dma((2,)),
            dma((14,)),
            dma((4,)),
            dma((4,)),
        ],
        compiler_params=pltpu.CompilerParams(
            collective_id=collective_id, has_side_effects=True, vmem_limit_bytes=60 << 20
        ),
        name="forward_pass",
    )(*operands)


SLOTS = 2 * RING + 4


def backward_plan():
    return tile_plan((4 * head_tiles() + 3 * unit_tiles()) * LANES)


def slot_of(route, tile):
    if route < 2:
        return route * RING + tile % RING
    return 2 * RING + (route - 2) * 2 + tile % 2


def ring_of(route):
    return RING if route < 2 else 2


def backward_kernel(
    plan,
    copies,
    d_shrunk,
    d_shrunk_turned,
    first_turned,
    tokens_turned,
    hidden,
    proj,
    raw,
    mixed,
    d_two,
    h_attn,
    first,
    tokens_in,
    factors,
    alphas,
    scales,
    gains,
    alpha_mlp_grad,
    bias,
    place_row,
    output,
    input_grad,
    block_output,
    grads,
    vectors,
    work,
    arrived,
    lefts,
    d_low,
    d_proj,
    first_part,
    core_in,
    stage_hidden,
    stage_rows,
    wide,
    outward,
    right,
    sum_k,
    sum_v,
    alpha_grad,
    unit_grad,
    query_grad,
    vector_sums,
    vector_in,
    send_sem,
    recv_sem,
    load_sem,
    unit_sem,
    raw_sem,
    result_sem,
    core_send,
    core_recv,
    vector_send,
    vector_recv,
):
    me = lax.axis_index("dp")
    core = lax.axis_index("tensor")
    inv_root = D ** (-0.5)
    rows = tokens_in.shape[0]
    own_rows = rows // 2
    own_at = pl.multiple_of(core * own_rows, own_rows)
    other_at = pl.multiple_of((1 - core) * own_rows, own_rows)
    heads = head_tiles()
    units = unit_tiles()
    block = D // 16
    unit_steps = units // 2
    shrink_steps = unit_steps - 1
    late_units = units // 4
    expand_steps = units - late_units
    attention_at = shrink_steps + expand_steps
    rare_units = 1 + late_units
    exchange_at = unit_steps
    attend_at = exchange_at + 3
    sequences = bias.shape[0]
    length = bias.shape[1]
    head_pairs = sequences * heads

    greet(me, core)

    def copy(source, target, sem):
        return pltpu.make_async_copy(source, target, sem)

    def chunks(total, size, body):
        def one(k, _):
            body(pl.ds(pl.multiple_of(k * size, size), size))
            return 0

        lax.fori_loop(0, total // size, one, 0)


    def piece(hop, route, tile):
        axis = ROUTES[route][3 - hop]
        slot = slot_of(route, tile)
        return pltpu.make_async_remote_copy(
            src_ref=work[hop].at[slot, 1],
            dst_ref=arrived[hop].at[slot],
            send_sem=send_sem.at[hop, slot],
            recv_sem=recv_sem.at[hop, slot],
            device_id={"dp": partner_of(me, PLACES[axis])},
            device_id_type=pl.DeviceIdType.MESH,
        )

    def free(hop, route, tile):
        @pl.when(tile >= ring_of(route))
        def _():
            piece(hop, route, tile - ring_of(route)).wait_send()

    def add(hop, route, tile):
        piece(hop - 1, route, tile).wait_recv()
        slot = slot_of(route, tile)
        total = work[hop - 1][slot, 0].astype(F32) + arrived[hop - 1][slot].astype(F32)
        if hop == 4:
            grads[:, lanes_of(plan, route, tile)] = total
            return
        half = total.shape[0] // 2
        free(hop, route, tile)
        work[hop][slot, 0] = total[:half].astype(BF16)
        work[hop][slot, 1] = total[half:].astype(BF16)
        piece(hop, route, tile).start()

    def keep_quarter(route, slot, quarter, part):
        axes = ROUTES[route][::-1]
        if route < 2:
            bits = [quarter >> 1, quarter & 1]
            at = bits[axes[1]] * 4 * block
            work[0][slot, bits[axes[0]], at : at + 4 * block, :] = part
            return
        for low in range(4):
            bits = [quarter >> 1, quarter & 1, low >> 1, low & 1]
            index = bits[axes[1]] * 4 + bits[axes[2]] * 2 + bits[axes[3]]
            work[0][slot, bits[axes[0]], index * block : (index + 1) * block, :] = part[
                low * block : (low + 1) * block
            ]

    def quarter_rows(quarter):
        return slice(quarter * 4 * block, (quarter + 1) * 4 * block)

    def often_product(tile):
        for route in (0, 1):
            free(0, route, tile)
        is_shrink = tile < shrink_steps
        is_expand = (tile >= shrink_steps) & (tile < attention_at)
        late = tile - attention_at
        is_outward = (late >= 0) & (late < 2)

        @pl.when(is_shrink)
        def _():
            right[0] = stage_hidden[tile % 2]

        @pl.when(is_expand)
        def _():
            unit = tile - shrink_steps + late_units
            right[0] = d_proj[:, pl.ds(pl.multiple_of(unit * 2 * LANES, 2 * LANES), 2 * LANES)]

        @pl.when(late >= 0)
        def _():
            first_tile = jnp.where(late < 2, 2 * late, 2 * late + 1)
            right[0] = wide[:rows, pl.ds(pl.multiple_of(first_tile * LANES, LANES), 2 * LANES)]

        which = jnp.where(is_expand | is_outward, 1, 0)
        scale = jnp.where(is_shrink | is_outward, 1.0, inv_root)
        for quarter in range(4):
            part = (nn(lefts[which, quarter_rows(quarter), :], right[0]) * scale).astype(BF16)
            for route in (0, 1):
                keep_quarter(
                    route, slot_of(route, tile), quarter, part[:, route * LANES : (route + 1) * LANES]
                )
        for route in (0, 1):
            piece(0, route, tile).start()

    def rare_product(tile):
        late = tile - rare_units

        @pl.when(tile == 0)
        def _():
            right[1] = stage_hidden[2]

        @pl.when((tile > 0) & (late < 0))
        def _():
            lanes = pl.ds(pl.multiple_of((tile - 1) * 2 * LANES, 2 * LANES), 2 * LANES)
            right[1] = d_proj[:, lanes]

        @pl.when(late == 0)
        def _():
            right[1, :, :LANES] = wide[:rows, (heads - 1) * LANES : heads * LANES]
            right[1, :, LANES:] = wide[:rows, (heads + 12) * LANES : (heads + 13) * LANES]

        @pl.when(late == 1)
        def _():
            right[1] = wide[:rows, (heads + 13) * LANES : (heads + 15) * LANES]

        for route in (2, 3):
            free(0, route, tile)
            of_units = (tile > 0) & (late < 0)
            of_outward = (late == 0) if route == 2 else (late < -rare_units)
            which = jnp.where(of_units | of_outward, 1, 0)
            scale = jnp.where((tile == 0) | of_outward, 1.0, inv_root)
            at = (route - 2) * LANES
            for quarter in range(4):
                part = nn(lefts[which, quarter_rows(quarter), :], right[1, :, at : at + LANES])
                keep_quarter(route, slot_of(route, tile), quarter, (part * scale).astype(BF16))
            piece(0, route, tile).start()


    def unit_copies(pair):
        slot = pair % 2
        unit = 2 * pair
        at = pl.multiple_of(slot * 6 * LANES, 2 * LANES)
        result = [
            (
                copies.at[:, pl.ds(pl.multiple_of(pair_tile(unit) * LANES, LANES), 4 * LANES)],
                wide.at[:, pl.ds(at, 4 * LANES)],
            )
        ]
        for k in range(2):
            tile = shrink_tile(unit + k)
            result.append(
                (
                    copies.at[:, pl.ds(pl.multiple_of(tile * LANES, LANES), LANES)],
                    wide.at[:, pl.ds(pl.multiple_of(at + (4 + k) * LANES, LANES), LANES)],
                )
            )
        lanes = pl.ds(pl.multiple_of(pair * 4 * LANES, 4 * LANES), 4 * LANES)
        for k in range(2):
            result.append(
                (
                    proj.at[pl.ds(k * own_rows, own_rows), lanes],
                    stage_rows.at[slot, :, pl.ds(k * 4 * LANES, 4 * LANES)],
                )
            )
        return [copy(source, target, unit_sem.at[k, slot]) for k, (source, target) in enumerate(result)]

    def hidden_copy(tile):
        lanes = pl.ds(pl.multiple_of((2 * tile + 2) * LANES, 2 * LANES), 2 * LANES)
        return copy(hidden.at[:, lanes], stage_hidden.at[tile % 2], unit_sem.at[5, tile % 2])

    def unit_pair(pair):
        slot = pair % 2
        for part in unit_copies(pair):
            part.wait()
        at = pl.multiple_of(slot * 6 * LANES, 2 * LANES)
        expand = wide[:, pl.ds(at, 4 * LANES)]
        down = wide[:, pl.ds(pl.multiple_of(at + 4 * LANES, 2 * LANES), 2 * LANES)]

        def some(row_at, row_from, proj_lanes):
            d_hidden = nn(d_low[row_at, :], down)
            for k in range(2):
                lanes = pl.ds(pl.multiple_of((2 * pair + k) * LANES, LANES), LANES)
                gain_up, gain_gate = gains[0:1, lanes], gains[1:2, lanes]
                start = proj_lanes + 2 * k * LANES
                proj_up = stage_rows[slot, row_from, start : start + LANES]
                proj_gate = stage_rows[slot, row_from, start + LANES : start + 2 * LANES]
                upstream = d_hidden[:, k * LANES : (k + 1) * LANES]
                gate = gain_gate * proj_gate
                sigmoid = jax.nn.sigmoid(gate)
                d_up = upstream * (gate * sigmoid)
                d_gate = upstream * (gain_up * proj_up) * sigmoid * (1.0 + gate * (1.0 - sigmoid))
                unit_grad[0:1, lanes] += jnp.sum(d_up * proj_up, axis=0, keepdims=True)
                unit_grad[1:2, lanes] += jnp.sum(d_gate * proj_gate, axis=0, keepdims=True)
                at = pl.multiple_of((2 * pair + k) * 2 * LANES, 2 * LANES)
                d_proj[row_at, pl.ds(at, LANES)] = (d_up * gain_up).astype(BF16)
                d_proj[row_at, pl.ds(pl.multiple_of(at + LANES, LANES), LANES)] = (
                    d_gate * gain_gate
                ).astype(BF16)
            lanes = pl.ds(pl.multiple_of(pair * 4 * LANES, 4 * LANES), 4 * LANES)
            first_part[row_at, :] += nt(d_proj[row_at, lanes], expand)

        size = own_rows // 2
        for half in range(2):

            def one(k, _, half=half):
                row_from = pl.multiple_of(k * size, size)
                row_at = pl.multiple_of(half * own_rows + row_from, size)
                some(pl.ds(row_at, size), pl.ds(row_from, size), half * 4 * LANES)
                return 0

            lax.fori_loop(0, 2, one, 0)


    def core_copy(source, target, which):
        return pltpu.make_async_remote_copy(
            src_ref=source,
            dst_ref=target,
            send_sem=core_send.at[which],
            recv_sem=core_recv.at[which],
            device_id={"tensor": 1 - core},
            device_id_type=pl.DeviceIdType.MESH,
        )

    def part_copy():
        return core_copy(first_part.at[pl.ds(other_at, own_rows)], core_in, 0)

    def branch_copy():
        own = d_low.at[pl.ds(own_at, own_rows)]
        return core_copy(own, own, 1)

    tokens_place = wide.at[pl.ds(0, own_rows), pl.ds(D, D)]
    rare, rarer = forward_plan()[2][0], forward_plan()[3][0]
    outward_tiles = ((rare + 1, 1, 0), (rarer + 1, 1, 1), (3 * heads - 1, 2, 2), (rare + 2, 1, 4))

    def load(k):
        if k == 0:
            return copy(d_two, stage_rows.at[0], load_sem.at[0])
        if k == 1:
            return copy(h_attn, stage_rows.at[1], load_sem.at[1])
        if k == 2:
            return copy(tokens_in.at[pl.ds(own_at, own_rows)], tokens_place, load_sem.at[2])
        if k == 3:
            return copy(
                mixed, wide.at[pl.ds(0, rows), pl.ds(0, heads * LANES)], load_sem.at[3]
            )
        if k == 4:
            return copy(first, first_part.at[pl.ds(other_at, own_rows)], load_sem.at[4])
        if k == 5:
            return copy(d_shrunk, d_low, load_sem.at[5])
        if k == 6:
            return copy(d_shrunk_turned, lefts.at[0], load_sem.at[6])
        if k == 7:
            return copy(first_turned, lefts.at[1], load_sem.at[7])
        if k == 8:
            return copy(tokens_turned, lefts.at[0], load_sem.at[8])
        if k == 9:
            return copy(hidden.at[:, pl.ds(0, 2 * LANES)], stage_hidden.at[2], load_sem.at[9])
        tile, width, at = outward_tiles[k - 10]
        return copy(
            copies.at[:, pl.ds(tile * LANES, width * LANES)],
            outward.at[:, pl.ds(at * LANES, width * LANES)],
            load_sem.at[k],
        )

    def branch_gradient():
        part_copy().wait_send()
        load(4).start()
        part_copy().wait_recv()
        for k in (0, 1, 2, 4):
            load(k).wait()
        alpha_attn, alpha_mlp = alphas[0:1, :], alphas[1:2, :]

        def some(at):
            here = pl.ds(pl.multiple_of(own_at + at.start, 64), 64)
            there = pl.ds(pl.multiple_of(other_at + at.start, 64), 64)
            part = (first_part[here, :] + core_in[at, :]) * inv_root
            d_first = (1.0 - alpha_mlp) * stage_rows[0, at, :] + part
            normed = stage_rows[1, at, :]
            d_one = row_norm_back(
                d_first, first_part[there, :], factors[at, LANES : LANES + 1]
            )
            inputs = wide[at, D : 2 * D].astype(F32)
            alpha_grad[0:1, :] += jnp.sum(d_one * (normed - inputs), axis=0, keepdims=True)
            stage_rows[0, at, :] = d_one
            d_low[here, :] = row_norm_back(alpha_attn * d_one, normed, factors[at, 0:1]).astype(
                BF16
            )

        chunks(own_rows, 64, some)
        branch_copy().start()


    def raw_copies(number):
        sequence, head = number // heads, number % heads
        at = pl.ds(pl.multiple_of(sequence * length, length), length)
        slot = number % 2
        target_rows = pl.ds(pl.multiple_of(slot * own_rows, own_rows), length)
        return [
            copy(
                raw.at[at, pl.ds(pl.multiple_of((k * heads + head) * LANES, LANES), LANES)],
                first_part.at[target_rows, pl.ds(k * LANES, LANES)],
                raw_sem.at[k, slot],
            )
            for k in range(3)
        ]

    def attend_one(number):
        sequence, head = number // heads, number % heads
        for part in raw_copies(number):
            part.wait()
        at = pl.ds(pl.multiple_of(sequence * length, length), length)
        source_rows = pl.ds(pl.multiple_of((number % 2) * own_rows, own_rows), length)
        head_lanes = pl.ds(pl.multiple_of(head * LANES, LANES), LANES)
        gain_lanes = pl.ds(pl.multiple_of((core * heads + head) * LANES, LANES), LANES)
        d_mixed = nn(d_low[at, :], outward[:, head_lanes]).astype(BF16)
        targets = [
            wide.at[at, pl.ds(pl.multiple_of(((k + 1) * heads + head) * LANES, LANES), LANES)]
            for k in range(3)
        ]
        total = attend_pair_back(
            *[first_part.at[source_rows, pl.ds(k * LANES, LANES)] for k in range(3)],
            d_mixed,
            scales[2:3, gain_lanes],
            bias.at[sequence],
            *targets,
            sum_k,
            sum_v,
        )
        query_grad[0:1, head_lanes] += total


    head_lanes = 3 * heads * LANES
    beyond = D - rows

    def inward_copies():
        first_lanes = (3 * heads - 1) * LANES
        result = []
        for row, number, at, lane in ((0, rows, 0, 0), (rows, beyond, 0, head_lanes)):
            for source, width in ((0, first_lanes), (rare * LANES, LANES)):
                offset = 0 if width == first_lanes else first_lanes
                result.append(
                    (
                        copies.at[pl.ds(row, number), pl.ds(source, width)],
                        d_proj.at[pl.ds(at, number), pl.ds(lane + offset, width)],
                    )
                )
        return [copy(source, target, load_sem.at[14 + k]) for k, (source, target) in enumerate(result)]

    order_lane = 2 * head_lanes

    def make_order():
        natural = place_row[...]

        def fill(at):
            here = lax.broadcasted_iota(jnp.int32, (LANES, D), 0) + at.start
            d_proj[at, order_lane : order_lane + D] = jnp.where(here == natural, 1.0, 0.0).astype(
                BF16
            )

        chunks(rows, LANES, fill)
        for k in range(beyond // LANES):
            here = lax.broadcasted_iota(jnp.int32, (LANES, D), 0) + rows + k * LANES
            at = slice(beyond + k * LANES, beyond + (k + 1) * LANES)
            d_proj[at, head_lanes : head_lanes + D] = jnp.where(here == natural, 1.0, 0.0).astype(
                BF16
            )

    def natural_parts(values):
        low = nt(values, d_proj[:, order_lane : order_lane + D])
        high = nt(values, d_proj[beyond : 2 * beyond, head_lanes : head_lanes + D])
        return low, high

    def input_part(number):
        at = pl.ds(pl.multiple_of(number * 256, 256), 256)
        upstream = wide[at, heads * LANES : 4 * heads * LANES]
        low = nt(upstream, d_proj[:, :head_lanes]) * inv_root
        d_low[at, :rows] = low.astype(BF16)
        high = nt(upstream, d_proj[:beyond, head_lanes : 2 * head_lanes]) * inv_root
        d_low[at, rows:] = high.astype(BF16)
        low, high = natural_parts(d_low[at, :])
        first_part[at, :rows] = low
        first_part[at, rows:] = high

    def residual_part():
        alpha_attn = alphas[0:1, :]

        def some(at):
            here = pl.ds(pl.multiple_of(own_at + at.start, 128), 128)
            residual = (1.0 - alpha_attn) * stage_rows[0, at, :]
            top = residual.astype(BF16)
            rest = (residual - top.astype(F32)).astype(BF16)
            for part in (top, rest):
                low, high = natural_parts(part)
                first_part[here, :rows] += low
                first_part[here, rows:] += high

        chunks(own_rows, 128, some)

    half_width = D // 2

    def input_copies():
        lanes = pl.ds(pl.multiple_of((1 - core) * half_width, LANES), half_width)
        return [
            core_copy(
                first_part.at[pl.ds(k * own_rows, own_rows), lanes],
                core_in.at[:, pl.ds(k * half_width, half_width)],
                2 + k,
            )
            for k in range(2)
        ]

    def input_copy(k):
        lanes = pl.ds(pl.multiple_of(core * half_width, LANES), half_width)
        at = pl.ds(k * own_rows, own_rows)
        return copy(first_part.at[at, lanes], input_grad.at[at], result_sem.at[k])

    def input_sum():
        lanes = pl.ds(pl.multiple_of(core * half_width, LANES), half_width)
        for k, part in enumerate(input_copies()):
            part.wait()
            at = pl.ds(k * own_rows, own_rows)
            first_part[at, lanes] += core_in[:, k * half_width : (k + 1) * half_width]
            input_copy(k).start()

    def output_load():
        return copy(output, d_low.at[pl.ds(other_at, own_rows)], load_sem.at[18])

    def output_order():
        output_load().wait()
        for k in range(own_rows // 256):
            source = pl.ds(pl.multiple_of(other_at + k * 256, 256), 256)
            target = pl.ds(pl.multiple_of(own_at + k * 256, 256), 256)
            low, high = natural_parts(d_low[source, :])
            d_low[target, :rows] = low.astype(BF16)
            d_low[target, rows:] = high.astype(BF16)
        output_copies()[0].start()
        output_copies()[1].start()

    def output_copies():
        own = pl.ds(own_at, own_rows)
        return (
            core_copy(d_low.at[own], block_output.at[own], 4),
            copy(d_low.at[own], block_output.at[own], result_sem.at[2]),
        )

    def vector_copy(k):
        if k == 0:
            device = {"tensor": 1 - core}
        else:
            device = {"dp": partner_of(me, PLACES[k - 1])}
        return pltpu.make_async_remote_copy(
            src_ref=vector_sums.at[k],
            dst_ref=vector_in.at[k],
            send_sem=vector_send.at[k],
            recv_sem=vector_recv.at[k],
            device_id=device,
            device_id_type=pl.DeviceIdType.MESH,
        )

    def vectors_start():
        alpha_grad[1:2, :] = alpha_mlp_grad[0:1, :]
        vector_sums[0] = jnp.zeros_like(vector_sums[0])
        values = alpha_grad[...]
        for _ in range(3):
            part = values.astype(BF16)
            low, high = natural_parts(part)
            vector_sums[0, :8, :rows] += low
            vector_sums[0, :8, rows:] += high
            values = values - part.astype(F32)
        vector_sums[0, 2:3, pl.ds(pl.multiple_of(core * heads * LANES, LANES), heads * LANES)] = (
            query_grad[0:1, :]
        )
        each = units * LANES // D
        for row in range(2):
            for k in range(2 * each):
                here = unit_grad[row : row + 1, (k % each) * D : (k % each + 1) * D]
                at = 3 + 2 * each * row + k
                vector_sums[0, at : at + 1, :] = jnp.where(core == k // each, here, 0.0)
        vector_copy(0).start()

    def vectors_add(k):
        vector_copy(k).wait()
        total = vector_sums[k] + vector_in[k]
        if k < len(PLACES):
            vector_sums[k + 1] = total
            vector_copy(k + 1).start()
        else:
            vectors[...] = total

    input_at = attention_at + 1
    parts = rows // 256


    for k in (5, 6, 9, 7):
        load(k).start()
    for part in unit_copies(0):
        part.start()
    hidden_copy(0).start()
    alpha_grad[...] = jnp.zeros_like(alpha_grad)
    unit_grad[...] = jnp.zeros_like(unit_grad)
    query_grad[...] = jnp.zeros_like(query_grad)
    first_part[...] = jnp.zeros_like(first_part)
    for k in (5, 6, 9, 7):
        load(k).wait()

    def step(index, _):
        for hop in range(4, 0, -1):
            for_tiles(index, hop, plan, functools.partial(add, hop))

        @pl.when(index < shrink_steps)
        def _():
            hidden_copy(index).wait()

        @pl.when(index == attention_at)
        def _():
            load(8).wait()
            chunks(rows, LANES, turn)

        @pl.when(index < plan[0][2])
        def _():
            often_product(index)

        @pl.when((index % EVERY == 0) & (index < plan[2][2] * EVERY))
        def _():
            rare_product(index // EVERY)

        @pl.when(index + 1 < shrink_steps)
        def _():
            hidden_copy(index + 1).start()

        @pl.when(index + 1 < unit_steps)
        def _():
            for part in unit_copies(index + 1):
                part.start()

        @pl.when(index < unit_steps)
        def _():
            unit_pair(index)

        @pl.when(index == exchange_at)
        def _():
            part_copy().start()
            for k in (0, 1, 2, 3, 8, 10, 11, 12, 13):
                load(k).start()

        @pl.when(index == exchange_at + 1)
        def _():
            branch_gradient()

        @pl.when(index == exchange_at + 2)
        def _():
            branch_copy().wait()
            for k in (3, 10, 11, 12, 13):
                load(k).wait()

        number = index - attend_at

        @pl.when((number >= -1) & (number < head_pairs - 1))
        def _():
            for part in raw_copies(number + 1):
                part.start()

        @pl.when((number >= 0) & (number < head_pairs))
        def _():
            attend_one(number)

        @pl.when(index == attention_at)
        def _():
            for part in inward_copies():
                part.start()
            make_order()
            vectors_start()

        for k in range(len(PLACES) + 1):

            @pl.when(index == attention_at + 1 + k)
            def _(k=k):
                vectors_add(k)

        @pl.when(index == input_at)
        def _():
            for part in inward_copies():
                part.wait()

        @pl.when((index >= input_at) & (index < input_at + parts))
        def _():
            input_part(index - input_at)

        @pl.when(index == input_at + parts)
        def _():
            output_load().start()
            residual_part()
            for part in input_copies():
                part.start()

        @pl.when(index == input_at + parts + 1)
        def _():
            output_order()

        @pl.when(index == input_at + parts + 2)
        def _():
            input_sum()

        return 0

    def turn(at):
        lefts[1, :, at] = d_low[at, :].astype(F32).T.astype(BF16)

    lax.fori_loop(0, steps_of(plan, 4), step, 0)
    for part in output_copies():
        part.wait()
    for k in range(2):
        input_copy(k).wait()
    for route, (_, _, number, _) in enumerate(plan):
        for tile in range(max(0, number - ring_of(route)), number):
            for hop in range(4):
                piece(hop, route, tile).wait_send()


def backward_pass(*operands, collective_id):
    plan = backward_plan()
    copies = operands[0]
    count = operands[1].shape[0]
    own = count // 2
    heads = head_tiles() * LANES
    units = unit_tiles() * LANES
    length = operands[18].shape[1]
    block = D // 16
    halves = [block * 8 >> hop for hop in range(4)]
    hbm = pl.BlockSpec(memory_space=pl.ANY)
    vmem = pl.BlockSpec(memory_space=pltpu.VMEM)
    dma = pltpu.SemaphoreType.DMA
    return pl.pallas_call(
        functools.partial(backward_kernel, plan),
        out_shape=[
            jax.ShapeDtypeStruct((count, D // 2), F32),
            jax.ShapeDtypeStruct((count, D), BF16),
            jax.ShapeDtypeStruct((block, 4 * heads + 3 * units), F32),
            jax.ShapeDtypeStruct((16, D), F32),
        ],
        in_specs=[hbm] * 13 + [vmem] * 7 + [hbm],
        out_specs=[hbm] * 2 + [vmem] * 2,
        scratch_shapes=[
            [pltpu.VMEM((SLOTS, 2, half, LANES), BF16) for half in halves],
            [pltpu.VMEM((SLOTS, half, LANES), BF16) for half in halves],
            pltpu.VMEM((2, D, count), BF16),
            pltpu.VMEM((count, D), BF16),
            pltpu.VMEM((count, 2 * units), BF16),
            pltpu.VMEM((count, D), F32),
            pltpu.VMEM((own, D), F32),
            pltpu.VMEM((3, count, 2 * LANES), BF16),
            pltpu.VMEM((2, own, D), F32),
            pltpu.VMEM((D, 4 * heads), BF16),
            pltpu.VMEM((D, heads), BF16),
            pltpu.VMEM((2, count, 2 * LANES), BF16),
            pltpu.VMEM((length, LANES), F32),
            pltpu.VMEM((length, LANES), F32),
            pltpu.VMEM((8, D), F32),
            pltpu.VMEM((8, units), F32),
            pltpu.VMEM((8, heads), F32),
            pltpu.VMEM((5, 16, D), F32),
            pltpu.VMEM((5, 16, D), F32),
            dma((4, SLOTS)),
            dma((4, SLOTS)),
            dma((19,)),
            dma((6, 2)),
            dma((3, 2)),
            dma((3,)),
            dma((5,)),
            dma((5,)),
            dma((5,)),
            dma((5,)),
        ],
        compiler_params=pltpu.CompilerParams(
            collective_id=collective_id, has_side_effects=True, vmem_limit_bytes=62 << 20
        ),
        name="backward_pass",
    )(*operands)


def sum_kernel(values, total, sums, arrived, send_sem, recv_sem):
    me = lax.axis_index("dp")
    greet(me)
    sums[0] = values[...]
    for k, bit in enumerate(PLACES):
        copy = pltpu.make_async_remote_copy(
            src_ref=sums.at[k],
            dst_ref=arrived.at[k],
            send_sem=send_sem.at[k],
            recv_sem=recv_sem.at[k],
            device_id={"dp": partner_of(me, bit)},
            device_id_type=pl.DeviceIdType.MESH,
        )
        copy.start()
        copy.wait()
        if k + 1 < len(PLACES):
            sums[k + 1] = sums[k] + arrived[k]
        else:
            total[...] = sums[k] + arrived[k]


def sum_all(values, count, collective_id):
    for bit in extra_bits(count):
        values = values + exchange(values, bit, count)
    vmem = pl.BlockSpec(memory_space=pltpu.VMEM)
    hops = len(PLACES)
    return pl.pallas_call(
        sum_kernel,
        out_shape=jax.ShapeDtypeStruct(values.shape, F32),
        in_specs=[vmem],
        out_specs=vmem,
        scratch_shapes=[
            pltpu.VMEM((hops, *values.shape), F32),
            pltpu.VMEM((hops, *values.shape), F32),
            pltpu.SemaphoreType.DMA((hops,)),
            pltpu.SemaphoreType.DMA((hops,)),
        ],
        compiler_params=pltpu.CompilerParams(
            collective_id=collective_id, has_side_effects=True, vmem_limit_bytes=16 << 20
        ),
        name="sum_all",
    )(values)


def columns_of(grads):
    plan = backward_plan()
    rows = grads.shape[0]
    heads, units = head_tiles(), unit_tiles()
    shrink_steps, late = units // 2 - 1, units // 4
    rare, rarer = plan[2][0], plan[3][0]

    def tiles(start, number):
        return grads[:, start * LANES : (start + number) * LANES]

    attention_at = 2 * (shrink_steps + units - late)
    pairs = tiles(2 * shrink_steps, 2 * (units - late)).reshape(rows, units - late, 2, LANES)
    shrink = jnp.concatenate([tiles(rare, 1), tiles(rarer, 1), tiles(0, 2 * shrink_steps)], axis=1)
    up = jnp.concatenate([tiles(rare + 1, late), pairs[:, :, 0].reshape(rows, -1)], axis=1)
    gate = jnp.concatenate([tiles(rarer + 1, late), pairs[:, :, 1].reshape(rows, -1)], axis=1)
    last = late + 1
    outward = jnp.concatenate([tiles(attention_at, 4), tiles(rare + last, 1)], axis=1)
    inward = jnp.concatenate(
        [
            tiles(attention_at + 4, 12),
            tiles(rarer + last, 1),
            tiles(rare + last + 1, 1),
            tiles(rarer + last + 1, 1),
        ],
        axis=1,
    )
    return inward, outward, up, gate, shrink


def per_device(
    tokens,
    cotangent,
    segment_ids,
    pad_mask,
    inward_master,
    inward_first,
    inward_second,
    outward_master,
    outward_first,
    outward_second,
    expand_master,
    expand_first,
    expand_second,
    shrink_master,
    shrink_first,
    shrink_second,
    alpha_master,
    alpha_first,
    alpha_second,
    scale_master,
    scale_first,
    scale_second,
):
    count = lax.axis_size("dp")
    me = lax.axis_index("dp")
    heads_width = inward_master.shape[2]

    small = jnp.concatenate([alpha_master, scale_master], axis=0).astype(BF16)
    small = jnp.pad(small, ((0, LANES - small.shape[0]), (0, 0))).T
    masters = (
        inward_master,
        outward_master.astype(BF16).T,
        expand_master,
        shrink_master.astype(BF16).T,
        small,
    )
    if extra_bits(count):
        masters = [gather_rest(master.astype(BF16), count) for master in masters]
    place_row = place_row_of(me, count)
    (
        copies,
        tokens_in,
        raw,
        mixed,
        h_attn,
        first,
        first_low,
        tokens_turned,
        first_turned,
        bias,
        d_two,
        output,
        d_shrunk,
        d_shrunk_turned,
        proj,
        hidden,
        factors,
        alphas,
        scale_rows,
        gains,
        alpha_mlp_grad,
    ) = forward_pass(
        *masters, tokens, cotangent, segment_ids, pad_mask, place_row, collective_id=0
    )

    input_grad, block_output, grads, vectors = backward_pass(
        copies.reshape(D, -1),
        d_shrunk,
        d_shrunk_turned,
        first_turned,
        tokens_turned,
        hidden,
        proj,
        raw,
        mixed,
        d_two,
        h_attn,
        first,
        tokens_in,
        factors,
        alphas,
        scale_rows,
        gains,
        alpha_mlp_grad,
        bias,
        place_row,
        output,
        collective_id=1,
    )
    grads = scatter_rest(grads, count)
    inward_grad, outward_grad, up_grad, gate_grad, shrink_grad = columns_of(grads)
    for bit in extra_bits(count):
        vectors = vectors + exchange(vectors, bit, count)
    width = D // count
    vectors = lax.dynamic_slice_in_dim(vectors, me * width, width, 1)
    alpha_grad, scale_grad = vectors[:2], vectors[2 : 2 + scale_master.shape[0]]

    outward_grad = outward_grad.T
    shrink_grad = shrink_grad.T
    expand_grad = jnp.stack([up_grad, gate_grad])
    inward_grad = jnp.stack(
        [inward_grad[:, k * heads_width : (k + 1) * heads_width] for k in range(3)]
    )
    inward_pre, inward_var = adam_step(
        inward_master, inward_first, inward_second, inward_grad, RATE_MATRIX
    )
    outward_pre, outward_var = adam_step(
        outward_master, outward_first, outward_second, outward_grad, RATE_MATRIX
    )
    expand_pre, expand_var = adam_step(
        expand_master, expand_first, expand_second, expand_grad, RATE_MATRIX
    )
    shrink_pre, shrink_var = adam_step(
        shrink_master, shrink_first, shrink_second, shrink_grad, RATE_MATRIX
    )
    alpha_new, alpha_var = adam_step(
        alpha_master, alpha_first, alpha_second, alpha_grad, RATE_ALPHA
    )
    scale_new, scale_var = adam_step(
        scale_master, scale_first, scale_second, scale_grad, RATE_SCALE
    )

    squares = [
        jnp.sum(pre * pre, axis=axis).reshape(-1)
        for pre, axis in ((inward_pre, 1), (outward_pre, 1), (expand_pre, 1), (shrink_pre, 1))
    ]
    sizes = [square.shape[0] for square in squares]
    squares = sum_all(jnp.concatenate(squares).reshape(8, -1), count, 2).reshape(-1)
    ends = np.cumsum(sizes)

    def renormed(pre, axis, which):
        mean = squares[int(ends[which]) - sizes[which] : int(ends[which])] / D
        kept = [size for k, size in enumerate(pre.shape) if k != axis]
        return pre * jnp.expand_dims(lax.rsqrt(mean + EPS_NORM).reshape(kept), axis)

    return (
        block_output,
        input_grad,
        inward_grad,
        inward_var,
        renormed(inward_pre, 1, 0),
        outward_grad,
        outward_var,
        renormed(outward_pre, 1, 1),
        expand_grad,
        expand_var,
        renormed(expand_pre, 1, 2),
        shrink_grad,
        shrink_var,
        renormed(shrink_pre, 1, 3),
        alpha_grad,
        alpha_var,
        alpha_new,
        scale_grad,
        scale_var,
        scale_new,
    )


def solution(mesh):
    rows = P("dp", None)
    deep = P(None, "dp", "tensor")
    flat = P("tensor", "dp")
    vector = P(None, "dp")
    in_specs = (rows,) * 4 + (deep,) * 3 + (flat,) * 3 + (deep,) * 3 + (flat,) * 3 + (vector,) * 6
    out_specs = (
        (rows, P("dp", "tensor"))
        + (deep,) * 3
        + (flat,) * 3
        + (deep,) * 3
        + (flat,) * 3
        + (vector,) * 6
    )
    return jax.shard_map(
        per_device, mesh=mesh, in_specs=in_specs, out_specs=out_specs, check_vma=False
    )
```

```python
import functools

import jax
import jax.numpy as jnp
import numpy as np
from jax import lax
from jax.experimental import pallas as pl
from jax.experimental.pallas import tpu as pltpu
from jax.sharding import PartitionSpec as P

D = 1280
HEADS = 20
HD = 64
FF = 5120
STEP = 10
LONGEST = 256


EPS_NORM = 1e-06
BETA_ONE = 0.9
BETA_TWO = 0.95
ADAM_EPS = 1e-08
RATE_MATRIX = 0.3
RATE_ALPHA = 0.08
RATE_SCALE = 0.25
MASKED = -1e30
F32 = jnp.float32
BF16 = jnp.bfloat16


def row_norm(values):
    factor = lax.rsqrt(jnp.mean(values * values, axis=-1, keepdims=True) + EPS_NORM)
    return (values * factor, factor)


def row_norm_back(upstream, normed, factor):
    return factor * (upstream - normed * jnp.mean(upstream * normed, axis=-1, keepdims=True))


def adam_step(master, first_moment, second_moment, gradient, rate):
    first_new = BETA_ONE * first_moment.astype(F32) + (1.0 - BETA_ONE) * gradient
    second_new = BETA_TWO * second_moment + (1.0 - BETA_TWO) * gradient * gradient
    ratio = (
        first_new
        / (1.0 - BETA_ONE**STEP)
        / (jnp.sqrt(second_new / (1.0 - BETA_TWO**STEP)) + ADAM_EPS)
    )
    return (master - rate * ratio, second_new)


LANES = 128
PLACES = (2, 1, 4, 8)
ROUTES = ((3, 2, 1, 0), (3, 2, 0, 1), (1, 0, 3, 2), (0, 1, 3, 2))
EVERY = 4
LAG = 2
RING = 4


def partner_of(me, bit):
    return me + bit - 2 * bit * ((me // bit) % 2)


def greet(me, core=None):
    barrier = pltpu.get_barrier_semaphore()
    partners = [{"dp": partner_of(me, bit)} for bit in PLACES]
    if core is not None:
        partners.append({"tensor": 1 - core})
    for partner in partners:
        pl.semaphore_signal(
            barrier, inc=1, device_id=partner, device_id_type=pl.DeviceIdType.MESH
        )
    pl.semaphore_wait(barrier, len(partners))


def tile_plan(columns):
    tiles = columns // LANES
    rare = tiles // 10
    often = (tiles - 2 * rare) // 2
    return (
        (0, 2, often, 1, 0),
        (1, 2, often, 1, 0),
        (2 * often, 1, rare, EVERY, 0),
        (2 * often + rare, 1, rare, EVERY, EVERY // 2),
    )


def for_tiles(step, hop, plan, body):
    for route, (_, _, number, every, start) in enumerate(plan):
        at = step - hop * LAG - start
        due = (at >= 0) & (at < number * every)
        if every > 1:
            due = due & (at % every == 0)

        @pl.when(due)
        def _():
            body(route, at // every)


def lanes_of(plan, route, tile):
    first, stride = plan[route][:2]
    return pl.ds(pl.multiple_of((first + stride * tile) * LANES, LANES), LANES)


def steps_of(plan, hops):
    return max(start + (number - 1) * every + 1 for _, _, number, every, start in plan) + hops * LAG


def extra_bits(count):
    return [bit for bit in (1 << k for k in range(4, count.bit_length() - 1))]


def exchange(array, bit, count):
    return lax.ppermute(array, "dp", [(i, i ^ bit) for i in range(count)])


def gather_rest(block, count):
    for bit in extra_bits(count)[::-1]:
        block = jnp.concatenate([block, exchange(block, bit, count)], axis=-2)
    return block


def scatter_rest(partial, count):
    for bit in extra_bits(count):
        half = partial.shape[0] // 2
        partial = partial[:half] + exchange(partial[half:], bit, count)
    return partial


def place_row_of(me, count):
    places = list(PLACES) + extra_bits(count)
    width = D // count
    placed = np.arange(D, dtype=np.int32)
    position, offset = placed // width, placed % width
    relative = np.zeros_like(position)
    for axis, bit in enumerate(places):
        relative = relative + ((position >> (len(places) - 1 - axis)) & 1) * bit
    return ((jnp.asarray(relative) ^ me) * width + jnp.asarray(offset))[None]


def nn(a, b):
    return lax.dot_general(a, b, (((1,), (0,)), ((), ())), preferred_element_type=F32)


def nt(a, b):
    return lax.dot_general(a, b, (((1,), (1,)), ((), ())), preferred_element_type=F32)


def tn(a, b):
    return lax.dot_general(a, b, (((0,), (0,)), ((), ())), preferred_element_type=F32)


def head_factors(raw, low_lanes):
    squares = raw * raw
    low = jnp.sum(jnp.where(low_lanes, squares, 0.0), axis=-1, keepdims=True)
    high = jnp.sum(jnp.where(low_lanes, 0.0, squares), axis=-1, keepdims=True)
    return jnp.where(low_lanes, lax.rsqrt(low + EPS_NORM), lax.rsqrt(high + EPS_NORM))


def head_sums(values, low_lanes):
    low = jnp.sum(jnp.where(low_lanes, values, 0.0), axis=-1, keepdims=True)
    high = jnp.sum(jnp.where(low_lanes, 0.0, values), axis=-1, keepdims=True)
    return jnp.where(low_lanes, low, high)


Q_TILE = 128


def key_range(tile):
    start = max(0, tile * Q_TILE - LONGEST)
    return start, (tile + 1) * Q_TILE


def attend_pair(query, key, value, gain, bias, mixed):
    length = query.shape[0]
    low_lanes = lax.broadcasted_iota(jnp.int32, (1, 2 * HD), 1) < HD
    query = (gain * (query * head_factors(query, low_lanes))).astype(BF16) * 8
    key = (gain * (key * head_factors(key, low_lanes))).astype(BF16)
    value = value.astype(BF16)
    zero = jnp.zeros_like(query)
    parts = (jnp.where(low_lanes, query, zero), jnp.where(low_lanes, zero, query))
    for tile in range(length // Q_TILE):
        start, end = key_range(tile)
        rows = slice(tile * Q_TILE, (tile + 1) * Q_TILE)
        tile_bias = bias[rows, start:end]
        results = []
        for part in parts:
            expo = jnp.exp(nt(part[rows], key[start:end]) + tile_bias)
            total = jnp.sum(expo, axis=-1, keepdims=True)
            results.append(nn(expo.astype(BF16), value[start:end]) * (1.0 / total))
        mixed[rows, :] = jnp.where(low_lanes, results[0], results[1]).astype(BF16)


def attend_pair_back(
    raw_q, raw_k, raw_v, d_mixed, gains, bias, d_raw_q, d_raw_k, d_raw_v, sum_k, sum_v
):
    length = raw_q.shape[0]
    low_lanes = lax.broadcasted_iota(jnp.int32, (1, 2 * HD), 1) < HD
    low_rows = lax.broadcasted_iota(jnp.int32, (2 * HD, 1), 0) < HD
    key_raw = raw_k[...]
    key_factor = head_factors(key_raw, low_lanes)
    key_unit = key_raw * key_factor
    key = (gains * key_unit).astype(BF16)
    key_eight = ((gains * key_unit).astype(BF16).astype(F32) * 8.0).T.astype(BF16)
    value = raw_v[...].astype(BF16)
    sum_k[...] = jnp.zeros_like(sum_k)
    sum_v[...] = jnp.zeros_like(sum_v)
    gain_total = jnp.zeros((1, 2 * HD), F32)

    def back(upstream, unit, factor):
        scaled = gains * upstream
        return (factor * (scaled - unit * head_sums(scaled * unit, low_lanes))).astype(BF16)

    for tile in range(length // Q_TILE):
        start, end = key_range(tile)
        rows = slice(tile * Q_TILE, (tile + 1) * Q_TILE)
        query_raw = raw_q[rows, :]
        query_factor = head_factors(query_raw, low_lanes)
        query_unit = query_raw * query_factor
        query = (gains * query_unit).astype(BF16) * 8
        upstream = d_mixed[rows]
        tile_bias = bias[start:end, rows]
        d_query = []
        for low in (True, False):
            lanes = low_lanes if low else jnp.logical_not(low_lanes)
            own_query = jnp.where(lanes, query, jnp.zeros_like(query))
            own_up = jnp.where(lanes, upstream, jnp.zeros_like(upstream))
            expo = jnp.exp(nt(key[start:end], own_query) + tile_bias)
            probs = expo * (1.0 / jnp.sum(expo, axis=0, keepdims=True))
            d_probs = nt(value[start:end], own_up)
            delta = jnp.sum(probs * d_probs, axis=0, keepdims=True)
            d_scores = (probs * (d_probs - delta)).astype(BF16)
            sum_v[start:end, :] += nn(probs.astype(BF16), own_up)
            sum_k[start:end, :] += nn(d_scores, own_query)
            d_query.append(nn(key_eight[:, start:end], d_scores))
        d_query = jnp.where(low_rows, d_query[0], d_query[1]).T
        gain_total += jnp.sum(d_query * query_unit, axis=0, keepdims=True)
        d_raw_q[rows, :] = back(d_query, query_unit, query_factor)
    d_key = sum_k[...]
    gain_total += jnp.sum(d_key * key_unit, axis=0, keepdims=True)
    d_raw_k[...] = back(d_key, key_unit, key_factor)
    d_raw_v[...] = sum_v[...].astype(BF16)
    return gain_total


ARRIVE = 4 * LAG
UNIT_GROUP = 4
FIRST_UNIT_PAIR = 8
RARE_UNITS = 3


def head_tiles():
    return HEADS * HD // 2 // LANES


def unit_tiles():
    return FF // 2 // LANES


def forward_plan():
    groups = unit_tiles() // UNIT_GROUP
    return tile_plan((2 * (FIRST_UNIT_PAIR + 5 * groups) + 2 * (RARE_UNITS + groups)) * LANES)


def pair_tile(unit):
    return 2 * (FIRST_UNIT_PAIR + 5 * (unit // UNIT_GROUP) + unit % UNIT_GROUP)


def shrink_tile_static(unit):
    plan = forward_plan()
    group, place = unit // UNIT_GROUP, unit % UNIT_GROUP
    if place < 2:
        return plan[2][0] + place * plan[2][2] + RARE_UNITS + group
    return 2 * (FIRST_UNIT_PAIR + 5 * group + UNIT_GROUP) + place - 2


def shrink_tile(unit):
    plan = forward_plan()
    group, place = unit // UNIT_GROUP, unit % UNIT_GROUP
    rare = plan[2][0] + place * plan[2][2] + RARE_UNITS + group
    often = 2 * (FIRST_UNIT_PAIR + 5 * group + UNIT_GROUP) + place - 2
    return jnp.where(place < 2, rare, often)


def forward_sources():
    plan = forward_plan()
    heads, units = head_tiles(), unit_tiles()
    rare, rarer = plan[2][0], plan[3][0]
    inward = [("inward", k // heads, k % heads) for k in range(3 * heads)]
    sources = dict(enumerate(inward[:-1]))
    sources[rare] = inward[-1]
    sources[rarer] = ("small", None, 0)
    for tile, place in ((rare + 1, 0), (rarer + 1, 1), (3 * heads - 1, 2), (3 * heads, 3), (rare + 2, 4)):
        sources[tile] = ("outward", None, place)
    for unit in range(units):
        sources[pair_tile(unit)] = ("expand", 0, unit)
        sources[pair_tile(unit) + 1] = ("expand", 1, unit)
        sources[shrink_tile_static(unit)] = ("shrink", None, unit)
    return sources


def shrink_tile_static(unit):
    plan = forward_plan()
    group, place = unit // UNIT_GROUP, unit % UNIT_GROUP
    if place < 2:
        return plan[2][0] + place * plan[2][2] + RARE_UNITS + group
    return 2 * (FIRST_UNIT_PAIR + 5 * group + UNIT_GROUP) + place - 2


def forward_kernel(
    plan,
    inward,
    outward,
    expand,
    shrink,
    small_copies,
    tokens,
    cotangent,
    segments,
    pads,
    place_row,
    out,
    tokens_out,
    raw_out,
    mixed_out,
    h_attn_out,
    first_out,
    first_low_out,
    tokens_turned_out,
    first_turned_out,
    bias_out,
    d_two_out,
    output_out,
    d_shrunk_out,
    d_shrunk_turned_out,
    proj_out,
    hidden_out,
    factors,
    alphas,
    scales,
    gains,
    alpha_grad,
    block,
    shrunk,
    place,
    tokens_in,
    cot_in,
    bias,
    turned_bias,
    raw,
    stage_pair,
    stage_one,
    stage_outward,
    mixed,
    branch_in,
    h_attn,
    first,
    first_low,
    stage_proj,
    stage_hidden,
    own_sem,
    send_sem,
    recv_sem,
    pair_sem,
    one_sem,
    outward_sem,
    proj_sem,
    hidden_sem,
    result_sem,
    core_send,
    core_recv,
):
    me = lax.axis_index("dp")
    core = lax.axis_index("tensor")
    inv_root = D ** (-0.5)
    rows = tokens.shape[0]
    own_rows = rows // 2
    own_at = pl.multiple_of(core * own_rows, own_rows)
    other_at = pl.multiple_of((1 - core) * own_rows, own_rows)
    heads = head_tiles()
    units = unit_tiles()
    attend_at = 3 * heads // 2 + ARRIVE + 1
    pairs_each = 2
    sequences, length = segments.shape
    head_pairs = sequences * heads
    branch_at = attend_at + -(-head_pairs // pairs_each)
    units_at = branch_at + 2

    cot_copy = pltpu.make_async_copy(cotangent.at[pl.ds(own_at, own_rows)], cot_in, result_sem.at[13])
    cot_copy.start()
    operands = {
        "inward": inward,
        "outward": outward,
        "expand": expand,
        "shrink": shrink,
        "small": small_copies,
    }
    for tile, (name, row_block, at) in forward_sources().items():
        source = operands[name] if row_block is None else operands[name].at[row_block]
        block[:, tile * LANES : (tile + 1) * LANES] = source[
            :, at * LANES : (at + 1) * LANES
        ].astype(BF16)
    unused = plan[3][0] + 2
    block[:, unused * LANES : (unused + 1) * LANES] = jnp.zeros((block.shape[0], LANES), BF16)
    own = pltpu.make_async_copy(block, out.at[0, 0, 0, 0], own_sem)
    own.start()
    greet(me, core)

    def piece(hop, route, tile):
        lanes = lanes_of(plan, route, tile)
        crossed, axis = ROUTES[route][:hop], ROUTES[route][hop]
        source = [slice(None) if k in crossed else 0 for k in range(4)]
        target = [1 if k == axis else source[k] for k in range(4)]
        if hop == 0:
            source_ref = block.at[:, lanes]
        else:
            source_ref = out.at[(*source, slice(None), lanes)]
        return pltpu.make_async_remote_copy(
            src_ref=source_ref,
            dst_ref=out.at[(*target, slice(None), lanes)],
            send_sem=send_sem.at[hop, route, tile % RING],
            recv_sem=recv_sem.at[hop, route, tile],
            device_id={"dp": partner_of(me, PLACES[axis])},
            device_id_type=pl.DeviceIdType.MESH,
        )

    def forward_hop(hop, route, tile):
        if hop > 0:
            piece(hop - 1, route, tile).wait_recv()
        if hop < 4:

            @pl.when(tile >= RING)
            def _():
                piece(hop, route, tile - RING).wait_send()

            piece(hop, route, tile).start()

    def staged(tile, width, target, sem):
        lanes = pl.ds(pl.multiple_of(tile * LANES, LANES), width * LANES)
        return pltpu.make_async_copy(out.at[:, :, :, :, :, lanes], target, sem)

    def pair_copy(tile, slot):
        return staged(tile, 2, stage_pair.at[slot], pair_sem.at[slot])

    def one_copy(tile, slot):
        return staged(tile, 1, stage_one.at[slot], one_sem.at[slot])

    rare = plan[2][0]
    rarer = plan[3][0]

    def outward_copies():
        return [
            staged(tile, width, stage_outward.at[:, :, :, :, :, pl.ds(at * LANES, width * LANES)], outward_sem.at[k])
            for k, (tile, width, at) in enumerate(
                ((rare + 1, 1, 0), (rarer + 1, 1, 1), (3 * heads - 1, 2, 2), (rare + 2, 1, 4))
            )
        ]

    def core_copy(source, target, which):
        return pltpu.make_async_remote_copy(
            src_ref=source,
            dst_ref=target,
            send_sem=core_send.at[which],
            recv_sem=core_recv.at[which],
            device_id={"tensor": 1 - core},
            device_id_type=pl.DeviceIdType.MESH,
        )

    def branch_copy():
        return core_copy(shrunk.at[pl.ds(0, own_rows)], branch_in, 0)

    def first_copy():
        return core_copy(
            first_low.at[pl.ds(own_at, own_rows)], first_low.at[pl.ds(own_at, own_rows)], 1
        )

    def shrunk_copy():
        return core_copy(shrunk.at[pl.ds(other_at, own_rows)], branch_in, 2)

    def d_shrunk_copy():
        own = first_low.at[pl.ds(own_at, own_rows)]
        return core_copy(own, own, 3)

    result_pairs = (
        (tokens_in, tokens_out),
        (raw, raw_out),
        (mixed, mixed_out),
        (h_attn, h_attn_out),
        (first, first_out),
        (first_low, first_low_out),
        (place.at[:, pl.ds(0, rows)], tokens_turned_out),
        (place.at[:, pl.ds(0, rows)], first_turned_out),
        (turned_bias, bias_out),
        (h_attn, d_two_out),
        (tokens_in.at[pl.ds(own_at, own_rows)], output_out),
        (first_low, d_shrunk_out),
        (place.at[:, pl.ds(0, rows)], d_shrunk_turned_out),
    )

    def result(k):
        return pltpu.make_async_copy(*result_pairs[k], result_sem.at[k])

    def chunks(total, size, body):
        def one(k, _):
            body(pl.ds(pl.multiple_of(k * size, size), size))
            return 0

        lax.fori_loop(0, total // size, one, 0)

    def make_order():
        natural = place_row[...]

        def fill(at):
            here = lax.broadcasted_iota(jnp.int32, (LANES, D), 0) + at.start
            place[at, :] = jnp.where(here == natural, 1.0, 0.0).astype(BF16)

        chunks(D, LANES, fill)

    def tokens_in_order(number):
        at = pl.ds(pl.multiple_of(number * 256, 256), 256)
        tokens_in[at, :] = nn(tokens[at, :], place[...]).astype(BF16)

    def cot_in_order():
        cot_copy.wait()

        def move(at):
            cot_in[at, :] = nn(cot_in[at, :], place[...]).astype(BF16)

        chunks(own_rows, 256, move)

    def column_of(row):
        return jnp.broadcast_to(row.astype(F32), (LANES, length)).T

    def make_bias():
        for sequence in range(sequences):
            segment = segments[sequence : sequence + 1, :]
            pad = pads[sequence : sequence + 1, :]
            own_segment = column_of(segment)
            for tile in range(length // LANES):
                lanes = slice(tile * LANES, (tile + 1) * LANES)
                query = lax.broadcasted_iota(jnp.int32, (length, LANES), 0)
                key = lax.broadcasted_iota(jnp.int32, (length, LANES), 1) + tile * LANES
                open_key = jnp.where(pad[:, lanes] == 0, segment[:, lanes], -1).astype(F32)
                allowed = ((own_segment == open_key) & (key <= query)) | (key == query)
                values = jnp.where(allowed, 0.0, MASKED)
                bias[sequence, :, lanes] = values
                turned_bias[sequence, lanes, :] = values.T
        result(8).start()

    def finish():
        shrunk_copy().start()
        result(3).wait()
        keep = jnp.where(
            core == 0, column_of(1 - pads[0:1, :]), column_of(1 - pads[1:2, :])
        )
        stage_proj[0, :own_rows, :LANES] = keep
        alpha = alphas[1:2, :]
        alpha_grad[...] = jnp.zeros_like(alpha_grad)
        shrunk_copy().wait()

        def some(at):
            here = pl.ds(pl.multiple_of(own_at + at.start, 64), 64)
            normed, factor = row_norm(shrunk[here, :] + branch_in[at, :])
            start = first[at, :]
            output, output_factor = row_norm(start + alpha * (normed - start))
            upstream = cot_in[at, :].astype(F32) * stage_proj[0, at, 0:1]
            d_two = row_norm_back(upstream, output, output_factor)
            alpha_grad[0:1, :] += jnp.sum(d_two * (normed - start), axis=0, keepdims=True)
            h_attn[at, :] = d_two
            tokens_in[here, :] = output.astype(BF16)
            first_low[here, :] = row_norm_back(alpha * d_two, normed, factor).astype(BF16)

        chunks(own_rows, 64, some)
        d_shrunk_copy().start()
        result(9).start()
        result(10).start()
        result(7).wait()
        d_shrunk_copy().wait()
        result(11).start()
        turn(first_low)
        result(12).start()
        for k in (9, 10, 11, 12):
            result(k).wait()

    def turn(source):
        def some(at):
            place[:, at] = source[at, :].astype(F32).T.astype(BF16)

        chunks(rows, LANES, some)

    def project(weights, lanes):
        def some(at):
            raw[at, lanes] = nn(tokens_in[at, :], weights) * inv_root

        chunks(rows, 256, some)

    def small_vectors():
        small = stage_one[1].reshape(D, LANES).astype(F32).T
        alphas[...] = small[: alphas.shape[0]]
        scales[...] = nt(small.astype(BF16), place[...])[: scales.shape[0]]
        each = units * LANES // D
        for row in range(2):
            for k in range(each):
                at = 3 + row * 2 * each + k
                gains[row : row + 1, k * D : (k + 1) * D] = jnp.where(
                    core == 0, scales[at : at + 1, :], scales[at + each : at + each + 1, :]
                )

    def attend_one(number):
        sequence, head = number // heads, number % heads
        at = pl.ds(pl.multiple_of(sequence * length, length), length)
        lanes = [
            pl.ds(pl.multiple_of((k * heads + head) * LANES, LANES), LANES) for k in range(3)
        ]
        gain_lanes = pl.ds(pl.multiple_of((core * heads + head) * LANES, LANES), LANES)
        attend_pair(
            raw[at, lanes[0]],
            raw[at, lanes[1]],
            raw[at, lanes[2]],
            scales[2:3, gain_lanes],
            bias.at[sequence],
            mixed.at[at, lanes[0]],
        )

    def branch():
        weights = stage_outward[...].reshape(D, heads * LANES)
        for target, source in ((0, other_at), (own_rows, own_at)):
            for k in range(2):
                half = own_rows // 2
                at = pl.ds(pl.multiple_of(source + k * half, half), half)
                shrunk[pl.ds(target + k * half, half), :] = nt(mixed[at, :], weights)
            if target == 0:
                branch_copy().start()

    def norms():
        branch_copy().wait()
        alpha = alphas[0:1, :]

        def some(at):
            total = shrunk[pl.ds(pl.multiple_of(own_rows + at.start, 64), 64), :] + branch_in[at, :]
            normed, factor = row_norm(total)
            here = pl.ds(pl.multiple_of(own_at + at.start, 64), 64)
            inputs = tokens_in[here, :].astype(F32)
            result, result_factor = row_norm(inputs + alpha * (normed - inputs))
            h_attn[at, :] = normed
            first[at, :] = result
            first_low[here, :] = result.astype(BF16)
            factors[at, :LANES] = jnp.broadcast_to(factor, (64, LANES))
            factors[at, LANES:] = jnp.broadcast_to(result_factor, (64, LANES))

        chunks(own_rows, 64, some)
        first_copy().start()
        for k in (3, 4):
            result(k).start()

    def gain_of(unit, row):
        return gains[row : row + 1, pl.ds(pl.multiple_of(unit * LANES, LANES), LANES)]

    def proj_copy(unit):
        lanes = pl.ds(pl.multiple_of(unit * 2 * LANES, 2 * LANES), 2 * LANES)
        slot = unit % 2
        return pltpu.make_async_copy(stage_proj.at[slot], proj_out.at[:, lanes], proj_sem.at[slot])

    def hidden_copy(unit):
        lanes = pl.ds(pl.multiple_of(unit * LANES, LANES), LANES)
        slot = unit % 2
        return pltpu.make_async_copy(
            stage_hidden.at[slot], hidden_out.at[:, lanes], hidden_sem.at[slot]
        )

    def fetch_unit(unit):
        pair_copy(pair_tile(unit), unit % 2).start()
        one_copy(shrink_tile(unit), unit % 2).start()

    def one_unit(unit):
        slot = unit % 2

        @pl.when(unit == 0)
        def _():
            first_copy().wait()
            result(5).start()
            shrunk[...] = jnp.zeros_like(shrunk)

        @pl.when(unit >= 2)
        def _():
            proj_copy(unit - 2).wait()
            hidden_copy(unit - 2).wait()

        pair_copy(0, slot).wait()
        one_copy(0, slot).wait()
        weights = stage_pair[slot].reshape(D, 2 * LANES)
        down = stage_one[slot].reshape(D, LANES)
        gain_up = gain_of(unit, 0)
        gain_gate = gain_of(unit, 1)

        def some(at):
            proj = nn(first_low[at, :], weights) * inv_root
            stage_proj[slot, at, :] = proj
            gate = gain_gate * proj[:, LANES:]
            hidden = (gain_up * proj[:, :LANES] * (gate * jax.nn.sigmoid(gate))).astype(BF16)
            stage_hidden[slot, at, :] = hidden
            shrunk[at, :] += nt(hidden, down)

        chunks(rows, 256, some)
        proj_copy(unit).start()
        hidden_copy(unit).start()

    def step(index, _):
        for hop in range(5):
            for_tiles(index, hop, plan, functools.partial(forward_hop, hop))

        @pl.when(index == LAG - 1)
        def _():
            own.wait()

        order_at = ARRIVE - rows // 256

        @pl.when(index == order_at - 1)
        def _():
            make_order()

        @pl.when((index >= order_at) & (index < ARRIVE))
        def _():
            tokens_in_order(index - order_at)

        @pl.when(index == ARRIVE)
        def _():
            result(0).start()

        pair = index - ARRIVE

        @pl.when((pair >= 0) & (pair < 3 * heads // 2))
        def _():
            pair_copy(2 * pair, pair % 2).start()

        @pl.when(pair == 0)
        def _():
            one_copy(rare, 0).start()

        @pl.when(pair == EVERY // 2)
        def _():
            one_copy(rarer, 1).start()

        @pl.when((pair >= 1) & (pair <= 3 * heads // 2))
        def _():
            done = pair - 1
            pair_copy(0, done % 2).wait()
            lanes = pl.ds(pl.multiple_of(done * 2 * LANES, 2 * LANES), 2 * LANES)
            project(stage_pair[done % 2].reshape(D, 2 * LANES), lanes)

        @pl.when(pair == 1)
        def _():
            one_copy(0, 0).wait()
            project(stage_one[0].reshape(D, LANES), pl.ds((3 * heads - 1) * LANES, LANES))

        @pl.when(pair == EVERY // 2 + 1)
        def _():
            one_copy(0, 1).wait()
            small_vectors()

        @pl.when(pair == 4)
        def _():
            cot_in_order()

        @pl.when(pair == 5)
        def _():
            make_bias()

        @pl.when(pair == 6)
        def _():
            turn(tokens_in)
            result(6).start()

        @pl.when(index == units_at + 1)
        def _():
            result(6).wait()
            turn(first_low)
            result(7).start()

        @pl.when(index == attend_at)
        def _():
            result(1).start()
            for copy in outward_copies():
                copy.start()

        @pl.when((index >= attend_at) & (index < branch_at))
        def _():
            for k in range(pairs_each):
                attend_one((index - attend_at) * pairs_each + k)

        @pl.when(index == branch_at)
        def _():
            result(2).start()
            for copy in outward_copies():
                copy.wait()
            branch()

        @pl.when(index == branch_at + 1)
        def _():
            norms()

        unit = index - units_at

        @pl.when((unit >= -1) & (unit < units - 1))
        def _():
            fetch_unit(unit + 1)

        @pl.when((unit >= 0) & (unit < units))
        def _():
            one_unit(unit)

        return 0

    lax.fori_loop(0, max(steps_of(plan, 4), units_at + units), step, 0)
    for unit in (units - 2, units - 1):
        proj_copy(unit).wait()
        hidden_copy(unit).wait()
    for k in (0, 1, 2, 4, 5, 8):
        result(k).wait()
    finish()
    for route, (_, _, number, _, _) in enumerate(plan):
        for tile in range(max(0, number - RING), number):
            for hop in range(4):
                piece(hop, route, tile).wait_send()


def forward_pass(*operands, collective_id):
    plan = forward_plan()
    rows = operands[1].shape[0]
    count = operands[5].shape[0]
    sequences, length = operands[7].shape
    columns = sum(entry[2] for entry in plan) * LANES
    own = count // 2
    heads = head_tiles() * LANES
    units = unit_tiles() * LANES
    most = max(entry[2] for entry in plan)
    place = (2, 2, 2, 2, rows)
    hbm = pl.BlockSpec(memory_space=pl.ANY)
    vmem = pl.BlockSpec(memory_space=pltpu.VMEM)
    dma = pltpu.SemaphoreType.DMA
    return pl.pallas_call(
        functools.partial(forward_kernel, plan),
        out_shape=[
            jax.ShapeDtypeStruct((*place, columns), BF16),
            jax.ShapeDtypeStruct((count, D), BF16),
            jax.ShapeDtypeStruct((count, 3 * heads), F32),
            jax.ShapeDtypeStruct((count, heads), BF16),
            jax.ShapeDtypeStruct((own, D), F32),
            jax.ShapeDtypeStruct((own, D), F32),
            jax.ShapeDtypeStruct((count, D), BF16),
            jax.ShapeDtypeStruct((D, count), BF16),
            jax.ShapeDtypeStruct((D, count), BF16),
            jax.ShapeDtypeStruct((sequences, length, length), F32),
            jax.ShapeDtypeStruct((own, D), F32),
            jax.ShapeDtypeStruct((own, D), BF16),
            jax.ShapeDtypeStruct((count, D), BF16),
            jax.ShapeDtypeStruct((D, count), BF16),
            jax.ShapeDtypeStruct((count, 2 * units), F32),
            jax.ShapeDtypeStruct((count, units), BF16),
            jax.ShapeDtypeStruct((own, 2 * LANES), F32),
            jax.ShapeDtypeStruct((8, D), F32),
            jax.ShapeDtypeStruct((16, D), F32),
            jax.ShapeDtypeStruct((8, units), F32),
            jax.ShapeDtypeStruct((8, D), F32),
        ],
        in_specs=[vmem] * 6 + [hbm] + [vmem] * 3,
        out_specs=[hbm] * 16 + [vmem] * 5,
        scratch_shapes=[
            pltpu.VMEM((rows, columns), BF16),
            pltpu.VMEM((count, D), F32),
            pltpu.VMEM((D, D), BF16),
            pltpu.VMEM((count, D), BF16),
            pltpu.VMEM((own, D), BF16),
            pltpu.VMEM((sequences, length, length), F32),
            pltpu.VMEM((sequences, length, length), F32),
            pltpu.VMEM((count, 3 * heads), F32),
            pltpu.VMEM((2, *place, 2 * LANES), BF16),
            pltpu.VMEM((2, *place, LANES), BF16),
            pltpu.VMEM((*place, heads), BF16),
            pltpu.VMEM((count, heads), BF16),
            pltpu.VMEM((own, D), F32),
            pltpu.VMEM((own, D), F32),
            pltpu.VMEM((own, D), F32),
            pltpu.VMEM((count, D), BF16),
            pltpu.VMEM((2, count, 2 * LANES), F32),
            pltpu.VMEM((2, count, LANES), BF16),
            dma,
            dma((4, 4, RING)),
            dma((4, 4, most)),
            dma((2,)),
            dma((2,)),
            dma((4,)),
            dma((2,)),
            dma((2,)),
            dma((14,)),
            dma((4,)),
            dma((4,)),
        ],
        compiler_params=pltpu.CompilerParams(
            collective_id=collective_id, has_side_effects=True, vmem_limit_bytes=60 << 20
        ),
        name="forward_pass",
    )(*operands)


SLOTS = 2 * RING + 4


def backward_plan():
    return tile_plan((4 * head_tiles() + 3 * unit_tiles()) * LANES)


def gradient_tile(route, tile):
    heads, units = head_tiles(), unit_tiles()
    shrink_steps, late = units // 2 - 1, units // 4
    outward, up = 3 * heads, 4 * heads
    gate, shrink = up + units, up + 2 * units
    if route < 2:
        unit = tile - shrink_steps + late
        last = tile - shrink_steps - (units - late)
        return jnp.where(
            tile < shrink_steps,
            shrink + 2 * tile + 2 + route,
            jnp.where(
                last < 0,
                (up, gate)[route] + unit,
                jnp.where(last < 2, outward + 2 * last + route, 2 * (last - 2) + route),
            ),
        )
    of_unit = (up, gate)[route - 2] + tile - 1
    if route == 2:
        last = jnp.where(tile == late + 1, outward + heads - 1, outward - 2)
    else:
        last = jnp.where(tile == late + 1, outward - 3, outward - 1)
    return jnp.where(tile == 0, shrink + route - 2, jnp.where(tile <= late, of_unit, last))


def slot_of(route, tile):
    if route < 2:
        return route * RING + tile % RING
    return 2 * RING + (route - 2) * 2 + tile % 2


def ring_of(route):
    return RING if route < 2 else 2


def backward_kernel(
    plan,
    copies,
    d_shrunk,
    d_shrunk_turned,
    first_turned,
    tokens_turned,
    hidden,
    proj,
    raw,
    mixed,
    d_two,
    h_attn,
    first,
    tokens_in,
    factors,
    alphas,
    scales,
    gains,
    alpha_mlp_grad,
    bias,
    place_row,
    output,
    input_grad,
    block_output,
    grads,
    vectors,
    work,
    arrived,
    lefts,
    d_low,
    d_proj,
    first_part,
    core_in,
    stage_hidden,
    stage_rows,
    wide,
    outward,
    right,
    sum_k,
    sum_v,
    alpha_grad,
    unit_grad,
    query_grad,
    vector_sums,
    vector_in,
    send_sem,
    recv_sem,
    load_sem,
    unit_sem,
    raw_sem,
    result_sem,
    core_send,
    core_recv,
    vector_send,
    vector_recv,
):
    me = lax.axis_index("dp")
    core = lax.axis_index("tensor")
    inv_root = D ** (-0.5)
    rows = tokens_in.shape[0]
    own_rows = rows // 2
    own_at = pl.multiple_of(core * own_rows, own_rows)
    other_at = pl.multiple_of((1 - core) * own_rows, own_rows)
    heads = head_tiles()
    units = unit_tiles()
    block = D // 16
    unit_steps = units // 2
    shrink_steps = unit_steps - 1
    late_units = units // 4
    expand_steps = units - late_units
    attention_at = shrink_steps + expand_steps
    rare_units = 1 + late_units
    exchange_at = unit_steps
    attend_at = exchange_at + 3
    sequences = bias.shape[0]
    length = bias.shape[1]
    head_pairs = sequences * heads

    greet(me, core)

    def copy(source, target, sem):
        return pltpu.make_async_copy(source, target, sem)

    def chunks(total, size, body):
        def one(k, _):
            body(pl.ds(pl.multiple_of(k * size, size), size))
            return 0

        lax.fori_loop(0, total // size, one, 0)


    def piece(hop, route, tile):
        axis = ROUTES[route][3 - hop]
        slot = slot_of(route, tile)
        return pltpu.make_async_remote_copy(
            src_ref=work[hop].at[slot, 1],
            dst_ref=arrived[hop].at[slot],
            send_sem=send_sem.at[hop, slot],
            recv_sem=recv_sem.at[hop, slot],
            device_id={"dp": partner_of(me, PLACES[axis])},
            device_id_type=pl.DeviceIdType.MESH,
        )

    def free(hop, route, tile):
        @pl.when(tile >= ring_of(route))
        def _():
            piece(hop, route, tile - ring_of(route)).wait_send()

    def add(hop, route, tile):
        piece(hop - 1, route, tile).wait_recv()
        slot = slot_of(route, tile)
        total = work[hop - 1][slot, 0].astype(F32) + arrived[hop - 1][slot].astype(F32)
        if hop == 4:
            place = gradient_tile(route, tile)
            grads[:, pl.ds(pl.multiple_of(place * LANES, LANES), LANES)] = total
            return
        half = total.shape[0] // 2
        free(hop, route, tile)
        work[hop][slot, 0] = total[:half].astype(BF16)
        work[hop][slot, 1] = total[half:].astype(BF16)
        piece(hop, route, tile).start()

    def keep_quarter(route, slot, quarter, part):
        axes = ROUTES[route][::-1]
        if route < 2:
            bits = [quarter >> 1, quarter & 1]
            at = bits[axes[1]] * 4 * block
            work[0][slot, bits[axes[0]], at : at + 4 * block, :] = part
            return
        for low in range(4):
            bits = [quarter >> 1, quarter & 1, low >> 1, low & 1]
            index = bits[axes[1]] * 4 + bits[axes[2]] * 2 + bits[axes[3]]
            work[0][slot, bits[axes[0]], index * block : (index + 1) * block, :] = part[
                low * block : (low + 1) * block
            ]

    def quarter_rows(quarter):
        return slice(quarter * 4 * block, (quarter + 1) * 4 * block)

    def often_product(tile):
        for route in (0, 1):
            free(0, route, tile)
        is_shrink = tile < shrink_steps
        is_expand = (tile >= shrink_steps) & (tile < attention_at)
        late = tile - attention_at
        is_outward = (late >= 0) & (late < 2)

        @pl.when(is_shrink)
        def _():
            right[0] = stage_hidden[tile % 2]

        @pl.when(is_expand)
        def _():
            unit = tile - shrink_steps + late_units
            right[0] = d_proj[:, pl.ds(pl.multiple_of(unit * 2 * LANES, 2 * LANES), 2 * LANES)]

        @pl.when(late >= 0)
        def _():
            first_tile = jnp.where(late < 2, 2 * late, 2 * late + 1)
            right[0] = wide[:rows, pl.ds(pl.multiple_of(first_tile * LANES, LANES), 2 * LANES)]

        which = jnp.where(is_expand | is_outward, 1, 0)
        scale = jnp.where(is_shrink | is_outward, 1.0, inv_root)
        product = (nn(lefts[which], right[0]) * scale).astype(BF16)
        for quarter in range(4):
            part = product[quarter_rows(quarter)]
            for route in (0, 1):
                keep_quarter(
                    route, slot_of(route, tile), quarter, part[:, route * LANES : (route + 1) * LANES]
                )
        for route in (0, 1):
            piece(0, route, tile).start()

    def rare_product(route, tile):
        late = tile - rare_units
        at = (route - 2) * LANES
        lanes = slice(at, at + LANES)

        @pl.when(tile == 0)
        def _():
            right[1, :, lanes] = stage_hidden[2, :, lanes]

        @pl.when((tile > 0) & (late < 0))
        def _():
            unit_lane = pl.multiple_of((tile - 1) * 2 * LANES + at, LANES)
            right[1, :, lanes] = d_proj[:, pl.ds(unit_lane, LANES)]

        @pl.when(late >= 0)
        def _():
            if route == 2:
                place = jnp.where(late == 0, heads - 1, heads + 13)
            else:
                place = heads + 12 + 2 * late
            right[1, :, lanes] = wide[:rows, pl.ds(pl.multiple_of(place * LANES, LANES), LANES)]

        free(0, route, tile)
        of_units = (tile > 0) & (late < 0)
        of_outward = (late == 0) if route == 2 else (late < -rare_units)
        which = jnp.where(of_units | of_outward, 1, 0)
        scale = jnp.where((tile == 0) | of_outward, 1.0, inv_root)
        product = (nn(lefts[which], right[1, :, lanes]) * scale).astype(BF16)
        for quarter in range(4):
            keep_quarter(route, slot_of(route, tile), quarter, product[quarter_rows(quarter)])
        piece(0, route, tile).start()


    def unit_copies(pair):
        slot = pair % 2
        unit = 2 * pair
        at = pl.multiple_of(slot * 6 * LANES, 2 * LANES)
        result = [
            (
                copies.at[:, pl.ds(pl.multiple_of(pair_tile(unit) * LANES, LANES), 4 * LANES)],
                wide.at[:, pl.ds(at, 4 * LANES)],
            )
        ]
        for k in range(2):
            tile = shrink_tile(unit + k)
            result.append(
                (
                    copies.at[:, pl.ds(pl.multiple_of(tile * LANES, LANES), LANES)],
                    wide.at[:, pl.ds(pl.multiple_of(at + (4 + k) * LANES, LANES), LANES)],
                )
            )
        lanes = pl.ds(pl.multiple_of(pair * 4 * LANES, 4 * LANES), 4 * LANES)
        for k in range(2):
            result.append(
                (
                    proj.at[pl.ds(k * own_rows, own_rows), lanes],
                    stage_rows.at[slot, :, pl.ds(k * 4 * LANES, 4 * LANES)],
                )
            )
        return [copy(source, target, unit_sem.at[k, slot]) for k, (source, target) in enumerate(result)]

    def hidden_copy(tile):
        lanes = pl.ds(pl.multiple_of((2 * tile + 2) * LANES, 2 * LANES), 2 * LANES)
        return copy(hidden.at[:, lanes], stage_hidden.at[tile % 2], unit_sem.at[5, tile % 2])

    def unit_pair(pair):
        slot = pair % 2
        for part in unit_copies(pair):
            part.wait()
        at_lane = pl.multiple_of(slot * 6 * LANES, 2 * LANES)
        down = wide[:, pl.ds(pl.multiple_of(at_lane + 4 * LANES, 2 * LANES), 2 * LANES)]

        for half in range(2):
            at = slice(half * own_rows, (half + 1) * own_rows)
            proj_lanes = half * 4 * LANES
            d_hidden = nn(d_low[at, :], down)
            for k in range(2):
                lanes = pl.ds(pl.multiple_of((2 * pair + k) * LANES, LANES), LANES)
                gain_up, gain_gate = gains[0:1, lanes], gains[1:2, lanes]
                start = proj_lanes + 2 * k * LANES
                proj_up = stage_rows[slot, :, start : start + LANES]
                proj_gate = stage_rows[slot, :, start + LANES : start + 2 * LANES]
                upstream = d_hidden[:, k * LANES : (k + 1) * LANES]
                gate = gain_gate * proj_gate
                sigmoid = jax.nn.sigmoid(gate)
                d_up = upstream * (gate * sigmoid)
                d_gate = upstream * (gain_up * proj_up) * sigmoid * (1.0 + gate * (1.0 - sigmoid))
                unit_grad[0:1, lanes] += jnp.sum(d_up * proj_up, axis=0, keepdims=True)
                unit_grad[1:2, lanes] += jnp.sum(d_gate * proj_gate, axis=0, keepdims=True)
                place = pl.multiple_of((2 * pair + k) * 2 * LANES, 2 * LANES)
                d_proj[at, pl.ds(place, LANES)] = (d_up * gain_up).astype(BF16)
                d_proj[at, pl.ds(pl.multiple_of(place + LANES, LANES), LANES)] = (
                    d_gate * gain_gate
                ).astype(BF16)
        expand_at = pl.ds(at_lane, 4 * LANES)
        lanes = pl.ds(pl.multiple_of(pair * 4 * LANES, 4 * LANES), 4 * LANES)
        upstream = d_proj[:, lanes]
        for k in range(D // 256):
            columns = slice(k * 256, (k + 1) * 256)
            first_part[:, columns] += nt(upstream, wide[columns, expand_at])


    def core_copy(source, target, which):
        return pltpu.make_async_remote_copy(
            src_ref=source,
            dst_ref=target,
            send_sem=core_send.at[which],
            recv_sem=core_recv.at[which],
            device_id={"tensor": 1 - core},
            device_id_type=pl.DeviceIdType.MESH,
        )

    def part_copy():
        return core_copy(first_part.at[pl.ds(other_at, own_rows)], core_in, 0)

    def branch_copy():
        own = d_low.at[pl.ds(own_at, own_rows)]
        return core_copy(own, own, 1)

    tokens_place = wide.at[pl.ds(0, own_rows), pl.ds(D, D)]
    rare, rarer = forward_plan()[2][0], forward_plan()[3][0]
    outward_tiles = ((rare + 1, 1, 0), (rarer + 1, 1, 1), (3 * heads - 1, 2, 2), (rare + 2, 1, 4))

    def load(k):
        if k == 0:
            return copy(d_two, stage_rows.at[0], load_sem.at[0])
        if k == 1:
            return copy(h_attn, stage_rows.at[1], load_sem.at[1])
        if k == 2:
            return copy(tokens_in.at[pl.ds(own_at, own_rows)], tokens_place, load_sem.at[2])
        if k == 3:
            return copy(
                mixed, wide.at[pl.ds(0, rows), pl.ds(0, heads * LANES)], load_sem.at[3]
            )
        if k == 4:
            return copy(first, first_part.at[pl.ds(other_at, own_rows)], load_sem.at[4])
        if k == 5:
            return copy(d_shrunk, d_low, load_sem.at[5])
        if k == 6:
            return copy(d_shrunk_turned, lefts.at[0], load_sem.at[6])
        if k == 7:
            return copy(first_turned, lefts.at[1], load_sem.at[7])
        if k == 8:
            return copy(tokens_turned, lefts.at[0], load_sem.at[8])
        if k == 9:
            return copy(hidden.at[:, pl.ds(0, 2 * LANES)], stage_hidden.at[2], load_sem.at[9])
        tile, width, at = outward_tiles[k - 10]
        return copy(
            copies.at[:, pl.ds(tile * LANES, width * LANES)],
            outward.at[:, pl.ds(at * LANES, width * LANES)],
            load_sem.at[k],
        )

    def branch_gradient():
        part_copy().wait_send()
        load(4).start()
        part_copy().wait_recv()
        for k in (0, 1, 2, 4):
            load(k).wait()
        alpha_attn, alpha_mlp = alphas[0:1, :], alphas[1:2, :]

        def some(at):
            here = pl.ds(pl.multiple_of(own_at + at.start, 64), 64)
            there = pl.ds(pl.multiple_of(other_at + at.start, 64), 64)
            part = (first_part[here, :] + core_in[at, :]) * inv_root
            d_first = (1.0 - alpha_mlp) * stage_rows[0, at, :] + part
            normed = stage_rows[1, at, :]
            d_one = row_norm_back(
                d_first, first_part[there, :], factors[at, LANES : LANES + 1]
            )
            inputs = wide[at, D : 2 * D].astype(F32)
            alpha_grad[0:1, :] += jnp.sum(d_one * (normed - inputs), axis=0, keepdims=True)
            stage_rows[0, at, :] = d_one
            d_low[here, :] = row_norm_back(alpha_attn * d_one, normed, factors[at, 0:1]).astype(
                BF16
            )

        chunks(own_rows, 64, some)
        branch_copy().start()


    def raw_copies(number):
        sequence, head = number // heads, number % heads
        at = pl.ds(pl.multiple_of(sequence * length, length), length)
        slot = number % 2
        target_rows = pl.ds(pl.multiple_of(slot * own_rows, own_rows), length)
        return [
            copy(
                raw.at[at, pl.ds(pl.multiple_of((k * heads + head) * LANES, LANES), LANES)],
                first_part.at[target_rows, pl.ds(k * LANES, LANES)],
                raw_sem.at[k, slot],
            )
            for k in range(3)
        ]

    def attend_one(number):
        sequence, head = number // heads, number % heads
        for part in raw_copies(number):
            part.wait()
        at = pl.ds(pl.multiple_of(sequence * length, length), length)
        source_rows = pl.ds(pl.multiple_of((number % 2) * own_rows, own_rows), length)
        head_lanes = pl.ds(pl.multiple_of(head * LANES, LANES), LANES)
        gain_lanes = pl.ds(pl.multiple_of((core * heads + head) * LANES, LANES), LANES)
        d_mixed = nn(d_low[at, :], outward[:, head_lanes]).astype(BF16)
        targets = [
            wide.at[at, pl.ds(pl.multiple_of(((k + 1) * heads + head) * LANES, LANES), LANES)]
            for k in range(3)
        ]
        total = attend_pair_back(
            *[first_part.at[source_rows, pl.ds(k * LANES, LANES)] for k in range(3)],
            d_mixed,
            scales[2:3, gain_lanes],
            bias.at[sequence],
            *targets,
            sum_k,
            sum_v,
        )
        query_grad[0:1, head_lanes] += total


    head_lanes = 3 * heads * LANES
    beyond = D - rows

    def inward_copies():
        first_lanes = (3 * heads - 1) * LANES
        result = []
        for row, number, at, lane in ((0, rows, 0, 0), (rows, beyond, 0, head_lanes)):
            for source, width in ((0, first_lanes), (rare * LANES, LANES)):
                offset = 0 if width == first_lanes else first_lanes
                result.append(
                    (
                        copies.at[pl.ds(row, number), pl.ds(source, width)],
                        d_proj.at[pl.ds(at, number), pl.ds(lane + offset, width)],
                    )
                )
        return [copy(source, target, load_sem.at[14 + k]) for k, (source, target) in enumerate(result)]

    order_lane = 2 * head_lanes

    def make_order():
        natural = place_row[...]

        def fill(at):
            here = lax.broadcasted_iota(jnp.int32, (LANES, D), 0) + at.start
            d_proj[at, order_lane : order_lane + D] = jnp.where(here == natural, 1.0, 0.0).astype(
                BF16
            )

        chunks(rows, LANES, fill)
        for k in range(beyond // LANES):
            here = lax.broadcasted_iota(jnp.int32, (LANES, D), 0) + rows + k * LANES
            at = slice(beyond + k * LANES, beyond + (k + 1) * LANES)
            d_proj[at, head_lanes : head_lanes + D] = jnp.where(here == natural, 1.0, 0.0).astype(
                BF16
            )

    def natural_parts(values):
        low = nt(values, d_proj[:, order_lane : order_lane + D])
        high = nt(values, d_proj[beyond : 2 * beyond, head_lanes : head_lanes + D])
        return low, high

    def input_part(number):
        at = pl.ds(pl.multiple_of(number * 256, 256), 256)
        upstream = wide[at, heads * LANES : 4 * heads * LANES]
        low = nt(upstream, d_proj[:, :head_lanes]) * inv_root
        d_low[at, :rows] = low.astype(BF16)
        high = nt(upstream, d_proj[:beyond, head_lanes : 2 * head_lanes]) * inv_root
        d_low[at, rows:] = high.astype(BF16)
        low, high = natural_parts(d_low[at, :])
        first_part[at, :rows] = low
        first_part[at, rows:] = high

    def residual_part():
        alpha_attn = alphas[0:1, :]

        def some(at):
            here = pl.ds(pl.multiple_of(own_at + at.start, 128), 128)
            residual = (1.0 - alpha_attn) * stage_rows[0, at, :]
            top = residual.astype(BF16)
            rest = (residual - top.astype(F32)).astype(BF16)
            for part in (top, rest):
                low, high = natural_parts(part)
                first_part[here, :rows] += low
                first_part[here, rows:] += high

        chunks(own_rows, 128, some)

    half_width = D // 2

    def input_copies():
        lanes = pl.ds(pl.multiple_of((1 - core) * half_width, LANES), half_width)
        return [
            core_copy(
                first_part.at[pl.ds(k * own_rows, own_rows), lanes],
                core_in.at[:, pl.ds(k * half_width, half_width)],
                2 + k,
            )
            for k in range(2)
        ]

    def input_copy(k):
        lanes = pl.ds(pl.multiple_of(core * half_width, LANES), half_width)
        at = pl.ds(k * own_rows, own_rows)
        return copy(first_part.at[at, lanes], input_grad.at[at], result_sem.at[k])

    def input_sum():
        lanes = pl.ds(pl.multiple_of(core * half_width, LANES), half_width)
        for k, part in enumerate(input_copies()):
            part.wait()
            at = pl.ds(k * own_rows, own_rows)
            first_part[at, lanes] += core_in[:, k * half_width : (k + 1) * half_width]
            input_copy(k).start()

    def output_load():
        return copy(output, d_low.at[pl.ds(other_at, own_rows)], load_sem.at[18])

    def output_order():
        output_load().wait()
        for k in range(own_rows // 256):
            source = pl.ds(pl.multiple_of(other_at + k * 256, 256), 256)
            target = pl.ds(pl.multiple_of(own_at + k * 256, 256), 256)
            low, high = natural_parts(d_low[source, :])
            d_low[target, :rows] = low.astype(BF16)
            d_low[target, rows:] = high.astype(BF16)
        output_copies()[0].start()
        output_copies()[1].start()

    def output_copies():
        own = pl.ds(own_at, own_rows)
        return (
            core_copy(d_low.at[own], block_output.at[own], 4),
            copy(d_low.at[own], block_output.at[own], result_sem.at[2]),
        )

    def vector_copy(k):
        if k == 0:
            device = {"tensor": 1 - core}
        else:
            device = {"dp": partner_of(me, PLACES[k - 1])}
        return pltpu.make_async_remote_copy(
            src_ref=vector_sums.at[k],
            dst_ref=vector_in.at[k],
            send_sem=vector_send.at[k],
            recv_sem=vector_recv.at[k],
            device_id=device,
            device_id_type=pl.DeviceIdType.MESH,
        )

    def vectors_start():
        alpha_grad[1:2, :] = alpha_mlp_grad[0:1, :]
        vector_sums[0] = jnp.zeros_like(vector_sums[0])
        values = alpha_grad[...]
        for _ in range(3):
            part = values.astype(BF16)
            low, high = natural_parts(part)
            vector_sums[0, :8, :rows] += low
            vector_sums[0, :8, rows:] += high
            values = values - part.astype(F32)
        vector_sums[0, 2:3, pl.ds(pl.multiple_of(core * heads * LANES, LANES), heads * LANES)] = (
            query_grad[0:1, :]
        )
        each = units * LANES // D
        for row in range(2):
            for k in range(2 * each):
                here = unit_grad[row : row + 1, (k % each) * D : (k % each + 1) * D]
                at = 3 + 2 * each * row + k
                vector_sums[0, at : at + 1, :] = jnp.where(core == k // each, here, 0.0)
        vector_copy(0).start()

    def vectors_add(k):
        vector_copy(k).wait()
        total = vector_sums[k] + vector_in[k]
        if k < len(PLACES):
            vector_sums[k + 1] = total
            vector_copy(k + 1).start()
        else:
            vectors[...] = total

    input_at = attention_at + 1
    parts = rows // 256


    for k in (5, 6, 9, 7):
        load(k).start()
    for part in unit_copies(0):
        part.start()
    hidden_copy(0).start()
    alpha_grad[...] = jnp.zeros_like(alpha_grad)
    unit_grad[...] = jnp.zeros_like(unit_grad)
    query_grad[...] = jnp.zeros_like(query_grad)
    first_part[...] = jnp.zeros_like(first_part)
    for k in (5, 6, 9, 7):
        load(k).wait()

    def step(index, _):
        for hop in range(4, 0, -1):
            for_tiles(index, hop, plan, functools.partial(add, hop))

        @pl.when(index < shrink_steps)
        def _():
            hidden_copy(index).wait()

        @pl.when(index == attention_at)
        def _():
            load(8).wait()
            chunks(rows, LANES, turn)

        @pl.when(index < plan[0][2])
        def _():
            often_product(index)

        for route in (2, 3):
            number, start = plan[route][2], plan[route][4]
            due = index - start

            @pl.when((due % EVERY == 0) & (due >= 0) & (due < number * EVERY))
            def _(route=route, due=due):
                rare_product(route, due // EVERY)

        @pl.when(index + 1 < shrink_steps)
        def _():
            hidden_copy(index + 1).start()

        @pl.when(index + 1 < unit_steps)
        def _():
            for part in unit_copies(index + 1):
                part.start()

        @pl.when(index < unit_steps)
        def _():
            unit_pair(index)

        @pl.when(index == exchange_at)
        def _():
            part_copy().start()
            for k in (0, 1, 2, 3, 8, 10, 11, 12, 13):
                load(k).start()

        @pl.when(index == exchange_at + 1)
        def _():
            branch_gradient()

        @pl.when(index == exchange_at + 2)
        def _():
            branch_copy().wait()
            for k in (3, 10, 11, 12, 13):
                load(k).wait()

        number = index - attend_at

        @pl.when((number >= -1) & (number < head_pairs - 1))
        def _():
            for part in raw_copies(number + 1):
                part.start()

        @pl.when((number >= 0) & (number < head_pairs))
        def _():
            attend_one(number)

        @pl.when(index == attention_at)
        def _():
            for part in inward_copies():
                part.start()
            make_order()
            vectors_start()

        for k in range(len(PLACES) + 1):

            @pl.when(index == attention_at + 1 + k)
            def _(k=k):
                vectors_add(k)

        @pl.when(index == input_at)
        def _():
            for part in inward_copies():
                part.wait()

        @pl.when((index >= input_at) & (index < input_at + parts))
        def _():
            input_part(index - input_at)

        @pl.when(index == input_at + parts)
        def _():
            output_load().start()
            residual_part()
            for part in input_copies():
                part.start()

        @pl.when(index == input_at + parts + 1)
        def _():
            output_order()

        @pl.when(index == input_at + parts + 2)
        def _():
            input_sum()

        return 0

    def turn(at):
        lefts[1, :, at] = d_low[at, :].astype(F32).T.astype(BF16)

    lax.fori_loop(0, steps_of(plan, 4), step, 0)
    for part in output_copies():
        part.wait()
    for k in range(2):
        input_copy(k).wait()
    for route, (_, _, number, _, _) in enumerate(plan):
        for tile in range(max(0, number - ring_of(route)), number):
            for hop in range(4):
                piece(hop, route, tile).wait_send()


def backward_pass(*operands, collective_id):
    plan = backward_plan()
    copies = operands[0]
    count = operands[1].shape[0]
    own = count // 2
    heads = head_tiles() * LANES
    units = unit_tiles() * LANES
    length = operands[18].shape[1]
    block = D // 16
    halves = [block * 8 >> hop for hop in range(4)]
    hbm = pl.BlockSpec(memory_space=pl.ANY)
    vmem = pl.BlockSpec(memory_space=pltpu.VMEM)
    dma = pltpu.SemaphoreType.DMA
    return pl.pallas_call(
        functools.partial(backward_kernel, plan),
        out_shape=[
            jax.ShapeDtypeStruct((count, D // 2), F32),
            jax.ShapeDtypeStruct((count, D), BF16),
            jax.ShapeDtypeStruct((block, 4 * heads + 3 * units), F32),
            jax.ShapeDtypeStruct((16, D), F32),
        ],
        in_specs=[hbm] * 13 + [vmem] * 7 + [hbm],
        out_specs=[hbm] * 2 + [vmem] * 2,
        scratch_shapes=[
            [pltpu.VMEM((SLOTS, 2, half, LANES), BF16) for half in halves],
            [pltpu.VMEM((SLOTS, half, LANES), BF16) for half in halves],
            pltpu.VMEM((2, D, count), BF16),
            pltpu.VMEM((count, D), BF16),
            pltpu.VMEM((count, 2 * units), BF16),
            pltpu.VMEM((count, D), F32),
            pltpu.VMEM((own, D), F32),
            pltpu.VMEM((3, count, 2 * LANES), BF16),
            pltpu.VMEM((2, own, D), F32),
            pltpu.VMEM((D, 4 * heads), BF16),
            pltpu.VMEM((D, heads), BF16),
            pltpu.VMEM((2, count, 2 * LANES), BF16),
            pltpu.VMEM((length, LANES), F32),
            pltpu.VMEM((length, LANES), F32),
            pltpu.VMEM((8, D), F32),
            pltpu.VMEM((8, units), F32),
            pltpu.VMEM((8, heads), F32),
            pltpu.VMEM((5, 16, D), F32),
            pltpu.VMEM((5, 16, D), F32),
            dma((4, SLOTS)),
            dma((4, SLOTS)),
            dma((19,)),
            dma((6, 2)),
            dma((3, 2)),
            dma((3,)),
            dma((5,)),
            dma((5,)),
            dma((5,)),
            dma((5,)),
        ],
        compiler_params=pltpu.CompilerParams(
            collective_id=collective_id, has_side_effects=True, vmem_limit_bytes=62 << 20
        ),
        name="backward_pass",
    )(*operands)


UPDATE_STEPS = 5
SQUARE_ROWS = 8


def update_parts(refs):
    grads, states = refs[:7], [refs[7 + 3 * k : 10 + 3 * k] for k in range(4)]
    pieces = [(0, 0), (0, 1), (0, 2), (1, None), (2, 0), (2, 1), (3, None)]
    return [
        (grad[...], *[ref[...] if at is None else ref[at] for ref in states[which]])
        for grad, (which, at) in zip(grads, pieces)
    ]


def squares_kernel(*refs):
    inputs, (total, sums, arrived, send_sem, recv_sem) = refs[:19], refs[19:]
    index = pl.program_id(0)
    me = lax.axis_index("dp")
    planes = (PLACES[:2], PLACES[2:])
    hops = [
        [(low,), (high,), (low, high)] for low, high in planes
    ]

    def partner(bits):
        device = me
        for bit in bits:
            device = device + partner_of(me, bit) - me
        return {"dp": device}

    @pl.when(index == 0)
    def _():
        barrier = pltpu.get_barrier_semaphore()
        for hop in hops:
            for bits in hop:
                pl.semaphore_signal(
                    barrier, inc=1, device_id=partner(bits), device_id_type=pl.DeviceIdType.MESH
                )
        pl.semaphore_wait(barrier, 6)
        sums[...] = jnp.zeros_like(sums)

    heads = head_tiles()
    places = [(0, k * heads) for k in range(4)] + [(1, 0), (2, 0), (3, 0)]
    for (at, start), (gradient, master, first, second) in zip(places, update_parts(inputs)):
        pre = adam_step(master, first, second, gradient, RATE_MATRIX)[0]
        row = jnp.sum(pre * pre, axis=0, keepdims=True)
        width = row.shape[1]
        lanes = pl.ds(pl.multiple_of(start * LANES + index * width, LANES), width)
        sums[0, at : at + 1, lanes] = row

    @pl.when(index == UPDATE_STEPS - 1)
    def _():
        for number, hop in enumerate(hops):
            copies = [
                pltpu.make_async_remote_copy(
                    src_ref=sums.at[number],
                    dst_ref=arrived.at[number, k],
                    send_sem=send_sem.at[number, k],
                    recv_sem=recv_sem.at[number, k],
                    device_id=partner(bits),
                    device_id_type=pl.DeviceIdType.MESH,
                )
                for k, bits in enumerate(hop)
            ]
            for copy in copies:
                copy.start()
            for copy in copies:
                copy.wait()
            result = (sums[number] + arrived[number, 0]) + (
                arrived[number, 1] + arrived[number, 2]
            )
            if number == 0:
                sums[1] = result
            else:
                total[...] = result


def update_kernel(*refs):
    inputs, squares, small, outputs = refs[:19], refs[19:26], refs[26:34], refs[34:]
    results, small_results = outputs[:12], outputs[12:]
    index = pl.program_id(0)
    places = [(0, 0), (0, 1), (0, 2), (1, None), (2, 0), (2, 1), (3, None)]
    for number, (gradient, master, first, second) in enumerate(update_parts(inputs)):
        pre, variance = adam_step(master, first, second, gradient, RATE_MATRIX)
        row = max(0, number - 3)
        factor = lax.rsqrt(squares[number][row : row + 1, :] / D + EPS_NORM)
        which, at = places[number]
        for target, value in zip(results[3 * which : 3 * which + 3], (gradient, variance, pre * factor)):
            if at is None:
                target[...] = value
            else:
                target[at] = value

    @pl.when(index == 0)
    def _():
        for k, rate in enumerate((RATE_ALPHA, RATE_SCALE)):
            gradient, master, first, second = [ref[...] for ref in small[4 * k : 4 * k + 4]]
            updated, variance = adam_step(master, first, second, gradient, rate)
            for target, value in zip(
                small_results[3 * k : 3 * k + 3], (gradient, variance, updated)
            ):
                target[...] = value


def update_specs(rows):
    heads, units = head_tiles(), unit_tiles()
    wide = units // UPDATE_STEPS * LANES

    def columns(width, start):
        return pl.BlockSpec((rows, width), lambda i: (0, start + i))

    grads = [columns(LANES, k * heads) for k in range(4)]
    grads += [columns(wide, (4 * heads + k * units) * LANES // wide) for k in range(3)]
    inward = pl.BlockSpec((3, rows, LANES), lambda i: (0, 0, i))
    outward = pl.BlockSpec((rows, LANES), lambda i: (0, i))
    expand = pl.BlockSpec((2, rows, wide), lambda i: (0, 0, i))
    shrink = pl.BlockSpec((rows, wide), lambda i: (0, i))
    states = [inward] * 3 + [outward] * 3 + [expand] * 3 + [shrink] * 3
    squares = [
        pl.BlockSpec((SQUARE_ROWS, LANES), lambda i, k=k: (0, k * heads + i)) for k in range(4)
    ]
    squares += [pl.BlockSpec((SQUARE_ROWS, wide), lambda i: (0, i))] * 3
    return grads, states, squares


def update(grads, states, small, count, collective_id):
    rows = grads.shape[0]
    grad_specs, state_specs, square_specs = update_specs(rows)
    units = unit_tiles() * LANES
    shape = (SQUARE_ROWS, units)
    squares = pl.pallas_call(
        squares_kernel,
        grid=(UPDATE_STEPS,),
        out_shape=jax.ShapeDtypeStruct(shape, F32),
        in_specs=grad_specs + state_specs,
        out_specs=pl.BlockSpec(shape, lambda i: (0, 0)),
        scratch_shapes=[
            pltpu.VMEM((2, *shape), F32),
            pltpu.VMEM((2, 3, *shape), F32),
            pltpu.SemaphoreType.DMA((2, 3)),
            pltpu.SemaphoreType.DMA((2, 3)),
        ],
        compiler_params=pltpu.CompilerParams(
            collective_id=collective_id, has_side_effects=True, vmem_limit_bytes=60 << 20
        ),
        name="sum_squares",
    )(*[grads] * 7, *states)
    for bit in extra_bits(count):
        squares = squares + exchange(squares, bit, count)
    out_shape = [
        jax.ShapeDtypeStruct(states[3 * k].shape, F32) for k in range(4) for _ in range(3)
    ]
    out_shape += [jax.ShapeDtypeStruct(small[4 * k].shape, F32) for k in range(2) for _ in range(3)]

    def whole(array):
        return pl.BlockSpec(array.shape, lambda i: (0, 0))

    return pl.pallas_call(
        update_kernel,
        grid=(UPDATE_STEPS,),
        out_shape=out_shape,
        in_specs=grad_specs + state_specs + square_specs + [whole(array) for array in small],
        out_specs=state_specs + [whole(small[4 * k]) for k in range(2) for _ in range(3)],
        compiler_params=pltpu.CompilerParams(vmem_limit_bytes=60 << 20),
        name="update",
    )(*[grads] * 7, *states, *[squares] * 7, *small)


def per_device(
    tokens,
    cotangent,
    segment_ids,
    pad_mask,
    inward_master,
    inward_first,
    inward_second,
    outward_master,
    outward_first,
    outward_second,
    expand_master,
    expand_first,
    expand_second,
    shrink_master,
    shrink_first,
    shrink_second,
    alpha_master,
    alpha_first,
    alpha_second,
    scale_master,
    scale_first,
    scale_second,
):
    count = lax.axis_size("dp")
    me = lax.axis_index("dp")
    heads_width = inward_master.shape[2]

    small = jnp.concatenate([alpha_master, scale_master], axis=0).astype(BF16)
    small = jnp.pad(small, ((0, LANES - small.shape[0]), (0, 0))).T
    masters = (
        inward_master,
        outward_master.T,
        expand_master,
        shrink_master.T,
        small,
    )
    if extra_bits(count):
        masters = [gather_rest(master.astype(BF16), count) for master in masters]
    place_row = place_row_of(me, count)
    (
        copies,
        tokens_in,
        raw,
        mixed,
        h_attn,
        first,
        first_low,
        tokens_turned,
        first_turned,
        bias,
        d_two,
        output,
        d_shrunk,
        d_shrunk_turned,
        proj,
        hidden,
        factors,
        alphas,
        scale_rows,
        gains,
        alpha_mlp_grad,
    ) = forward_pass(
        *masters, tokens, cotangent, segment_ids, pad_mask, place_row, collective_id=0
    )

    input_grad, block_output, grads, vectors = backward_pass(
        copies.reshape(D, -1),
        d_shrunk,
        d_shrunk_turned,
        first_turned,
        tokens_turned,
        hidden,
        proj,
        raw,
        mixed,
        d_two,
        h_attn,
        first,
        tokens_in,
        factors,
        alphas,
        scale_rows,
        gains,
        alpha_mlp_grad,
        bias,
        place_row,
        output,
        collective_id=1,
    )
    grads = scatter_rest(grads, count)
    for bit in extra_bits(count):
        vectors = vectors + exchange(vectors, bit, count)
    width = D // count
    vectors = lax.dynamic_slice_in_dim(vectors, me * width, width, 1)
    alpha_grad, scale_grad = vectors[:2], vectors[2 : 2 + scale_master.shape[0]]

    states = (
        inward_master,
        inward_first,
        inward_second,
        outward_master.T,
        outward_first.T,
        outward_second.T,
        expand_master,
        expand_first,
        expand_second,
        shrink_master.T,
        shrink_first.T,
        shrink_second.T,
    )
    small = (
        alpha_grad,
        alpha_master,
        alpha_first,
        alpha_second,
        scale_grad,
        scale_master,
        scale_first,
        scale_second,
    )
    results = list(update(grads, states, small, count, 2))
    for k in (*range(3, 6), *range(9, 12)):
        results[k] = results[k].T
    return block_output, input_grad, *results


def solution(mesh):
    rows = P("dp", None)
    deep = P(None, "dp", "tensor")
    flat = P("tensor", "dp")
    vector = P(None, "dp")
    in_specs = (rows,) * 4 + (deep,) * 3 + (flat,) * 3 + (deep,) * 3 + (flat,) * 3 + (vector,) * 6
    out_specs = (
        (rows, P("dp", "tensor"))
        + (deep,) * 3
        + (flat,) * 3
        + (deep,) * 3
        + (flat,) * 3
        + (vector,) * 6
    )
    return jax.shard_map(
        per_device, mesh=mesh, in_specs=in_specs, out_specs=out_specs, check_vma=False
    )
```

```python
import functools

import jax
import jax.numpy as jnp
import numpy as np
from jax import lax
from jax.experimental import pallas as pl
from jax.experimental.pallas import tpu as pltpu
from jax.sharding import PartitionSpec as P

D = 1280
HEADS = 20
HD = 64
FF = 5120
STEP = 10
LONGEST = 256


EPS_NORM = 1e-06
BETA_ONE = 0.9
BETA_TWO = 0.95
ADAM_EPS = 1e-08
RATE_MATRIX = 0.3
RATE_ALPHA = 0.08
RATE_SCALE = 0.25
MASKED = -1e30
F32 = jnp.float32
BF16 = jnp.bfloat16


def row_norm(values):
    factor = lax.rsqrt(jnp.mean(values * values, axis=-1, keepdims=True) + EPS_NORM)
    return (values * factor, factor)


def row_norm_back(upstream, normed, factor):
    return factor * (upstream - normed * jnp.mean(upstream * normed, axis=-1, keepdims=True))


def adam_step(master, first_moment, second_moment, gradient, rate):
    first_new = BETA_ONE * first_moment.astype(F32) + (1.0 - BETA_ONE) * gradient
    second_new = BETA_TWO * second_moment + (1.0 - BETA_TWO) * gradient * gradient
    root = jnp.sqrt(second_new * (1.0 / (1.0 - BETA_TWO**STEP)))
    ratio = first_new * (rate / (1.0 - BETA_ONE**STEP)) / (root + ADAM_EPS)
    return (master - ratio, second_new)


LANES = 128
PLACES = (2, 1, 4, 8)
ROUTES = ((3, 2, 1, 0), (3, 2, 0, 1), (1, 0, 3, 2), (0, 1, 3, 2))
EVERY = 4
LAG = 2
RING = 4


def partner_of(me, bit):
    return me + bit - 2 * bit * ((me // bit) % 2)


def greet(me, core=None):
    barrier = pltpu.get_barrier_semaphore()
    partners = [{"dp": partner_of(me, bit)} for bit in PLACES]
    if core is not None:
        partners.append({"tensor": 1 - core})
    for partner in partners:
        pl.semaphore_signal(
            barrier, inc=1, device_id=partner, device_id_type=pl.DeviceIdType.MESH
        )
    pl.semaphore_wait(barrier, len(partners))


def tile_plan(columns):
    tiles = columns // LANES
    rare = tiles // 10
    often = (tiles - 2 * rare) // 2
    return (
        (0, 2, often, 1, 0),
        (1, 2, often, 1, 0),
        (2 * often, 1, rare, EVERY, 0),
        (2 * often + rare, 1, rare, EVERY, EVERY // 2),
    )


def for_tiles(step, hop, plan, body):
    for route, (_, _, number, every, start) in enumerate(plan):
        at = step - hop * LAG - start
        due = (at >= 0) & (at < number * every)
        if every > 1:
            due = due & (at % every == 0)

        @pl.when(due)
        def _():
            body(route, at // every)


def lanes_of(plan, route, tile):
    first, stride = plan[route][:2]
    return pl.ds(pl.multiple_of((first + stride * tile) * LANES, LANES), LANES)


def steps_of(plan, hops):
    return max(start + (number - 1) * every + 1 for _, _, number, every, start in plan) + hops * LAG


def extra_bits(count):
    return [bit for bit in (1 << k for k in range(4, count.bit_length() - 1))]


def exchange(array, bit, count):
    return lax.ppermute(array, "dp", [(i, i ^ bit) for i in range(count)])


def gather_rest(block, count):
    for bit in extra_bits(count)[::-1]:
        block = jnp.concatenate([block, exchange(block, bit, count)], axis=-2)
    return block


def scatter_rest(partial, count):
    for bit in extra_bits(count):
        half = partial.shape[0] // 2
        partial = partial[:half] + exchange(partial[half:], bit, count)
    return partial


def place_rows_of(count):
    places = list(PLACES) + extra_bits(count)
    width = D // count
    placed = np.arange(D, dtype=np.int32)
    position, offset = placed // width, placed % width
    relative = np.zeros_like(position)
    for axis, bit in enumerate(places):
        relative = relative + ((position >> (len(places) - 1 - axis)) & 1) * bit
    return np.stack([relative, offset])


def natural_row(place_row, me):
    count = lax.axis_size("dp")
    return (place_row[0:1, :] ^ me) * (D // count) + place_row[1:2, :]


def nn(a, b):
    return lax.dot_general(a, b, (((1,), (0,)), ((), ())), preferred_element_type=F32)


def nt(a, b):
    return lax.dot_general(a, b, (((1,), (1,)), ((), ())), preferred_element_type=F32)


def tn(a, b):
    return lax.dot_general(a, b, (((0,), (0,)), ((), ())), preferred_element_type=F32)


def head_factors(raw, low_lanes):
    squares = raw * raw
    low = jnp.sum(jnp.where(low_lanes, squares, 0.0), axis=-1, keepdims=True)
    high = jnp.sum(jnp.where(low_lanes, 0.0, squares), axis=-1, keepdims=True)
    return jnp.where(low_lanes, lax.rsqrt(low + EPS_NORM), lax.rsqrt(high + EPS_NORM))


def head_sums(values, low_lanes):
    low = jnp.sum(jnp.where(low_lanes, values, 0.0), axis=-1, keepdims=True)
    high = jnp.sum(jnp.where(low_lanes, 0.0, values), axis=-1, keepdims=True)
    return jnp.where(low_lanes, low, high)


Q_TILE = 128


def key_range(tile):
    start = max(0, tile * Q_TILE - LONGEST)
    return start, (tile + 1) * Q_TILE


def attend_pair(query, key, value, gain, bias, mixed):
    length = query.shape[0]
    low_lanes = lax.broadcasted_iota(jnp.int32, (1, 2 * HD), 1) < HD
    query = (gain * (query * head_factors(query, low_lanes))).astype(BF16) * 8
    key = (gain * (key * head_factors(key, low_lanes))).astype(BF16)
    value = value.astype(BF16)
    zero = jnp.zeros_like(query)
    parts = (jnp.where(low_lanes, query, zero), jnp.where(low_lanes, zero, query))
    for tile in range(length // Q_TILE):
        start, end = key_range(tile)
        rows = slice(tile * Q_TILE, (tile + 1) * Q_TILE)
        tile_bias = bias[rows, start:end]
        results = []
        for part in parts:
            expo = jnp.exp(nt(part[rows], key[start:end]) + tile_bias)
            total = jnp.sum(expo, axis=-1, keepdims=True)
            results.append(nn(expo.astype(BF16), value[start:end]) * (1.0 / total))
        mixed[rows, :] = jnp.where(low_lanes, results[0], results[1]).astype(BF16)


def attend_pair_back(
    raw_q, raw_k, raw_v, d_mixed, gains, bias, d_raw_q, d_raw_k, d_raw_v, sum_k, sum_v
):
    length = raw_q.shape[0]
    low_lanes = lax.broadcasted_iota(jnp.int32, (1, 2 * HD), 1) < HD
    low_rows = lax.broadcasted_iota(jnp.int32, (2 * HD, 1), 0) < HD
    key_raw = raw_k[...]
    key_factor = head_factors(key_raw, low_lanes)
    key_unit = key_raw * key_factor
    key = (gains * key_unit).astype(BF16)
    key_eight = ((gains * key_unit).astype(BF16).astype(F32) * 8.0).T.astype(BF16)
    value = raw_v[...].astype(BF16)
    sum_k[...] = jnp.zeros_like(sum_k)
    sum_v[...] = jnp.zeros_like(sum_v)
    gain_total = jnp.zeros((1, 2 * HD), F32)

    def back(upstream, unit, factor):
        scaled = gains * upstream
        return (factor * (scaled - unit * head_sums(scaled * unit, low_lanes))).astype(BF16)

    for tile in range(length // Q_TILE):
        start, end = key_range(tile)
        rows = slice(tile * Q_TILE, (tile + 1) * Q_TILE)
        query_raw = raw_q[rows, :]
        query_factor = head_factors(query_raw, low_lanes)
        query_unit = query_raw * query_factor
        query = (gains * query_unit).astype(BF16) * 8
        upstream = d_mixed[rows]
        tile_bias = bias[start:end, rows]
        d_query = []
        for low in (True, False):
            lanes = low_lanes if low else jnp.logical_not(low_lanes)
            own_query = jnp.where(lanes, query, jnp.zeros_like(query))
            own_up = jnp.where(lanes, upstream, jnp.zeros_like(upstream))
            expo = jnp.exp(nt(key[start:end], own_query) + tile_bias)
            probs = expo * (1.0 / jnp.sum(expo, axis=0, keepdims=True))
            d_probs = nt(value[start:end], own_up)
            delta = jnp.sum(probs * d_probs, axis=0, keepdims=True)
            d_scores = (probs * (d_probs - delta)).astype(BF16)
            sum_v[start:end, :] += nn(probs.astype(BF16), own_up)
            sum_k[start:end, :] += nn(d_scores, own_query)
            d_query.append(nn(key_eight[:, start:end], d_scores))
        d_query = jnp.where(low_rows, d_query[0], d_query[1]).T
        gain_total += jnp.sum(d_query * query_unit, axis=0, keepdims=True)
        d_raw_q[rows, :] = back(d_query, query_unit, query_factor)
    d_key = sum_k[...]
    gain_total += jnp.sum(d_key * key_unit, axis=0, keepdims=True)
    d_raw_k[...] = back(d_key, key_unit, key_factor)
    d_raw_v[...] = sum_v[...].astype(BF16)
    return gain_total


ARRIVE = 4 * LAG
UNIT_GROUP = 4
FIRST_UNIT_PAIR = 8
RARE_UNITS = 3


def head_tiles():
    return HEADS * HD // 2 // LANES


def unit_tiles():
    return FF // 2 // LANES


def forward_plan():
    groups = unit_tiles() // UNIT_GROUP
    return tile_plan((2 * (FIRST_UNIT_PAIR + 5 * groups) + 2 * (RARE_UNITS + groups)) * LANES)


def pair_tile(unit):
    return 2 * (FIRST_UNIT_PAIR + 5 * (unit // UNIT_GROUP) + unit % UNIT_GROUP)


def shrink_tile_static(unit):
    plan = forward_plan()
    group, place = unit // UNIT_GROUP, unit % UNIT_GROUP
    if place < 2:
        return plan[2][0] + place * plan[2][2] + RARE_UNITS + group
    return 2 * (FIRST_UNIT_PAIR + 5 * group + UNIT_GROUP) + place - 2


def shrink_tile(unit):
    plan = forward_plan()
    group, place = unit // UNIT_GROUP, unit % UNIT_GROUP
    rare = plan[2][0] + place * plan[2][2] + RARE_UNITS + group
    often = 2 * (FIRST_UNIT_PAIR + 5 * group + UNIT_GROUP) + place - 2
    return jnp.where(place < 2, rare, often)


def forward_sources():
    plan = forward_plan()
    heads, units = head_tiles(), unit_tiles()
    rare, rarer = plan[2][0], plan[3][0]
    inward = [("inward", k // heads, k % heads) for k in range(3 * heads)]
    sources = dict(enumerate(inward[:-1]))
    sources[rare] = inward[-1]
    sources[rarer] = ("small", None, 0)
    for tile, place in ((rare + 1, 0), (rarer + 1, 1), (3 * heads - 1, 2), (3 * heads, 3), (rare + 2, 4)):
        sources[tile] = ("outward", None, place)
    for unit in range(units):
        sources[pair_tile(unit)] = ("expand", 0, unit)
        sources[pair_tile(unit) + 1] = ("expand", 1, unit)
        sources[shrink_tile_static(unit)] = ("shrink", None, unit)
    return sources


def shrink_tile_static(unit):
    plan = forward_plan()
    group, place = unit // UNIT_GROUP, unit % UNIT_GROUP
    if place < 2:
        return plan[2][0] + place * plan[2][2] + RARE_UNITS + group
    return 2 * (FIRST_UNIT_PAIR + 5 * group + UNIT_GROUP) + place - 2


def forward_kernel(
    plan,
    inward,
    outward,
    expand,
    shrink,
    small_copies,
    tokens,
    cotangent,
    segments,
    pads,
    place_row,
    out,
    tokens_out,
    raw_out,
    mixed_out,
    h_attn_out,
    first_out,
    first_low_out,
    tokens_turned_out,
    first_turned_out,
    bias_out,
    d_two_out,
    output_out,
    d_shrunk_out,
    d_shrunk_turned_out,
    proj_out,
    hidden_out,
    factors,
    alphas,
    scales,
    gains,
    alpha_grad,
    block,
    shrunk,
    place,
    tokens_in,
    cot_in,
    bias,
    turned_bias,
    raw,
    stage_pair,
    stage_one,
    stage_outward,
    mixed,
    branch_in,
    h_attn,
    first,
    first_low,
    stage_proj,
    stage_hidden,
    keep,
    own_sem,
    send_sem,
    recv_sem,
    pair_sem,
    one_sem,
    outward_sem,
    proj_sem,
    hidden_sem,
    result_sem,
    core_send,
    core_recv,
):
    me = lax.axis_index("dp")
    core = lax.axis_index("tensor")
    inv_root = D ** (-0.5)
    rows = tokens.shape[0]
    own_rows = rows // 2
    own_at = pl.multiple_of(core * own_rows, own_rows)
    other_at = pl.multiple_of((1 - core) * own_rows, own_rows)
    heads = head_tiles()
    units = unit_tiles()
    attend_at = 3 * heads // 2 + ARRIVE + 1
    pairs_each = 2
    sequences, length = segments.shape
    head_pairs = sequences * heads
    branch_at = attend_at + -(-head_pairs // pairs_each)
    units_at = branch_at + 2

    cot_copy = pltpu.make_async_copy(cotangent.at[pl.ds(own_at, own_rows)], cot_in, result_sem.at[13])
    cot_copy.start()
    operands = {
        "inward": inward,
        "outward": outward,
        "expand": expand,
        "shrink": shrink,
        "small": small_copies,
    }
    for tile, (name, row_block, at) in forward_sources().items():
        source = operands[name] if row_block is None else operands[name].at[row_block]
        block[:, tile * LANES : (tile + 1) * LANES] = source[
            :, at * LANES : (at + 1) * LANES
        ].astype(BF16)
    unused = plan[3][0] + 2
    block[:, unused * LANES : (unused + 1) * LANES] = jnp.zeros((block.shape[0], LANES), BF16)
    own = pltpu.make_async_copy(block, out.at[0, 0, 0, 0], own_sem)
    own.start()
    greet(me, core)

    def piece(hop, route, tile):
        lanes = lanes_of(plan, route, tile)
        crossed, axis = ROUTES[route][:hop], ROUTES[route][hop]
        source = [slice(None) if k in crossed else 0 for k in range(4)]
        target = [1 if k == axis else source[k] for k in range(4)]
        if hop == 0:
            source_ref = block.at[:, lanes]
        else:
            source_ref = out.at[(*source, slice(None), lanes)]
        return pltpu.make_async_remote_copy(
            src_ref=source_ref,
            dst_ref=out.at[(*target, slice(None), lanes)],
            send_sem=send_sem.at[hop, route, tile % RING],
            recv_sem=recv_sem.at[hop, route, tile],
            device_id={"dp": partner_of(me, PLACES[axis])},
            device_id_type=pl.DeviceIdType.MESH,
        )

    def forward_hop(hop, route, tile):
        if hop > 0:
            piece(hop - 1, route, tile).wait_recv()
        if hop < 4:

            @pl.when(tile >= RING)
            def _():
                piece(hop, route, tile - RING).wait_send()

            piece(hop, route, tile).start()

    def staged(tile, width, target, sem):
        lanes = pl.ds(pl.multiple_of(tile * LANES, LANES), width * LANES)
        return pltpu.make_async_copy(out.at[:, :, :, :, :, lanes], target, sem)

    def lanes_half(number):
        return pl.ds(pl.multiple_of((number % 2) * LANES, LANES), LANES)

    def pair_copy(tile, slot):
        return staged(tile, 2, stage_pair.at[slot], pair_sem.at[slot])

    def one_copy(tile, number):
        target = stage_one.at[(number // 2) % 2, :, :, :, :, :, lanes_half(number)]
        return staged(tile, 1, target, one_sem.at[number % 2])

    rare = plan[2][0]
    rarer = plan[3][0]

    def outward_copies():
        return [
            staged(tile, width, stage_outward.at[:, :, :, :, :, pl.ds(at * LANES, width * LANES)], outward_sem.at[k])
            for k, (tile, width, at) in enumerate(
                ((rare + 1, 1, 0), (rarer + 1, 1, 1), (3 * heads - 1, 2, 2), (rare + 2, 1, 4))
            )
        ]

    def core_copy(source, target, which):
        return pltpu.make_async_remote_copy(
            src_ref=source,
            dst_ref=target,
            send_sem=core_send.at[which],
            recv_sem=core_recv.at[which],
            device_id={"tensor": 1 - core},
            device_id_type=pl.DeviceIdType.MESH,
        )

    def branch_copy():
        return core_copy(shrunk.at[pl.ds(0, own_rows)], branch_in, 0)

    def first_copy():
        return core_copy(
            first_low.at[pl.ds(own_at, own_rows)], first_low.at[pl.ds(own_at, own_rows)], 1
        )

    half_rows = own_rows // 2

    def shrunk_copy(k):
        source = pl.ds(pl.multiple_of(other_at + k * half_rows, half_rows), half_rows)
        return core_copy(shrunk.at[source], branch_in.at[pl.ds(k * half_rows, half_rows)], 2 + k)

    def d_shrunk_copy(k):
        at = pl.ds(pl.multiple_of(own_at + k * half_rows, half_rows), half_rows)
        return core_copy(first_low.at[at], first_low.at[at], 4 + k)

    result_pairs = (
        (tokens_in, tokens_out),
        (raw, raw_out),
        (mixed, mixed_out),
        (h_attn, h_attn_out),
        (first, first_out),
        (first_low, first_low_out),
        (place.at[:, pl.ds(0, rows)], tokens_turned_out),
        (place.at[:, pl.ds(0, rows)], first_turned_out),
        (turned_bias, bias_out),
        (h_attn, d_two_out),
        (tokens_in.at[pl.ds(own_at, own_rows)], output_out),
        (first_low, d_shrunk_out),
        (place.at[:, pl.ds(0, rows)], d_shrunk_turned_out),
    )

    def result(k):
        return pltpu.make_async_copy(*result_pairs[k], result_sem.at[k])

    def chunks(total, size, body):
        def one(k, _):
            body(pl.ds(pl.multiple_of(k * size, size), size))
            return 0

        lax.fori_loop(0, total // size, one, 0)

    def make_order():
        natural = natural_row(place_row, me)

        def fill(at):
            here = lax.broadcasted_iota(jnp.int32, (LANES, D), 0) + at.start
            place[at, :] = jnp.where(here == natural, 1.0, 0.0).astype(BF16)

        chunks(D, LANES, fill)

    def tokens_in_order(number):
        at = pl.ds(pl.multiple_of(number * 256, 256), 256)
        tokens_in[at, :] = nn(tokens[at, :], place[...]).astype(BF16)

    def cot_in_order():
        cot_copy.wait()

        def move(at):
            cot_in[at, :] = nn(cot_in[at, :], place[...]).astype(BF16)

        chunks(own_rows, 256, move)

    def column_of(row):
        return jnp.broadcast_to(row.astype(F32), (LANES, length)).T

    def make_bias():
        for sequence in range(sequences):
            segment = segments[sequence : sequence + 1, :]
            pad = pads[sequence : sequence + 1, :]
            own_segment = column_of(segment)
            for tile in range(length // LANES):
                lanes = slice(tile * LANES, (tile + 1) * LANES)
                query = lax.broadcasted_iota(jnp.int32, (length, LANES), 0)
                key = lax.broadcasted_iota(jnp.int32, (length, LANES), 1) + tile * LANES
                open_key = jnp.where(pad[:, lanes] == 0, segment[:, lanes], -1).astype(F32)
                allowed = ((own_segment == open_key) & (key <= query)) | (key == query)
                values = jnp.where(allowed, 0.0, MASKED)
                bias[sequence, :, lanes] = values
                turned_bias[sequence, lanes, :] = values.T
        result(8).start()
        keep[...] = jnp.where(core == 0, column_of(1 - pads[0:1, :]), column_of(1 - pads[1:2, :]))

    def finish():
        alpha = alphas[1:2, :]
        alpha_grad[...] = jnp.zeros_like(alpha_grad)

        def some(at):
            here = pl.ds(pl.multiple_of(own_at + at.start, 64), 64)
            normed, factor = row_norm(shrunk[here, :] + branch_in[at, :])
            start = first[at, :]
            output, output_factor = row_norm(start + alpha * (normed - start))
            upstream = cot_in[at, :].astype(F32) * keep[at, 0:1]
            d_two = row_norm_back(upstream, output, output_factor)
            alpha_grad[0:1, :] += jnp.sum(d_two * (normed - start), axis=0, keepdims=True)
            h_attn[at, :] = d_two
            tokens_in[here, :] = output.astype(BF16)
            first_low[here, :] = row_norm_back(alpha * d_two, normed, factor).astype(BF16)

        def span(k, size, start, body):
            def one(j, _):
                body(pl.ds(pl.multiple_of(start + k * half_rows + j * size, size), size))
                return 0

            lax.fori_loop(0, half_rows // size, one, 0)

        for k in range(2):
            shrunk_copy(k).wait()
            span(k, 64, 0, some)
            d_shrunk_copy(k).start()
        result(9).start()
        result(10).start()
        for k in range(2):
            span(k, LANES, own_at, lambda at: turn_rows(first_low, at))
        for k in range(2):
            d_shrunk_copy(k).wait()
            span(k, LANES, other_at, lambda at: turn_rows(first_low, at))
        result(12).start()
        result(11).start()
        for k in (9, 10, 11, 12):
            result(k).wait()

    def turn_rows(source, at):
        place[:, at] = source[at, :].astype(F32).T.astype(BF16)

    def turn(source):
        chunks(rows, LANES, functools.partial(turn_rows, source))

    def project(weights, lanes):
        def some(at):
            raw[at, lanes] = nn(tokens_in[at, :], weights) * inv_root

        chunks(rows, 256, some)

    def small_vectors():
        small = stage_one[0, :, :, :, :, :, LANES:].reshape(D, LANES).astype(F32).T
        alphas[...] = small[: alphas.shape[0]]
        scales[...] = nt(small.astype(BF16), place[...])[: scales.shape[0]]
        each = units * LANES // D
        for row in range(2):
            for k in range(each):
                at = 3 + row * 2 * each + k
                gains[row : row + 1, k * D : (k + 1) * D] = jnp.where(
                    core == 0, scales[at : at + 1, :], scales[at + each : at + each + 1, :]
                )

    def attend_one(number):
        sequence, head = number // heads, number % heads
        at = pl.ds(pl.multiple_of(sequence * length, length), length)
        lanes = [
            pl.ds(pl.multiple_of((k * heads + head) * LANES, LANES), LANES) for k in range(3)
        ]
        gain_lanes = pl.ds(pl.multiple_of((core * heads + head) * LANES, LANES), LANES)
        attend_pair(
            raw[at, lanes[0]],
            raw[at, lanes[1]],
            raw[at, lanes[2]],
            scales[2:3, gain_lanes],
            bias.at[sequence],
            mixed.at[at, lanes[0]],
        )

    def branch():
        weights = stage_outward[...].reshape(D, heads * LANES)
        for target, source in ((0, other_at), (own_rows, own_at)):
            for k in range(2):
                half = own_rows // 2
                at = pl.ds(pl.multiple_of(source + k * half, half), half)
                shrunk[pl.ds(target + k * half, half), :] = nt(mixed[at, :], weights)
            if target == 0:
                branch_copy().start()

    def norms():
        branch_copy().wait()
        alpha = alphas[0:1, :]

        def some(at):
            total = shrunk[pl.ds(pl.multiple_of(own_rows + at.start, 64), 64), :] + branch_in[at, :]
            normed, factor = row_norm(total)
            here = pl.ds(pl.multiple_of(own_at + at.start, 64), 64)
            inputs = tokens_in[here, :].astype(F32)
            result, result_factor = row_norm(inputs + alpha * (normed - inputs))
            h_attn[at, :] = normed
            first[at, :] = result
            first_low[here, :] = result.astype(BF16)
            factors[at, :LANES] = jnp.broadcast_to(factor, (64, LANES))
            factors[at, LANES:] = jnp.broadcast_to(result_factor, (64, LANES))

        chunks(own_rows, 64, some)
        first_copy().start()
        for k in (3, 4):
            result(k).start()

    def gain_of(unit, row):
        return gains[row : row + 1, pl.ds(pl.multiple_of(unit * LANES, LANES), LANES)]

    def proj_copy(unit):
        lanes = pl.ds(pl.multiple_of(unit * 2 * LANES, 2 * LANES), 2 * LANES)
        slot = unit % 2
        return pltpu.make_async_copy(stage_proj.at[slot], proj_out.at[:, lanes], proj_sem.at[slot])

    def hidden_copy(pair):
        lanes = pl.ds(pl.multiple_of(pair * 2 * LANES, 2 * LANES), 2 * LANES)
        slot = pair % 2
        return pltpu.make_async_copy(
            stage_hidden.at[slot], hidden_out.at[:, lanes], hidden_sem.at[slot]
        )

    def fetch_unit(unit):
        pair_copy(pair_tile(unit), unit % 2).start()
        one_copy(shrink_tile(unit), unit).start()

    def add_shrunk(pair):
        down = stage_one[pair % 2].reshape(D, 2 * LANES)
        for part, start in enumerate((other_at, own_at)):
            at = pl.ds(start, own_rows)
            values = stage_hidden[pair % 2, at, :]
            for k in range(D // 256):
                columns = slice(k * 256, (k + 1) * 256)
                shrunk[at, columns] += nt(values, down[columns])
            if part == 0:

                @pl.when(pair == units // 2 - 1)
                def _():
                    result(5).wait()
                    for k in range(2):
                        shrunk_copy(k).start()

        hidden_copy(pair).start()

    def one_unit(unit):
        slot = unit % 2
        pair = unit // 2

        @pl.when(unit == 0)
        def _():
            first_copy().wait()
            result(5).start()
            shrunk[...] = jnp.zeros_like(shrunk)

        @pl.when(unit >= 2)
        def _():
            proj_copy(unit - 2).wait()

        @pl.when((unit >= 4) & (slot == 0))
        def _():
            hidden_copy(pair - 2).wait()

        pair_copy(0, slot).wait()
        one_copy(0, unit).wait()
        weights = stage_pair[slot].reshape(D, 2 * LANES)
        gain_up = gain_of(unit, 0)
        gain_gate = gain_of(unit, 1)

        def some(at):
            proj = nn(first_low[at, :], weights) * inv_root
            stage_proj[slot, at, :] = proj
            gate = gain_gate * proj[:, LANES:]
            hidden = (gain_up * proj[:, :LANES] * (gate * jax.nn.sigmoid(gate))).astype(BF16)
            stage_hidden[pair % 2, at, lanes_half(unit)] = hidden

        chunks(rows, own_rows, some)
        proj_copy(unit).start()

        @pl.when(slot == 1)
        def _():
            add_shrunk(pair)

    def step(index, _):
        for hop in range(5):
            for_tiles(index, hop, plan, functools.partial(forward_hop, hop))

        @pl.when(index == LAG - 1)
        def _():
            own.wait()

        order_at = ARRIVE - rows // 256

        @pl.when(index == order_at - 1)
        def _():
            make_order()

        @pl.when((index >= order_at) & (index < ARRIVE))
        def _():
            tokens_in_order(index - order_at)

        @pl.when(index == ARRIVE)
        def _():
            result(0).start()

        pair = index - ARRIVE

        @pl.when((pair >= 0) & (pair < 3 * heads // 2))
        def _():
            pair_copy(2 * pair, pair % 2).start()

        @pl.when(pair == 0)
        def _():
            one_copy(rare, 0).start()

        @pl.when(pair == EVERY // 2)
        def _():
            one_copy(rarer, 1).start()

        @pl.when((pair >= 1) & (pair <= 3 * heads // 2))
        def _():
            done = pair - 1
            pair_copy(0, done % 2).wait()
            lanes = pl.ds(pl.multiple_of(done * 2 * LANES, 2 * LANES), 2 * LANES)
            project(stage_pair[done % 2].reshape(D, 2 * LANES), lanes)

        @pl.when(pair == 1)
        def _():
            one_copy(0, 0).wait()
            weights = stage_one[0, :, :, :, :, :, :LANES].reshape(D, LANES)
            project(weights, pl.ds((3 * heads - 1) * LANES, LANES))

        @pl.when(pair == EVERY // 2 + 1)
        def _():
            one_copy(0, 1).wait()
            small_vectors()

        @pl.when(pair == 4)
        def _():
            cot_in_order()

        @pl.when(pair == 5)
        def _():
            make_bias()

        @pl.when(pair == 6)
        def _():
            turn(tokens_in)
            result(6).start()

        @pl.when(index == units_at + 1)
        def _():
            result(6).wait()
            turn(first_low)
            result(7).start()

        @pl.when(index == attend_at)
        def _():
            result(1).start()
            for copy in outward_copies():
                copy.start()

        @pl.when((index >= attend_at) & (index < branch_at))
        def _():
            for k in range(pairs_each):
                attend_one((index - attend_at) * pairs_each + k)

        @pl.when(index == branch_at)
        def _():
            result(2).start()
            for copy in outward_copies():
                copy.wait()
            branch()

        @pl.when(index == branch_at + 1)
        def _():
            norms()

        unit = index - units_at

        @pl.when((unit >= -1) & (unit < units - 1))
        def _():
            fetch_unit(unit + 1)

        @pl.when((unit >= 0) & (unit < units))
        def _():
            one_unit(unit)

        return 0

    lax.fori_loop(0, max(steps_of(plan, 4), units_at + units), step, 0)
    for unit in (units - 2, units - 1):
        proj_copy(unit).wait()
    for pair in (units // 2 - 2, units // 2 - 1):
        hidden_copy(pair).wait()
    for k in (0, 1, 2, 3, 4, 7, 8):
        result(k).wait()
    finish()
    for route, (_, _, number, _, _) in enumerate(plan):
        for tile in range(max(0, number - RING), number):
            for hop in range(4):
                piece(hop, route, tile).wait_send()


def forward_pass(*operands, collective_id):
    plan = forward_plan()
    rows = operands[1].shape[0]
    count = operands[5].shape[0]
    sequences, length = operands[7].shape
    columns = sum(entry[2] for entry in plan) * LANES
    own = count // 2
    heads = head_tiles() * LANES
    units = unit_tiles() * LANES
    most = max(entry[2] for entry in plan)
    place = (2, 2, 2, 2, rows)
    hbm = pl.BlockSpec(memory_space=pl.ANY)
    vmem = pl.BlockSpec(memory_space=pltpu.VMEM)
    dma = pltpu.SemaphoreType.DMA
    return pl.pallas_call(
        functools.partial(forward_kernel, plan),
        out_shape=[
            jax.ShapeDtypeStruct((*place, columns), BF16),
            jax.ShapeDtypeStruct((count, D), BF16),
            jax.ShapeDtypeStruct((count, 3 * heads), F32),
            jax.ShapeDtypeStruct((count, heads), BF16),
            jax.ShapeDtypeStruct((own, D), F32),
            jax.ShapeDtypeStruct((own, D), F32),
            jax.ShapeDtypeStruct((count, D), BF16),
            jax.ShapeDtypeStruct((D, count), BF16),
            jax.ShapeDtypeStruct((D, count), BF16),
            jax.ShapeDtypeStruct((sequences, length, length), F32),
            jax.ShapeDtypeStruct((own, D), F32),
            jax.ShapeDtypeStruct((own, D), BF16),
            jax.ShapeDtypeStruct((count, D), BF16),
            jax.ShapeDtypeStruct((D, count), BF16),
            jax.ShapeDtypeStruct((count, 2 * units), F32),
            jax.ShapeDtypeStruct((count, units), BF16),
            jax.ShapeDtypeStruct((own, 2 * LANES), F32),
            jax.ShapeDtypeStruct((8, D), F32),
            jax.ShapeDtypeStruct((16, D), F32),
            jax.ShapeDtypeStruct((8, units), F32),
            jax.ShapeDtypeStruct((8, D), F32),
        ],
        in_specs=[vmem] * 6 + [hbm] + [vmem] * 3,
        out_specs=[hbm] * 16 + [vmem] * 5,
        scratch_shapes=[
            pltpu.VMEM((rows, columns), BF16),
            pltpu.VMEM((count, D), F32),
            pltpu.VMEM((D, D), BF16),
            pltpu.VMEM((count, D), BF16),
            pltpu.VMEM((own, D), BF16),
            pltpu.VMEM((sequences, length, length), F32),
            pltpu.VMEM((sequences, length, length), F32),
            pltpu.VMEM((count, 3 * heads), F32),
            pltpu.VMEM((2, *place, 2 * LANES), BF16),
            pltpu.VMEM((2, *place, 2 * LANES), BF16),
            pltpu.VMEM((*place, heads), BF16),
            pltpu.VMEM((count, heads), BF16),
            pltpu.VMEM((own, D), F32),
            pltpu.VMEM((own, D), F32),
            pltpu.VMEM((own, D), F32),
            pltpu.VMEM((count, D), BF16),
            pltpu.VMEM((2, count, 2 * LANES), F32),
            pltpu.VMEM((2, count, 2 * LANES), BF16),
            pltpu.VMEM((own, LANES), F32),
            dma,
            dma((4, 4, RING)),
            dma((4, 4, most)),
            dma((2,)),
            dma((2,)),
            dma((4,)),
            dma((2,)),
            dma((2,)),
            dma((14,)),
            dma((6,)),
            dma((6,)),
        ],
        compiler_params=pltpu.CompilerParams(
            collective_id=collective_id, has_side_effects=True, vmem_limit_bytes=60 << 20
        ),
        name="forward_pass",
    )(*operands)


SLOTS = 2 * RING + 4


def backward_plan():
    return tile_plan((4 * head_tiles() + 3 * unit_tiles()) * LANES)


def gradient_tile(route, tile):
    heads, units = head_tiles(), unit_tiles()
    shrink_steps, late = units // 2 - 1, units // 4
    outward, up = 3 * heads, 4 * heads
    gate, shrink = up + units, up + 2 * units
    if route < 2:
        unit = tile - shrink_steps + late
        last = tile - shrink_steps - (units - late)
        return jnp.where(
            tile < shrink_steps,
            shrink + 2 * tile + 2 + route,
            jnp.where(
                last < 0,
                (up, gate)[route] + unit,
                jnp.where(last < 2, outward + 2 * last + route, 2 * (last - 2) + route),
            ),
        )
    of_unit = (up, gate)[route - 2] + tile - 1
    if route == 2:
        last = jnp.where(tile == late + 1, outward + heads - 1, outward - 2)
    else:
        last = jnp.where(tile == late + 1, outward - 3, outward - 1)
    return jnp.where(tile == 0, shrink + route - 2, jnp.where(tile <= late, of_unit, last))


def slot_of(route, tile):
    if route < 2:
        return route * RING + tile % RING
    return 2 * RING + (route - 2) * 2 + tile % 2


def ring_of(route):
    return RING if route < 2 else 2


def backward_kernel(
    plan,
    copies,
    d_shrunk,
    d_shrunk_turned,
    first_turned,
    tokens_turned,
    hidden,
    proj,
    raw,
    mixed,
    d_two,
    h_attn,
    first,
    tokens_in,
    factors,
    alphas,
    scales,
    gains,
    alpha_mlp_grad,
    bias,
    place_row,
    output,
    input_grad,
    block_output,
    grads,
    vectors,
    work,
    arrived,
    lefts,
    d_low,
    d_proj,
    first_part,
    core_in,
    stage_hidden,
    stage_rows,
    wide,
    outward,
    right,
    sum_k,
    sum_v,
    alpha_grad,
    unit_grad,
    query_grad,
    vector_sums,
    vector_in,
    send_sem,
    recv_sem,
    load_sem,
    unit_sem,
    raw_sem,
    result_sem,
    core_send,
    core_recv,
    vector_send,
    vector_recv,
):
    me = lax.axis_index("dp")
    core = lax.axis_index("tensor")
    inv_root = D ** (-0.5)
    rows = tokens_in.shape[0]
    own_rows = rows // 2
    own_at = pl.multiple_of(core * own_rows, own_rows)
    other_at = pl.multiple_of((1 - core) * own_rows, own_rows)
    heads = head_tiles()
    units = unit_tiles()
    block = D // 16
    unit_steps = units // 2
    shrink_steps = unit_steps - 1
    late_units = units // 4
    expand_steps = units - late_units
    attention_at = shrink_steps + expand_steps
    rare_units = 1 + late_units
    exchange_at = unit_steps
    attend_at = exchange_at + 3
    sequences = bias.shape[0]
    length = bias.shape[1]
    head_pairs = sequences * heads

    greet(me, core)

    def copy(source, target, sem):
        return pltpu.make_async_copy(source, target, sem)

    def chunks(total, size, body):
        def one(k, _):
            body(pl.ds(pl.multiple_of(k * size, size), size))
            return 0

        lax.fori_loop(0, total // size, one, 0)


    def piece(hop, route, tile):
        axis = ROUTES[route][3 - hop]
        slot = slot_of(route, tile)
        return pltpu.make_async_remote_copy(
            src_ref=work[hop].at[slot, 1],
            dst_ref=arrived[hop].at[slot],
            send_sem=send_sem.at[hop, slot],
            recv_sem=recv_sem.at[hop, slot],
            device_id={"dp": partner_of(me, PLACES[axis])},
            device_id_type=pl.DeviceIdType.MESH,
        )

    def free(hop, route, tile):
        @pl.when(tile >= ring_of(route))
        def _():
            piece(hop, route, tile - ring_of(route)).wait_send()

    def add(hop, route, tile):
        piece(hop - 1, route, tile).wait_recv()
        slot = slot_of(route, tile)
        total = work[hop - 1][slot, 0].astype(F32) + arrived[hop - 1][slot].astype(F32)
        if hop == 4:
            place = gradient_tile(route, tile)
            grads[:, pl.ds(pl.multiple_of(place * LANES, LANES), LANES)] = total
            return
        half = total.shape[0] // 2
        free(hop, route, tile)
        work[hop][slot, 0] = total[:half].astype(BF16)
        work[hop][slot, 1] = total[half:].astype(BF16)
        piece(hop, route, tile).start()

    def keep_quarter(route, slot, quarter, part):
        axes = ROUTES[route][::-1]
        if route < 2:
            bits = [quarter >> 1, quarter & 1]
            at = bits[axes[1]] * 4 * block
            work[0][slot, bits[axes[0]], at : at + 4 * block, :] = part
            return
        for low in range(4):
            bits = [quarter >> 1, quarter & 1, low >> 1, low & 1]
            index = bits[axes[1]] * 4 + bits[axes[2]] * 2 + bits[axes[3]]
            work[0][slot, bits[axes[0]], index * block : (index + 1) * block, :] = part[
                low * block : (low + 1) * block
            ]

    def quarter_rows(quarter):
        return slice(quarter * 4 * block, (quarter + 1) * 4 * block)

    def often_product(tile):
        for route in (0, 1):
            free(0, route, tile)
        is_shrink = tile < shrink_steps
        is_expand = (tile >= shrink_steps) & (tile < attention_at)
        late = tile - attention_at
        is_outward = (late >= 0) & (late < 2)

        @pl.when(is_shrink)
        def _():
            right[0] = stage_hidden[tile % 2]

        @pl.when(is_expand)
        def _():
            unit = tile - shrink_steps + late_units
            right[0] = d_proj[:, pl.ds(pl.multiple_of(unit * 2 * LANES, 2 * LANES), 2 * LANES)]

        @pl.when(late >= 0)
        def _():
            first_tile = jnp.where(late < 2, 2 * late, 2 * late + 1)
            right[0] = wide[:rows, pl.ds(pl.multiple_of(first_tile * LANES, LANES), 2 * LANES)]

        which = jnp.where(is_expand | is_outward, 1, 0)
        scale = jnp.where(is_shrink | is_outward, 1.0, inv_root)
        product = (nn(lefts[which], right[0]) * scale).astype(BF16)
        for quarter in range(4):
            part = product[quarter_rows(quarter)]
            for route in (0, 1):
                keep_quarter(
                    route, slot_of(route, tile), quarter, part[:, route * LANES : (route + 1) * LANES]
                )
        for route in (0, 1):
            piece(0, route, tile).start()

    def rare_product(route, tile):
        late = tile - rare_units
        at = (route - 2) * LANES
        lanes = slice(at, at + LANES)

        @pl.when(tile == 0)
        def _():
            right[1, :, lanes] = stage_hidden[2, :, lanes]

        @pl.when((tile > 0) & (late < 0))
        def _():
            unit_lane = pl.multiple_of((tile - 1) * 2 * LANES + at, LANES)
            right[1, :, lanes] = d_proj[:, pl.ds(unit_lane, LANES)]

        @pl.when(late >= 0)
        def _():
            if route == 2:
                place = jnp.where(late == 0, heads - 1, heads + 13)
            else:
                place = heads + 12 + 2 * late
            right[1, :, lanes] = wide[:rows, pl.ds(pl.multiple_of(place * LANES, LANES), LANES)]

        free(0, route, tile)
        of_units = (tile > 0) & (late < 0)
        of_outward = (late == 0) if route == 2 else (late < -rare_units)
        which = jnp.where(of_units | of_outward, 1, 0)
        scale = jnp.where((tile == 0) | of_outward, 1.0, inv_root)
        product = (nn(lefts[which], right[1, :, lanes]) * scale).astype(BF16)
        for quarter in range(4):
            keep_quarter(route, slot_of(route, tile), quarter, product[quarter_rows(quarter)])
        piece(0, route, tile).start()


    def unit_copies(pair):
        slot = pair % 2
        unit = 2 * pair
        at = pl.multiple_of(slot * 6 * LANES, 2 * LANES)
        result = [
            (
                copies.at[:, pl.ds(pl.multiple_of(pair_tile(unit) * LANES, LANES), 4 * LANES)],
                wide.at[:, pl.ds(at, 4 * LANES)],
            )
        ]
        for k in range(2):
            tile = shrink_tile(unit + k)
            result.append(
                (
                    copies.at[:, pl.ds(pl.multiple_of(tile * LANES, LANES), LANES)],
                    wide.at[:, pl.ds(pl.multiple_of(at + (4 + k) * LANES, LANES), LANES)],
                )
            )
        lanes = pl.ds(pl.multiple_of(pair * 4 * LANES, 4 * LANES), 4 * LANES)
        for k in range(2):
            result.append(
                (
                    proj.at[pl.ds(k * own_rows, own_rows), lanes],
                    stage_rows.at[slot, :, pl.ds(k * 4 * LANES, 4 * LANES)],
                )
            )
        return [copy(source, target, unit_sem.at[k, slot]) for k, (source, target) in enumerate(result)]

    def hidden_copy(tile):
        lanes = pl.ds(pl.multiple_of((2 * tile + 2) * LANES, 2 * LANES), 2 * LANES)
        return copy(hidden.at[:, lanes], stage_hidden.at[tile % 2], unit_sem.at[5, tile % 2])

    def unit_pair(pair):
        slot = pair % 2
        for part in unit_copies(pair):
            part.wait()
        at_lane = pl.multiple_of(slot * 6 * LANES, 2 * LANES)
        down = wide[:, pl.ds(pl.multiple_of(at_lane + 4 * LANES, 2 * LANES), 2 * LANES)]

        for half in range(2):
            at = slice(half * own_rows, (half + 1) * own_rows)
            proj_lanes = half * 4 * LANES
            d_hidden = nn(d_low[at, :], down)
            for k in range(2):
                lanes = pl.ds(pl.multiple_of((2 * pair + k) * LANES, LANES), LANES)
                gain_up, gain_gate = gains[0:1, lanes], gains[1:2, lanes]
                start = proj_lanes + 2 * k * LANES
                proj_up = stage_rows[slot, :, start : start + LANES]
                proj_gate = stage_rows[slot, :, start + LANES : start + 2 * LANES]
                upstream = d_hidden[:, k * LANES : (k + 1) * LANES]
                gate = gain_gate * proj_gate
                sigmoid = jax.nn.sigmoid(gate)
                d_up = upstream * (gate * sigmoid)
                d_gate = upstream * (gain_up * proj_up) * sigmoid * (1.0 + gate * (1.0 - sigmoid))
                unit_grad[0:1, lanes] += jnp.sum(d_up * proj_up, axis=0, keepdims=True)
                unit_grad[1:2, lanes] += jnp.sum(d_gate * proj_gate, axis=0, keepdims=True)
                place = pl.multiple_of((2 * pair + k) * 2 * LANES, 2 * LANES)
                d_proj[at, pl.ds(place, LANES)] = (d_up * gain_up).astype(BF16)
                d_proj[at, pl.ds(pl.multiple_of(place + LANES, LANES), LANES)] = (
                    d_gate * gain_gate
                ).astype(BF16)
        expand_at = pl.ds(at_lane, 4 * LANES)
        lanes = pl.ds(pl.multiple_of(pair * 4 * LANES, 4 * LANES), 4 * LANES)
        upstream = d_proj[:, lanes]
        for k in range(D // 256):
            columns = slice(k * 256, (k + 1) * 256)
            first_part[:, columns] += nt(upstream, wide[columns, expand_at])


    def core_copy(source, target, which):
        return pltpu.make_async_remote_copy(
            src_ref=source,
            dst_ref=target,
            send_sem=core_send.at[which],
            recv_sem=core_recv.at[which],
            device_id={"tensor": 1 - core},
            device_id_type=pl.DeviceIdType.MESH,
        )

    def part_copy():
        return core_copy(first_part.at[pl.ds(other_at, own_rows)], core_in, 0)

    def branch_copy():
        own = d_low.at[pl.ds(own_at, own_rows)]
        return core_copy(own, own, 1)

    tokens_place = wide.at[pl.ds(0, own_rows), pl.ds(D, D)]
    rare, rarer = forward_plan()[2][0], forward_plan()[3][0]
    outward_tiles = ((rare + 1, 1, 0), (rarer + 1, 1, 1), (3 * heads - 1, 2, 2), (rare + 2, 1, 4))

    def load(k):
        if k == 0:
            return copy(d_two, stage_rows.at[0], load_sem.at[0])
        if k == 1:
            return copy(h_attn, stage_rows.at[1], load_sem.at[1])
        if k == 2:
            return copy(tokens_in.at[pl.ds(own_at, own_rows)], tokens_place, load_sem.at[2])
        if k == 3:
            return copy(
                mixed, wide.at[pl.ds(0, rows), pl.ds(0, heads * LANES)], load_sem.at[3]
            )
        if k == 4:
            return copy(first, first_part.at[pl.ds(other_at, own_rows)], load_sem.at[4])
        if k == 5:
            return copy(d_shrunk, d_low, load_sem.at[5])
        if k == 6:
            return copy(d_shrunk_turned, lefts.at[0], load_sem.at[6])
        if k == 7:
            return copy(first_turned, lefts.at[1], load_sem.at[7])
        if k == 8:
            return copy(tokens_turned, lefts.at[0], load_sem.at[8])
        if k == 9:
            return copy(hidden.at[:, pl.ds(0, 2 * LANES)], stage_hidden.at[2], load_sem.at[9])
        tile, width, at = outward_tiles[k - 10]
        return copy(
            copies.at[:, pl.ds(tile * LANES, width * LANES)],
            outward.at[:, pl.ds(at * LANES, width * LANES)],
            load_sem.at[k],
        )

    def branch_gradient():
        part_copy().wait_send()
        load(4).start()
        part_copy().wait_recv()
        for k in (0, 1, 2, 4):
            load(k).wait()
        alpha_attn, alpha_mlp = alphas[0:1, :], alphas[1:2, :]

        def some(at):
            here = pl.ds(pl.multiple_of(own_at + at.start, 64), 64)
            there = pl.ds(pl.multiple_of(other_at + at.start, 64), 64)
            part = (first_part[here, :] + core_in[at, :]) * inv_root
            d_first = (1.0 - alpha_mlp) * stage_rows[0, at, :] + part
            normed = stage_rows[1, at, :]
            d_one = row_norm_back(
                d_first, first_part[there, :], factors[at, LANES : LANES + 1]
            )
            inputs = wide[at, D : 2 * D].astype(F32)
            alpha_grad[0:1, :] += jnp.sum(d_one * (normed - inputs), axis=0, keepdims=True)
            stage_rows[0, at, :] = d_one
            d_low[here, :] = row_norm_back(alpha_attn * d_one, normed, factors[at, 0:1]).astype(
                BF16
            )

        chunks(own_rows, 64, some)
        branch_copy().start()


    def raw_copies(number):
        sequence, head = number // heads, number % heads
        at = pl.ds(pl.multiple_of(sequence * length, length), length)
        slot = number % 2
        target_rows = pl.ds(pl.multiple_of(slot * own_rows, own_rows), length)
        return [
            copy(
                raw.at[at, pl.ds(pl.multiple_of((k * heads + head) * LANES, LANES), LANES)],
                first_part.at[target_rows, pl.ds(k * LANES, LANES)],
                raw_sem.at[k, slot],
            )
            for k in range(3)
        ]

    def attend_one(number):
        sequence, head = number // heads, number % heads
        for part in raw_copies(number):
            part.wait()
        at = pl.ds(pl.multiple_of(sequence * length, length), length)
        source_rows = pl.ds(pl.multiple_of((number % 2) * own_rows, own_rows), length)
        head_lanes = pl.ds(pl.multiple_of(head * LANES, LANES), LANES)
        gain_lanes = pl.ds(pl.multiple_of((core * heads + head) * LANES, LANES), LANES)
        d_mixed = nn(d_low[at, :], outward[:, head_lanes]).astype(BF16)
        targets = [
            wide.at[at, pl.ds(pl.multiple_of(((k + 1) * heads + head) * LANES, LANES), LANES)]
            for k in range(3)
        ]
        total = attend_pair_back(
            *[first_part.at[source_rows, pl.ds(k * LANES, LANES)] for k in range(3)],
            d_mixed,
            scales[2:3, gain_lanes],
            bias.at[sequence],
            *targets,
            sum_k,
            sum_v,
        )
        query_grad[0:1, head_lanes] += total


    head_lanes = 3 * heads * LANES
    beyond = D - rows

    def inward_copies():
        first_lanes = (3 * heads - 1) * LANES
        result = []
        for row, number, at, lane in ((0, rows, 0, 0), (rows, beyond, 0, head_lanes)):
            for source, width in ((0, first_lanes), (rare * LANES, LANES)):
                offset = 0 if width == first_lanes else first_lanes
                result.append(
                    (
                        copies.at[pl.ds(row, number), pl.ds(source, width)],
                        d_proj.at[pl.ds(at, number), pl.ds(lane + offset, width)],
                    )
                )
        return [copy(source, target, load_sem.at[14 + k]) for k, (source, target) in enumerate(result)]

    order_lane = 2 * head_lanes

    def make_order():
        natural = natural_row(place_row, me)

        def fill(at):
            here = lax.broadcasted_iota(jnp.int32, (LANES, D), 0) + at.start
            d_proj[at, order_lane : order_lane + D] = jnp.where(here == natural, 1.0, 0.0).astype(
                BF16
            )

        chunks(rows, LANES, fill)
        for k in range(beyond // LANES):
            here = lax.broadcasted_iota(jnp.int32, (LANES, D), 0) + rows + k * LANES
            at = slice(beyond + k * LANES, beyond + (k + 1) * LANES)
            d_proj[at, head_lanes : head_lanes + D] = jnp.where(here == natural, 1.0, 0.0).astype(
                BF16
            )

    def natural_parts(values):
        low = nt(values, d_proj[:, order_lane : order_lane + D])
        high = nt(values, d_proj[beyond : 2 * beyond, head_lanes : head_lanes + D])
        return low, high

    def input_part(number):
        at = pl.ds(pl.multiple_of(number * 256, 256), 256)
        upstream = wide[at, heads * LANES : 4 * heads * LANES]
        low = nt(upstream, d_proj[:, :head_lanes]) * inv_root
        d_low[at, :rows] = low.astype(BF16)
        high = nt(upstream, d_proj[:beyond, head_lanes : 2 * head_lanes]) * inv_root
        d_low[at, rows:] = high.astype(BF16)
        low, high = natural_parts(d_low[at, :])
        first_part[at, :rows] = low
        first_part[at, rows:] = high

    def residual_part():
        alpha_attn = alphas[0:1, :]

        def some(at):
            here = pl.ds(pl.multiple_of(own_at + at.start, 128), 128)
            residual = (1.0 - alpha_attn) * stage_rows[0, at, :]
            top = residual.astype(BF16)
            rest = (residual - top.astype(F32)).astype(BF16)
            for part in (top, rest):
                low, high = natural_parts(part)
                first_part[here, :rows] += low
                first_part[here, rows:] += high

        chunks(own_rows, 128, some)

    half_width = D // 2

    def input_copies():
        lanes = pl.ds(pl.multiple_of((1 - core) * half_width, LANES), half_width)
        return [
            core_copy(
                first_part.at[pl.ds(k * own_rows, own_rows), lanes],
                core_in.at[:, pl.ds(k * half_width, half_width)],
                2 + k,
            )
            for k in range(2)
        ]

    def input_copy(k):
        lanes = pl.ds(pl.multiple_of(core * half_width, LANES), half_width)
        at = pl.ds(k * own_rows, own_rows)
        return copy(first_part.at[at, lanes], input_grad.at[at], result_sem.at[k])

    def input_sum():
        lanes = pl.ds(pl.multiple_of(core * half_width, LANES), half_width)
        for k, part in enumerate(input_copies()):
            part.wait()
            at = pl.ds(k * own_rows, own_rows)
            first_part[at, lanes] += core_in[:, k * half_width : (k + 1) * half_width]
            input_copy(k).start()

    def output_load():
        return copy(output, d_low.at[pl.ds(other_at, own_rows)], load_sem.at[18])

    def output_order():
        output_load().wait()
        for k in range(own_rows // 256):
            source = pl.ds(pl.multiple_of(other_at + k * 256, 256), 256)
            target = pl.ds(pl.multiple_of(own_at + k * 256, 256), 256)
            low, high = natural_parts(d_low[source, :])
            d_low[target, :rows] = low.astype(BF16)
            d_low[target, rows:] = high.astype(BF16)
        output_copies()[0].start()
        output_copies()[1].start()

    def output_copies():
        own = pl.ds(own_at, own_rows)
        return (
            core_copy(d_low.at[own], block_output.at[own], 4),
            copy(d_low.at[own], block_output.at[own], result_sem.at[2]),
        )

    def vector_copy(k):
        if k == 0:
            device = {"tensor": 1 - core}
        else:
            device = {"dp": partner_of(me, PLACES[k - 1])}
        return pltpu.make_async_remote_copy(
            src_ref=vector_sums.at[k],
            dst_ref=vector_in.at[k],
            send_sem=vector_send.at[k],
            recv_sem=vector_recv.at[k],
            device_id=device,
            device_id_type=pl.DeviceIdType.MESH,
        )

    def vectors_start():
        alpha_grad[1:2, :] = alpha_mlp_grad[0:1, :]
        vector_sums[0] = jnp.zeros_like(vector_sums[0])
        values = alpha_grad[...]
        for _ in range(3):
            part = values.astype(BF16)
            low, high = natural_parts(part)
            vector_sums[0, :8, :rows] += low
            vector_sums[0, :8, rows:] += high
            values = values - part.astype(F32)
        vector_sums[0, 2:3, pl.ds(pl.multiple_of(core * heads * LANES, LANES), heads * LANES)] = (
            query_grad[0:1, :]
        )
        each = units * LANES // D
        for row in range(2):
            for k in range(2 * each):
                here = unit_grad[row : row + 1, (k % each) * D : (k % each + 1) * D]
                at = 3 + 2 * each * row + k
                vector_sums[0, at : at + 1, :] = jnp.where(core == k // each, here, 0.0)
        vector_copy(0).start()

    def vectors_add(k):
        vector_copy(k).wait()
        total = vector_sums[k] + vector_in[k]
        if k < len(PLACES):
            vector_sums[k + 1] = total
            vector_copy(k + 1).start()
        else:
            vectors[...] = total

    input_at = attention_at + 1
    parts = rows // 256


    load(6).start()
    hidden_copy(0).start()
    for k in (9, 5):
        load(k).start()
    for part in unit_copies(0):
        part.start()
    load(7).start()
    alpha_grad[...] = jnp.zeros_like(alpha_grad)
    unit_grad[...] = jnp.zeros_like(unit_grad)
    query_grad[...] = jnp.zeros_like(query_grad)
    first_part[...] = jnp.zeros_like(first_part)
    load(6).wait()

    def step(index, _):
        for hop in range(4, 0, -1):
            for_tiles(index, hop, plan, functools.partial(add, hop))

        @pl.when(index < shrink_steps)
        def _():
            hidden_copy(index).wait()

        @pl.when(index == attention_at)
        def _():
            load(8).wait()
            chunks(rows, LANES, turn)

        @pl.when(index < plan[0][2])
        def _():
            often_product(index)

        @pl.when(index == 0)
        def _():
            for k in (9, 5):
                load(k).wait()

        @pl.when(index == EVERY - 1)
        def _():
            load(7).wait()

        for route in (2, 3):
            number, start = plan[route][2], plan[route][4]
            due = index - start

            @pl.when((due % EVERY == 0) & (due >= 0) & (due < number * EVERY))
            def _(route=route, due=due):
                rare_product(route, due // EVERY)

        @pl.when(index + 1 < shrink_steps)
        def _():
            hidden_copy(index + 1).start()

        @pl.when(index + 1 < unit_steps)
        def _():
            for part in unit_copies(index + 1):
                part.start()

        @pl.when(index < unit_steps)
        def _():
            unit_pair(index)

        @pl.when(index == exchange_at)
        def _():
            part_copy().start()
            for k in (0, 1, 2, 3, 8, 10, 11, 12, 13):
                load(k).start()

        @pl.when(index == exchange_at + 1)
        def _():
            branch_gradient()

        @pl.when(index == exchange_at + 2)
        def _():
            branch_copy().wait()
            for k in (3, 10, 11, 12, 13):
                load(k).wait()

        number = index - attend_at

        @pl.when((number >= -1) & (number < head_pairs - 1))
        def _():
            for part in raw_copies(number + 1):
                part.start()

        @pl.when((number >= 0) & (number < head_pairs))
        def _():
            attend_one(number)

        @pl.when(index == attention_at)
        def _():
            for part in inward_copies():
                part.start()
            make_order()
            vectors_start()

        for k in range(len(PLACES) + 1):

            @pl.when(index == attention_at + 1 + k)
            def _(k=k):
                vectors_add(k)

        @pl.when(index == input_at)
        def _():
            for part in inward_copies():
                part.wait()

        @pl.when((index >= input_at) & (index < input_at + parts))
        def _():
            input_part(index - input_at)

        @pl.when(index == input_at + parts)
        def _():
            output_load().start()
            residual_part()
            for part in input_copies():
                part.start()

        @pl.when(index == input_at + parts + 1)
        def _():
            output_order()

        @pl.when(index == input_at + parts + 2)
        def _():
            input_sum()

        return 0

    def turn(at):
        lefts[1, :, at] = d_low[at, :].astype(F32).T.astype(BF16)

    lax.fori_loop(0, steps_of(plan, 4), step, 0)
    for part in output_copies():
        part.wait()
    for k in range(2):
        input_copy(k).wait()
    for route, (_, _, number, _, _) in enumerate(plan):
        for tile in range(max(0, number - ring_of(route)), number):
            for hop in range(4):
                piece(hop, route, tile).wait_send()


def backward_pass(*operands, collective_id):
    plan = backward_plan()
    copies = operands[0]
    count = operands[1].shape[0]
    own = count // 2
    heads = head_tiles() * LANES
    units = unit_tiles() * LANES
    length = operands[18].shape[1]
    block = D // 16
    halves = [block * 8 >> hop for hop in range(4)]
    hbm = pl.BlockSpec(memory_space=pl.ANY)
    vmem = pl.BlockSpec(memory_space=pltpu.VMEM)
    dma = pltpu.SemaphoreType.DMA
    return pl.pallas_call(
        functools.partial(backward_kernel, plan),
        out_shape=[
            jax.ShapeDtypeStruct((count, D // 2), F32),
            jax.ShapeDtypeStruct((count, D), BF16),
            jax.ShapeDtypeStruct((block, 4 * heads + 3 * units), F32),
            jax.ShapeDtypeStruct((16, D), F32),
        ],
        in_specs=[hbm] * 13 + [vmem] * 7 + [hbm],
        out_specs=[hbm] * 2 + [vmem] * 2,
        scratch_shapes=[
            [pltpu.VMEM((SLOTS, 2, half, LANES), BF16) for half in halves],
            [pltpu.VMEM((SLOTS, half, LANES), BF16) for half in halves],
            pltpu.VMEM((2, D, count), BF16),
            pltpu.VMEM((count, D), BF16),
            pltpu.VMEM((count, 2 * units), BF16),
            pltpu.VMEM((count, D), F32),
            pltpu.VMEM((own, D), F32),
            pltpu.VMEM((3, count, 2 * LANES), BF16),
            pltpu.VMEM((2, own, D), F32),
            pltpu.VMEM((D, 4 * heads), BF16),
            pltpu.VMEM((D, heads), BF16),
            pltpu.VMEM((2, count, 2 * LANES), BF16),
            pltpu.VMEM((length, LANES), F32),
            pltpu.VMEM((length, LANES), F32),
            pltpu.VMEM((8, D), F32),
            pltpu.VMEM((8, units), F32),
            pltpu.VMEM((8, heads), F32),
            pltpu.VMEM((5, 16, D), F32),
            pltpu.VMEM((5, 16, D), F32),
            dma((4, SLOTS)),
            dma((4, SLOTS)),
            dma((19,)),
            dma((6, 2)),
            dma((3, 2)),
            dma((3,)),
            dma((5,)),
            dma((5,)),
            dma((5,)),
            dma((5,)),
        ],
        compiler_params=pltpu.CompilerParams(
            collective_id=collective_id, has_side_effects=True, vmem_limit_bytes=62 << 20
        ),
        name="backward_pass",
    )(*operands)


SQUARE_ROWS = 4


def update_pieces():
    heads, units = head_tiles() * LANES, unit_tiles() * LANES
    pieces = [(k * heads, heads, 0, k, 0, k * heads) for k in range(3)]
    pieces.append((3 * heads, heads, 1, None, 0, 3 * heads))
    pieces += [(4 * heads + k * units, units, 2, k, 1 + k, 0) for k in range(2)]
    pieces.append((4 * heads + 2 * units, units, 3, None, 3, 0))
    return pieces


def update_loads(grads, states, held_grads, held_states, sem):
    pairs = []
    ends = {0: 0, 1: 3, 2: 4, 3: 6}
    sizes = {0: 3, 1: 1, 2: 2, 3: 1}
    pieces = update_pieces()
    for which in range(4):
        start, width = pieces[ends[which]][:2]
        lanes = pl.ds(start, width * sizes[which])
        pairs.append((grads.at[:, lanes], held_grads.at[:, lanes]))
        pairs += list(zip(states[3 * which : 3 * which + 3], held_states[3 * which : 3 * which + 3]))
    return [pltpu.make_async_copy(source, target, sem.at[k]) for k, (source, target) in enumerate(pairs)]


def for_update_tiles(loads, held_grads, held_states, body, after=None):
    waited = -1
    for piece in update_pieces():
        start, width, which, block, _, _ = piece
        if which != waited:
            for load in loads[4 * which : 4 * which + 4]:
                load.wait()
            waited = which

        def one(k, _, start=start, which=which, block=block, piece=piece):
            lane = pl.multiple_of(k * LANES, LANES)
            here = pl.ds(lane, LANES)
            values = [
                ref[:, here] if block is None else ref[block, :, here]
                for ref in held_states[3 * which : 3 * which + 3]
            ]
            gradient = held_grads[:, pl.ds(pl.multiple_of(start + lane, LANES), LANES)]
            body(piece, lane, gradient, *values)
            return 0

        lax.fori_loop(0, width // LANES, one, 0)
        if after is not None and block in (None, (2, 0, 1, 0)[which]):
            after(which)


def squares_kernel(*refs):
    grads, states, total, held_grads, held_states = refs[0], refs[1:13], refs[13], refs[14], refs[15]
    sums, arrived, load_sem, send_sem, recv_sem = refs[16:]
    loads = update_loads(grads, states, held_grads, held_states, load_sem)
    for load in loads:
        load.start()
    me = lax.axis_index("dp")
    low, high = PLACES[:2]
    hops = [[(low,), (high,), (low, high)], *[[(bit,)] for bit in PLACES[2:]]]

    def partner(bits):
        device = me
        for bit in bits:
            device = device + partner_of(me, bit) - me
        return {"dp": device}

    barrier = pltpu.get_barrier_semaphore()
    for hop in hops:
        for bits in hop:
            pl.semaphore_signal(
                barrier, inc=1, device_id=partner(bits), device_id_type=pl.DeviceIdType.MESH
            )
    pl.semaphore_wait(barrier, sum(len(hop) for hop in hops))

    def body(piece, lane, gradient, master, first, second):
        pre = adam_step(master, first, second, gradient, RATE_MATRIX)[0]
        row, start = piece[4:]
        lanes = pl.ds(pl.multiple_of(start + lane, LANES), LANES)
        sums[0, row : row + 1, lanes] = jnp.sum(pre * pre, axis=0, keepdims=True)

    for_update_tiles(loads, held_grads, held_states, body)
    for number, hop in enumerate(hops):
        copies = [
            pltpu.make_async_remote_copy(
                src_ref=sums.at[number],
                dst_ref=arrived.at[number, k],
                send_sem=send_sem.at[number, k],
                recv_sem=recv_sem.at[number, k],
                device_id=partner(bits),
                device_id_type=pl.DeviceIdType.MESH,
            )
            for k, bits in enumerate(hop)
        ]
        for copy in copies:
            copy.start()
        for copy in copies:
            copy.wait()
        if len(hop) == 3:
            result = (sums[number] + arrived[number, 0]) + (
                arrived[number, 1] + arrived[number, 2]
            )
        else:
            result = sums[number] + arrived[number, 0]
        if number + 1 < len(hops):
            sums[number + 1] = result
        else:
            total[...] = result


def update_kernel(*refs):
    grads, states, squares, small, outputs = refs[0], refs[1:13], refs[13], refs[14:21], refs[21:39]
    held_grads, held_states, held_results, load_sem, store_sem = refs[39:]
    results, small_results = outputs[:12], outputs[12:]
    loads = update_loads(grads, states, held_grads, held_states, load_sem)
    for load in loads:
        load.start()

    def store(k):
        return pltpu.make_async_copy(held_results[k], results[k], store_sem.at[k])

    for k, rate in enumerate((RATE_ALPHA, RATE_SCALE)):
        master, first, second = [ref[...] for ref in small[3 * k + 1 : 3 * k + 4]]
        gradient = small[0][...][2 * k : 2 * k + master.shape[0]]
        updated, variance = adam_step(master, first, second, gradient, rate)
        for target, value in zip(small_results[3 * k : 3 * k + 3], (gradient, variance, updated)):
            target[...] = value

    def body(piece, lane, gradient, master, first, second):
        _, _, which, block, row, start = piece
        pre, variance = adam_step(master, first, second, gradient, RATE_MATRIX)
        lanes = pl.ds(pl.multiple_of(start + lane, LANES), LANES)
        factor = lax.rsqrt(squares[row : row + 1, lanes] / D + EPS_NORM)
        here = pl.ds(lane, LANES)
        for target, value in zip(
            held_results[3 * which : 3 * which + 3], (gradient, variance, pre * factor)
        ):
            if block is None:
                target[:, here] = value
            else:
                target[block, :, here] = value

    def after(which):
        for k in range(3 * which, 3 * which + 3):
            store(k).start()

    for_update_tiles(loads, held_grads, held_states, body, after)
    for k in range(12):
        store(k).wait()


def update(grads, states, small, count, collective_id):
    rows = grads.shape[0]
    units = unit_tiles() * LANES
    shape = (SQUARE_ROWS, units)
    hbm = pl.BlockSpec(memory_space=pl.ANY)
    vmem = pl.BlockSpec(memory_space=pltpu.VMEM)
    dma = pltpu.SemaphoreType.DMA
    held = [pltpu.VMEM(grads.shape, F32), [pltpu.VMEM(state.shape, state.dtype) for state in states]]
    squares = pl.pallas_call(
        squares_kernel,
        out_shape=jax.ShapeDtypeStruct(shape, F32),
        in_specs=[hbm] * 13,
        out_specs=vmem,
        scratch_shapes=held
        + [
            pltpu.VMEM((3, *shape), F32),
            pltpu.VMEM((3, 3, *shape), F32),
            dma((16,)),
            dma((3, 3)),
            dma((3, 3)),
        ],
        compiler_params=pltpu.CompilerParams(
            collective_id=collective_id, has_side_effects=True, vmem_limit_bytes=60 << 20
        ),
        name="sum_squares",
    )(grads, *states)
    for bit in extra_bits(count):
        squares = squares + exchange(squares, bit, count)
    results = [
        jax.ShapeDtypeStruct(states[3 * k].shape, F32) for k in range(4) for _ in range(3)
    ]
    small_results = [
        jax.ShapeDtypeStruct(small[3 * k + 1].shape, F32) for k in range(2) for _ in range(3)
    ]
    return pl.pallas_call(
        update_kernel,
        out_shape=results + small_results,
        in_specs=[hbm] * 13 + [vmem] * 8,
        out_specs=[hbm] * 12 + [vmem] * 6,
        scratch_shapes=held
        + [[pltpu.VMEM(result.shape, F32) for result in results], dma((16,)), dma((12,))],
        compiler_params=pltpu.CompilerParams(vmem_limit_bytes=60 << 20),
        name="update",
    )(grads, *states, squares, *small)


def per_device(
    tokens,
    cotangent,
    segment_ids,
    pad_mask,
    inward_master,
    inward_first,
    inward_second,
    outward_master,
    outward_first,
    outward_second,
    expand_master,
    expand_first,
    expand_second,
    shrink_master,
    shrink_first,
    shrink_second,
    alpha_master,
    alpha_first,
    alpha_second,
    scale_master,
    scale_first,
    scale_second,
):
    count = lax.axis_size("dp")
    me = lax.axis_index("dp")
    heads_width = inward_master.shape[2]

    small = jnp.concatenate([alpha_master, scale_master], axis=0).astype(BF16)
    small = jnp.pad(small, ((0, LANES - small.shape[0]), (0, 0))).T
    masters = (
        inward_master,
        outward_master.T,
        expand_master,
        shrink_master.T,
        small,
    )
    if extra_bits(count):
        masters = [gather_rest(master.astype(BF16), count) for master in masters]
    place_row = jnp.asarray(place_rows_of(count))
    (
        copies,
        tokens_in,
        raw,
        mixed,
        h_attn,
        first,
        first_low,
        tokens_turned,
        first_turned,
        bias,
        d_two,
        output,
        d_shrunk,
        d_shrunk_turned,
        proj,
        hidden,
        factors,
        alphas,
        scale_rows,
        gains,
        alpha_mlp_grad,
    ) = forward_pass(
        *masters, tokens, cotangent, segment_ids, pad_mask, place_row, collective_id=0
    )

    input_grad, block_output, grads, vectors = backward_pass(
        copies.reshape(D, -1),
        d_shrunk,
        d_shrunk_turned,
        first_turned,
        tokens_turned,
        hidden,
        proj,
        raw,
        mixed,
        d_two,
        h_attn,
        first,
        tokens_in,
        factors,
        alphas,
        scale_rows,
        gains,
        alpha_mlp_grad,
        bias,
        place_row,
        output,
        collective_id=1,
    )
    grads = scatter_rest(grads, count)
    for bit in extra_bits(count):
        vectors = vectors + exchange(vectors, bit, count)
    width = D // count
    vectors = lax.dynamic_slice_in_dim(vectors, me * width, width, 1)

    states = (
        inward_master,
        inward_first,
        inward_second,
        outward_master.T,
        outward_first.T,
        outward_second.T,
        expand_master,
        expand_first,
        expand_second,
        shrink_master.T,
        shrink_first.T,
        shrink_second.T,
    )
    small = (
        vectors,
        alpha_master,
        alpha_first,
        alpha_second,
        scale_master,
        scale_first,
        scale_second,
    )
    results = list(update(grads, states, small, count, 2))
    for k in (*range(3, 6), *range(9, 12)):
        results[k] = results[k].T
    return block_output, input_grad, *results


def solution(mesh):
    rows = P("dp", None)
    deep = P(None, "dp", "tensor")
    flat = P("tensor", "dp")
    vector = P(None, "dp")
    in_specs = (rows,) * 4 + (deep,) * 3 + (flat,) * 3 + (deep,) * 3 + (flat,) * 3 + (vector,) * 6
    out_specs = (
        (rows, P("dp", "tensor"))
        + (deep,) * 3
        + (flat,) * 3
        + (deep,) * 3
        + (flat,) * 3
        + (vector,) * 6
    )
    return jax.shard_map(
        per_device, mesh=mesh, in_specs=in_specs, out_specs=out_specs, check_vma=False
    )
```

```python
import functools

import jax
import jax.numpy as jnp
import numpy as np
from jax import lax
from jax.experimental import pallas as pl
from jax.experimental.pallas import tpu as pltpu
from jax.sharding import PartitionSpec as P

D = 1280
HEADS = 20
HD = 64
FF = 5120
STEP = 10
LONGEST = 256


EPS_NORM = 1e-06
BETA_ONE = 0.9
BETA_TWO = 0.95
ADAM_EPS = 1e-08
RATE_MATRIX = 0.3
RATE_ALPHA = 0.08
RATE_SCALE = 0.25
MASKED = -1e30
F32 = jnp.float32
BF16 = jnp.bfloat16


def row_norm(values):
    factor = lax.rsqrt(jnp.mean(values * values, axis=-1, keepdims=True) + EPS_NORM)
    return (values * factor, factor)


def row_norm_back(upstream, normed, factor):
    return factor * (upstream - normed * jnp.mean(upstream * normed, axis=-1, keepdims=True))


def adam_step(master, first_moment, second_moment, gradient, rate):
    first_new = BETA_ONE * first_moment.astype(F32) + (1.0 - BETA_ONE) * gradient
    second_new = BETA_TWO * second_moment + (1.0 - BETA_TWO) * gradient * gradient
    root = jnp.sqrt(second_new * (1.0 / (1.0 - BETA_TWO**STEP)))
    ratio = first_new * (rate / (1.0 - BETA_ONE**STEP)) / (root + ADAM_EPS)
    return (master - ratio, second_new)


LANES = 128
PLACES = (2, 1, 4, 8)
ROUTES = ((3, 2, 1, 0), (3, 2, 0, 1), (1, 0, 3, 2), (0, 1, 3, 2))
EVERY = 4
LAG = 2
RING = 4


def partner_of(me, bit):
    return me + bit - 2 * bit * ((me // bit) % 2)


def partner_across(me, bits):
    device = me
    for bit in bits:
        device = device + partner_of(me, bit) - me
    return {"dp": device}


ROUNDS = (
    ((PLACES[0],), (PLACES[1],), (PLACES[0], PLACES[1])),
    ((PLACES[2],), (PLACES[3],), (PLACES[2], PLACES[3])),
)


def round_copies(me, number, sums, arrived, send_sem, recv_sem):
    return [
        pltpu.make_async_remote_copy(
            src_ref=sums.at[number],
            dst_ref=arrived.at[number, k],
            send_sem=send_sem.at[number, k],
            recv_sem=recv_sem.at[number, k],
            device_id=partner_across(me, bits),
            device_id_type=pl.DeviceIdType.MESH,
        )
        for k, bits in enumerate(ROUNDS[number])
    ]


def round_start(*parts):
    for copy in round_copies(*parts):
        copy.start()


def round_sum(me, number, sums, arrived, send_sem, recv_sem):
    for copy in round_copies(me, number, sums, arrived, send_sem, recv_sem):
        copy.wait()
    total = sums[number] + arrived[number, 0]
    for k in range(1, len(ROUNDS[number])):
        total = total + arrived[number, k]
    return total


def greet(me, core=None, diagonal=False):
    barrier = pltpu.get_barrier_semaphore()
    partners = [{"dp": partner_of(me, bit)} for bit in PLACES]
    if diagonal:
        partners += [partner_across(me, PLACES[:2]), partner_across(me, PLACES[2:])]
    if core is not None:
        partners.append({"tensor": 1 - core})
    for partner in partners:
        pl.semaphore_signal(
            barrier, inc=1, device_id=partner, device_id_type=pl.DeviceIdType.MESH
        )
    pl.semaphore_wait(barrier, len(partners))


def tile_plan(columns):
    tiles = columns // LANES
    rare = tiles // 10
    often = (tiles - 2 * rare) // 2
    return (
        (0, 2, often, 1, 0),
        (1, 2, often, 1, 0),
        (2 * often, 1, rare, EVERY, 0),
        (2 * often + rare, 1, rare, EVERY, EVERY // 2),
    )


def for_tiles(step, hop, plan, body):
    for route, (_, _, number, every, start) in enumerate(plan):
        at = step - hop * LAG - start
        due = (at >= 0) & (at < number * every)
        if every > 1:
            due = due & (at % every == 0)

        @pl.when(due)
        def _():
            body(route, at // every)


def lanes_of(plan, route, tile):
    first, stride = plan[route][:2]
    return pl.ds(pl.multiple_of((first + stride * tile) * LANES, LANES), LANES)


def steps_of(plan, hops):
    return max(start + (number - 1) * every + 1 for _, _, number, every, start in plan) + hops * LAG


def extra_bits(count):
    return [bit for bit in (1 << k for k in range(4, count.bit_length() - 1))]


def exchange(array, bit, count):
    return lax.ppermute(array, "dp", [(i, i ^ bit) for i in range(count)])


def gather_rest(block, count):
    for bit in extra_bits(count)[::-1]:
        block = jnp.concatenate([block, exchange(block, bit, count)], axis=-2)
    return block


def scatter_rest(partial, count):
    for bit in extra_bits(count):
        half = partial.shape[0] // 2
        partial = partial[:half] + exchange(partial[half:], bit, count)
    return partial


def place_rows_of(count):
    places = list(PLACES) + extra_bits(count)
    width = D // count
    placed = np.arange(D, dtype=np.int32)
    position, offset = placed // width, placed % width
    relative = np.zeros_like(position)
    for axis, bit in enumerate(places):
        relative = relative + ((position >> (len(places) - 1 - axis)) & 1) * bit
    return np.stack([relative, offset])


def natural_row(place_row, me):
    count = lax.axis_size("dp")
    return (place_row[0:1, :] ^ me) * (D // count) + place_row[1:2, :]


def nn(a, b):
    return lax.dot_general(a, b, (((1,), (0,)), ((), ())), preferred_element_type=F32)


def nt(a, b):
    return lax.dot_general(a, b, (((1,), (1,)), ((), ())), preferred_element_type=F32)


def tn(a, b):
    return lax.dot_general(a, b, (((0,), (0,)), ((), ())), preferred_element_type=F32)


def head_factors(raw, low_lanes):
    squares = raw * raw
    low = jnp.sum(jnp.where(low_lanes, squares, 0.0), axis=-1, keepdims=True)
    high = jnp.sum(jnp.where(low_lanes, 0.0, squares), axis=-1, keepdims=True)
    return jnp.where(low_lanes, lax.rsqrt(low + EPS_NORM), lax.rsqrt(high + EPS_NORM))


def head_sums(values, low_lanes):
    low = jnp.sum(jnp.where(low_lanes, values, 0.0), axis=-1, keepdims=True)
    high = jnp.sum(jnp.where(low_lanes, 0.0, values), axis=-1, keepdims=True)
    return jnp.where(low_lanes, low, high)


Q_TILE = 128


def key_range(tile):
    start = max(0, tile * Q_TILE - LONGEST)
    return start, (tile + 1) * Q_TILE


def attend_pair(query, key, value, gain, bias, mixed):
    length = query.shape[0]
    low_lanes = lax.broadcasted_iota(jnp.int32, (1, 2 * HD), 1) < HD
    query = (gain * (query * head_factors(query, low_lanes))).astype(BF16) * 8
    key = (gain * (key * head_factors(key, low_lanes))).astype(BF16)
    value = value.astype(BF16)
    zero = jnp.zeros_like(query)
    parts = (jnp.where(low_lanes, query, zero), jnp.where(low_lanes, zero, query))
    for tile in range(length // Q_TILE):
        start, end = key_range(tile)
        rows = slice(tile * Q_TILE, (tile + 1) * Q_TILE)
        tile_bias = bias[rows, start:end]
        results = []
        for part in parts:
            expo = jnp.exp(nt(part[rows], key[start:end]) + tile_bias)
            total = jnp.sum(expo, axis=-1, keepdims=True)
            results.append(nn(expo.astype(BF16), value[start:end]) * (1.0 / total))
        mixed[rows, :] = jnp.where(low_lanes, results[0], results[1]).astype(BF16)


def attend_pair_back(
    raw_q, raw_k, raw_v, d_mixed, gains, bias, d_raw_q, d_raw_k, d_raw_v, sum_k, sum_v
):
    length = raw_q.shape[0]
    low_lanes = lax.broadcasted_iota(jnp.int32, (1, 2 * HD), 1) < HD
    low_rows = lax.broadcasted_iota(jnp.int32, (2 * HD, 1), 0) < HD
    key_raw = raw_k[...]
    key_factor = head_factors(key_raw, low_lanes)
    key_unit = key_raw * key_factor
    key = (gains * key_unit).astype(BF16)
    key_eight = ((gains * key_unit).astype(BF16).astype(F32) * 8.0).T.astype(BF16)
    value = raw_v[...].astype(BF16)
    sum_k[...] = jnp.zeros_like(sum_k)
    sum_v[...] = jnp.zeros_like(sum_v)
    gain_total = jnp.zeros((1, 2 * HD), F32)

    def back(upstream, unit, factor):
        scaled = gains * upstream
        return (factor * (scaled - unit * head_sums(scaled * unit, low_lanes))).astype(BF16)

    for tile in range(length // Q_TILE):
        start, end = key_range(tile)
        rows = slice(tile * Q_TILE, (tile + 1) * Q_TILE)
        query_raw = raw_q[rows, :]
        query_factor = head_factors(query_raw, low_lanes)
        query_unit = query_raw * query_factor
        query = (gains * query_unit).astype(BF16) * 8
        upstream = d_mixed[rows]
        tile_bias = bias[start:end, rows]
        d_query = []
        for low in (True, False):
            lanes = low_lanes if low else jnp.logical_not(low_lanes)
            own_query = jnp.where(lanes, query, jnp.zeros_like(query))
            own_up = jnp.where(lanes, upstream, jnp.zeros_like(upstream))
            expo = jnp.exp(nt(key[start:end], own_query) + tile_bias)
            probs = expo * (1.0 / jnp.sum(expo, axis=0, keepdims=True))
            d_probs = nt(value[start:end], own_up)
            delta = jnp.sum(probs * d_probs, axis=0, keepdims=True)
            d_scores = (probs * (d_probs - delta)).astype(BF16)
            sum_v[start:end, :] += nn(probs.astype(BF16), own_up)
            sum_k[start:end, :] += nn(d_scores, own_query)
            d_query.append(nn(key_eight[:, start:end], d_scores))
        d_query = jnp.where(low_rows, d_query[0], d_query[1]).T
        gain_total += jnp.sum(d_query * query_unit, axis=0, keepdims=True)
        d_raw_q[rows, :] = back(d_query, query_unit, query_factor)
    d_key = sum_k[...]
    gain_total += jnp.sum(d_key * key_unit, axis=0, keepdims=True)
    d_raw_k[...] = back(d_key, key_unit, key_factor)
    d_raw_v[...] = sum_v[...].astype(BF16)
    return gain_total


ARRIVE = 4 * LAG
UNIT_GROUP = 4
FIRST_UNIT_PAIR = 8
RARE_UNITS = 3


def head_tiles():
    return HEADS * HD // 2 // LANES


def unit_tiles():
    return FF // 2 // LANES


def forward_plan():
    groups = unit_tiles() // UNIT_GROUP
    return tile_plan((2 * (FIRST_UNIT_PAIR + 5 * groups) + 2 * (RARE_UNITS + groups)) * LANES)


def pair_tile(unit):
    return 2 * (FIRST_UNIT_PAIR + 5 * (unit // UNIT_GROUP) + unit % UNIT_GROUP)


def shrink_tile_static(unit):
    plan = forward_plan()
    group, place = unit // UNIT_GROUP, unit % UNIT_GROUP
    if place < 2:
        return plan[2][0] + place * plan[2][2] + RARE_UNITS + group
    return 2 * (FIRST_UNIT_PAIR + 5 * group + UNIT_GROUP) + place - 2


def shrink_tile(unit):
    plan = forward_plan()
    group, place = unit // UNIT_GROUP, unit % UNIT_GROUP
    rare = plan[2][0] + place * plan[2][2] + RARE_UNITS + group
    often = 2 * (FIRST_UNIT_PAIR + 5 * group + UNIT_GROUP) + place - 2
    return jnp.where(place < 2, rare, often)


def forward_sources():
    plan = forward_plan()
    heads, units = head_tiles(), unit_tiles()
    rare, rarer = plan[2][0], plan[3][0]
    inward = [("inward", k // heads, k % heads) for k in range(3 * heads)]
    sources = dict(enumerate(inward[:-1]))
    sources[rare] = inward[-1]
    sources[rarer] = ("small", None, 0)
    for tile, place in ((rare + 1, 0), (rarer + 1, 1), (3 * heads - 1, 2), (3 * heads, 3), (rare + 2, 4)):
        sources[tile] = ("outward", None, place)
    for unit in range(units):
        sources[pair_tile(unit)] = ("expand", 0, unit)
        sources[pair_tile(unit) + 1] = ("expand", 1, unit)
        sources[shrink_tile_static(unit)] = ("shrink", None, unit)
    return sources


def shrink_tile_static(unit):
    plan = forward_plan()
    group, place = unit // UNIT_GROUP, unit % UNIT_GROUP
    if place < 2:
        return plan[2][0] + place * plan[2][2] + RARE_UNITS + group
    return 2 * (FIRST_UNIT_PAIR + 5 * group + UNIT_GROUP) + place - 2


def forward_kernel(
    plan,
    inward,
    outward,
    expand,
    shrink,
    small_copies,
    tokens,
    cotangent,
    segments,
    pads,
    place_row,
    out,
    tokens_out,
    raw_out,
    mixed_out,
    h_attn_out,
    first_out,
    first_low_out,
    tokens_turned_out,
    first_turned_out,
    bias_out,
    d_two_out,
    output_out,
    d_shrunk_out,
    d_shrunk_turned_out,
    proj_out,
    hidden_out,
    factors,
    alphas,
    scales,
    gains,
    alpha_grad,
    block,
    shrunk,
    place,
    tokens_in,
    cot_in,
    bias,
    turned_bias,
    raw,
    stage_pair,
    stage_one,
    stage_outward,
    mixed,
    branch_in,
    h_attn,
    first,
    first_low,
    stage_proj,
    stage_hidden,
    keep,
    own_sem,
    send_sem,
    recv_sem,
    pair_sem,
    one_sem,
    outward_sem,
    proj_sem,
    hidden_sem,
    result_sem,
    core_send,
    core_recv,
):
    me = lax.axis_index("dp")
    core = lax.axis_index("tensor")
    inv_root = D ** (-0.5)
    rows = tokens.shape[0]
    own_rows = rows // 2
    own_at = pl.multiple_of(core * own_rows, own_rows)
    other_at = pl.multiple_of((1 - core) * own_rows, own_rows)
    heads = head_tiles()
    units = unit_tiles()
    attend_at = 3 * heads // 2 + ARRIVE + 1
    pairs_each = 2
    sequences, length = segments.shape
    head_pairs = sequences * heads
    branch_at = attend_at + -(-head_pairs // pairs_each)
    units_at = branch_at + 2

    cot_copy = pltpu.make_async_copy(cotangent.at[pl.ds(own_at, own_rows)], cot_in, result_sem.at[13])
    cot_copy.start()
    operands = {
        "inward": inward,
        "outward": outward,
        "expand": expand,
        "shrink": shrink,
        "small": small_copies,
    }
    for tile, (name, row_block, at) in forward_sources().items():
        source = operands[name] if row_block is None else operands[name].at[row_block]
        block[:, tile * LANES : (tile + 1) * LANES] = source[
            :, at * LANES : (at + 1) * LANES
        ].astype(BF16)
    unused = plan[3][0] + 2
    block[:, unused * LANES : (unused + 1) * LANES] = jnp.zeros((block.shape[0], LANES), BF16)
    own = pltpu.make_async_copy(block, out.at[0, 0, 0, 0], own_sem)
    own.start()
    greet(me, core)

    def piece(hop, route, tile):
        lanes = lanes_of(plan, route, tile)
        crossed, axis = ROUTES[route][:hop], ROUTES[route][hop]
        source = [slice(None) if k in crossed else 0 for k in range(4)]
        target = [1 if k == axis else source[k] for k in range(4)]
        if hop == 0:
            source_ref = block.at[:, lanes]
        else:
            source_ref = out.at[(*source, slice(None), lanes)]
        return pltpu.make_async_remote_copy(
            src_ref=source_ref,
            dst_ref=out.at[(*target, slice(None), lanes)],
            send_sem=send_sem.at[hop, route, tile % RING],
            recv_sem=recv_sem.at[hop, route, tile],
            device_id={"dp": partner_of(me, PLACES[axis])},
            device_id_type=pl.DeviceIdType.MESH,
        )

    def forward_hop(hop, route, tile):
        if hop > 0:
            piece(hop - 1, route, tile).wait_recv()
        if hop < 4:

            @pl.when(tile >= RING)
            def _():
                piece(hop, route, tile - RING).wait_send()

            piece(hop, route, tile).start()

    def staged(tile, width, target, sem):
        lanes = pl.ds(pl.multiple_of(tile * LANES, LANES), width * LANES)
        return pltpu.make_async_copy(out.at[:, :, :, :, :, lanes], target, sem)

    def lanes_half(number):
        return pl.ds(pl.multiple_of((number % 2) * LANES, LANES), LANES)

    def pair_copy(tile, slot):
        return staged(tile, 2, stage_pair.at[slot], pair_sem.at[slot])

    def one_copy(tile, number):
        target = stage_one.at[(number // 2) % 2, :, :, :, :, :, lanes_half(number)]
        return staged(tile, 1, target, one_sem.at[number % 4])

    rare = plan[2][0]
    rarer = plan[3][0]

    def outward_copies():
        return [
            staged(tile, width, stage_outward.at[:, :, :, :, :, pl.ds(at * LANES, width * LANES)], outward_sem.at[k])
            for k, (tile, width, at) in enumerate(
                ((rare + 1, 1, 0), (rarer + 1, 1, 1), (3 * heads - 1, 2, 2), (rare + 2, 1, 4))
            )
        ]

    def core_copy(source, target, which):
        return pltpu.make_async_remote_copy(
            src_ref=source,
            dst_ref=target,
            send_sem=core_send.at[which],
            recv_sem=core_recv.at[which],
            device_id={"tensor": 1 - core},
            device_id_type=pl.DeviceIdType.MESH,
        )

    def branch_copy():
        return core_copy(shrunk.at[pl.ds(0, own_rows)], branch_in, 0)

    def first_copy():
        return core_copy(
            first_low.at[pl.ds(own_at, own_rows)], first_low.at[pl.ds(own_at, own_rows)], 1
        )

    half_rows = own_rows // 2

    def shrunk_copy(k):
        at = pl.ds(pl.multiple_of(other_at + k * half_rows, half_rows), half_rows)
        return core_copy(tokens_in.at[at], tokens_in.at[at], 2 + k)

    def d_shrunk_copy(k):
        at = pl.ds(pl.multiple_of(own_at + k * half_rows, half_rows), half_rows)
        return core_copy(first_low.at[at], first_low.at[at], 4 + k)

    result_pairs = (
        (tokens_in, tokens_out),
        (raw, raw_out),
        (mixed, mixed_out),
        (h_attn, h_attn_out),
        (first, first_out),
        (first_low, first_low_out),
        (place.at[:, pl.ds(0, rows)], tokens_turned_out),
        (place.at[:, pl.ds(0, rows)], first_turned_out),
        (turned_bias, bias_out),
        (h_attn, d_two_out),
        (tokens_in.at[pl.ds(own_at, own_rows)], output_out),
        (first_low, d_shrunk_out),
        (place.at[:, pl.ds(0, rows)], d_shrunk_turned_out),
    )

    def result(k):
        return pltpu.make_async_copy(*result_pairs[k], result_sem.at[k])

    def chunks(total, size, body):
        def one(k, _):
            body(pl.ds(pl.multiple_of(k * size, size), size))
            return 0

        lax.fori_loop(0, total // size, one, 0)

    def make_order():
        natural = natural_row(place_row, me)

        def fill(at):
            here = lax.broadcasted_iota(jnp.int32, (LANES, D), 0) + at.start
            place[at, :] = jnp.where(here == natural, 1.0, 0.0).astype(BF16)

        chunks(D, LANES, fill)

    def tokens_in_order(number):
        at = pl.ds(pl.multiple_of(number * 256, 256), 256)
        tokens_in[at, :] = nn(tokens[at, :], place[...]).astype(BF16)

    def cot_in_order():
        cot_copy.wait()

        def move(at):
            cot_in[at, :] = nn(cot_in[at, :], place[...]).astype(BF16)

        chunks(own_rows, 256, move)

    def column_of(row):
        return jnp.broadcast_to(row.astype(F32), (LANES, length)).T

    def make_bias():
        for sequence in range(sequences):
            segment = segments[sequence : sequence + 1, :]
            pad = pads[sequence : sequence + 1, :]
            own_segment = column_of(segment)
            for tile in range(length // LANES):
                lanes = slice(tile * LANES, (tile + 1) * LANES)
                query = lax.broadcasted_iota(jnp.int32, (length, LANES), 0)
                key = lax.broadcasted_iota(jnp.int32, (length, LANES), 1) + tile * LANES
                open_key = jnp.where(pad[:, lanes] == 0, segment[:, lanes], -1).astype(F32)
                allowed = ((own_segment == open_key) & (key <= query)) | (key == query)
                values = jnp.where(allowed, 0.0, MASKED)
                bias[sequence, :, lanes] = values
                turned_bias[sequence, lanes, :] = values.T
        result(8).start()
        keep[...] = jnp.where(core == 0, column_of(1 - pads[0:1, :]), column_of(1 - pads[1:2, :]))

    def finish():
        alpha = alphas[1:2, :]
        alpha_grad[...] = jnp.zeros_like(alpha_grad)

        def some(at):
            here = pl.ds(pl.multiple_of(own_at + at.start, 64), 64)
            normed, factor = row_norm(shrunk[here, :] + tokens_in[here, :].astype(F32))
            start = first[at, :]
            output, output_factor = row_norm(start + alpha * (normed - start))
            upstream = cot_in[at, :].astype(F32) * keep[at, 0:1]
            d_two = row_norm_back(upstream, output, output_factor)
            alpha_grad[0:1, :] += jnp.sum(d_two * (normed - start), axis=0, keepdims=True)
            h_attn[at, :] = d_two
            tokens_in[here, :] = output.astype(BF16)
            first_low[here, :] = row_norm_back(alpha * d_two, normed, factor).astype(BF16)

        for k in range(2):
            shrunk_copy(k).wait()
            span(k, 64, 0, some)
            d_shrunk_copy(k).start()
        result(9).start()
        result(10).start()
        for k in range(2):
            span(k, LANES, own_at, lambda at: turn_rows(first_low, at))
        for k in range(2):
            d_shrunk_copy(k).wait()
            span(k, LANES, other_at, lambda at: turn_rows(first_low, at))
        result(12).start()
        result(11).start()
        for k in (9, 10, 11, 12):
            result(k).wait()

    def turn_rows(source, at):
        place[:, at] = source[at, :].astype(F32).T.astype(BF16)

    def turn(source):
        chunks(rows, LANES, functools.partial(turn_rows, source))

    def project(weights, lanes):
        def some(at):
            raw[at, lanes] = nn(tokens_in[at, :], weights) * inv_root

        chunks(rows, 256, some)

    def small_vectors():
        small = stage_one[0, :, :, :, :, :, LANES:].reshape(D, LANES).astype(F32).T
        alphas[...] = small[: alphas.shape[0]]
        scales[...] = nt(small.astype(BF16), place[...])[: scales.shape[0]]
        each = units * LANES // D
        for row in range(2):
            for k in range(each):
                at = 3 + row * 2 * each + k
                gains[row : row + 1, k * D : (k + 1) * D] = jnp.where(
                    core == 0, scales[at : at + 1, :], scales[at + each : at + each + 1, :]
                )

    def attend_one(number):
        sequence, head = number // heads, number % heads
        at = pl.ds(pl.multiple_of(sequence * length, length), length)
        lanes = [
            pl.ds(pl.multiple_of((k * heads + head) * LANES, LANES), LANES) for k in range(3)
        ]
        gain_lanes = pl.ds(pl.multiple_of((core * heads + head) * LANES, LANES), LANES)
        attend_pair(
            raw[at, lanes[0]],
            raw[at, lanes[1]],
            raw[at, lanes[2]],
            scales[2:3, gain_lanes],
            bias.at[sequence],
            mixed.at[at, lanes[0]],
        )

    def branch():
        weights = stage_outward[...].reshape(D, heads * LANES)
        for target, source in ((0, other_at), (own_rows, own_at)):
            for k in range(2):
                half = own_rows // 2
                at = pl.ds(pl.multiple_of(source + k * half, half), half)
                shrunk[pl.ds(target + k * half, half), :] = nt(mixed[at, :], weights)
            if target == 0:
                branch_copy().start()

    def norms():
        branch_copy().wait()
        alpha = alphas[0:1, :]

        def some(at):
            total = shrunk[pl.ds(pl.multiple_of(own_rows + at.start, 64), 64), :] + branch_in[at, :]
            normed, factor = row_norm(total)
            here = pl.ds(pl.multiple_of(own_at + at.start, 64), 64)
            inputs = tokens_in[here, :].astype(F32)
            result, result_factor = row_norm(inputs + alpha * (normed - inputs))
            h_attn[at, :] = normed
            first[at, :] = result
            first_low[here, :] = result.astype(BF16)
            factors[at, :LANES] = jnp.broadcast_to(factor, (64, LANES))
            factors[at, LANES:] = jnp.broadcast_to(result_factor, (64, LANES))

        chunks(own_rows, 64, some)
        result(0).wait()
        first_copy().start()
        for k in (3, 4):
            result(k).start()

    def gain_of(unit, row):
        return gains[row : row + 1, pl.ds(pl.multiple_of(unit * LANES, LANES), LANES)]

    def proj_copy(unit):
        lanes = pl.ds(pl.multiple_of(unit * 2 * LANES, 2 * LANES), 2 * LANES)
        slot = unit % 2
        return pltpu.make_async_copy(stage_proj.at[slot], proj_out.at[:, lanes], proj_sem.at[slot])

    def hidden_copy(pair):
        lanes = pl.ds(pl.multiple_of(pair * 2 * LANES, 2 * LANES), 2 * LANES)
        slot = pair % 2
        return pltpu.make_async_copy(
            stage_hidden.at[slot], hidden_out.at[:, lanes], hidden_sem.at[slot]
        )

    def fetch_shrink(pair):
        for k in range(2):
            one_copy(shrink_tile(2 * pair + k), 2 * pair + k).start()

    def span(k, size, start, body):
        def one(j, _):
            body(pl.ds(pl.multiple_of(start + k * half_rows + j * size, size), size))
            return 0

        lax.fori_loop(0, half_rows // size, one, 0)

    def add_shrunk(pair):
        for k in range(2):
            one_copy(0, 2 * pair + k).wait()
        down = stage_one[pair % 2].reshape(D, 2 * LANES)
        for part, start in enumerate((other_at, own_at)):
            at = pl.ds(start, own_rows)
            values = stage_hidden[pair % 2, at, :]
            for k in range(D // 256):
                columns = slice(k * 256, (k + 1) * 256)
                shrunk[at, columns] += nt(values, down[columns])
            if part == 0:

                @pl.when(pair == units // 2 - 1)
                def _():
                    result(5).wait()
                    def lower(rows_at):
                        tokens_in[rows_at, :] = shrunk[rows_at, :].astype(BF16)

                    for k in range(2):
                        span(k, 64, other_at, lower)
                        shrunk_copy(k).start()

        hidden_copy(pair).start()

    def one_unit(unit):
        slot = unit % 2
        pair = unit // 2

        @pl.when(unit == 0)
        def _():
            first_copy().wait()
            result(5).start()
            shrunk[...] = jnp.zeros_like(shrunk)

        @pl.when(unit >= 2)
        def _():
            proj_copy(unit - 2).wait()

        @pl.when((unit >= 4) & (slot == 0))
        def _():
            hidden_copy(pair - 2).wait()

        pair_copy(0, slot).wait()
        weights = stage_pair[slot].reshape(D, 2 * LANES)
        gain_up = gain_of(unit, 0)
        gain_gate = gain_of(unit, 1)

        def some(at):
            proj = nn(first_low[at, :], weights) * inv_root
            stage_proj[slot, at, :] = proj
            gate = gain_gate * proj[:, LANES:]
            hidden = (gain_up * proj[:, :LANES] * (gate * jax.nn.sigmoid(gate))).astype(BF16)
            stage_hidden[pair % 2, at, lanes_half(unit)] = hidden

        chunks(rows, own_rows, some)
        proj_copy(unit).start()

    def step(index, _):
        for hop in range(5):
            for_tiles(index, hop, plan, functools.partial(forward_hop, hop))

        @pl.when(index == LAG - 1)
        def _():
            own.wait()

        order_at = ARRIVE - rows // 256

        @pl.when(index == order_at - 1)
        def _():
            make_order()

        @pl.when((index >= order_at) & (index < ARRIVE))
        def _():
            tokens_in_order(index - order_at)

        @pl.when(index == ARRIVE)
        def _():
            result(0).start()

        pair = index - ARRIVE

        @pl.when((pair >= 0) & (pair < 3 * heads // 2))
        def _():
            pair_copy(2 * pair, pair % 2).start()

        @pl.when(pair == 0)
        def _():
            one_copy(rare, 0).start()

        @pl.when(pair == EVERY // 2)
        def _():
            one_copy(rarer, 1).start()

        @pl.when((pair >= 1) & (pair <= 3 * heads // 2))
        def _():
            done = pair - 1
            pair_copy(0, done % 2).wait()
            lanes = pl.ds(pl.multiple_of(done * 2 * LANES, 2 * LANES), 2 * LANES)
            project(stage_pair[done % 2].reshape(D, 2 * LANES), lanes)

        @pl.when(pair == 1)
        def _():
            one_copy(0, 0).wait()
            weights = stage_one[0, :, :, :, :, :, :LANES].reshape(D, LANES)
            project(weights, pl.ds((3 * heads - 1) * LANES, LANES))

        @pl.when(pair == EVERY // 2 + 1)
        def _():
            one_copy(0, 1).wait()
            small_vectors()

        @pl.when(pair == 4)
        def _():
            cot_in_order()

        @pl.when(pair == 5)
        def _():
            make_bias()

        @pl.when(pair == 6)
        def _():
            turn(tokens_in)
            result(6).start()

        @pl.when(index == units_at + 1)
        def _():
            result(6).wait()
            turn(first_low)
            result(7).start()

        @pl.when(index == attend_at)
        def _():
            result(1).start()
            for copy in outward_copies():
                copy.start()

        @pl.when((index >= attend_at) & (index < branch_at))
        def _():
            for k in range(pairs_each):
                attend_one((index - attend_at) * pairs_each + k)

        @pl.when(index == branch_at)
        def _():
            result(2).start()
            for copy in outward_copies():
                copy.wait()
            branch()

        @pl.when(index == branch_at + 1)
        def _():
            norms()

        due = index - units_at

        @pl.when(due == -1)
        def _():
            pair_copy(pair_tile(0), 0).start()

        for k in range(2):
            early = 2 * due - 1 + k
            unit = jnp.where(due <= 2, early, due + 2) if k == 1 else early

            @pl.when((due >= 0) & (unit >= 0) & (unit < units) & ((due <= 2) | (k == 1)))
            def _(unit=unit):
                @pl.when(unit + 1 < units)
                def _():
                    pair_copy(pair_tile(unit + 1), (unit + 1) % 2).start()

                one_unit(unit)

        down_at = due - 1
        for k in range(2):

            @pl.when((down_at >= k - 1) & ((down_at + 1 - k) % 4 == 0) & (down_at - k < units - 1))
            def _(k=k):
                fetch_shrink((down_at + 1 - k) // 2 + k)

            @pl.when((down_at >= k) & ((down_at - k) % 4 == 0) & (down_at - k < units))
            def _(k=k):
                add_shrunk((down_at - k) // 2 + k)

        return 0

    lax.fori_loop(0, max(steps_of(plan, 4), units_at + units - 1), step, 0)
    for unit in (units - 2, units - 1):
        proj_copy(unit).wait()
    for pair in (units // 2 - 2, units // 2 - 1):
        hidden_copy(pair).wait()
    for k in (1, 2, 3, 4, 7, 8):
        result(k).wait()
    finish()
    for route, (_, _, number, _, _) in enumerate(plan):
        for tile in range(max(0, number - RING), number):
            for hop in range(4):
                piece(hop, route, tile).wait_send()


def forward_pass(*operands, collective_id):
    plan = forward_plan()
    rows = operands[1].shape[0]
    count = operands[5].shape[0]
    sequences, length = operands[7].shape
    columns = sum(entry[2] for entry in plan) * LANES
    own = count // 2
    heads = head_tiles() * LANES
    units = unit_tiles() * LANES
    most = max(entry[2] for entry in plan)
    place = (2, 2, 2, 2, rows)
    hbm = pl.BlockSpec(memory_space=pl.ANY)
    vmem = pl.BlockSpec(memory_space=pltpu.VMEM)
    dma = pltpu.SemaphoreType.DMA
    return pl.pallas_call(
        functools.partial(forward_kernel, plan),
        out_shape=[
            jax.ShapeDtypeStruct((*place, columns), BF16),
            jax.ShapeDtypeStruct((count, D), BF16),
            jax.ShapeDtypeStruct((count, 3 * heads), F32),
            jax.ShapeDtypeStruct((count, heads), BF16),
            jax.ShapeDtypeStruct((own, D), F32),
            jax.ShapeDtypeStruct((own, D), F32),
            jax.ShapeDtypeStruct((count, D), BF16),
            jax.ShapeDtypeStruct((D, count), BF16),
            jax.ShapeDtypeStruct((D, count), BF16),
            jax.ShapeDtypeStruct((sequences, length, length), F32),
            jax.ShapeDtypeStruct((own, D), F32),
            jax.ShapeDtypeStruct((own, D), BF16),
            jax.ShapeDtypeStruct((count, D), BF16),
            jax.ShapeDtypeStruct((D, count), BF16),
            jax.ShapeDtypeStruct((count, 2 * units), F32),
            jax.ShapeDtypeStruct((count, units), BF16),
            jax.ShapeDtypeStruct((own, 2 * LANES), F32),
            jax.ShapeDtypeStruct((8, D), F32),
            jax.ShapeDtypeStruct((16, D), F32),
            jax.ShapeDtypeStruct((8, units), F32),
            jax.ShapeDtypeStruct((8, D), F32),
        ],
        in_specs=[vmem] * 6 + [hbm] + [vmem] * 3,
        out_specs=[hbm] * 16 + [vmem] * 5,
        scratch_shapes=[
            pltpu.VMEM((rows, columns), BF16),
            pltpu.VMEM((count, D), F32),
            pltpu.VMEM((D, D), BF16),
            pltpu.VMEM((count, D), BF16),
            pltpu.VMEM((own, D), BF16),
            pltpu.VMEM((sequences, length, length), F32),
            pltpu.VMEM((sequences, length, length), F32),
            pltpu.VMEM((count, 3 * heads), F32),
            pltpu.VMEM((2, *place, 2 * LANES), BF16),
            pltpu.VMEM((2, *place, 2 * LANES), BF16),
            pltpu.VMEM((*place, heads), BF16),
            pltpu.VMEM((count, heads), BF16),
            pltpu.VMEM((own, D), F32),
            pltpu.VMEM((own, D), F32),
            pltpu.VMEM((own, D), F32),
            pltpu.VMEM((count, D), BF16),
            pltpu.VMEM((2, count, 2 * LANES), F32),
            pltpu.VMEM((2, count, 2 * LANES), BF16),
            pltpu.VMEM((own, LANES), F32),
            dma,
            dma((4, 4, RING)),
            dma((4, 4, most)),
            dma((2,)),
            dma((4,)),
            dma((4,)),
            dma((2,)),
            dma((2,)),
            dma((14,)),
            dma((6,)),
            dma((6,)),
        ],
        compiler_params=pltpu.CompilerParams(
            collective_id=collective_id, has_side_effects=True, vmem_limit_bytes=60 << 20
        ),
        name="forward_pass",
    )(*operands)


SLOTS = 2 * RING + 4


def backward_plan():
    return tile_plan((4 * head_tiles() + 3 * unit_tiles()) * LANES)


def gradient_tile(route, tile):
    heads, units = head_tiles(), unit_tiles()
    shrink_steps, late = units // 2 - 1, units // 4
    outward, up = 3 * heads, 4 * heads
    gate, shrink = up + units, up + 2 * units
    if route < 2:
        unit = tile - shrink_steps + late
        last = tile - shrink_steps - (units - late)
        return jnp.where(
            tile < shrink_steps,
            shrink + 2 * tile + 2 + route,
            jnp.where(
                last < 0,
                (up, gate)[route] + unit,
                jnp.where(last < 2, outward + 2 * last + route, 2 * (last - 2) + route),
            ),
        )
    of_unit = (up, gate)[route - 2] + tile - 1
    if route == 2:
        last = jnp.where(tile == late + 1, outward + heads - 1, outward - 2)
    else:
        last = jnp.where(tile == late + 1, outward - 3, outward - 1)
    return jnp.where(tile == 0, shrink + route - 2, jnp.where(tile <= late, of_unit, last))


def slot_of(route, tile):
    if route < 2:
        return route * RING + tile % RING
    return 2 * RING + (route - 2) * 2 + tile % 2


def ring_of(route):
    return RING if route < 2 else 2


def backward_kernel(plan, fused, *refs):
    if fused:
        extra = (refs[21:33], refs[37], *refs[-9:])
        refs = (*refs[:21], *refs[33:37], *refs[38:-9])
    else:
        extra = None
    backward_steps(plan, extra, *refs)


def backward_steps(
    plan,
    extra,
    copies,
    d_shrunk,
    d_shrunk_turned,
    first_turned,
    tokens_turned,
    hidden,
    proj,
    raw,
    mixed,
    d_two,
    h_attn,
    first,
    tokens_in,
    factors,
    alphas,
    scales,
    gains,
    alpha_mlp_grad,
    bias,
    place_row,
    output,
    input_grad,
    block_output,
    grads,
    vectors,
    work,
    arrived,
    lefts,
    d_low,
    d_proj,
    first_part,
    core_in,
    stage_hidden,
    stage_rows,
    wide,
    outward,
    right,
    sum_k,
    sum_v,
    alpha_grad,
    unit_grad,
    query_grad,
    vector_sums,
    vector_in,
    send_sem,
    recv_sem,
    load_sem,
    unit_sem,
    raw_sem,
    result_sem,
    core_send,
    core_recv,
    vector_send,
    vector_recv,
):
    me = lax.axis_index("dp")
    core = lax.axis_index("tensor")
    inv_root = D ** (-0.5)
    rows = tokens_in.shape[0]
    own_rows = rows // 2
    own_at = pl.multiple_of(core * own_rows, own_rows)
    other_at = pl.multiple_of((1 - core) * own_rows, own_rows)
    heads = head_tiles()
    units = unit_tiles()
    block = D // 16
    unit_steps = units // 2
    shrink_steps = unit_steps - 1
    late_units = units // 4
    expand_steps = units - late_units
    attention_at = shrink_steps + expand_steps
    rare_units = 1 + late_units
    exchange_at = unit_steps
    attend_at = exchange_at + 3
    sequences = bias.shape[0]
    length = bias.shape[1]
    head_pairs = sequences * heads

    greet(me, core, diagonal=extra is not None)

    def copy(source, target, sem):
        return pltpu.make_async_copy(source, target, sem)

    def chunks(total, size, body):
        def one(k, _):
            body(pl.ds(pl.multiple_of(k * size, size), size))
            return 0

        lax.fori_loop(0, total // size, one, 0)


    def piece(hop, route, tile):
        axis = ROUTES[route][3 - hop]
        slot = slot_of(route, tile)
        return pltpu.make_async_remote_copy(
            src_ref=work[hop].at[slot, 1],
            dst_ref=arrived[hop].at[slot],
            send_sem=send_sem.at[hop, slot],
            recv_sem=recv_sem.at[hop, slot],
            device_id={"dp": partner_of(me, PLACES[axis])},
            device_id_type=pl.DeviceIdType.MESH,
        )

    def free(hop, route, tile):
        @pl.when(tile >= ring_of(route))
        def _():
            piece(hop, route, tile - ring_of(route)).wait_send()

    def add(hop, route, tile):
        piece(hop - 1, route, tile).wait_recv()
        slot = slot_of(route, tile)
        total = work[hop - 1][slot, 0].astype(F32) + arrived[hop - 1][slot].astype(F32)
        if hop == 4:
            place = gradient_tile(route, tile)
            grads[:, pl.ds(pl.multiple_of(place * LANES, LANES), LANES)] = total
            return
        half = total.shape[0] // 2
        free(hop, route, tile)
        work[hop][slot, 0] = total[:half].astype(BF16)
        work[hop][slot, 1] = total[half:].astype(BF16)
        piece(hop, route, tile).start()

    def keep_quarter(route, slot, quarter, part):
        axes = ROUTES[route][::-1]
        if route < 2:
            bits = [quarter >> 1, quarter & 1]
            at = bits[axes[1]] * 4 * block
            work[0][slot, bits[axes[0]], at : at + 4 * block, :] = part
            return
        for low in range(4):
            bits = [quarter >> 1, quarter & 1, low >> 1, low & 1]
            index = bits[axes[1]] * 4 + bits[axes[2]] * 2 + bits[axes[3]]
            work[0][slot, bits[axes[0]], index * block : (index + 1) * block, :] = part[
                low * block : (low + 1) * block
            ]

    def quarter_rows(quarter):
        return slice(quarter * 4 * block, (quarter + 1) * 4 * block)

    def often_product(tile):
        for route in (0, 1):
            free(0, route, tile)
        is_shrink = tile < shrink_steps
        is_expand = (tile >= shrink_steps) & (tile < attention_at)
        late = tile - attention_at
        is_outward = (late >= 0) & (late < 2)

        @pl.when(is_shrink)
        def _():
            right[0] = stage_hidden[tile % 2]

        @pl.when(is_expand)
        def _():
            unit = tile - shrink_steps + late_units
            right[0] = d_proj[:, pl.ds(pl.multiple_of(unit * 2 * LANES, 2 * LANES), 2 * LANES)]

        @pl.when(late >= 0)
        def _():
            first_tile = jnp.where(late < 2, 2 * late, 2 * late + 1)
            right[0] = wide[:rows, pl.ds(pl.multiple_of(first_tile * LANES, LANES), 2 * LANES)]

        which = jnp.where(is_expand | is_outward, 1, 0)
        scale = jnp.where(is_shrink | is_outward, 1.0, inv_root)
        product = (nn(lefts[which], right[0]) * scale).astype(BF16)
        for quarter in range(4):
            part = product[quarter_rows(quarter)]
            for route in (0, 1):
                keep_quarter(
                    route, slot_of(route, tile), quarter, part[:, route * LANES : (route + 1) * LANES]
                )
        for route in (0, 1):
            piece(0, route, tile).start()

    def rare_product(route, tile):
        late = tile - rare_units
        at = (route - 2) * LANES
        lanes = slice(at, at + LANES)

        @pl.when(tile == 0)
        def _():
            right[1, :, lanes] = stage_hidden[2, :, lanes]

        @pl.when((tile > 0) & (late < 0))
        def _():
            unit_lane = pl.multiple_of((tile - 1) * 2 * LANES + at, LANES)
            right[1, :, lanes] = d_proj[:, pl.ds(unit_lane, LANES)]

        @pl.when(late >= 0)
        def _():
            if route == 2:
                place = jnp.where(late == 0, heads - 1, heads + 13)
            else:
                place = heads + 12 + 2 * late
            right[1, :, lanes] = wide[:rows, pl.ds(pl.multiple_of(place * LANES, LANES), LANES)]

        free(0, route, tile)
        of_units = (tile > 0) & (late < 0)
        of_outward = (late == 0) if route == 2 else (late < -rare_units)
        which = jnp.where(of_units | of_outward, 1, 0)
        scale = jnp.where((tile == 0) | of_outward, 1.0, inv_root)
        product = (nn(lefts[which], right[1, :, lanes]) * scale).astype(BF16)
        for quarter in range(4):
            keep_quarter(route, slot_of(route, tile), quarter, product[quarter_rows(quarter)])
        piece(0, route, tile).start()


    def unit_copies(pair):
        slot = pair % 2
        unit = 2 * pair
        at = pl.multiple_of(slot * 6 * LANES, 2 * LANES)
        result = [
            (
                copies.at[:, pl.ds(pl.multiple_of(pair_tile(unit) * LANES, LANES), 4 * LANES)],
                wide.at[:, pl.ds(at, 4 * LANES)],
            )
        ]
        for k in range(2):
            tile = shrink_tile(unit + k)
            result.append(
                (
                    copies.at[:, pl.ds(pl.multiple_of(tile * LANES, LANES), LANES)],
                    wide.at[:, pl.ds(pl.multiple_of(at + (4 + k) * LANES, LANES), LANES)],
                )
            )
        lanes = pl.ds(pl.multiple_of(pair * 4 * LANES, 4 * LANES), 4 * LANES)
        for k in range(2):
            result.append(
                (
                    proj.at[pl.ds(k * own_rows, own_rows), lanes],
                    stage_rows.at[slot, :, pl.ds(k * 4 * LANES, 4 * LANES)],
                )
            )
        return [copy(source, target, unit_sem.at[k, slot]) for k, (source, target) in enumerate(result)]

    def hidden_copy(tile):
        lanes = pl.ds(pl.multiple_of((2 * tile + 2) * LANES, 2 * LANES), 2 * LANES)
        return copy(hidden.at[:, lanes], stage_hidden.at[tile % 2], unit_sem.at[5, tile % 2])

    def unit_pair(pair):
        slot = pair % 2
        for part in unit_copies(pair):
            part.wait()
        at_lane = pl.multiple_of(slot * 6 * LANES, 2 * LANES)
        down = wide[:, pl.ds(pl.multiple_of(at_lane + 4 * LANES, 2 * LANES), 2 * LANES)]

        for half in range(2):
            at = slice(half * own_rows, (half + 1) * own_rows)
            proj_lanes = half * 4 * LANES
            d_hidden = nn(d_low[at, :], down)
            for k in range(2):
                lanes = pl.ds(pl.multiple_of((2 * pair + k) * LANES, LANES), LANES)
                gain_up, gain_gate = gains[0:1, lanes], gains[1:2, lanes]
                start = proj_lanes + 2 * k * LANES
                proj_up = stage_rows[slot, :, start : start + LANES]
                proj_gate = stage_rows[slot, :, start + LANES : start + 2 * LANES]
                upstream = d_hidden[:, k * LANES : (k + 1) * LANES]
                gate = gain_gate * proj_gate
                sigmoid = jax.nn.sigmoid(gate)
                d_up = upstream * (gate * sigmoid)
                d_gate = upstream * (gain_up * proj_up) * sigmoid * (1.0 + gate * (1.0 - sigmoid))
                unit_grad[0:1, lanes] += jnp.sum(d_up * proj_up, axis=0, keepdims=True)
                unit_grad[1:2, lanes] += jnp.sum(d_gate * proj_gate, axis=0, keepdims=True)
                place = pl.multiple_of((2 * pair + k) * 2 * LANES, 2 * LANES)
                d_proj[at, pl.ds(place, LANES)] = (d_up * gain_up).astype(BF16)
                d_proj[at, pl.ds(pl.multiple_of(place + LANES, LANES), LANES)] = (
                    d_gate * gain_gate
                ).astype(BF16)
        expand_at = pl.ds(at_lane, 4 * LANES)
        lanes = pl.ds(pl.multiple_of(pair * 4 * LANES, 4 * LANES), 4 * LANES)
        upstream = d_proj[:, lanes]
        for k in range(D // 256):
            columns = slice(k * 256, (k + 1) * 256)
            first_part[:, columns] += nt(upstream, wide[columns, expand_at])


    def core_copy(source, target, which):
        return pltpu.make_async_remote_copy(
            src_ref=source,
            dst_ref=target,
            send_sem=core_send.at[which],
            recv_sem=core_recv.at[which],
            device_id={"tensor": 1 - core},
            device_id_type=pl.DeviceIdType.MESH,
        )

    def part_copy():
        return core_copy(first_part.at[pl.ds(other_at, own_rows)], core_in, 0)

    def branch_copy():
        own = d_low.at[pl.ds(own_at, own_rows)]
        return core_copy(own, own, 1)

    tokens_place = wide.at[pl.ds(0, own_rows), pl.ds(D, D)]
    rare, rarer = forward_plan()[2][0], forward_plan()[3][0]
    outward_tiles = ((rare + 1, 1, 0), (rarer + 1, 1, 1), (3 * heads - 1, 2, 2), (rare + 2, 1, 4))

    def load(k):
        if k == 0:
            return copy(d_two, stage_rows.at[0], load_sem.at[0])
        if k == 1:
            return copy(h_attn, stage_rows.at[1], load_sem.at[1])
        if k == 2:
            return copy(tokens_in.at[pl.ds(own_at, own_rows)], tokens_place, load_sem.at[2])
        if k == 3:
            return copy(
                mixed, wide.at[pl.ds(0, rows), pl.ds(0, heads * LANES)], load_sem.at[3]
            )
        if k == 4:
            return copy(first, first_part.at[pl.ds(other_at, own_rows)], load_sem.at[4])
        if k == 5:
            return copy(d_shrunk, d_low, load_sem.at[5])
        if k == 6:
            return copy(d_shrunk_turned, lefts.at[0], load_sem.at[6])
        if k == 7:
            return copy(first_turned, lefts.at[1], load_sem.at[7])
        if k == 8:
            return copy(tokens_turned, lefts.at[0], load_sem.at[8])
        if k == 9:
            return copy(hidden.at[:, pl.ds(0, 2 * LANES)], stage_hidden.at[2], load_sem.at[9])
        tile, width, at = outward_tiles[k - 10]
        return copy(
            copies.at[:, pl.ds(tile * LANES, width * LANES)],
            outward.at[:, pl.ds(at * LANES, width * LANES)],
            load_sem.at[k],
        )

    def branch_gradient():
        part_copy().wait_send()
        load(4).start()
        part_copy().wait_recv()
        for k in (0, 1, 2, 4):
            load(k).wait()
        alpha_attn, alpha_mlp = alphas[0:1, :], alphas[1:2, :]

        def some(at):
            here = pl.ds(pl.multiple_of(own_at + at.start, 64), 64)
            there = pl.ds(pl.multiple_of(other_at + at.start, 64), 64)
            part = (first_part[here, :] + core_in[at, :]) * inv_root
            d_first = (1.0 - alpha_mlp) * stage_rows[0, at, :] + part
            normed = stage_rows[1, at, :]
            d_one = row_norm_back(
                d_first, first_part[there, :], factors[at, LANES : LANES + 1]
            )
            inputs = wide[at, D : 2 * D].astype(F32)
            alpha_grad[0:1, :] += jnp.sum(d_one * (normed - inputs), axis=0, keepdims=True)
            stage_rows[0, at, :] = d_one
            d_low[here, :] = row_norm_back(alpha_attn * d_one, normed, factors[at, 0:1]).astype(
                BF16
            )

        chunks(own_rows, 64, some)
        branch_copy().start()


    def raw_copies(number):
        sequence, head = number // heads, number % heads
        at = pl.ds(pl.multiple_of(sequence * length, length), length)
        slot = number % 2
        target_rows = pl.ds(pl.multiple_of(slot * own_rows, own_rows), length)
        return [
            copy(
                raw.at[at, pl.ds(pl.multiple_of((k * heads + head) * LANES, LANES), LANES)],
                first_part.at[target_rows, pl.ds(k * LANES, LANES)],
                raw_sem.at[k, slot],
            )
            for k in range(3)
        ]

    def attend_one(number):
        sequence, head = number // heads, number % heads
        for part in raw_copies(number):
            part.wait()
        at = pl.ds(pl.multiple_of(sequence * length, length), length)
        source_rows = pl.ds(pl.multiple_of((number % 2) * own_rows, own_rows), length)
        head_lanes = pl.ds(pl.multiple_of(head * LANES, LANES), LANES)
        gain_lanes = pl.ds(pl.multiple_of((core * heads + head) * LANES, LANES), LANES)
        d_mixed = nn(d_low[at, :], outward[:, head_lanes]).astype(BF16)
        targets = [
            wide.at[at, pl.ds(pl.multiple_of(((k + 1) * heads + head) * LANES, LANES), LANES)]
            for k in range(3)
        ]
        total = attend_pair_back(
            *[first_part.at[source_rows, pl.ds(k * LANES, LANES)] for k in range(3)],
            d_mixed,
            scales[2:3, gain_lanes],
            bias.at[sequence],
            *targets,
            sum_k,
            sum_v,
        )
        query_grad[0:1, head_lanes] += total


    head_lanes = 3 * heads * LANES
    beyond = D - rows

    def inward_copies():
        first_lanes = (3 * heads - 1) * LANES
        result = []
        for row, number, at, lane in ((0, rows, 0, 0), (rows, beyond, 0, head_lanes)):
            for source, width in ((0, first_lanes), (rare * LANES, LANES)):
                offset = 0 if width == first_lanes else first_lanes
                result.append(
                    (
                        copies.at[pl.ds(row, number), pl.ds(source, width)],
                        d_proj.at[pl.ds(at, number), pl.ds(lane + offset, width)],
                    )
                )
        return [copy(source, target, load_sem.at[14 + k]) for k, (source, target) in enumerate(result)]

    order_lane = 2 * head_lanes

    def make_order():
        natural = natural_row(place_row, me)

        def fill(at):
            here = lax.broadcasted_iota(jnp.int32, (LANES, D), 0) + at.start
            d_proj[at, order_lane : order_lane + D] = jnp.where(here == natural, 1.0, 0.0).astype(
                BF16
            )

        chunks(rows, LANES, fill)
        for k in range(beyond // LANES):
            here = lax.broadcasted_iota(jnp.int32, (LANES, D), 0) + rows + k * LANES
            at = slice(beyond + k * LANES, beyond + (k + 1) * LANES)
            d_proj[at, head_lanes : head_lanes + D] = jnp.where(here == natural, 1.0, 0.0).astype(
                BF16
            )

    def natural_parts(values):
        low = nt(values, d_proj[:, order_lane : order_lane + D])
        high = nt(values, d_proj[beyond : 2 * beyond, head_lanes : head_lanes + D])
        return low, high

    def input_part(number):
        at = pl.ds(pl.multiple_of(number * 256, 256), 256)
        upstream = wide[at, heads * LANES : 4 * heads * LANES]
        low = nt(upstream, d_proj[:, :head_lanes]) * inv_root
        d_low[at, :rows] = low.astype(BF16)
        high = nt(upstream, d_proj[:beyond, head_lanes : 2 * head_lanes]) * inv_root
        d_low[at, rows:] = high.astype(BF16)
        low, high = natural_parts(d_low[at, :])
        first_part[at, :rows] = low
        first_part[at, rows:] = high

    def residual_part():
        alpha_attn = alphas[0:1, :]

        def some(at):
            here = pl.ds(pl.multiple_of(own_at + at.start, 128), 128)
            residual = (1.0 - alpha_attn) * stage_rows[0, at, :]
            top = residual.astype(BF16)
            rest = (residual - top.astype(F32)).astype(BF16)
            for part in (top, rest):
                low, high = natural_parts(part)
                first_part[here, :rows] += low
                first_part[here, rows:] += high

        chunks(own_rows, 128, some)

    half_width = D // 2

    def input_copies():
        lanes = pl.ds(pl.multiple_of((1 - core) * half_width, LANES), half_width)
        return [
            core_copy(
                first_part.at[pl.ds(k * own_rows, own_rows), lanes],
                core_in.at[:, pl.ds(k * half_width, half_width)],
                2 + k,
            )
            for k in range(2)
        ]

    def input_copy(k):
        lanes = pl.ds(pl.multiple_of(core * half_width, LANES), half_width)
        at = pl.ds(k * own_rows, own_rows)
        return copy(first_part.at[at, lanes], input_grad.at[at], result_sem.at[k])

    def input_sum():
        lanes = pl.ds(pl.multiple_of(core * half_width, LANES), half_width)
        for k, part in enumerate(input_copies()):
            part.wait()
            at = pl.ds(k * own_rows, own_rows)
            first_part[at, lanes] += core_in[:, k * half_width : (k + 1) * half_width]
            input_copy(k).start()

    def output_load():
        return copy(output, d_low.at[pl.ds(other_at, own_rows)], load_sem.at[18])

    def output_order():
        output_load().wait()
        for k in range(own_rows // 256):
            source = pl.ds(pl.multiple_of(other_at + k * 256, 256), 256)
            target = pl.ds(pl.multiple_of(own_at + k * 256, 256), 256)
            low, high = natural_parts(d_low[source, :])
            d_low[target, :rows] = low.astype(BF16)
            d_low[target, rows:] = high.astype(BF16)
        output_copies()[0].start()
        output_copies()[1].start()

    def output_copies():
        own = pl.ds(own_at, own_rows)
        return (
            core_copy(d_low.at[own], block_output.at[own], 4),
            copy(d_low.at[own], block_output.at[own], result_sem.at[2]),
        )

    def vector_copy(k):
        if k == 0:
            device = {"tensor": 1 - core}
        else:
            device = {"dp": partner_of(me, PLACES[k - 1])}
        return pltpu.make_async_remote_copy(
            src_ref=vector_sums.at[k],
            dst_ref=vector_in.at[k],
            send_sem=vector_send.at[k],
            recv_sem=vector_recv.at[k],
            device_id=device,
            device_id_type=pl.DeviceIdType.MESH,
        )

    def vectors_start():
        alpha_grad[1:2, :] = alpha_mlp_grad[0:1, :]
        vector_sums[0] = jnp.zeros_like(vector_sums[0])
        values = alpha_grad[...]
        for _ in range(3):
            part = values.astype(BF16)
            low, high = natural_parts(part)
            vector_sums[0, :8, :rows] += low
            vector_sums[0, :8, rows:] += high
            values = values - part.astype(F32)
        vector_sums[0, 2:3, pl.ds(pl.multiple_of(core * heads * LANES, LANES), heads * LANES)] = (
            query_grad[0:1, :]
        )
        each = units * LANES // D
        for row in range(2):
            for k in range(2 * each):
                here = unit_grad[row : row + 1, (k % each) * D : (k % each + 1) * D]
                at = 3 + 2 * each * row + k
                vector_sums[0, at : at + 1, :] = jnp.where(core == k // each, here, 0.0)
        vector_copy(0).start()

    def vectors_add(k):
        vector_copy(k).wait()
        total = vector_sums[k] + vector_in[k]
        if k < len(PLACES):
            vector_sums[k + 1] = total
            vector_copy(k + 1).start()
        else:
            vectors[...] = total

    input_at = attention_at + 1
    parts = rows // 256


    squares_at = input_at + parts + 3
    if extra is not None:
        states, squares, *scratch = extra
        early, last, state_sem = scratch[:4], scratch[4:8], scratch[8]

    def state_loads():
        pairs = []
        for start, width, which, place, _, _ in update_pieces():
            for offset in range(0, width, D):
                part = min(width, D)
                number, lane = (start + offset) // D, (start + offset) % D
                source_lanes, lanes = pl.ds(offset, part), pl.ds(lane, part)
                at = pl.ds(number * block, block)
                targets = (
                    first_part.at[at, lanes],
                    wide.at[at, lanes],
                    stage_rows.at[number // 4, pl.ds(number % 4 * block, block), lanes],
                )
                for state, target in zip(states[3 * which : 3 * which + 3], targets):
                    if place is None:
                        source = state.at[:, source_lanes]
                    else:
                        source = state.at[place, :, source_lanes]
                    pairs.append((source, target))
        return [copy(source, target, state_sem.at[k]) for k, (source, target) in enumerate(pairs)]

    def square_row(target, row, first_tile, begin=0, end=units):
        def one(k, _):
            tile = first_tile + k
            number = tile // (D // LANES)
            lanes = pl.ds(pl.multiple_of(tile % (D // LANES) * LANES, LANES), LANES)
            at = pl.ds(pl.multiple_of(number * block, block), block)
            there = pl.ds(pl.multiple_of(number % 4 * block, block), block)
            pre = adam_step(
                first_part[at, lanes],
                wide[at, lanes],
                stage_rows[number // 4, there, lanes],
                grads[:, pl.ds(pl.multiple_of(tile * LANES, LANES), LANES)],
                RATE_MATRIX,
            )[0]
            here = pl.ds(pl.multiple_of(k * LANES, LANES), LANES)
            target[0, row : row + 1, here] = jnp.sum(pre * pre, axis=0, keepdims=True)
            return 0

        lax.fori_loop(begin, end, one, 0)

    def early_squares(index):
        @pl.when(index == squares_at)
        def _():
            early[0][...] = jnp.zeros_like(early[0])
            for k in range(2):
                input_copy(k).wait()
            for load in state_loads():
                load.start()

        @pl.when(index == squares_at + 2)
        def _():
            for load in state_loads():
                load.wait()

        for row in range(3):

            @pl.when(index == squares_at + 2 + row)
            def _(row=row):
                square_row(early[0], row, 4 * heads + row * units)

        @pl.when(index == squares_at + 4)
        def _():
            round_start(me, 0, *early)

        for number, ranges in enumerate((((0, 6), (12, 14), (15, units)), ((6, 10), (14, 15)))):

            @pl.when(index == squares_at + 5 + number)
            def _(ranges=ranges):
                for begin, end in ranges:
                    square_row(last[0], 0, 0, begin, end)

        for number in range(len(ROUNDS)):

            @pl.when(index == squares_at + 5 + number)
            def _(number=number):
                total = round_sum(me, number, *early)
                if number + 1 < len(ROUNDS):
                    early[0][number + 1] = total
                    round_start(me, number + 1, *early)
                else:
                    squares[1:4, :] = total[:3]

    def last_squares():
        square_row(last[0], 0, 0, 10, 12)
        for number in range(len(ROUNDS)):
            round_start(me, number, *last)
            total = round_sum(me, number, *last)
            if number + 1 < len(ROUNDS):
                last[0][number + 1] = total
            else:
                squares[0:1, :] = total


    load(6).start()
    hidden_copy(0).start()
    for k in (9, 5):
        load(k).start()
    for part in unit_copies(0):
        part.start()
    load(7).start()
    alpha_grad[...] = jnp.zeros_like(alpha_grad)
    unit_grad[...] = jnp.zeros_like(unit_grad)
    query_grad[...] = jnp.zeros_like(query_grad)
    first_part[...] = jnp.zeros_like(first_part)
    load(6).wait()

    def step(index, _):
        for hop in range(4, 0, -1):
            for_tiles(index, hop, plan, functools.partial(add, hop))

        @pl.when(index < shrink_steps)
        def _():
            hidden_copy(index).wait()

        @pl.when(index == attention_at)
        def _():
            load(8).wait()
            chunks(rows, LANES, turn)

        @pl.when(index < plan[0][2])
        def _():
            often_product(index)

        @pl.when(index == 0)
        def _():
            for k in (9, 5):
                load(k).wait()

        @pl.when(index == EVERY - 1)
        def _():
            load(7).wait()

        for route in (2, 3):
            number, start = plan[route][2], plan[route][4]
            due = index - start

            @pl.when((due % EVERY == 0) & (due >= 0) & (due < number * EVERY))
            def _(route=route, due=due):
                rare_product(route, due // EVERY)

        @pl.when(index + 1 < shrink_steps)
        def _():
            hidden_copy(index + 1).start()

        @pl.when(index + 1 < unit_steps)
        def _():
            for part in unit_copies(index + 1):
                part.start()

        @pl.when(index < unit_steps)
        def _():
            unit_pair(index)

        @pl.when(index == exchange_at)
        def _():
            part_copy().start()
            for k in (0, 1, 2, 3, 8, 10, 11, 12, 13):
                load(k).start()

        @pl.when(index == exchange_at + 1)
        def _():
            branch_gradient()

        @pl.when(index == exchange_at + 2)
        def _():
            branch_copy().wait()
            for k in (3, 10, 11, 12, 13):
                load(k).wait()

        number = index - attend_at

        @pl.when((number >= -1) & (number < head_pairs - 1))
        def _():
            for part in raw_copies(number + 1):
                part.start()

        @pl.when((number >= 0) & (number < head_pairs))
        def _():
            attend_one(number)

        @pl.when(index == attention_at)
        def _():
            for part in inward_copies():
                part.start()
            make_order()
            vectors_start()

        for k in range(len(PLACES) + 1):

            @pl.when(index == attention_at + 1 + k)
            def _(k=k):
                vectors_add(k)

        @pl.when(index == input_at)
        def _():
            for part in inward_copies():
                part.wait()

        @pl.when((index >= input_at) & (index < input_at + parts))
        def _():
            input_part(index - input_at)

        @pl.when(index == input_at + parts)
        def _():
            output_load().start()
            residual_part()
            for part in input_copies():
                part.start()

        @pl.when(index == input_at + parts + 1)
        def _():
            output_order()

        @pl.when(index == input_at + parts + 2)
        def _():
            input_sum()

        if extra is not None:
            early_squares(index)
        return 0

    def turn(at):
        lefts[1, :, at] = d_low[at, :].astype(F32).T.astype(BF16)

    lax.fori_loop(0, steps_of(plan, 4), step, 0)
    if extra is not None:
        last_squares()
    for part in output_copies():
        part.wait()
    if extra is None:
        for k in range(2):
            input_copy(k).wait()
    for route, (_, _, number, _, _) in enumerate(plan):
        for tile in range(max(0, number - ring_of(route)), number):
            for hop in range(4):
                piece(hop, route, tile).wait_send()


def backward_pass(*operands, states, collective_id):
    fused = len(states) > 0
    plan = backward_plan()
    copies = operands[0]
    count = operands[1].shape[0]
    own = count // 2
    heads = head_tiles() * LANES
    units = unit_tiles() * LANES
    length = operands[18].shape[1]
    block = D // 16
    halves = [block * 8 >> hop for hop in range(4)]
    hbm = pl.BlockSpec(memory_space=pl.ANY)
    vmem = pl.BlockSpec(memory_space=pltpu.VMEM)
    dma = pltpu.SemaphoreType.DMA
    round_scratch = []
    for height in (SQUARE_ROWS, 1):
        round_scratch += [
            pltpu.VMEM((3, height, units), F32),
            pltpu.VMEM((3, 3, height, units), F32),
            dma((3, 3)),
            dma((3, 3)),
        ]
    round_scratch.append(dma((30,)))
    return pl.pallas_call(
        functools.partial(backward_kernel, plan, fused),
        out_shape=[
            jax.ShapeDtypeStruct((count, D // 2), F32),
            jax.ShapeDtypeStruct((count, D), BF16),
            jax.ShapeDtypeStruct((block, 4 * heads + 3 * units), F32),
            jax.ShapeDtypeStruct((16, D), F32),
        ]
        + [jax.ShapeDtypeStruct((SQUARE_ROWS, units), F32)] * fused,
        in_specs=[hbm] * 13 + [vmem] * 7 + [hbm] + [hbm] * len(states),
        out_specs=[hbm] * 2 + [vmem] * (2 + fused),
        scratch_shapes=[
            [pltpu.VMEM((SLOTS, 2, half, LANES), BF16) for half in halves],
            [pltpu.VMEM((SLOTS, half, LANES), BF16) for half in halves],
            pltpu.VMEM((2, D, count), BF16),
            pltpu.VMEM((count, D), BF16),
            pltpu.VMEM((count, 2 * units), BF16),
            pltpu.VMEM((count, D), F32),
            pltpu.VMEM((own, D), F32),
            pltpu.VMEM((3, count, 2 * LANES), BF16),
            pltpu.VMEM((2, own, D), F32),
            pltpu.VMEM((D, 4 * heads), BF16),
            pltpu.VMEM((D, heads), BF16),
            pltpu.VMEM((2, count, 2 * LANES), BF16),
            pltpu.VMEM((length, LANES), F32),
            pltpu.VMEM((length, LANES), F32),
            pltpu.VMEM((8, D), F32),
            pltpu.VMEM((8, units), F32),
            pltpu.VMEM((8, heads), F32),
            pltpu.VMEM((5, 16, D), F32),
            pltpu.VMEM((5, 16, D), F32),
            dma((4, SLOTS)),
            dma((4, SLOTS)),
            dma((19,)),
            dma((6, 2)),
            dma((3, 2)),
            dma((3,)),
            dma((5,)),
            dma((5,)),
            dma((5,)),
            dma((5,)),
        ]
        + round_scratch * fused,
        compiler_params=pltpu.CompilerParams(
            collective_id=collective_id, has_side_effects=True, vmem_limit_bytes=62 << 20
        ),
        name="backward_pass",
    )(*operands, *states)


SQUARE_ROWS = 4


def update_pieces():
    heads, units = head_tiles() * LANES, unit_tiles() * LANES
    pieces = [(k * heads, heads, 0, k, 0, k * heads) for k in range(3)]
    pieces.append((3 * heads, heads, 1, None, 0, 3 * heads))
    pieces += [(4 * heads + k * units, units, 2, k, 1 + k, 0) for k in range(2)]
    pieces.append((4 * heads + 2 * units, units, 3, None, 3, 0))
    return pieces


def update_loads(grads, states, held_grads, held_states, sem):
    pairs = []
    ends = {0: 0, 1: 3, 2: 4, 3: 6}
    sizes = {0: 3, 1: 1, 2: 2, 3: 1}
    pieces = update_pieces()
    for which in range(4):
        start, width = pieces[ends[which]][:2]
        lanes = pl.ds(start, width * sizes[which])
        pairs.append((grads.at[:, lanes], held_grads.at[:, lanes]))
        pairs += list(zip(states[3 * which : 3 * which + 3], held_states[3 * which : 3 * which + 3]))
    return [pltpu.make_async_copy(source, target, sem.at[k]) for k, (source, target) in enumerate(pairs)]


def for_update_tiles(loads, held_grads, held_states, body, after=None):
    waited = -1
    for piece in update_pieces():
        start, width, which, block, _, _ = piece
        if which != waited:
            for load in loads[4 * which : 4 * which + 4]:
                load.wait()
            waited = which

        def one(k, _, start=start, which=which, block=block, piece=piece):
            lane = pl.multiple_of(k * LANES, LANES)
            here = pl.ds(lane, LANES)
            values = [
                ref[:, here] if block is None else ref[block, :, here]
                for ref in held_states[3 * which : 3 * which + 3]
            ]
            gradient = held_grads[:, pl.ds(pl.multiple_of(start + lane, LANES), LANES)]
            body(piece, lane, gradient, *values)
            return 0

        lax.fori_loop(0, width // LANES, one, 0)
        if after is not None and block in (None, (2, 0, 1, 0)[which]):
            after(which)


def squares_kernel(*refs):
    grads, states, total, held_grads, held_states = refs[0], refs[1:13], refs[13], refs[14], refs[15]
    sums, arrived, load_sem, send_sem, recv_sem = refs[16:]
    loads = update_loads(grads, states, held_grads, held_states, load_sem)
    for load in loads:
        load.start()
    me = lax.axis_index("dp")
    low, high = PLACES[:2]
    hops = [[(low,), (high,), (low, high)], *[[(bit,)] for bit in PLACES[2:]]]

    def partner(bits):
        device = me
        for bit in bits:
            device = device + partner_of(me, bit) - me
        return {"dp": device}

    barrier = pltpu.get_barrier_semaphore()
    for hop in hops:
        for bits in hop:
            pl.semaphore_signal(
                barrier, inc=1, device_id=partner(bits), device_id_type=pl.DeviceIdType.MESH
            )
    pl.semaphore_wait(barrier, sum(len(hop) for hop in hops))

    def body(piece, lane, gradient, master, first, second):
        pre = adam_step(master, first, second, gradient, RATE_MATRIX)[0]
        row, start = piece[4:]
        lanes = pl.ds(pl.multiple_of(start + lane, LANES), LANES)
        sums[0, row : row + 1, lanes] = jnp.sum(pre * pre, axis=0, keepdims=True)

    for_update_tiles(loads, held_grads, held_states, body)
    for number, hop in enumerate(hops):
        copies = [
            pltpu.make_async_remote_copy(
                src_ref=sums.at[number],
                dst_ref=arrived.at[number, k],
                send_sem=send_sem.at[number, k],
                recv_sem=recv_sem.at[number, k],
                device_id=partner(bits),
                device_id_type=pl.DeviceIdType.MESH,
            )
            for k, bits in enumerate(hop)
        ]
        for copy in copies:
            copy.start()
        for copy in copies:
            copy.wait()
        if len(hop) == 3:
            result = (sums[number] + arrived[number, 0]) + (
                arrived[number, 1] + arrived[number, 2]
            )
        else:
            result = sums[number] + arrived[number, 0]
        if number + 1 < len(hops):
            sums[number + 1] = result
        else:
            total[...] = result


def update_kernel(*refs):
    grads, states, squares, small, outputs = refs[0], refs[1:13], refs[13], refs[14:21], refs[21:39]
    held_grads, held_states, held_results, load_sem, store_sem = refs[39:]
    results, small_results = outputs[:12], outputs[12:]
    loads = update_loads(grads, states, held_grads, held_states, load_sem)
    for load in loads:
        load.start()

    def store(k):
        return pltpu.make_async_copy(held_results[k], results[k], store_sem.at[k])

    for k, rate in enumerate((RATE_ALPHA, RATE_SCALE)):
        master, first, second = [ref[...] for ref in small[3 * k + 1 : 3 * k + 4]]
        gradient = small[0][...][2 * k : 2 * k + master.shape[0]]
        updated, variance = adam_step(master, first, second, gradient, rate)
        for target, value in zip(small_results[3 * k : 3 * k + 3], (gradient, variance, updated)):
            target[...] = value

    def body(piece, lane, gradient, master, first, second):
        _, _, which, block, row, start = piece
        pre, variance = adam_step(master, first, second, gradient, RATE_MATRIX)
        lanes = pl.ds(pl.multiple_of(start + lane, LANES), LANES)
        factor = lax.rsqrt(squares[row : row + 1, lanes] / D + EPS_NORM)
        here = pl.ds(lane, LANES)
        for target, value in zip(
            held_results[3 * which : 3 * which + 3], (gradient, variance, pre * factor)
        ):
            if block is None:
                target[:, here] = value
            else:
                target[block, :, here] = value

    def after(which):
        for k in range(3 * which, 3 * which + 3):
            store(k).start()

    for_update_tiles(loads, held_grads, held_states, body, after)
    for k in range(12):
        store(k).wait()


def update(grads, states, small, squares, count, collective_id):
    rows = grads.shape[0]
    units = unit_tiles() * LANES
    shape = (SQUARE_ROWS, units)
    hbm = pl.BlockSpec(memory_space=pl.ANY)
    vmem = pl.BlockSpec(memory_space=pltpu.VMEM)
    dma = pltpu.SemaphoreType.DMA
    held = [pltpu.VMEM(grads.shape, F32), [pltpu.VMEM(state.shape, state.dtype) for state in states]]
    if squares is None:
        squares = pl.pallas_call(
            squares_kernel,
            out_shape=jax.ShapeDtypeStruct(shape, F32),
            in_specs=[hbm] * 13,
            out_specs=vmem,
            scratch_shapes=held
            + [
                pltpu.VMEM((3, *shape), F32),
                pltpu.VMEM((3, 3, *shape), F32),
                dma((16,)),
                dma((3, 3)),
                dma((3, 3)),
            ],
            compiler_params=pltpu.CompilerParams(
                collective_id=collective_id, has_side_effects=True, vmem_limit_bytes=60 << 20
            ),
            name="sum_squares",
        )(grads, *states)
        for bit in extra_bits(count):
            squares = squares + exchange(squares, bit, count)
    results = [
        jax.ShapeDtypeStruct(states[3 * k].shape, F32) for k in range(4) for _ in range(3)
    ]
    small_results = [
        jax.ShapeDtypeStruct(small[3 * k + 1].shape, F32) for k in range(2) for _ in range(3)
    ]
    return pl.pallas_call(
        update_kernel,
        out_shape=results + small_results,
        in_specs=[hbm] * 13 + [vmem] * 8,
        out_specs=[hbm] * 12 + [vmem] * 6,
        scratch_shapes=held
        + [[pltpu.VMEM(result.shape, F32) for result in results], dma((16,)), dma((12,))],
        compiler_params=pltpu.CompilerParams(vmem_limit_bytes=60 << 20),
        name="update",
    )(grads, *states, squares, *small)


def per_device(
    tokens,
    cotangent,
    segment_ids,
    pad_mask,
    inward_master,
    inward_first,
    inward_second,
    outward_master,
    outward_first,
    outward_second,
    expand_master,
    expand_first,
    expand_second,
    shrink_master,
    shrink_first,
    shrink_second,
    alpha_master,
    alpha_first,
    alpha_second,
    scale_master,
    scale_first,
    scale_second,
):
    count = lax.axis_size("dp")
    me = lax.axis_index("dp")
    heads_width = inward_master.shape[2]

    small = jnp.concatenate([alpha_master, scale_master], axis=0).astype(BF16)
    small = jnp.pad(small, ((0, LANES - small.shape[0]), (0, 0))).T
    masters = (
        inward_master,
        outward_master.T,
        expand_master,
        shrink_master.T,
        small,
    )
    if extra_bits(count):
        masters = [gather_rest(master.astype(BF16), count) for master in masters]
    place_row = jnp.asarray(place_rows_of(count))
    (
        copies,
        tokens_in,
        raw,
        mixed,
        h_attn,
        first,
        first_low,
        tokens_turned,
        first_turned,
        bias,
        d_two,
        output,
        d_shrunk,
        d_shrunk_turned,
        proj,
        hidden,
        factors,
        alphas,
        scale_rows,
        gains,
        alpha_mlp_grad,
    ) = forward_pass(
        *masters, tokens, cotangent, segment_ids, pad_mask, place_row, collective_id=0
    )

    states = (
        inward_master,
        inward_first,
        inward_second,
        outward_master.T,
        outward_first.T,
        outward_second.T,
        expand_master,
        expand_first,
        expand_second,
        shrink_master.T,
        shrink_first.T,
        shrink_second.T,
    )

    input_grad, block_output, grads, vectors, *squares = backward_pass(
        copies.reshape(D, -1),
        d_shrunk,
        d_shrunk_turned,
        first_turned,
        tokens_turned,
        hidden,
        proj,
        raw,
        mixed,
        d_two,
        h_attn,
        first,
        tokens_in,
        factors,
        alphas,
        scale_rows,
        gains,
        alpha_mlp_grad,
        bias,
        place_row,
        output,
        states=() if extra_bits(count) else states,
        collective_id=1,
    )
    grads = scatter_rest(grads, count)
    for bit in extra_bits(count):
        vectors = vectors + exchange(vectors, bit, count)
    width = D // count
    vectors = lax.dynamic_slice_in_dim(vectors, me * width, width, 1)

    small = (
        vectors,
        alpha_master,
        alpha_first,
        alpha_second,
        scale_master,
        scale_first,
        scale_second,
    )
    results = list(update(grads, states, small, squares[0] if squares else None, count, 2))
    for k in (*range(3, 6), *range(9, 12)):
        results[k] = results[k].T
    return block_output, input_grad, *results


def solution(mesh):
    rows = P("dp", None)
    deep = P(None, "dp", "tensor")
    flat = P("tensor", "dp")
    vector = P(None, "dp")
    in_specs = (rows,) * 4 + (deep,) * 3 + (flat,) * 3 + (deep,) * 3 + (flat,) * 3 + (vector,) * 6
    out_specs = (
        (rows, P("dp", "tensor"))
        + (deep,) * 3
        + (flat,) * 3
        + (deep,) * 3
        + (flat,) * 3
        + (vector,) * 6
    )
    return jax.shard_map(
        per_device, mesh=mesh, in_specs=in_specs, out_specs=out_specs, check_vma=False
    )
```

```python
import functools

import jax
import jax.numpy as jnp
import numpy as np
from jax import lax
from jax.experimental import pallas as pl
from jax.experimental.pallas import tpu as pltpu
from jax.sharding import PartitionSpec as P

D = 1280
HEADS = 20
HD = 64
FF = 5120
STEP = 10
LONGEST = 256


EPS_NORM = 1e-06
BETA_ONE = 0.9
BETA_TWO = 0.95
ADAM_EPS = 1e-08
RATE_MATRIX = 0.3
RATE_ALPHA = 0.08
RATE_SCALE = 0.25
MASKED = -1e30
F32 = jnp.float32
BF16 = jnp.bfloat16


def row_norm(values):
    factor = lax.rsqrt(jnp.mean(values * values, axis=-1, keepdims=True) + EPS_NORM)
    return (values * factor, factor)


def row_norm_back(upstream, normed, factor):
    return factor * (upstream - normed * jnp.mean(upstream * normed, axis=-1, keepdims=True))


def adam_step(master, first_moment, second_moment, gradient, rate):
    first_new = BETA_ONE * first_moment.astype(F32) + (1.0 - BETA_ONE) * gradient
    second_new = BETA_TWO * second_moment + (1.0 - BETA_TWO) * gradient * gradient
    root = jnp.sqrt(second_new * (1.0 / (1.0 - BETA_TWO**STEP)))
    ratio = first_new * (rate / (1.0 - BETA_ONE**STEP)) / (root + ADAM_EPS)
    return (master - ratio, second_new)


LANES = 128
PLACES = (2, 1, 4, 8)
ROUTES = ((3, 2, 1, 0), (3, 2, 0, 1), (1, 0, 3, 2), (0, 1, 3, 2))
EVERY = 4
LAG = 2
RING = 4


def partner_of(me, bit):
    return me + bit - 2 * bit * ((me // bit) % 2)


def partner_across(me, bits):
    device = me
    for bit in bits:
        device = device + partner_of(me, bit) - me
    return {"dp": device}


ROUNDS = (
    ((PLACES[0],), (PLACES[1],), (PLACES[0], PLACES[1])),
    ((PLACES[2],), (PLACES[3],), (PLACES[2], PLACES[3])),
)


def round_copies(me, number, sums, arrived, send_sem, recv_sem):
    return [
        pltpu.make_async_remote_copy(
            src_ref=sums.at[number],
            dst_ref=arrived.at[number, k],
            send_sem=send_sem.at[number, k],
            recv_sem=recv_sem.at[number, k],
            device_id=partner_across(me, bits),
            device_id_type=pl.DeviceIdType.MESH,
        )
        for k, bits in enumerate(ROUNDS[number])
    ]


def round_start(*parts):
    for copy in round_copies(*parts):
        copy.start()


def round_sum(me, number, sums, arrived, send_sem, recv_sem):
    for copy in round_copies(me, number, sums, arrived, send_sem, recv_sem):
        copy.wait()
    total = sums[number] + arrived[number, 0]
    for k in range(1, len(ROUNDS[number])):
        total = total + arrived[number, k]
    return total


def greet_start(me, core=None, diagonal=False):
    barrier = pltpu.get_barrier_semaphore()
    partners = [{"dp": partner_of(me, bit)} for bit in PLACES]
    if diagonal:
        partners += [partner_across(me, PLACES[:2]), partner_across(me, PLACES[2:])]
    if core is not None:
        partners.append({"tensor": 1 - core})
    for partner in partners:
        pl.semaphore_signal(
            barrier, inc=1, device_id=partner, device_id_type=pl.DeviceIdType.MESH
        )
    return len(partners)


def greet_wait(number):
    pl.semaphore_wait(pltpu.get_barrier_semaphore(), number)


def tile_plan(columns):
    tiles = columns // LANES
    rare = tiles // 10
    often = (tiles - 2 * rare) // 2
    return (
        (0, 2, often, 1, 0),
        (1, 2, often, 1, 0),
        (2 * often, 1, rare, EVERY, 0),
        (2 * often + rare, 1, rare, EVERY, EVERY // 2),
    )


def for_tiles(step, hop, plan, body):
    for route, (_, _, number, every, start) in enumerate(plan):
        at = step - hop * LAG - start
        due = (at >= 0) & (at < number * every)
        if every > 1:
            due = due & (at % every == 0)

        @pl.when(due)
        def _():
            body(route, at // every)


def lanes_of(plan, route, tile):
    first, stride = plan[route][:2]
    return pl.ds(pl.multiple_of((first + stride * tile) * LANES, LANES), LANES)


def steps_of(plan, hops):
    return max(start + (number - 1) * every + 1 for _, _, number, every, start in plan) + hops * LAG


def extra_bits(count):
    return [bit for bit in (1 << k for k in range(4, count.bit_length() - 1))]


def exchange(array, bit, count):
    return lax.ppermute(array, "dp", [(i, i ^ bit) for i in range(count)])


def gather_rest(block, count):
    for bit in extra_bits(count)[::-1]:
        block = jnp.concatenate([block, exchange(block, bit, count)], axis=-2)
    return block


def scatter_rest(partial, count):
    for bit in extra_bits(count):
        half = partial.shape[0] // 2
        partial = partial[:half] + exchange(partial[half:], bit, count)
    return partial


def place_rows_of(count):
    places = list(PLACES) + extra_bits(count)
    width = D // count
    placed = np.arange(D, dtype=np.int32)
    position, offset = placed // width, placed % width
    relative = np.zeros_like(position)
    for axis, bit in enumerate(places):
        relative = relative + ((position >> (len(places) - 1 - axis)) & 1) * bit
    return np.stack([relative, offset])


def natural_row(place_row, me):
    count = lax.axis_size("dp")
    return (place_row[0:1, :] ^ me) * (D // count) + place_row[1:2, :]


def nn(a, b):
    return lax.dot_general(a, b, (((1,), (0,)), ((), ())), preferred_element_type=F32)


def nt(a, b):
    return lax.dot_general(a, b, (((1,), (1,)), ((), ())), preferred_element_type=F32)


def tn(a, b):
    return lax.dot_general(a, b, (((0,), (0,)), ((), ())), preferred_element_type=F32)


def head_factors(raw, low_lanes):
    squares = raw * raw
    low = jnp.sum(jnp.where(low_lanes, squares, 0.0), axis=-1, keepdims=True)
    high = jnp.sum(jnp.where(low_lanes, 0.0, squares), axis=-1, keepdims=True)
    return jnp.where(low_lanes, lax.rsqrt(low + EPS_NORM), lax.rsqrt(high + EPS_NORM))


def head_sums(values, low_lanes):
    low = jnp.sum(jnp.where(low_lanes, values, 0.0), axis=-1, keepdims=True)
    high = jnp.sum(jnp.where(low_lanes, 0.0, values), axis=-1, keepdims=True)
    return jnp.where(low_lanes, low, high)


Q_TILE = 128


def key_range(tile):
    start = max(0, tile * Q_TILE - LONGEST)
    return start, (tile + 1) * Q_TILE


def attend_pair(query, key, value, gain, bias, mixed):
    length = query.shape[0]
    low_lanes = lax.broadcasted_iota(jnp.int32, (1, 2 * HD), 1) < HD
    query = (gain * (query * head_factors(query, low_lanes))).astype(BF16) * 8
    key = (gain * (key * head_factors(key, low_lanes))).astype(BF16)
    value = value.astype(BF16)
    zero = jnp.zeros_like(query)
    parts = (jnp.where(low_lanes, query, zero), jnp.where(low_lanes, zero, query))
    for tile in range(length // Q_TILE):
        start, end = key_range(tile)
        rows = slice(tile * Q_TILE, (tile + 1) * Q_TILE)
        tile_bias = bias[rows, start:end]
        results = []
        for part in parts:
            expo = jnp.exp(nt(part[rows], key[start:end]) + tile_bias)
            total = jnp.sum(expo, axis=-1, keepdims=True)
            results.append(nn(expo.astype(BF16), value[start:end]) * (1.0 / total))
        mixed[rows, :] = jnp.where(low_lanes, results[0], results[1]).astype(BF16)


def attend_pair_back(
    raw_q, raw_k, raw_v, d_mixed, gains, bias, d_raw_q, d_raw_k, d_raw_v, sum_k, sum_v
):
    length = raw_q.shape[0]
    low_lanes = lax.broadcasted_iota(jnp.int32, (1, 2 * HD), 1) < HD
    low_rows = lax.broadcasted_iota(jnp.int32, (2 * HD, 1), 0) < HD
    key_raw = raw_k[...]
    key_factor = head_factors(key_raw, low_lanes)
    key_unit = key_raw * key_factor
    key = (gains * key_unit).astype(BF16)
    key_eight = ((gains * key_unit).astype(BF16).astype(F32) * 8.0).T.astype(BF16)
    value = raw_v[...].astype(BF16)
    sum_k[...] = jnp.zeros_like(sum_k)
    sum_v[...] = jnp.zeros_like(sum_v)
    gain_total = jnp.zeros((1, 2 * HD), F32)

    def back(upstream, unit, factor):
        scaled = gains * upstream
        return (factor * (scaled - unit * head_sums(scaled * unit, low_lanes))).astype(BF16)

    for tile in range(length // Q_TILE):
        start, end = key_range(tile)
        rows = slice(tile * Q_TILE, (tile + 1) * Q_TILE)
        query_raw = raw_q[rows, :]
        query_factor = head_factors(query_raw, low_lanes)
        query_unit = query_raw * query_factor
        query = (gains * query_unit).astype(BF16) * 8
        upstream = d_mixed[rows]
        tile_bias = bias[start:end, rows]
        d_query = []
        for low in (True, False):
            lanes = low_lanes if low else jnp.logical_not(low_lanes)
            own_query = jnp.where(lanes, query, jnp.zeros_like(query))
            own_up = jnp.where(lanes, upstream, jnp.zeros_like(upstream))
            expo = jnp.exp(nt(key[start:end], own_query) + tile_bias)
            probs = expo * (1.0 / jnp.sum(expo, axis=0, keepdims=True))
            d_probs = nt(value[start:end], own_up)
            delta = jnp.sum(probs * d_probs, axis=0, keepdims=True)
            d_scores = (probs * (d_probs - delta)).astype(BF16)
            sum_v[start:end, :] += nn(probs.astype(BF16), own_up)
            sum_k[start:end, :] += nn(d_scores, own_query)
            d_query.append(nn(key_eight[:, start:end], d_scores))
        d_query = jnp.where(low_rows, d_query[0], d_query[1]).T
        gain_total += jnp.sum(d_query * query_unit, axis=0, keepdims=True)
        d_raw_q[rows, :] = back(d_query, query_unit, query_factor)
    d_key = sum_k[...]
    gain_total += jnp.sum(d_key * key_unit, axis=0, keepdims=True)
    d_raw_k[...] = back(d_key, key_unit, key_factor)
    d_raw_v[...] = sum_v[...].astype(BF16)
    return gain_total


ARRIVE = 4 * LAG
UNIT_GROUP = 4
FIRST_UNIT_PAIR = 8
RARE_UNITS = 3


def head_tiles():
    return HEADS * HD // 2 // LANES


def unit_tiles():
    return FF // 2 // LANES


def forward_plan():
    groups = unit_tiles() // UNIT_GROUP
    return tile_plan((2 * (FIRST_UNIT_PAIR + 5 * groups) + 2 * (RARE_UNITS + groups)) * LANES)


def pair_tile(unit):
    return 2 * (FIRST_UNIT_PAIR + 5 * (unit // UNIT_GROUP) + unit % UNIT_GROUP)


def shrink_tile_static(unit):
    plan = forward_plan()
    group, place = unit // UNIT_GROUP, unit % UNIT_GROUP
    if place < 2:
        return plan[2][0] + place * plan[2][2] + RARE_UNITS + group
    return 2 * (FIRST_UNIT_PAIR + 5 * group + UNIT_GROUP) + place - 2


def shrink_tile(unit):
    plan = forward_plan()
    group, place = unit // UNIT_GROUP, unit % UNIT_GROUP
    rare = plan[2][0] + place * plan[2][2] + RARE_UNITS + group
    often = 2 * (FIRST_UNIT_PAIR + 5 * group + UNIT_GROUP) + place - 2
    return jnp.where(place < 2, rare, often)


def forward_sources():
    plan = forward_plan()
    heads, units = head_tiles(), unit_tiles()
    rare, rarer = plan[2][0], plan[3][0]
    inward = [("inward", k // heads, k % heads) for k in range(3 * heads)]
    sources = dict(enumerate(inward[:-1]))
    sources[rare] = inward[-1]
    sources[rarer] = ("small", None, 0)
    for tile, place in ((rare + 1, 0), (rarer + 1, 1), (3 * heads - 1, 2), (3 * heads, 3), (rare + 2, 4)):
        sources[tile] = ("outward", None, place)
    for unit in range(units):
        sources[pair_tile(unit)] = ("expand", 0, unit)
        sources[pair_tile(unit) + 1] = ("expand", 1, unit)
        sources[shrink_tile_static(unit)] = ("shrink", None, unit)
    return sources


def shrink_tile_static(unit):
    plan = forward_plan()
    group, place = unit // UNIT_GROUP, unit % UNIT_GROUP
    if place < 2:
        return plan[2][0] + place * plan[2][2] + RARE_UNITS + group
    return 2 * (FIRST_UNIT_PAIR + 5 * group + UNIT_GROUP) + place - 2


def forward_kernel(
    plan,
    inward,
    outward,
    expand,
    shrink,
    small_copies,
    tokens,
    cotangent,
    segments,
    pads,
    place_row,
    out,
    tokens_out,
    raw_out,
    mixed_out,
    h_attn_out,
    first_out,
    first_low_out,
    tokens_turned_out,
    first_turned_out,
    bias_out,
    d_two_out,
    output_out,
    d_shrunk_out,
    d_shrunk_turned_out,
    proj_out,
    hidden_out,
    factors,
    alphas,
    scales,
    gains,
    alpha_grad,
    block,
    shrunk,
    place,
    tokens_in,
    cot_in,
    bias,
    turned_bias,
    raw,
    stage_pair,
    stage_one,
    stage_outward,
    mixed,
    branch_in,
    h_attn,
    first,
    first_low,
    stage_proj,
    stage_hidden,
    keep,
    own_sem,
    send_sem,
    recv_sem,
    pair_sem,
    one_sem,
    outward_sem,
    proj_sem,
    hidden_sem,
    result_sem,
    core_send,
    core_recv,
):
    me = lax.axis_index("dp")
    core = lax.axis_index("tensor")
    inv_root = D ** (-0.5)
    rows = tokens.shape[0]
    own_rows = rows // 2
    own_at = pl.multiple_of(core * own_rows, own_rows)
    other_at = pl.multiple_of((1 - core) * own_rows, own_rows)
    heads = head_tiles()
    units = unit_tiles()
    attend_at = 3 * heads // 2 + ARRIVE + 1
    pairs_each = 2
    sequences, length = segments.shape
    head_pairs = sequences * heads
    branch_at = attend_at + -(-head_pairs // pairs_each)
    units_at = branch_at + 2

    greeted = greet_start(me, core)
    cot_copy = pltpu.make_async_copy(cotangent.at[pl.ds(own_at, own_rows)], cot_in, result_sem.at[13])
    cot_copy.start()
    operands = {
        "inward": inward,
        "outward": outward,
        "expand": expand,
        "shrink": shrink,
        "small": small_copies,
    }
    for tile, (name, row_block, at) in forward_sources().items():
        source = operands[name] if row_block is None else operands[name].at[row_block]
        block[:, tile * LANES : (tile + 1) * LANES] = source[
            :, at * LANES : (at + 1) * LANES
        ].astype(BF16)
    unused = plan[3][0] + 2
    block[:, unused * LANES : (unused + 1) * LANES] = jnp.zeros((block.shape[0], LANES), BF16)
    own = pltpu.make_async_copy(block, out.at[0, 0, 0, 0], own_sem)
    own.start()
    greet_wait(greeted)

    def piece(hop, route, tile):
        lanes = lanes_of(plan, route, tile)
        crossed, axis = ROUTES[route][:hop], ROUTES[route][hop]
        source = [slice(None) if k in crossed else 0 for k in range(4)]
        target = [1 if k == axis else source[k] for k in range(4)]
        if hop == 0:
            source_ref = block.at[:, lanes]
        else:
            source_ref = out.at[(*source, slice(None), lanes)]
        return pltpu.make_async_remote_copy(
            src_ref=source_ref,
            dst_ref=out.at[(*target, slice(None), lanes)],
            send_sem=send_sem.at[hop, route, tile % RING],
            recv_sem=recv_sem.at[hop, route, tile],
            device_id={"dp": partner_of(me, PLACES[axis])},
            device_id_type=pl.DeviceIdType.MESH,
        )

    def forward_hop(hop, route, tile):
        if hop > 0:
            piece(hop - 1, route, tile).wait_recv()
        if hop < 4:

            @pl.when(tile >= RING)
            def _():
                piece(hop, route, tile - RING).wait_send()

            piece(hop, route, tile).start()

    def staged(tile, width, target, sem):
        lanes = pl.ds(pl.multiple_of(tile * LANES, LANES), width * LANES)
        return pltpu.make_async_copy(out.at[:, :, :, :, :, lanes], target, sem)

    def lanes_half(number):
        return pl.ds(pl.multiple_of((number % 2) * LANES, LANES), LANES)

    def pair_copy(tile, slot):
        return staged(tile, 2, stage_pair.at[slot], pair_sem.at[slot])

    def one_copy(tile, number):
        target = stage_one.at[(number // 2) % 2, :, :, :, :, :, lanes_half(number)]
        return staged(tile, 1, target, one_sem.at[number % 4])

    rare = plan[2][0]
    rarer = plan[3][0]

    def outward_copies():
        return [
            staged(tile, width, stage_outward.at[:, :, :, :, :, pl.ds(at * LANES, width * LANES)], outward_sem.at[k])
            for k, (tile, width, at) in enumerate(
                ((rare + 1, 1, 0), (rarer + 1, 1, 1), (3 * heads - 1, 2, 2), (rare + 2, 1, 4))
            )
        ]

    def core_copy(source, target, which):
        return pltpu.make_async_remote_copy(
            src_ref=source,
            dst_ref=target,
            send_sem=core_send.at[which],
            recv_sem=core_recv.at[which],
            device_id={"tensor": 1 - core},
            device_id_type=pl.DeviceIdType.MESH,
        )

    def branch_copy():
        return core_copy(shrunk.at[pl.ds(0, own_rows)], branch_in, 0)

    def first_copy():
        return core_copy(
            first_low.at[pl.ds(own_at, own_rows)], first_low.at[pl.ds(own_at, own_rows)], 1
        )

    half_rows = own_rows // 2

    def shrunk_copy(k):
        at = pl.ds(pl.multiple_of(other_at + k * half_rows, half_rows), half_rows)
        return core_copy(tokens_in.at[at], tokens_in.at[at], 2 + k)

    def d_shrunk_copy(k):
        at = pl.ds(pl.multiple_of(own_at + k * half_rows, half_rows), half_rows)
        return core_copy(first_low.at[at], first_low.at[at], 4 + k)

    result_pairs = (
        (tokens_in, tokens_out),
        (raw, raw_out),
        (mixed, mixed_out),
        (h_attn, h_attn_out),
        (first, first_out),
        (first_low, first_low_out),
        (place.at[:, pl.ds(0, rows)], tokens_turned_out),
        (place.at[:, pl.ds(0, rows)], first_turned_out),
        (turned_bias, bias_out),
        (h_attn, d_two_out),
        (tokens_in.at[pl.ds(own_at, own_rows)], output_out),
        (first_low, d_shrunk_out),
        (place.at[:, pl.ds(0, rows)], d_shrunk_turned_out),
    )

    def result(k):
        return pltpu.make_async_copy(*result_pairs[k], result_sem.at[k])

    def chunks(total, size, body):
        def one(k, _):
            body(pl.ds(pl.multiple_of(k * size, size), size))
            return 0

        lax.fori_loop(0, total // size, one, 0)

    def make_order():
        natural = natural_row(place_row, me)

        def fill(at):
            here = lax.broadcasted_iota(jnp.int32, (LANES, D), 0) + at.start
            place[at, :] = jnp.where(here == natural, 1.0, 0.0).astype(BF16)

        chunks(D, LANES, fill)

    def tokens_in_order(number):
        at = pl.ds(pl.multiple_of(number * 256, 256), 256)
        tokens_in[at, :] = nn(tokens[at, :], place[...]).astype(BF16)

    def cot_in_order():
        cot_copy.wait()

        def move(at):
            cot_in[at, :] = nn(cot_in[at, :], place[...]).astype(BF16)

        chunks(own_rows, 256, move)

    def column_of(row):
        return jnp.broadcast_to(row.astype(F32), (LANES, length)).T

    def make_bias():
        for sequence in range(sequences):
            segment = segments[sequence : sequence + 1, :]
            pad = pads[sequence : sequence + 1, :]
            own_segment = column_of(segment)
            for tile in range(length // LANES):
                lanes = slice(tile * LANES, (tile + 1) * LANES)
                query = lax.broadcasted_iota(jnp.int32, (length, LANES), 0)
                key = lax.broadcasted_iota(jnp.int32, (length, LANES), 1) + tile * LANES
                open_key = jnp.where(pad[:, lanes] == 0, segment[:, lanes], -1).astype(F32)
                allowed = ((own_segment == open_key) & (key <= query)) | (key == query)
                values = jnp.where(allowed, 0.0, MASKED)
                bias[sequence, :, lanes] = values
                turned_bias[sequence, lanes, :] = values.T
        result(8).start()
        keep[...] = jnp.where(core == 0, column_of(1 - pads[0:1, :]), column_of(1 - pads[1:2, :]))

    def finish():
        alpha = alphas[1:2, :]
        alpha_grad[...] = jnp.zeros_like(alpha_grad)

        def some(at):
            here = pl.ds(pl.multiple_of(own_at + at.start, 64), 64)
            normed, factor = row_norm(shrunk[here, :] + tokens_in[here, :].astype(F32))
            start = first[at, :]
            output, output_factor = row_norm(start + alpha * (normed - start))
            upstream = cot_in[at, :].astype(F32) * keep[at, 0:1]
            d_two = row_norm_back(upstream, output, output_factor)
            alpha_grad[0:1, :] += jnp.sum(d_two * (normed - start), axis=0, keepdims=True)
            h_attn[at, :] = d_two
            tokens_in[here, :] = output.astype(BF16)
            first_low[here, :] = row_norm_back(alpha * d_two, normed, factor).astype(BF16)

        for k in range(2):
            shrunk_copy(k).wait()
            span(k, 64, 0, some)
            d_shrunk_copy(k).start()
        result(9).start()
        result(10).start()
        for k in range(2):
            span(k, LANES, own_at, lambda at: turn_rows(first_low, at))
        for k in range(2):
            d_shrunk_copy(k).wait()
            span(k, LANES, other_at, lambda at: turn_rows(first_low, at))
        result(12).start()
        result(11).start()
        for k in (9, 10, 11, 12):
            result(k).wait()

    def turn_rows(source, at):
        place[:, at] = source[at, :].astype(F32).T.astype(BF16)

    def turn(source):
        chunks(rows, LANES, functools.partial(turn_rows, source))

    def project(weights, lanes):
        def some(at):
            raw[at, lanes] = nn(tokens_in[at, :], weights) * inv_root

        chunks(rows, 256, some)

    def small_vectors():
        small = stage_one[0, :, :, :, :, :, LANES:].reshape(D, LANES).astype(F32).T
        alphas[...] = small[: alphas.shape[0]]
        scales[...] = nt(small.astype(BF16), place[...])[: scales.shape[0]]
        each = units * LANES // D
        for row in range(2):
            for k in range(each):
                at = 3 + row * 2 * each + k
                gains[row : row + 1, k * D : (k + 1) * D] = jnp.where(
                    core == 0, scales[at : at + 1, :], scales[at + each : at + each + 1, :]
                )

    def attend_one(number):
        sequence, head = number // heads, number % heads
        at = pl.ds(pl.multiple_of(sequence * length, length), length)
        lanes = [
            pl.ds(pl.multiple_of((k * heads + head) * LANES, LANES), LANES) for k in range(3)
        ]
        gain_lanes = pl.ds(pl.multiple_of((core * heads + head) * LANES, LANES), LANES)
        attend_pair(
            raw[at, lanes[0]],
            raw[at, lanes[1]],
            raw[at, lanes[2]],
            scales[2:3, gain_lanes],
            bias.at[sequence],
            mixed.at[at, lanes[0]],
        )

    def branch():
        weights = stage_outward[...].reshape(D, heads * LANES)
        for target, source in ((0, other_at), (own_rows, own_at)):
            for k in range(2):
                half = own_rows // 2
                at = pl.ds(pl.multiple_of(source + k * half, half), half)
                shrunk[pl.ds(target + k * half, half), :] = nt(mixed[at, :], weights)
            if target == 0:
                branch_copy().start()

    def norms():
        branch_copy().wait()
        alpha = alphas[0:1, :]

        def some(at):
            total = shrunk[pl.ds(pl.multiple_of(own_rows + at.start, 64), 64), :] + branch_in[at, :]
            normed, factor = row_norm(total)
            here = pl.ds(pl.multiple_of(own_at + at.start, 64), 64)
            inputs = tokens_in[here, :].astype(F32)
            result, result_factor = row_norm(inputs + alpha * (normed - inputs))
            h_attn[at, :] = normed
            first[at, :] = result
            first_low[here, :] = result.astype(BF16)
            factors[at, :LANES] = jnp.broadcast_to(factor, (64, LANES))
            factors[at, LANES:] = jnp.broadcast_to(result_factor, (64, LANES))

        chunks(own_rows, 64, some)
        result(0).wait()
        first_copy().start()
        for k in (3, 4):
            result(k).start()

    def gain_of(unit, row):
        return gains[row : row + 1, pl.ds(pl.multiple_of(unit * LANES, LANES), LANES)]

    def proj_copy(unit):
        lanes = pl.ds(pl.multiple_of(unit * 2 * LANES, 2 * LANES), 2 * LANES)
        slot = unit % 2
        return pltpu.make_async_copy(stage_proj.at[slot], proj_out.at[:, lanes], proj_sem.at[slot])

    def hidden_copy(pair):
        lanes = pl.ds(pl.multiple_of(pair * 2 * LANES, 2 * LANES), 2 * LANES)
        slot = pair % 2
        return pltpu.make_async_copy(
            stage_hidden.at[slot], hidden_out.at[:, lanes], hidden_sem.at[slot]
        )

    def fetch_shrink(pair):
        for k in range(2):
            one_copy(shrink_tile(2 * pair + k), 2 * pair + k).start()

    def span(k, size, start, body):
        def one(j, _):
            body(pl.ds(pl.multiple_of(start + k * half_rows + j * size, size), size))
            return 0

        lax.fori_loop(0, half_rows // size, one, 0)

    def add_shrunk(pair):
        for k in range(2):
            one_copy(0, 2 * pair + k).wait()
        down = stage_one[pair % 2].reshape(D, 2 * LANES)
        for part, start in enumerate((other_at, own_at)):
            at = pl.ds(start, own_rows)
            values = stage_hidden[pair % 2, at, :]
            for k in range(D // 256):
                columns = slice(k * 256, (k + 1) * 256)
                shrunk[at, columns] += nt(values, down[columns])
            if part == 0:

                @pl.when(pair == units // 2 - 1)
                def _():
                    result(5).wait()
                    def lower(rows_at):
                        tokens_in[rows_at, :] = shrunk[rows_at, :].astype(BF16)

                    for k in range(2):
                        span(k, 64, other_at, lower)
                        shrunk_copy(k).start()

        hidden_copy(pair).start()

    def one_unit(unit):
        slot = unit % 2
        pair = unit // 2

        @pl.when(unit == 0)
        def _():
            first_copy().wait()
            result(5).start()
            shrunk[...] = jnp.zeros_like(shrunk)

        @pl.when(unit >= 2)
        def _():
            proj_copy(unit - 2).wait()

        @pl.when((unit >= 4) & (slot == 0))
        def _():
            hidden_copy(pair - 2).wait()

        pair_copy(0, slot).wait()
        weights = stage_pair[slot].reshape(D, 2 * LANES)
        gain_up = gain_of(unit, 0)
        gain_gate = gain_of(unit, 1)

        def some(at):
            proj = nn(first_low[at, :], weights) * inv_root
            stage_proj[slot, at, :] = proj
            gate = gain_gate * proj[:, LANES:]
            hidden = (gain_up * proj[:, :LANES] * (gate * jax.nn.sigmoid(gate))).astype(BF16)
            stage_hidden[pair % 2, at, lanes_half(unit)] = hidden

        chunks(rows, own_rows, some)
        proj_copy(unit).start()

    def step(index, _):
        for hop in range(5):
            for_tiles(index, hop, plan, functools.partial(forward_hop, hop))

        @pl.when(index == LAG - 1)
        def _():
            own.wait()

        order_at = ARRIVE - rows // 256

        @pl.when(index == order_at - 1)
        def _():
            make_order()

        @pl.when((index >= order_at) & (index < ARRIVE))
        def _():
            tokens_in_order(index - order_at)

        @pl.when(index == ARRIVE)
        def _():
            result(0).start()

        pair = index - ARRIVE

        @pl.when((pair >= 0) & (pair < 3 * heads // 2))
        def _():
            pair_copy(2 * pair, pair % 2).start()

        @pl.when(pair == 0)
        def _():
            one_copy(rare, 0).start()

        @pl.when(pair == EVERY // 2)
        def _():
            one_copy(rarer, 1).start()

        @pl.when((pair >= 1) & (pair <= 3 * heads // 2))
        def _():
            done = pair - 1
            pair_copy(0, done % 2).wait()
            lanes = pl.ds(pl.multiple_of(done * 2 * LANES, 2 * LANES), 2 * LANES)
            project(stage_pair[done % 2].reshape(D, 2 * LANES), lanes)

        @pl.when(pair == 1)
        def _():
            one_copy(0, 0).wait()
            weights = stage_one[0, :, :, :, :, :, :LANES].reshape(D, LANES)
            project(weights, pl.ds((3 * heads - 1) * LANES, LANES))

        @pl.when(pair == EVERY // 2 + 1)
        def _():
            one_copy(0, 1).wait()
            small_vectors()

        @pl.when(pair == 4)
        def _():
            cot_in_order()

        @pl.when(pair == 5)
        def _():
            make_bias()

        @pl.when(pair == 6)
        def _():
            turn(tokens_in)
            result(6).start()

        @pl.when(index == units_at + 1)
        def _():
            result(6).wait()
            turn(first_low)
            result(7).start()

        @pl.when(index == attend_at)
        def _():
            result(1).start()
            for copy in outward_copies():
                copy.start()

        @pl.when((index >= attend_at) & (index < branch_at))
        def _():
            for k in range(pairs_each):
                attend_one((index - attend_at) * pairs_each + k)

        @pl.when(index == branch_at)
        def _():
            result(2).start()
            for copy in outward_copies():
                copy.wait()
            branch()

        @pl.when(index == branch_at + 1)
        def _():
            norms()

        due = index - units_at

        @pl.when(due == -1)
        def _():
            pair_copy(pair_tile(0), 0).start()

        for k in range(2):
            early = 2 * due - 1 + k
            unit = jnp.where(due <= 2, early, due + 2) if k == 1 else early

            @pl.when((due >= 0) & (unit >= 0) & (unit < units) & ((due <= 2) | (k == 1)))
            def _(unit=unit):
                @pl.when(unit + 1 < units)
                def _():
                    pair_copy(pair_tile(unit + 1), (unit + 1) % 2).start()

                one_unit(unit)

        down_at = due - 1
        for k in range(2):

            @pl.when((down_at >= k - 1) & ((down_at + 1 - k) % 4 == 0) & (down_at - k < units - 1))
            def _(k=k):
                fetch_shrink((down_at + 1 - k) // 2 + k)

            @pl.when((down_at >= k) & ((down_at - k) % 4 == 0) & (down_at - k < units))
            def _(k=k):
                add_shrunk((down_at - k) // 2 + k)

        return 0

    lax.fori_loop(0, max(steps_of(plan, 4), units_at + units - 1), step, 0)
    for unit in (units - 2, units - 1):
        proj_copy(unit).wait()
    for pair in (units // 2 - 2, units // 2 - 1):
        hidden_copy(pair).wait()
    for k in (1, 2, 3, 4, 7, 8):
        result(k).wait()
    finish()
    for route, (_, _, number, _, _) in enumerate(plan):
        for tile in range(max(0, number - RING), number):
            for hop in range(4):
                piece(hop, route, tile).wait_send()


def forward_pass(*operands, collective_id):
    plan = forward_plan()
    rows = operands[1].shape[0]
    count = operands[5].shape[0]
    sequences, length = operands[7].shape
    columns = sum(entry[2] for entry in plan) * LANES
    own = count // 2
    heads = head_tiles() * LANES
    units = unit_tiles() * LANES
    most = max(entry[2] for entry in plan)
    place = (2, 2, 2, 2, rows)
    hbm = pl.BlockSpec(memory_space=pl.ANY)
    vmem = pl.BlockSpec(memory_space=pltpu.VMEM)
    dma = pltpu.SemaphoreType.DMA
    return pl.pallas_call(
        functools.partial(forward_kernel, plan),
        out_shape=[
            jax.ShapeDtypeStruct((*place, columns), BF16),
            jax.ShapeDtypeStruct((count, D), BF16),
            jax.ShapeDtypeStruct((count, 3 * heads), F32),
            jax.ShapeDtypeStruct((count, heads), BF16),
            jax.ShapeDtypeStruct((own, D), F32),
            jax.ShapeDtypeStruct((own, D), F32),
            jax.ShapeDtypeStruct((count, D), BF16),
            jax.ShapeDtypeStruct((D, count), BF16),
            jax.ShapeDtypeStruct((D, count), BF16),
            jax.ShapeDtypeStruct((sequences, length, length), F32),
            jax.ShapeDtypeStruct((own, D), F32),
            jax.ShapeDtypeStruct((own, D), BF16),
            jax.ShapeDtypeStruct((count, D), BF16),
            jax.ShapeDtypeStruct((D, count), BF16),
            jax.ShapeDtypeStruct((count, 2 * units), F32),
            jax.ShapeDtypeStruct((count, units), BF16),
            jax.ShapeDtypeStruct((own, 2 * LANES), F32),
            jax.ShapeDtypeStruct((8, D), F32),
            jax.ShapeDtypeStruct((16, D), F32),
            jax.ShapeDtypeStruct((8, units), F32),
            jax.ShapeDtypeStruct((8, D), F32),
        ],
        in_specs=[vmem] * 6 + [hbm] + [vmem] * 3,
        out_specs=[hbm] * 16 + [vmem] * 5,
        scratch_shapes=[
            pltpu.VMEM((rows, columns), BF16),
            pltpu.VMEM((count, D), F32),
            pltpu.VMEM((D, D), BF16),
            pltpu.VMEM((count, D), BF16),
            pltpu.VMEM((own, D), BF16),
            pltpu.VMEM((sequences, length, length), F32),
            pltpu.VMEM((sequences, length, length), F32),
            pltpu.VMEM((count, 3 * heads), F32),
            pltpu.VMEM((2, *place, 2 * LANES), BF16),
            pltpu.VMEM((2, *place, 2 * LANES), BF16),
            pltpu.VMEM((*place, heads), BF16),
            pltpu.VMEM((count, heads), BF16),
            pltpu.VMEM((own, D), F32),
            pltpu.VMEM((own, D), F32),
            pltpu.VMEM((own, D), F32),
            pltpu.VMEM((count, D), BF16),
            pltpu.VMEM((2, count, 2 * LANES), F32),
            pltpu.VMEM((2, count, 2 * LANES), BF16),
            pltpu.VMEM((own, LANES), F32),
            dma,
            dma((4, 4, RING)),
            dma((4, 4, most)),
            dma((2,)),
            dma((4,)),
            dma((4,)),
            dma((2,)),
            dma((2,)),
            dma((14,)),
            dma((6,)),
            dma((6,)),
        ],
        compiler_params=pltpu.CompilerParams(
            collective_id=collective_id, has_side_effects=True, vmem_limit_bytes=60 << 20
        ),
        name="forward_pass",
    )(*operands)


SLOTS = 2 * RING + 4


def backward_plan():
    return tile_plan((4 * head_tiles() + 3 * unit_tiles()) * LANES)


def gradient_tile(route, tile):
    heads, units = head_tiles(), unit_tiles()
    shrink_steps, late = units // 2 - 1, units // 4
    outward, up = 3 * heads, 4 * heads
    gate, shrink = up + units, up + 2 * units
    if route < 2:
        unit = tile - shrink_steps + late
        last = tile - shrink_steps - (units - late)
        return jnp.where(
            tile < shrink_steps,
            shrink + 2 * tile + 2 + route,
            jnp.where(
                last < 0,
                (up, gate)[route] + unit,
                jnp.where(last < 2, outward + 2 * last + route, 2 * (last - 2) + route),
            ),
        )
    of_unit = (up, gate)[route - 2] + tile - 1
    if route == 2:
        last = jnp.where(tile == late + 1, outward + heads - 1, outward - 2)
    else:
        last = jnp.where(tile == late + 1, outward - 3, outward - 1)
    return jnp.where(tile == 0, shrink + route - 2, jnp.where(tile <= late, of_unit, last))


def slot_of(route, tile):
    if route < 2:
        return route * RING + tile % RING
    return 2 * RING + (route - 2) * 2 + tile % 2


def ring_of(route):
    return RING if route < 2 else 2


def backward_kernel(plan, fused, *refs):
    if fused:
        extra = (refs[21:33], refs[37], *refs[-9:])
        refs = (*refs[:21], *refs[33:37], *refs[38:-9])
    else:
        extra = None
    backward_steps(plan, extra, *refs)


def backward_steps(
    plan,
    extra,
    copies,
    d_shrunk,
    d_shrunk_turned,
    first_turned,
    tokens_turned,
    hidden,
    proj,
    raw,
    mixed,
    d_two,
    h_attn,
    first,
    tokens_in,
    factors,
    alphas,
    scales,
    gains,
    alpha_mlp_grad,
    bias,
    place_row,
    output,
    input_grad,
    block_output,
    grads,
    vectors,
    work,
    arrived,
    lefts,
    d_low,
    d_proj,
    first_part,
    core_in,
    stage_hidden,
    stage_rows,
    wide,
    outward,
    right,
    sum_k,
    sum_v,
    alpha_grad,
    unit_grad,
    query_grad,
    vector_sums,
    vector_in,
    send_sem,
    recv_sem,
    load_sem,
    unit_sem,
    raw_sem,
    result_sem,
    core_send,
    core_recv,
    vector_send,
    vector_recv,
):
    me = lax.axis_index("dp")
    core = lax.axis_index("tensor")
    inv_root = D ** (-0.5)
    rows = tokens_in.shape[0]
    own_rows = rows // 2
    own_at = pl.multiple_of(core * own_rows, own_rows)
    other_at = pl.multiple_of((1 - core) * own_rows, own_rows)
    heads = head_tiles()
    units = unit_tiles()
    block = D // 16
    unit_steps = units // 2
    shrink_steps = unit_steps - 1
    late_units = units // 4
    expand_steps = units - late_units
    attention_at = shrink_steps + expand_steps
    rare_units = 1 + late_units
    exchange_at = unit_steps
    attend_at = exchange_at + 3
    sequences = bias.shape[0]
    length = bias.shape[1]
    head_pairs = sequences * heads

    greeted = greet_start(me, core, diagonal=extra is not None)

    def copy(source, target, sem):
        return pltpu.make_async_copy(source, target, sem)

    def chunks(total, size, body):
        def one(k, _):
            body(pl.ds(pl.multiple_of(k * size, size), size))
            return 0

        lax.fori_loop(0, total // size, one, 0)


    def piece(hop, route, tile):
        axis = ROUTES[route][3 - hop]
        slot = slot_of(route, tile)
        return pltpu.make_async_remote_copy(
            src_ref=work[hop].at[slot, 1],
            dst_ref=arrived[hop].at[slot],
            send_sem=send_sem.at[hop, slot],
            recv_sem=recv_sem.at[hop, slot],
            device_id={"dp": partner_of(me, PLACES[axis])},
            device_id_type=pl.DeviceIdType.MESH,
        )

    def free(hop, route, tile):
        @pl.when(tile >= ring_of(route))
        def _():
            piece(hop, route, tile - ring_of(route)).wait_send()

    def add(hop, route, tile):
        piece(hop - 1, route, tile).wait_recv()
        slot = slot_of(route, tile)
        total = work[hop - 1][slot, 0].astype(F32) + arrived[hop - 1][slot].astype(F32)
        if hop == 4:
            place = gradient_tile(route, tile)
            grads[:, pl.ds(pl.multiple_of(place * LANES, LANES), LANES)] = total
            return
        half = total.shape[0] // 2
        free(hop, route, tile)
        work[hop][slot, 0] = total[:half].astype(BF16)
        work[hop][slot, 1] = total[half:].astype(BF16)
        piece(hop, route, tile).start()

    def keep_quarter(route, slot, quarter, part):
        axes = ROUTES[route][::-1]
        if route < 2:
            bits = [quarter >> 1, quarter & 1]
            at = bits[axes[1]] * 4 * block
            work[0][slot, bits[axes[0]], at : at + 4 * block, :] = part
            return
        for low in range(4):
            bits = [quarter >> 1, quarter & 1, low >> 1, low & 1]
            index = bits[axes[1]] * 4 + bits[axes[2]] * 2 + bits[axes[3]]
            work[0][slot, bits[axes[0]], index * block : (index + 1) * block, :] = part[
                low * block : (low + 1) * block
            ]

    def quarter_rows(quarter):
        return slice(quarter * 4 * block, (quarter + 1) * 4 * block)

    def often_product(tile):
        for route in (0, 1):
            free(0, route, tile)
        is_shrink = tile < shrink_steps
        is_expand = (tile >= shrink_steps) & (tile < attention_at)
        late = tile - attention_at
        is_outward = (late >= 0) & (late < 2)

        @pl.when(is_shrink)
        def _():
            right[0] = stage_hidden[tile % 2]

        @pl.when(is_expand)
        def _():
            unit = tile - shrink_steps + late_units
            right[0] = d_proj[:, pl.ds(pl.multiple_of(unit * 2 * LANES, 2 * LANES), 2 * LANES)]

        @pl.when(late >= 0)
        def _():
            first_tile = jnp.where(late < 2, 2 * late, 2 * late + 1)
            right[0] = wide[:rows, pl.ds(pl.multiple_of(first_tile * LANES, LANES), 2 * LANES)]

        which = jnp.where(is_expand | is_outward, 1, 0)
        scale = jnp.where(is_shrink | is_outward, 1.0, inv_root)
        product = (nn(lefts[which], right[0]) * scale).astype(BF16)
        for quarter in range(4):
            part = product[quarter_rows(quarter)]
            for route in (0, 1):
                keep_quarter(
                    route, slot_of(route, tile), quarter, part[:, route * LANES : (route + 1) * LANES]
                )
        for route in (0, 1):
            piece(0, route, tile).start()

    def rare_product(route, tile):
        late = tile - rare_units
        at = (route - 2) * LANES
        lanes = slice(at, at + LANES)

        @pl.when(tile == 0)
        def _():
            right[1, :, lanes] = stage_hidden[2, :, lanes]

        @pl.when((tile > 0) & (late < 0))
        def _():
            unit_lane = pl.multiple_of((tile - 1) * 2 * LANES + at, LANES)
            right[1, :, lanes] = d_proj[:, pl.ds(unit_lane, LANES)]

        @pl.when(late >= 0)
        def _():
            if route == 2:
                place = jnp.where(late == 0, heads - 1, heads + 13)
            else:
                place = heads + 12 + 2 * late
            right[1, :, lanes] = wide[:rows, pl.ds(pl.multiple_of(place * LANES, LANES), LANES)]

        free(0, route, tile)
        of_units = (tile > 0) & (late < 0)
        of_outward = (late == 0) if route == 2 else (late < -rare_units)
        which = jnp.where(of_units | of_outward, 1, 0)
        scale = jnp.where((tile == 0) | of_outward, 1.0, inv_root)
        product = (nn(lefts[which], right[1, :, lanes]) * scale).astype(BF16)
        for quarter in range(4):
            keep_quarter(route, slot_of(route, tile), quarter, product[quarter_rows(quarter)])
        piece(0, route, tile).start()


    def unit_copies(pair):
        slot = pair % 2
        unit = 2 * pair
        at = pl.multiple_of(slot * 6 * LANES, 2 * LANES)
        result = [
            (
                copies.at[:, pl.ds(pl.multiple_of(pair_tile(unit) * LANES, LANES), 4 * LANES)],
                wide.at[:, pl.ds(at, 4 * LANES)],
            )
        ]
        for k in range(2):
            tile = shrink_tile(unit + k)
            result.append(
                (
                    copies.at[:, pl.ds(pl.multiple_of(tile * LANES, LANES), LANES)],
                    wide.at[:, pl.ds(pl.multiple_of(at + (4 + k) * LANES, LANES), LANES)],
                )
            )
        lanes = pl.ds(pl.multiple_of(pair * 4 * LANES, 4 * LANES), 4 * LANES)
        for k in range(2):
            result.append(
                (
                    proj.at[pl.ds(k * own_rows, own_rows), lanes],
                    stage_rows.at[slot, :, pl.ds(k * 4 * LANES, 4 * LANES)],
                )
            )
        return [copy(source, target, unit_sem.at[k, slot]) for k, (source, target) in enumerate(result)]

    def hidden_copy(tile):
        lanes = pl.ds(pl.multiple_of((2 * tile + 2) * LANES, 2 * LANES), 2 * LANES)
        return copy(hidden.at[:, lanes], stage_hidden.at[tile % 2], unit_sem.at[5, tile % 2])

    def unit_pair(pair):
        slot = pair % 2
        for part in unit_copies(pair):
            part.wait()
        at_lane = pl.multiple_of(slot * 6 * LANES, 2 * LANES)
        down = wide[:, pl.ds(pl.multiple_of(at_lane + 4 * LANES, 2 * LANES), 2 * LANES)]

        for half in range(2):
            at = slice(half * own_rows, (half + 1) * own_rows)
            proj_lanes = half * 4 * LANES
            d_hidden = nn(d_low[at, :], down)
            for k in range(2):
                lanes = pl.ds(pl.multiple_of((2 * pair + k) * LANES, LANES), LANES)
                gain_up, gain_gate = gains[0:1, lanes], gains[1:2, lanes]
                start = proj_lanes + 2 * k * LANES
                proj_up = stage_rows[slot, :, start : start + LANES]
                proj_gate = stage_rows[slot, :, start + LANES : start + 2 * LANES]
                upstream = d_hidden[:, k * LANES : (k + 1) * LANES]
                gate = gain_gate * proj_gate
                sigmoid = jax.nn.sigmoid(gate)
                d_up = upstream * (gate * sigmoid)
                d_gate = upstream * (gain_up * proj_up) * sigmoid * (1.0 + gate * (1.0 - sigmoid))
                unit_grad[0:1, lanes] += jnp.sum(d_up * proj_up, axis=0, keepdims=True)
                unit_grad[1:2, lanes] += jnp.sum(d_gate * proj_gate, axis=0, keepdims=True)
                place = pl.multiple_of((2 * pair + k) * 2 * LANES, 2 * LANES)
                d_proj[at, pl.ds(place, LANES)] = (d_up * gain_up).astype(BF16)
                d_proj[at, pl.ds(pl.multiple_of(place + LANES, LANES), LANES)] = (
                    d_gate * gain_gate
                ).astype(BF16)
        expand_at = pl.ds(at_lane, 4 * LANES)
        lanes = pl.ds(pl.multiple_of(pair * 4 * LANES, 4 * LANES), 4 * LANES)
        upstream = d_proj[:, lanes]
        for k in range(D // 256):
            columns = slice(k * 256, (k + 1) * 256)
            first_part[:, columns] += nt(upstream, wide[columns, expand_at])


    def core_copy(source, target, which):
        return pltpu.make_async_remote_copy(
            src_ref=source,
            dst_ref=target,
            send_sem=core_send.at[which],
            recv_sem=core_recv.at[which],
            device_id={"tensor": 1 - core},
            device_id_type=pl.DeviceIdType.MESH,
        )

    def part_copy():
        return core_copy(first_part.at[pl.ds(other_at, own_rows)], core_in, 0)

    def branch_copy():
        own = d_low.at[pl.ds(own_at, own_rows)]
        return core_copy(own, own, 1)

    tokens_place = wide.at[pl.ds(0, own_rows), pl.ds(D, D)]
    rare, rarer = forward_plan()[2][0], forward_plan()[3][0]
    outward_tiles = ((rare + 1, 1, 0), (rarer + 1, 1, 1), (3 * heads - 1, 2, 2), (rare + 2, 1, 4))

    def load(k):
        if k == 0:
            return copy(d_two, stage_rows.at[0], load_sem.at[0])
        if k == 1:
            return copy(h_attn, stage_rows.at[1], load_sem.at[1])
        if k == 2:
            return copy(tokens_in.at[pl.ds(own_at, own_rows)], tokens_place, load_sem.at[2])
        if k == 3:
            return copy(
                mixed, wide.at[pl.ds(0, rows), pl.ds(0, heads * LANES)], load_sem.at[3]
            )
        if k == 4:
            return copy(first, first_part.at[pl.ds(other_at, own_rows)], load_sem.at[4])
        if k == 5:
            return copy(d_shrunk, d_low, load_sem.at[5])
        if k == 6:
            return copy(d_shrunk_turned, lefts.at[0], load_sem.at[6])
        if k == 7:
            return copy(first_turned, lefts.at[1], load_sem.at[7])
        if k == 8:
            return copy(tokens_turned, lefts.at[0], load_sem.at[8])
        if k == 9:
            return copy(hidden.at[:, pl.ds(0, 2 * LANES)], stage_hidden.at[2], load_sem.at[9])
        tile, width, at = outward_tiles[k - 10]
        return copy(
            copies.at[:, pl.ds(tile * LANES, width * LANES)],
            outward.at[:, pl.ds(at * LANES, width * LANES)],
            load_sem.at[k],
        )

    def branch_gradient():
        part_copy().wait_send()
        load(4).start()
        part_copy().wait_recv()
        for k in (0, 1, 2, 4):
            load(k).wait()
        alpha_attn, alpha_mlp = alphas[0:1, :], alphas[1:2, :]

        def some(at):
            here = pl.ds(pl.multiple_of(own_at + at.start, 64), 64)
            there = pl.ds(pl.multiple_of(other_at + at.start, 64), 64)
            part = (first_part[here, :] + core_in[at, :]) * inv_root
            d_first = (1.0 - alpha_mlp) * stage_rows[0, at, :] + part
            normed = stage_rows[1, at, :]
            d_one = row_norm_back(
                d_first, first_part[there, :], factors[at, LANES : LANES + 1]
            )
            inputs = wide[at, D : 2 * D].astype(F32)
            alpha_grad[0:1, :] += jnp.sum(d_one * (normed - inputs), axis=0, keepdims=True)
            stage_rows[0, at, :] = d_one
            d_low[here, :] = row_norm_back(alpha_attn * d_one, normed, factors[at, 0:1]).astype(
                BF16
            )

        chunks(own_rows, 64, some)
        branch_copy().start()


    def raw_copies(number):
        sequence, head = number // heads, number % heads
        at = pl.ds(pl.multiple_of(sequence * length, length), length)
        slot = number % 2
        target_rows = pl.ds(pl.multiple_of(slot * own_rows, own_rows), length)
        return [
            copy(
                raw.at[at, pl.ds(pl.multiple_of((k * heads + head) * LANES, LANES), LANES)],
                first_part.at[target_rows, pl.ds(k * LANES, LANES)],
                raw_sem.at[k, slot],
            )
            for k in range(3)
        ]

    def attend_one(number):
        sequence, head = number // heads, number % heads
        for part in raw_copies(number):
            part.wait()
        at = pl.ds(pl.multiple_of(sequence * length, length), length)
        source_rows = pl.ds(pl.multiple_of((number % 2) * own_rows, own_rows), length)
        head_lanes = pl.ds(pl.multiple_of(head * LANES, LANES), LANES)
        gain_lanes = pl.ds(pl.multiple_of((core * heads + head) * LANES, LANES), LANES)
        d_mixed = nn(d_low[at, :], outward[:, head_lanes]).astype(BF16)
        targets = [
            wide.at[at, pl.ds(pl.multiple_of(((k + 1) * heads + head) * LANES, LANES), LANES)]
            for k in range(3)
        ]
        total = attend_pair_back(
            *[first_part.at[source_rows, pl.ds(k * LANES, LANES)] for k in range(3)],
            d_mixed,
            scales[2:3, gain_lanes],
            bias.at[sequence],
            *targets,
            sum_k,
            sum_v,
        )
        query_grad[0:1, head_lanes] += total


    head_lanes = 3 * heads * LANES
    beyond = D - rows

    def inward_copies():
        first_lanes = (3 * heads - 1) * LANES
        result = []
        for row, number, at, lane in ((0, rows, 0, 0), (rows, beyond, 0, head_lanes)):
            for source, width in ((0, first_lanes), (rare * LANES, LANES)):
                offset = 0 if width == first_lanes else first_lanes
                result.append(
                    (
                        copies.at[pl.ds(row, number), pl.ds(source, width)],
                        d_proj.at[pl.ds(at, number), pl.ds(lane + offset, width)],
                    )
                )
        return [copy(source, target, load_sem.at[14 + k]) for k, (source, target) in enumerate(result)]

    order_lane = 2 * head_lanes

    def make_order():
        natural = natural_row(place_row, me)

        def fill(at):
            here = lax.broadcasted_iota(jnp.int32, (LANES, D), 0) + at.start
            d_proj[at, order_lane : order_lane + D] = jnp.where(here == natural, 1.0, 0.0).astype(
                BF16
            )

        chunks(rows, LANES, fill)
        for k in range(beyond // LANES):
            here = lax.broadcasted_iota(jnp.int32, (LANES, D), 0) + rows + k * LANES
            at = slice(beyond + k * LANES, beyond + (k + 1) * LANES)
            d_proj[at, head_lanes : head_lanes + D] = jnp.where(here == natural, 1.0, 0.0).astype(
                BF16
            )

    def natural_parts(values):
        low = nt(values, d_proj[:, order_lane : order_lane + D])
        high = nt(values, d_proj[beyond : 2 * beyond, head_lanes : head_lanes + D])
        return low, high

    def input_part(number):
        at = pl.ds(pl.multiple_of(number * 256, 256), 256)
        upstream = wide[at, heads * LANES : 4 * heads * LANES]
        low = nt(upstream, d_proj[:, :head_lanes]) * inv_root
        d_low[at, :rows] = low.astype(BF16)
        high = nt(upstream, d_proj[:beyond, head_lanes : 2 * head_lanes]) * inv_root
        d_low[at, rows:] = high.astype(BF16)
        low, high = natural_parts(d_low[at, :])
        first_part[at, :rows] = low
        first_part[at, rows:] = high

    def residual_part():
        alpha_attn = alphas[0:1, :]

        def some(at):
            here = pl.ds(pl.multiple_of(own_at + at.start, 128), 128)
            residual = (1.0 - alpha_attn) * stage_rows[0, at, :]
            top = residual.astype(BF16)
            rest = (residual - top.astype(F32)).astype(BF16)
            for part in (top, rest):
                low, high = natural_parts(part)
                first_part[here, :rows] += low
                first_part[here, rows:] += high

        chunks(own_rows, 128, some)

    half_width = D // 2

    def input_copies():
        lanes = pl.ds(pl.multiple_of((1 - core) * half_width, LANES), half_width)
        return [
            core_copy(
                first_part.at[pl.ds(k * own_rows, own_rows), lanes],
                core_in.at[:, pl.ds(k * half_width, half_width)],
                2 + k,
            )
            for k in range(2)
        ]

    def input_copy(k):
        lanes = pl.ds(pl.multiple_of(core * half_width, LANES), half_width)
        at = pl.ds(k * own_rows, own_rows)
        return copy(first_part.at[at, lanes], input_grad.at[at], result_sem.at[k])

    def input_sum():
        lanes = pl.ds(pl.multiple_of(core * half_width, LANES), half_width)
        for k, part in enumerate(input_copies()):
            part.wait()
            at = pl.ds(k * own_rows, own_rows)
            first_part[at, lanes] += core_in[:, k * half_width : (k + 1) * half_width]
            input_copy(k).start()

    def output_load():
        return copy(output, d_low.at[pl.ds(other_at, own_rows)], load_sem.at[18])

    def output_order():
        output_load().wait()
        for k in range(own_rows // 256):
            source = pl.ds(pl.multiple_of(other_at + k * 256, 256), 256)
            target = pl.ds(pl.multiple_of(own_at + k * 256, 256), 256)
            low, high = natural_parts(d_low[source, :])
            d_low[target, :rows] = low.astype(BF16)
            d_low[target, rows:] = high.astype(BF16)
        output_copies()[0].start()
        output_copies()[1].start()

    def output_copies():
        own = pl.ds(own_at, own_rows)
        return (
            core_copy(d_low.at[own], block_output.at[own], 4),
            copy(d_low.at[own], block_output.at[own], result_sem.at[2]),
        )

    def vector_copy(k):
        if k == 0:
            device = {"tensor": 1 - core}
        else:
            device = {"dp": partner_of(me, PLACES[k - 1])}
        return pltpu.make_async_remote_copy(
            src_ref=vector_sums.at[k],
            dst_ref=vector_in.at[k],
            send_sem=vector_send.at[k],
            recv_sem=vector_recv.at[k],
            device_id=device,
            device_id_type=pl.DeviceIdType.MESH,
        )

    def vectors_start():
        alpha_grad[1:2, :] = alpha_mlp_grad[0:1, :]
        vector_sums[0] = jnp.zeros_like(vector_sums[0])
        values = alpha_grad[...]
        for _ in range(3):
            part = values.astype(BF16)
            low, high = natural_parts(part)
            vector_sums[0, :8, :rows] += low
            vector_sums[0, :8, rows:] += high
            values = values - part.astype(F32)
        vector_sums[0, 2:3, pl.ds(pl.multiple_of(core * heads * LANES, LANES), heads * LANES)] = (
            query_grad[0:1, :]
        )
        each = units * LANES // D
        for row in range(2):
            for k in range(2 * each):
                here = unit_grad[row : row + 1, (k % each) * D : (k % each + 1) * D]
                at = 3 + 2 * each * row + k
                vector_sums[0, at : at + 1, :] = jnp.where(core == k // each, here, 0.0)
        vector_copy(0).start()

    def vectors_add(k):
        vector_copy(k).wait()
        total = vector_sums[k] + vector_in[k]
        if k < len(PLACES):
            vector_sums[k + 1] = total
            vector_copy(k + 1).start()
        else:
            vectors[...] = total

    input_at = attention_at + 1
    parts = rows // 256


    squares_at = input_at + parts + 3
    if extra is not None:
        states, squares, *scratch = extra
        early, last, state_sem = scratch[:4], scratch[4:8], scratch[8]

    def state_loads():
        pairs = []
        for start, width, which, place, _, _ in update_pieces():
            for offset in range(0, width, D):
                part = min(width, D)
                number, lane = (start + offset) // D, (start + offset) % D
                source_lanes, lanes = pl.ds(offset, part), pl.ds(lane, part)
                at = pl.ds(number * block, block)
                targets = (
                    first_part.at[at, lanes],
                    wide.at[at, lanes],
                    stage_rows.at[number // 4, pl.ds(number % 4 * block, block), lanes],
                )
                for state, target in zip(states[3 * which : 3 * which + 3], targets):
                    if place is None:
                        source = state.at[:, source_lanes]
                    else:
                        source = state.at[place, :, source_lanes]
                    pairs.append((source, target))
        return [copy(source, target, state_sem.at[k]) for k, (source, target) in enumerate(pairs)]

    def square_row(target, row, first_tile, begin=0, end=units):
        def one(k, _):
            tile = first_tile + k
            number = tile // (D // LANES)
            lanes = pl.ds(pl.multiple_of(tile % (D // LANES) * LANES, LANES), LANES)
            at = pl.ds(pl.multiple_of(number * block, block), block)
            there = pl.ds(pl.multiple_of(number % 4 * block, block), block)
            pre = adam_step(
                first_part[at, lanes],
                wide[at, lanes],
                stage_rows[number // 4, there, lanes],
                grads[:, pl.ds(pl.multiple_of(tile * LANES, LANES), LANES)],
                RATE_MATRIX,
            )[0]
            here = pl.ds(pl.multiple_of(k * LANES, LANES), LANES)
            target[0, row : row + 1, here] = jnp.sum(pre * pre, axis=0, keepdims=True)
            return 0

        lax.fori_loop(begin, end, one, 0)

    def early_squares(index):
        @pl.when(index == squares_at)
        def _():
            early[0][...] = jnp.zeros_like(early[0])
            for k in range(2):
                input_copy(k).wait()
            for load in state_loads():
                load.start()

        @pl.when(index == squares_at + 2)
        def _():
            for load in state_loads():
                load.wait()

        for row in range(3):

            @pl.when(index == squares_at + 2 + row)
            def _(row=row):
                square_row(early[0], row, 4 * heads + row * units)

        @pl.when(index == squares_at + 4)
        def _():
            round_start(me, 0, *early)

        for number, ranges in enumerate((((0, 6), (12, 14), (15, units)), ((6, 10), (14, 15)))):

            @pl.when(index == squares_at + 5 + number)
            def _(ranges=ranges):
                for begin, end in ranges:
                    square_row(last[0], 0, 0, begin, end)

        for number in range(len(ROUNDS)):

            @pl.when(index == squares_at + 5 + number)
            def _(number=number):
                total = round_sum(me, number, *early)
                if number + 1 < len(ROUNDS):
                    early[0][number + 1] = total
                    round_start(me, number + 1, *early)
                else:
                    squares[1:4, :] = total[:3]

    def last_squares():
        square_row(last[0], 0, 0, 10, 12)
        for number in range(len(ROUNDS)):
            round_start(me, number, *last)
            total = round_sum(me, number, *last)
            if number + 1 < len(ROUNDS):
                last[0][number + 1] = total
            else:
                squares[0:1, :] = total


    load(6).start()
    hidden_copy(0).start()
    for k in (9, 5):
        load(k).start()
    for part in unit_copies(0):
        part.start()
    load(7).start()
    alpha_grad[...] = jnp.zeros_like(alpha_grad)
    unit_grad[...] = jnp.zeros_like(unit_grad)
    query_grad[...] = jnp.zeros_like(query_grad)
    first_part[...] = jnp.zeros_like(first_part)
    load(6).wait()
    greet_wait(greeted)

    def step(index, _):
        for hop in range(4, 0, -1):
            for_tiles(index, hop, plan, functools.partial(add, hop))

        @pl.when(index < shrink_steps)
        def _():
            hidden_copy(index).wait()

        @pl.when(index == attention_at)
        def _():
            load(8).wait()
            chunks(rows, LANES, turn)

        @pl.when(index < plan[0][2])
        def _():
            often_product(index)

        @pl.when(index == 0)
        def _():
            for k in (9, 5):
                load(k).wait()

        @pl.when(index == EVERY - 1)
        def _():
            load(7).wait()

        for route in (2, 3):
            number, start = plan[route][2], plan[route][4]
            due = index - start

            @pl.when((due % EVERY == 0) & (due >= 0) & (due < number * EVERY))
            def _(route=route, due=due):
                rare_product(route, due // EVERY)

        @pl.when(index + 1 < shrink_steps)
        def _():
            hidden_copy(index + 1).start()

        @pl.when(index + 1 < unit_steps)
        def _():
            for part in unit_copies(index + 1):
                part.start()

        @pl.when(index < unit_steps)
        def _():
            unit_pair(index)

        @pl.when(index == exchange_at)
        def _():
            part_copy().start()
            for k in (0, 1, 2, 3, 8, 10, 11, 12, 13):
                load(k).start()

        @pl.when(index == exchange_at + 1)
        def _():
            branch_gradient()

        @pl.when(index == exchange_at + 2)
        def _():
            branch_copy().wait()
            for k in (3, 10, 11, 12, 13):
                load(k).wait()

        number = index - attend_at

        @pl.when((number >= -1) & (number < head_pairs - 1))
        def _():
            for part in raw_copies(number + 1):
                part.start()

        @pl.when((number >= 0) & (number < head_pairs))
        def _():
            attend_one(number)

        @pl.when(index == attention_at)
        def _():
            for part in inward_copies():
                part.start()
            make_order()
            vectors_start()

        for k in range(len(PLACES) + 1):

            @pl.when(index == attention_at + 1 + k)
            def _(k=k):
                vectors_add(k)

        @pl.when(index == input_at)
        def _():
            for part in inward_copies():
                part.wait()

        @pl.when((index >= input_at) & (index < input_at + parts))
        def _():
            input_part(index - input_at)

        @pl.when(index == input_at + parts)
        def _():
            output_load().start()
            residual_part()
            for part in input_copies():
                part.start()

        @pl.when(index == input_at + parts + 1)
        def _():
            output_order()

        @pl.when(index == input_at + parts + 2)
        def _():
            input_sum()

        if extra is not None:
            early_squares(index)
        return 0

    def turn(at):
        lefts[1, :, at] = d_low[at, :].astype(F32).T.astype(BF16)

    lax.fori_loop(0, steps_of(plan, 4), step, 0)
    if extra is not None:
        last_squares()
    for part in output_copies():
        part.wait()
    if extra is None:
        for k in range(2):
            input_copy(k).wait()
    for route, (_, _, number, _, _) in enumerate(plan):
        for tile in range(max(0, number - ring_of(route)), number):
            for hop in range(4):
                piece(hop, route, tile).wait_send()


def backward_pass(*operands, states, collective_id):
    fused = len(states) > 0
    plan = backward_plan()
    copies = operands[0]
    count = operands[1].shape[0]
    own = count // 2
    heads = head_tiles() * LANES
    units = unit_tiles() * LANES
    length = operands[18].shape[1]
    block = D // 16
    halves = [block * 8 >> hop for hop in range(4)]
    hbm = pl.BlockSpec(memory_space=pl.ANY)
    vmem = pl.BlockSpec(memory_space=pltpu.VMEM)
    dma = pltpu.SemaphoreType.DMA
    round_scratch = []
    for height in (SQUARE_ROWS, 1):
        round_scratch += [
            pltpu.VMEM((3, height, units), F32),
            pltpu.VMEM((3, 3, height, units), F32),
            dma((3, 3)),
            dma((3, 3)),
        ]
    round_scratch.append(dma((30,)))
    return pl.pallas_call(
        functools.partial(backward_kernel, plan, fused),
        out_shape=[
            jax.ShapeDtypeStruct((count, D // 2), F32),
            jax.ShapeDtypeStruct((count, D), BF16),
            jax.ShapeDtypeStruct((block, 4 * heads + 3 * units), F32),
            jax.ShapeDtypeStruct((16, D), F32),
        ]
        + [jax.ShapeDtypeStruct((SQUARE_ROWS, units), F32)] * fused,
        in_specs=[hbm] * 13 + [vmem] * 7 + [hbm] + [hbm] * len(states),
        out_specs=[hbm] * 2 + [vmem] * (2 + fused),
        scratch_shapes=[
            [pltpu.VMEM((SLOTS, 2, half, LANES), BF16) for half in halves],
            [pltpu.VMEM((SLOTS, half, LANES), BF16) for half in halves],
            pltpu.VMEM((2, D, count), BF16),
            pltpu.VMEM((count, D), BF16),
            pltpu.VMEM((count, 2 * units), BF16),
            pltpu.VMEM((count, D), F32),
            pltpu.VMEM((own, D), F32),
            pltpu.VMEM((3, count, 2 * LANES), BF16),
            pltpu.VMEM((2, own, D), F32),
            pltpu.VMEM((D, 4 * heads), BF16),
            pltpu.VMEM((D, heads), BF16),
            pltpu.VMEM((2, count, 2 * LANES), BF16),
            pltpu.VMEM((length, LANES), F32),
            pltpu.VMEM((length, LANES), F32),
            pltpu.VMEM((8, D), F32),
            pltpu.VMEM((8, units), F32),
            pltpu.VMEM((8, heads), F32),
            pltpu.VMEM((5, 16, D), F32),
            pltpu.VMEM((5, 16, D), F32),
            dma((4, SLOTS)),
            dma((4, SLOTS)),
            dma((19,)),
            dma((6, 2)),
            dma((3, 2)),
            dma((3,)),
            dma((5,)),
            dma((5,)),
            dma((5,)),
            dma((5,)),
        ]
        + round_scratch * fused,
        compiler_params=pltpu.CompilerParams(
            collective_id=collective_id, has_side_effects=True, vmem_limit_bytes=62 << 20
        ),
        name="backward_pass",
    )(*operands, *states)


SQUARE_ROWS = 4


def update_pieces():
    heads, units = head_tiles() * LANES, unit_tiles() * LANES
    pieces = [(k * heads, heads, 0, k, 0, k * heads) for k in range(3)]
    pieces.append((3 * heads, heads, 1, None, 0, 3 * heads))
    pieces += [(4 * heads + k * units, units, 2, k, 1 + k, 0) for k in range(2)]
    pieces.append((4 * heads + 2 * units, units, 3, None, 3, 0))
    return pieces


def update_loads(grads, states, held_grads, held_states, sem):
    pairs = []
    ends = {0: 0, 1: 3, 2: 4, 3: 6}
    sizes = {0: 3, 1: 1, 2: 2, 3: 1}
    pieces = update_pieces()
    for which in range(4):
        start, width = pieces[ends[which]][:2]
        lanes = pl.ds(start, width * sizes[which])
        pairs.append((grads.at[:, lanes], held_grads.at[:, lanes]))
        pairs += list(zip(states[3 * which : 3 * which + 3], held_states[3 * which : 3 * which + 3]))
    return [pltpu.make_async_copy(source, target, sem.at[k]) for k, (source, target) in enumerate(pairs)]


def for_update_tiles(loads, held_grads, held_states, body, after=None):
    waited = -1
    for piece in update_pieces():
        start, width, which, block, _, _ = piece
        if which != waited:
            for load in loads[4 * which : 4 * which + 4]:
                load.wait()
            waited = which

        def one(k, _, start=start, which=which, block=block, piece=piece):
            lane = pl.multiple_of(k * LANES, LANES)
            here = pl.ds(lane, LANES)
            values = [
                ref[:, here] if block is None else ref[block, :, here]
                for ref in held_states[3 * which : 3 * which + 3]
            ]
            gradient = held_grads[:, pl.ds(pl.multiple_of(start + lane, LANES), LANES)]
            body(piece, lane, gradient, *values)
            return 0

        lax.fori_loop(0, width // LANES, one, 0)
        if after is not None and block in (None, (2, 0, 1, 0)[which]):
            after(which)


def squares_kernel(*refs):
    grads, states, total, held_grads, held_states = refs[0], refs[1:13], refs[13], refs[14], refs[15]
    sums, arrived, load_sem, send_sem, recv_sem = refs[16:]
    loads = update_loads(grads, states, held_grads, held_states, load_sem)
    for load in loads:
        load.start()
    me = lax.axis_index("dp")
    low, high = PLACES[:2]
    hops = [[(low,), (high,), (low, high)], *[[(bit,)] for bit in PLACES[2:]]]

    def partner(bits):
        device = me
        for bit in bits:
            device = device + partner_of(me, bit) - me
        return {"dp": device}

    barrier = pltpu.get_barrier_semaphore()
    for hop in hops:
        for bits in hop:
            pl.semaphore_signal(
                barrier, inc=1, device_id=partner(bits), device_id_type=pl.DeviceIdType.MESH
            )
    pl.semaphore_wait(barrier, sum(len(hop) for hop in hops))

    def body(piece, lane, gradient, master, first, second):
        pre = adam_step(master, first, second, gradient, RATE_MATRIX)[0]
        row, start = piece[4:]
        lanes = pl.ds(pl.multiple_of(start + lane, LANES), LANES)
        sums[0, row : row + 1, lanes] = jnp.sum(pre * pre, axis=0, keepdims=True)

    for_update_tiles(loads, held_grads, held_states, body)
    for number, hop in enumerate(hops):
        copies = [
            pltpu.make_async_remote_copy(
                src_ref=sums.at[number],
                dst_ref=arrived.at[number, k],
                send_sem=send_sem.at[number, k],
                recv_sem=recv_sem.at[number, k],
                device_id=partner(bits),
                device_id_type=pl.DeviceIdType.MESH,
            )
            for k, bits in enumerate(hop)
        ]
        for copy in copies:
            copy.start()
        for copy in copies:
            copy.wait()
        if len(hop) == 3:
            result = (sums[number] + arrived[number, 0]) + (
                arrived[number, 1] + arrived[number, 2]
            )
        else:
            result = sums[number] + arrived[number, 0]
        if number + 1 < len(hops):
            sums[number + 1] = result
        else:
            total[...] = result


def update_kernel(*refs):
    grads, states, squares, small, outputs = refs[0], refs[1:13], refs[13], refs[14:21], refs[21:39]
    held_grads, held_states, held_results, load_sem, store_sem = refs[39:]
    results, small_results = outputs[:12], outputs[12:]
    loads = update_loads(grads, states, held_grads, held_states, load_sem)
    for load in loads:
        load.start()

    def store(k):
        return pltpu.make_async_copy(held_results[k], results[k], store_sem.at[k])

    for k, rate in enumerate((RATE_ALPHA, RATE_SCALE)):
        master, first, second = [ref[...] for ref in small[3 * k + 1 : 3 * k + 4]]
        gradient = small[0][...][2 * k : 2 * k + master.shape[0]]
        updated, variance = adam_step(master, first, second, gradient, rate)
        for target, value in zip(small_results[3 * k : 3 * k + 3], (gradient, variance, updated)):
            target[...] = value

    def body(piece, lane, gradient, master, first, second):
        _, _, which, block, row, start = piece
        pre, variance = adam_step(master, first, second, gradient, RATE_MATRIX)
        lanes = pl.ds(pl.multiple_of(start + lane, LANES), LANES)
        factor = lax.rsqrt(squares[row : row + 1, lanes] / D + EPS_NORM)
        here = pl.ds(lane, LANES)
        for target, value in zip(
            held_results[3 * which : 3 * which + 3], (gradient, variance, pre * factor)
        ):
            if block is None:
                target[:, here] = value
            else:
                target[block, :, here] = value

    def after(which):
        for k in range(3 * which, 3 * which + 3):
            store(k).start()

    for_update_tiles(loads, held_grads, held_states, body, after)
    for k in range(12):
        store(k).wait()


def update(grads, states, small, squares, count, collective_id):
    rows = grads.shape[0]
    units = unit_tiles() * LANES
    shape = (SQUARE_ROWS, units)
    hbm = pl.BlockSpec(memory_space=pl.ANY)
    vmem = pl.BlockSpec(memory_space=pltpu.VMEM)
    dma = pltpu.SemaphoreType.DMA
    held = [pltpu.VMEM(grads.shape, F32), [pltpu.VMEM(state.shape, state.dtype) for state in states]]
    if squares is None:
        squares = pl.pallas_call(
            squares_kernel,
            out_shape=jax.ShapeDtypeStruct(shape, F32),
            in_specs=[hbm] * 13,
            out_specs=vmem,
            scratch_shapes=held
            + [
                pltpu.VMEM((3, *shape), F32),
                pltpu.VMEM((3, 3, *shape), F32),
                dma((16,)),
                dma((3, 3)),
                dma((3, 3)),
            ],
            compiler_params=pltpu.CompilerParams(
                collective_id=collective_id, has_side_effects=True, vmem_limit_bytes=60 << 20
            ),
            name="sum_squares",
        )(grads, *states)
        for bit in extra_bits(count):
            squares = squares + exchange(squares, bit, count)
    results = [
        jax.ShapeDtypeStruct(states[3 * k].shape, F32) for k in range(4) for _ in range(3)
    ]
    small_results = [
        jax.ShapeDtypeStruct(small[3 * k + 1].shape, F32) for k in range(2) for _ in range(3)
    ]
    return pl.pallas_call(
        update_kernel,
        out_shape=results + small_results,
        in_specs=[hbm] * 13 + [vmem] * 8,
        out_specs=[hbm] * 12 + [vmem] * 6,
        scratch_shapes=held
        + [[pltpu.VMEM(result.shape, F32) for result in results], dma((16,)), dma((12,))],
        compiler_params=pltpu.CompilerParams(vmem_limit_bytes=60 << 20),
        name="update",
    )(grads, *states, squares, *small)


def per_device(
    tokens,
    cotangent,
    segment_ids,
    pad_mask,
    inward_master,
    inward_first,
    inward_second,
    outward_master,
    outward_first,
    outward_second,
    expand_master,
    expand_first,
    expand_second,
    shrink_master,
    shrink_first,
    shrink_second,
    alpha_master,
    alpha_first,
    alpha_second,
    scale_master,
    scale_first,
    scale_second,
):
    count = lax.axis_size("dp")
    me = lax.axis_index("dp")
    heads_width = inward_master.shape[2]

    small = jnp.concatenate([alpha_master, scale_master], axis=0).astype(BF16)
    small = jnp.pad(small, ((0, LANES - small.shape[0]), (0, 0))).T
    masters = (
        inward_master,
        outward_master.T,
        expand_master,
        shrink_master.T,
        small,
    )
    if extra_bits(count):
        masters = [gather_rest(master.astype(BF16), count) for master in masters]
    place_row = jnp.asarray(place_rows_of(count))
    (
        copies,
        tokens_in,
        raw,
        mixed,
        h_attn,
        first,
        first_low,
        tokens_turned,
        first_turned,
        bias,
        d_two,
        output,
        d_shrunk,
        d_shrunk_turned,
        proj,
        hidden,
        factors,
        alphas,
        scale_rows,
        gains,
        alpha_mlp_grad,
    ) = forward_pass(
        *masters, tokens, cotangent, segment_ids, pad_mask, place_row, collective_id=0
    )

    states = (
        inward_master,
        inward_first,
        inward_second,
        outward_master.T,
        outward_first.T,
        outward_second.T,
        expand_master,
        expand_first,
        expand_second,
        shrink_master.T,
        shrink_first.T,
        shrink_second.T,
    )

    input_grad, block_output, grads, vectors, *squares = backward_pass(
        copies.reshape(D, -1),
        d_shrunk,
        d_shrunk_turned,
        first_turned,
        tokens_turned,
        hidden,
        proj,
        raw,
        mixed,
        d_two,
        h_attn,
        first,
        tokens_in,
        factors,
        alphas,
        scale_rows,
        gains,
        alpha_mlp_grad,
        bias,
        place_row,
        output,
        states=() if extra_bits(count) else states,
        collective_id=1,
    )
    grads = scatter_rest(grads, count)
    for bit in extra_bits(count):
        vectors = vectors + exchange(vectors, bit, count)
    width = D // count
    vectors = lax.dynamic_slice_in_dim(vectors, me * width, width, 1)

    small = (
        vectors,
        alpha_master,
        alpha_first,
        alpha_second,
        scale_master,
        scale_first,
        scale_second,
    )
    results = list(update(grads, states, small, squares[0] if squares else None, count, 2))
    for k in (*range(3, 6), *range(9, 12)):
        results[k] = results[k].T
    return block_output, input_grad, *results


def solution(mesh):
    rows = P("dp", None)
    deep = P(None, "dp", "tensor")
    flat = P("tensor", "dp")
    vector = P(None, "dp")
    in_specs = (rows,) * 4 + (deep,) * 3 + (flat,) * 3 + (deep,) * 3 + (flat,) * 3 + (vector,) * 6
    out_specs = (
        (rows, P("dp", "tensor"))
        + (deep,) * 3
        + (flat,) * 3
        + (deep,) * 3
        + (flat,) * 3
        + (vector,) * 6
    )
    return jax.shard_map(
        per_device, mesh=mesh, in_specs=in_specs, out_specs=out_specs, check_vma=False
    )
```
